32 devices in a mesh: grp: 2 (over y), wide: 16 (over z, x, core), narrow: 1.
Axes of the slice: x: 2, y: 2, z: 4, core: 2. Of those that a mesh axis runs over, the one named last changes fastest.
Arguments:
- pairwise_state: bfloat16 [256, 128, 128], P(('grp', 'wide'), 'narrow'), parts along dimension 0, may hold values from -6 to 6
- homolog_features: bfloat16 [128, 128, 256], P('grp', 'wide'), parts along dimension 0, may hold values from -6 to 6
- residue_chain_index: int32 [256], P('grp'), parts along dimension 0, may hold values from 0 to 3, as said below
- resolved_residue_mask: int32 [256], P('grp'), parts along dimension 0, may hold values 0 or 1
- alignment_mask: bfloat16 [128, 128], P('grp', 'wide'), parts along dimension 0, may hold values from 0 to 1
- relative_offset_table: bfloat16 [66, 128], replicated, may hold values from -3 to 3
- homolog_to_sides_matrix: bfloat16 [256, 64], replicated, may hold values from -0.375 to 0.375
- outer_mean_output_weight: bfloat16 [1024, 128], replicated, may hold values from -0.1875 to 0.1875
- triangle_projection_weight: bfloat16 [2, 128, 640], replicated, may hold values from -0.5 to 0.5
- triangle_output_weight: bfloat16 [2, 128, 128], replicated, may hold values from -0.5 to 0.5
Outputs:
- new_pair: bfloat16 [256, 128, 128], P(('grp', 'wide'), 'narrow'), parts along dimension 0
The draws below stay inside these ranges and needn't reach their ends.
There are 2 independent parts, one for each index of `grp`. The reference program is written for one: setup_inputs(seed, part) draws one part's arguments, and reference() takes and returns one part's arrays. A program takes and returns all parts, laid end to end along the dimension named above; an argument that names none is the same for every part. Nothing has to cross between parts.
Inputs may be any that keep to these rules, and one draw needn't show every extreme that they name: `residue_chain_index`: chain numbers never fall along the residues, so each chain is one contiguous run; the first residue is in chain 0 and the last in chain 4 - 1; some chains may be empty.
All inputs are finite; a program needn't handle non-finite values.
Results may differ from the reference program's by a relative error of at most 0.009.
Values may be sent and summed in bfloat16 or wider, within the bound.
No kernel may reach another device: no remote copies, remote signals or barrier semaphores. Data moves between devices by JAX's collectives and lax.ppermute only.
A program may use at most 64 MiB of HBM per device.

```python
import jax
import jax.numpy as jnp
from jax import lax

CZ = 128
FEATURE_SIZE = 256
PRODUCT_FEATURES = 32
C_TRI = 128
RELMAX = 32
CHAINS = 4
HOMOLOG_TOTAL = 64
AMINO_TOTAL = 128


def draw_residue_chain_index(key, part):
    key = jax.random.fold_in(key, 7)
    cut_points = jax.random.randint(key, (CHAINS - 1,), 1, AMINO_TOTAL)
    positions = jnp.arange(AMINO_TOTAL, dtype=jnp.int32)
    return jnp.sum((positions[:, None] >= cut_points[None, :]).astype(jnp.int32), axis=1).astype(jnp.int32)


def draw_alignment_mask(key, part):
    key = jax.random.fold_in(key, 11)
    span_key, start_key, scale_key, entry_key = jax.random.split(key, 4)
    spans = jax.random.randint(span_key, (HOMOLOG_TOTAL,), AMINO_TOTAL // 8, AMINO_TOTAL + 1)
    starts = jax.random.randint(start_key, (HOMOLOG_TOTAL,), 0, AMINO_TOTAL - spans + 1)
    positions = jnp.arange(AMINO_TOTAL, dtype=jnp.int32)
    covered = (positions[None, :] >= starts[:, None]) & (positions[None, :] < (starts + spans)[:, None])
    query_row = jnp.arange(HOMOLOG_TOTAL, dtype=jnp.int32)[:, None] == 0
    covered = covered | query_row
    seq_scale = jnp.exp(jax.random.uniform(scale_key, (HOMOLOG_TOTAL, 1), jnp.float32, -2.302585, 0.0))
    seq_scale = jnp.where(query_row, 1.0, seq_scale)
    entry_scale = jax.random.uniform(entry_key, (HOMOLOG_TOTAL, AMINO_TOTAL), jnp.float32, 0.5, 1.0)
    weights = jnp.where(covered, seq_scale * entry_scale, 0.0)
    return weights.astype(jnp.bfloat16)


def set_ends(drawn, rng, smallest, top_value):
    longest = drawn.shape.index(max(drawn.shape))
    spots = []
    for shift in (0, 1):
        where = [jax.random.randint(jax.random.fold_in(rng, axis), (), 0, length) for axis, length in enumerate(drawn.shape)]
        where[longest] = (where[longest] + shift) % drawn.shape[longest]
        spots.append(tuple(where))
    return drawn.at[spots[0]].set(smallest).at[spots[1]].set(top_value)


def levels(stream_key, shape, cuts, least, high):
    level, own = 1.0, jax.random.fold_in(stream_key, 6)
    for axis_at, shards_of in cuts:
        heights = jnp.exp(jax.random.uniform(jax.random.fold_in(own, axis_at), (shards_of,), jnp.float32, least / len(cuts), high / len(cuts)))
        level = level * jnp.repeat(heights, shape[axis_at] // shards_of).reshape([-1 if axis == axis_at else 1 for axis in range(len(shape))])
    return level


def scatter_about(rng, shape, deviation, most, shards=(), kind=jnp.bfloat16):
    result = jax.random.normal(rng, shape, jnp.float32) * deviation
    if len(shards) > 0:
        result = levels(rng, shape, shards, -0.22, 0.18) * result
    return jnp.clip(result, min=-most, max=most).astype(kind)


def setup_inputs(seed: int = 0, part: int = 0) -> dict:
    keys = jax.random.split(jax.random.key(seed), 11)
    part_keys = jax.random.split(jax.random.fold_in(keys[10], part), 11)
    return {
        "pairwise_state": scatter_about(part_keys[0], (AMINO_TOTAL, AMINO_TOTAL, CZ), 1.0, 6.0, ((0, 16),)),
        "homolog_features": scatter_about(part_keys[1], (HOMOLOG_TOTAL, AMINO_TOTAL, FEATURE_SIZE), 1.0, 6.0, ((1, 16),)),
        "residue_chain_index": draw_residue_chain_index(jax.random.fold_in(jax.random.fold_in(keys[10], part), 71), part),
        "resolved_residue_mask": set_ends((jax.random.randint(part_keys[3], (AMINO_TOTAL,), 0, 16) < 15).astype(jnp.int32), jax.random.fold_in(part_keys[3], 1), 0, 1),
        "alignment_mask": draw_alignment_mask(jax.random.fold_in(jax.random.fold_in(keys[10], part), 71), part),
        "relative_offset_table": scatter_about(keys[5], (2 * RELMAX + 2, CZ), 0.5, 3.0),
        "homolog_to_sides_matrix": scatter_about(keys[6], (FEATURE_SIZE, 2 * PRODUCT_FEATURES), FEATURE_SIZE ** -0.5, 0.375),
        "outer_mean_output_weight": scatter_about(keys[7], (PRODUCT_FEATURES * PRODUCT_FEATURES, CZ), (PRODUCT_FEATURES * PRODUCT_FEATURES) ** -0.5, 0.1875),
        "triangle_projection_weight": scatter_about(keys[8], (2, CZ, 4 * C_TRI + CZ), CZ ** -0.5, 0.5),
        "triangle_output_weight": scatter_about(keys[9], (2, C_TRI, CZ), C_TRI ** -0.5, 0.5),
    }


EPSILON = 1e-05

def apply_layer_norm(values, axis_dim):
    center = values - lax.optimization_barrier(jnp.mean(values, axis=axis_dim, keepdims=True))
    spread = lax.optimization_barrier(jnp.mean(center * center, axis=axis_dim, keepdims=True))
    return center * lax.rsqrt(spread + EPSILON)

def rounded_values(values):
    return lax.optimization_barrier(values.astype(jnp.bfloat16)).astype(jnp.float32)

def outgoing_plane(planes):
    return rounded_values(jnp.dot(planes[0], planes[1].T))

def incoming_plane(planes):
    return rounded_values(jnp.dot(planes[0].T, planes[1]))

def triangle(stream, pair_live, proj_weight, out_weight, incoming):
    normed = rounded_values(apply_layer_norm(stream, 2))
    weight_f = proj_weight.astype(jnp.float32)

    def project(first, width):
        return jnp.einsum('ijd,dc->ijc', normed, weight_f[:, first:first + width])
    left_side = rounded_values(jax.nn.sigmoid(project(0, C_TRI)) * project(C_TRI, C_TRI) * pair_live[:, :, None])
    right_side = rounded_values(jax.nn.sigmoid(project(2 * C_TRI, C_TRI)) * project(3 * C_TRI, C_TRI) * pair_live[:, :, None])
    gate = jax.nn.sigmoid(project(4 * C_TRI, CZ))
    planes = (jnp.moveaxis(left_side, 2, 0), jnp.moveaxis(right_side, 2, 0))
    if incoming:
        mixed = lax.map(incoming_plane, planes)
    else:
        mixed = lax.map(outgoing_plane, planes)
    blended_standardize = rounded_values(apply_layer_norm(mixed, 0))
    update = jnp.einsum('cij,cd->ijd', blended_standardize, out_weight.astype(jnp.float32))
    return stream + gate * update

def reference(pairwise_state, homolog_features, residue_chain_index, resolved_residue_mask, alignment_mask, relative_offset_table, homolog_to_sides_matrix, outer_mean_output_weight, triangle_projection_weight, triangle_output_weight):
    residue_present = resolved_residue_mask.astype(jnp.float32)
    present_flags = alignment_mask.astype(jnp.float32) * residue_present[None, :]
    alignment_normed = rounded_values(apply_layer_norm(homolog_features.astype(jnp.float32), 2))
    projected_rows = jnp.einsum('tna,ak->tnk', alignment_normed, homolog_to_sides_matrix.astype(jnp.float32)) * present_flags[:, :, None]
    projected_rows = rounded_values(projected_rows)
    left_proj = projected_rows[:, :, :PRODUCT_FEATURES]
    right_proj = projected_rows[:, :, PRODUCT_FEATURES:]
    counts = jnp.dot(present_flags.T, present_flags)
    weight_opm = outer_mean_output_weight.astype(jnp.float32)

    def opm_row(left_row):
        outer = jnp.einsum('sc,sjd->jcd', left_row, right_proj)
        outer = rounded_values(outer.reshape(outer.shape[0], PRODUCT_FEATURES * PRODUCT_FEATURES))
        return jnp.dot(outer, weight_opm)
    opm = lax.map(opm_row, jnp.moveaxis(left_proj, 1, 0))
    positions = jnp.arange(residue_chain_index.shape[0], dtype=jnp.int32)
    offset = jnp.clip(positions[:, None] - positions[None, :], -RELMAX, RELMAX) + RELMAX
    bin_index = jnp.where(residue_chain_index[:, None] == residue_chain_index[None, :], offset, 2 * RELMAX + 1).astype(jnp.int32)
    relpos = jnp.take(relative_offset_table, bin_index, axis=0).astype(jnp.float32)
    stream = pairwise_state.astype(jnp.float32) + relpos + opm / jnp.maximum(counts, 1.0)[:, :, None]
    pair_live = residue_present[:, None] * residue_present[None, :]
    stream = triangle(stream, pair_live, triangle_projection_weight[0], triangle_output_weight[0], False)
    stream = triangle(stream, pair_live, triangle_projection_weight[1], triangle_output_weight[1], True)
    return stream.astype(jnp.bfloat16)
```

```python
import jax
import jax.numpy as jnp
from jax import lax
from jax.sharding import PartitionSpec as P

RELMAX = 32


EPSILON = 1e-05


def apply_layer_norm(values, axis_dim):
    center = values - jnp.mean(values, axis=axis_dim, keepdims=True)
    spread = jnp.mean(center * center, axis=axis_dim, keepdims=True)
    return center * lax.rsqrt(spread + EPSILON)


def gather_wide(block):
    n = lax.axis_size("wide")
    if n % 4 or n < 8:
        return lax.all_gather(block, "wide", axis=0)
    outer = n // 4
    me = lax.axis_index("wide")
    high, mid, low = me // 4, (me // 2) % 2, me % 2
    arrived = [block]
    for shift in range(1, outer):
        perm = [(w, ((w // 4 + shift) % outer) * 4 + w % 4) for w in range(n)]
        arrived.append(lax.ppermute(block, "wide", perm))
    held = jnp.zeros((outer,) + block.shape, block.dtype)
    for shift, piece in enumerate(arrived):
        held = lax.dynamic_update_index_in_dim(held, piece, (high - shift + outer) % outer, 0)
    other = lax.ppermute(held, "wide", [(w, w ^ 2) for w in range(n)])
    held = jnp.stack(
        [jnp.where(mid == 0, held, other), jnp.where(mid == 0, other, held)], axis=1
    )
    other = lax.ppermute(held, "wide", [(w, w ^ 1) for w in range(n)])
    held = jnp.stack(
        [jnp.where(low == 0, held, other), jnp.where(low == 0, other, held)], axis=2
    )
    return held.reshape((n,) + block.shape)


def triangle(stream, pair_live, proj_weight, out_weight, incoming):
    rows = stream.shape[0]
    cols = stream.shape[1]
    width = out_weight.shape[0]
    wide_count = lax.axis_size("wide")
    core_count = lax.axis_size("narrow")
    devices = wide_count * core_count
    per_dev = width // devices
    normed = apply_layer_norm(stream, 2).astype(jnp.bfloat16)
    blocks = [proj_weight[:, index * width : (index + 1) * width] for index in range(4)]

    def project(block):
        return jnp.einsum("ijd,dc->cij", normed, block, preferred_element_type=jnp.float32)

    left_side = (jax.nn.sigmoid(project(blocks[0])) * project(blocks[1]) * pair_live[None]).astype(
        jnp.bfloat16
    )
    right_side = (jax.nn.sigmoid(project(blocks[2])) * project(blocks[3]) * pair_live[None]).astype(
        jnp.bfloat16
    )
    gate = jax.nn.sigmoid(
        jnp.einsum(
            "ijd,dc->ijc", normed, proj_weight[:, 4 * width :], preferred_element_type=jnp.float32
        )
    )
    form = "cki,ckj->cij" if incoming else "cik,cjk->cij"
    both = jnp.stack(
        [
            left_side.reshape(devices, per_dev, rows * cols),
            right_side.reshape(devices, per_dev, rows * cols),
        ],
        axis=1,
    ).reshape(devices, 2 * per_dev, rows * cols)
    both = lax.all_to_all(both, ("wide", "narrow"), split_axis=0, concat_axis=0, tiled=True)
    both = both.reshape(wide_count, core_count, 2, per_dev, rows, cols)
    both = jnp.transpose(both, (2, 3, 0, 4, 1, 5)).reshape(
        2, per_dev, wide_count * rows, core_count * cols
    )
    mixed = jnp.einsum(form, both[0], both[1], preferred_element_type=jnp.float32).astype(
        jnp.bfloat16
    )
    spread_out = mixed.reshape(per_dev, wide_count, rows, core_count, cols)
    spread_out = jnp.transpose(spread_out, (1, 3, 0, 2, 4)).reshape(
        wide_count * core_count * per_dev, rows * cols
    )
    returned = lax.all_to_all(
        spread_out, ("wide", "narrow"), split_axis=0, concat_axis=0, tiled=True
    ).reshape(width, rows, cols)
    blended_standardize = apply_layer_norm(returned.astype(jnp.float32), 0).astype(jnp.bfloat16)
    update = jnp.einsum(
        "cij,cd->ijd", blended_standardize, out_weight, preferred_element_type=jnp.float32
    )
    return stream + gate * update


def per_device(
    pairwise_state,
    homolog_features,
    residue_chain_index,
    resolved_residue_mask,
    alignment_mask,
    relative_offset_table,
    homolog_to_sides_matrix,
    outer_mean_output_weight,
    triangle_projection_weight,
    triangle_output_weight,
):
    rows = pairwise_state.shape[0]
    cols = pairwise_state.shape[1]
    row_start = lax.axis_index("wide") * rows
    col_start = lax.axis_index("narrow") * cols
    residue_present = resolved_residue_mask.astype(jnp.float32)
    row_present = lax.dynamic_slice_in_dim(residue_present, row_start, rows)
    col_live = lax.dynamic_slice_in_dim(residue_present, col_start, cols)
    present_flags = alignment_mask.astype(jnp.float32) * row_present[None, :]
    alignment_normed = apply_layer_norm(homolog_features.astype(jnp.float32), 2).astype(
        jnp.bfloat16
    )
    projected_rows = jnp.einsum(
        "tna,ak->tnk", alignment_normed, homolog_to_sides_matrix, preferred_element_type=jnp.float32
    )
    projected_rows = (projected_rows * present_flags[:, :, None]).astype(jnp.bfloat16)
    half_width = projected_rows.shape[2] // 2
    homologs = projected_rows.shape[0]
    left_proj = projected_rows[:, :, :half_width]
    right_proj = projected_rows[:, :, half_width:]
    live_flags = present_flags.astype(jnp.bfloat16)
    packed = jnp.concatenate(
        [jnp.transpose(right_proj, (1, 0, 2)).reshape(rows, homologs * half_width), live_flags.T],
        axis=1,
    )
    gathered = gather_wide(packed).reshape(-1, packed.shape[1])
    gathered = lax.dynamic_slice_in_dim(gathered, col_start, cols, 0)
    right_mine = jnp.transpose(
        gathered[:, : homologs * half_width].reshape(cols, homologs, half_width), (1, 0, 2)
    )
    live_mine = gathered[:, homologs * half_width :].T
    counts = jnp.dot(live_flags.T, live_mine, preferred_element_type=jnp.float32)

    def opm_row(left_row):
        outer = jnp.einsum("sc,sjd->jcd", left_row, right_mine, preferred_element_type=jnp.float32)
        outer = outer.reshape(cols, half_width * half_width).astype(jnp.bfloat16)
        return jnp.dot(outer, outer_mean_output_weight, preferred_element_type=jnp.float32)

    opm = lax.map(opm_row, jnp.transpose(left_proj, (1, 0, 2)))
    row_pos = row_start + jnp.arange(rows, dtype=jnp.int32)
    col_pos = col_start + jnp.arange(cols, dtype=jnp.int32)
    row_chain = lax.dynamic_slice_in_dim(residue_chain_index, row_start, rows)
    col_chain = lax.dynamic_slice_in_dim(residue_chain_index, col_start, cols)
    offset = jnp.clip(row_pos[:, None] - col_pos[None, :], -RELMAX, RELMAX) + RELMAX
    bin_index = jnp.where(row_chain[:, None] == col_chain[None, :], offset, 2 * RELMAX + 1)
    bin_count = relative_offset_table.shape[0]
    one_hot = (
        bin_index[:, :, None] == jnp.arange(bin_count, dtype=jnp.int32)[None, None, :]
    ).astype(jnp.bfloat16)
    relpos = jnp.einsum(
        "ijb,bc->ijc", one_hot, relative_offset_table, preferred_element_type=jnp.float32
    )
    stream = (
        pairwise_state.astype(jnp.float32) + relpos + opm / jnp.maximum(counts, 1.0)[:, :, None]
    )
    pair_live = row_present[:, None] * col_live[None, :]
    for turn_index in range(2):
        stream = triangle(
            stream,
            pair_live,
            triangle_projection_weight[turn_index],
            triangle_output_weight[turn_index],
            turn_index == 1,
        )
    return stream.astype(jnp.bfloat16)


def solution(mesh):
    return jax.shard_map(
        per_device,
        mesh=mesh,
        in_specs=(
            P(("grp", "wide"), "narrow", None),
            P("grp", "wide", None),
            P("grp"),
            P("grp"),
            P("grp", "wide"),
            P(),
            P(),
            P(),
            P(),
            P(),
        ),
        out_specs=P(("grp", "wide"), "narrow", None),
        check_vma=False,
    )
```

```python
import jax
import jax.numpy as jnp
from jax import lax
from jax.sharding import PartitionSpec as P

RELMAX = 32


EPSILON = 1e-05


def apply_layer_norm(values, axis_dim):
    center = values - jnp.mean(values, axis=axis_dim, keepdims=True)
    spread = jnp.mean(center * center, axis=axis_dim, keepdims=True)
    return center * lax.rsqrt(spread + EPSILON)


def gather_wide(block):
    n = lax.axis_size("wide")
    if n % 4 or n < 8:
        return lax.all_gather(block, "wide", axis=0)
    outer = n // 4
    me = lax.axis_index("wide")
    high, mid, low = me // 4, (me // 2) % 2, me % 2
    arrived = [block]
    for shift in range(1, outer):
        perm = [(w, ((w // 4 + shift) % outer) * 4 + w % 4) for w in range(n)]
        arrived.append(lax.ppermute(block, "wide", perm))
    held = jnp.zeros((outer,) + block.shape, block.dtype)
    for shift, piece in enumerate(arrived):
        held = lax.dynamic_update_index_in_dim(held, piece, (high - shift + outer) % outer, 0)
    other = lax.ppermute(held, "wide", [(w, w ^ 2) for w in range(n)])
    held = jnp.stack(
        [jnp.where(mid == 0, held, other), jnp.where(mid == 0, other, held)], axis=1
    )
    other = lax.ppermute(held, "wide", [(w, w ^ 1) for w in range(n)])
    held = jnp.stack(
        [jnp.where(low == 0, held, other), jnp.where(low == 0, other, held)], axis=2
    )
    return held.reshape((n,) + block.shape)


def chip_exchange(blocks):
    chips = blocks.shape[0]
    count = lax.axis_size("wide")
    here = lax.axis_index("wide") // 2
    held = lax.dynamic_update_index_in_dim(
        jnp.zeros_like(blocks), lax.dynamic_index_in_dim(blocks, here, 0, False), here, 0
    )
    arrived = []
    for step in range(chips - 1, 0, -1):
        piece = lax.dynamic_index_in_dim(blocks, here ^ step, 0, False)
        pairs = [(w, w ^ (2 * step)) for w in range(count)]
        arrived.append((step, lax.ppermute(piece, "wide", pairs)))
    for step, piece in arrived:
        held = lax.dynamic_update_index_in_dim(held, piece, here ^ step, 0)
    return held


def core_swap(block):
    count = lax.axis_size("wide")
    return lax.ppermute(block, "wide", [(w, w ^ 1) for w in range(count)])


def planes_by_chip(left_side, right_side, incoming):
    width, rows, cols = left_side.shape
    chips = lax.axis_size("wide") // 2
    per_chip = width // chips
    core = lax.axis_index("wide") % 2
    both = jnp.stack(
        [left_side.reshape(chips, per_chip, rows, cols), right_side.reshape(chips, per_chip, rows, cols)],
        axis=1,
    )
    both = jnp.transpose(chip_exchange(both), (1, 2, 0, 3, 4))
    if incoming:
        both = both.reshape(2, per_chip, chips * rows, cols)
        partial = jnp.einsum("cki,ckj->cij", both[0], both[1], preferred_element_type=jnp.float32)
        partial = partial.reshape(per_chip, chips, 2, rows, cols)
        mine = jnp.where(core == 0, partial[:, :, 0], partial[:, :, 1])
        theirs = jnp.where(core == 0, partial[:, :, 1], partial[:, :, 0])
        mixed = mine + core_swap(theirs)
    else:
        left = both[0].reshape(per_chip, chips * rows, cols)
        mine = both[1]
        theirs = core_swap(mine)
        right = jnp.stack(
            [jnp.where(core == 0, mine, theirs), jnp.where(core == 0, theirs, mine)], axis=2
        ).reshape(per_chip, 2 * chips * rows, cols)
        mixed = jnp.einsum("cik,cjk->cij", left, right, preferred_element_type=jnp.float32)
        mixed = mixed.reshape(per_chip, chips, rows, cols)
    mixed = jnp.transpose(mixed.astype(jnp.bfloat16), (1, 0, 2, 3))
    return chip_exchange(mixed).reshape(width, rows, cols)


def planes_by_device(left_side, right_side, incoming):
    width, rows, cols = left_side.shape
    wide_count = lax.axis_size("wide")
    core_count = lax.axis_size("narrow")
    devices = wide_count * core_count
    per_dev = width // devices
    both = jnp.stack(
        [
            left_side.reshape(devices, per_dev, rows * cols),
            right_side.reshape(devices, per_dev, rows * cols),
        ],
        axis=1,
    ).reshape(devices, 2 * per_dev, rows * cols)
    both = lax.all_to_all(both, ("wide", "narrow"), split_axis=0, concat_axis=0, tiled=True)
    both = both.reshape(wide_count, core_count, 2, per_dev, rows, cols)
    both = jnp.transpose(both, (2, 3, 0, 4, 1, 5)).reshape(
        2, per_dev, wide_count * rows, core_count * cols
    )
    form = "cki,ckj->cij" if incoming else "cik,cjk->cij"
    mixed = jnp.einsum(form, both[0], both[1], preferred_element_type=jnp.float32).astype(
        jnp.bfloat16
    )
    spread_out = mixed.reshape(per_dev, wide_count, rows, core_count, cols)
    spread_out = jnp.transpose(spread_out, (1, 3, 0, 2, 4)).reshape(
        wide_count * core_count * per_dev, rows * cols
    )
    return lax.all_to_all(
        spread_out, ("wide", "narrow"), split_axis=0, concat_axis=0, tiled=True
    ).reshape(width, rows, cols)


def triangle(stream, pair_live, proj_weight, out_weight, incoming):
    width = out_weight.shape[0]
    wide_count = lax.axis_size("wide")
    by_chip = lax.axis_size("narrow") == 1 and wide_count in (4, 8, 16)
    normed = apply_layer_norm(stream, 2).astype(jnp.bfloat16)
    blocks = [proj_weight[:, index * width : (index + 1) * width] for index in range(4)]

    def project(block):
        return jnp.einsum("ijd,dc->cij", normed, block, preferred_element_type=jnp.float32)

    left_side = (jax.nn.sigmoid(project(blocks[0])) * project(blocks[1]) * pair_live[None]).astype(
        jnp.bfloat16
    )
    right_side = (jax.nn.sigmoid(project(blocks[2])) * project(blocks[3]) * pair_live[None]).astype(
        jnp.bfloat16
    )
    gate = jax.nn.sigmoid(
        jnp.einsum(
            "ijd,dc->ijc", normed, proj_weight[:, 4 * width :], preferred_element_type=jnp.float32
        )
    )
    planes = planes_by_chip if by_chip else planes_by_device
    returned = planes(left_side, right_side, incoming)
    blended_standardize = apply_layer_norm(returned.astype(jnp.float32), 0).astype(jnp.bfloat16)
    update = jnp.einsum(
        "cij,cd->ijd", blended_standardize, out_weight, preferred_element_type=jnp.float32
    )
    return stream + gate * update


def per_device(
    pairwise_state,
    homolog_features,
    residue_chain_index,
    resolved_residue_mask,
    alignment_mask,
    relative_offset_table,
    homolog_to_sides_matrix,
    outer_mean_output_weight,
    triangle_projection_weight,
    triangle_output_weight,
):
    rows = pairwise_state.shape[0]
    cols = pairwise_state.shape[1]
    row_start = lax.axis_index("wide") * rows
    col_start = lax.axis_index("narrow") * cols
    residue_present = resolved_residue_mask.astype(jnp.float32)
    row_present = lax.dynamic_slice_in_dim(residue_present, row_start, rows)
    col_live = lax.dynamic_slice_in_dim(residue_present, col_start, cols)
    present_flags = alignment_mask.astype(jnp.float32) * row_present[None, :]
    alignment_normed = apply_layer_norm(homolog_features.astype(jnp.float32), 2).astype(
        jnp.bfloat16
    )
    projected_rows = jnp.einsum(
        "tna,ak->tnk", alignment_normed, homolog_to_sides_matrix, preferred_element_type=jnp.float32
    )
    projected_rows = (projected_rows * present_flags[:, :, None]).astype(jnp.bfloat16)
    half_width = projected_rows.shape[2] // 2
    homologs = projected_rows.shape[0]
    left_proj = projected_rows[:, :, :half_width]
    right_proj = projected_rows[:, :, half_width:]
    live_flags = present_flags.astype(jnp.bfloat16)
    packed = jnp.concatenate(
        [jnp.transpose(right_proj, (1, 0, 2)).reshape(rows, homologs * half_width), live_flags.T],
        axis=1,
    )
    gathered = gather_wide(packed).reshape(-1, packed.shape[1])
    gathered = lax.dynamic_slice_in_dim(gathered, col_start, cols, 0)
    right_mine = jnp.transpose(
        gathered[:, : homologs * half_width].reshape(cols, homologs, half_width), (1, 0, 2)
    )
    live_mine = gathered[:, homologs * half_width :].T
    counts = jnp.dot(live_flags.T, live_mine, preferred_element_type=jnp.float32)

    def opm_row(left_row):
        outer = jnp.einsum("sc,sjd->jcd", left_row, right_mine, preferred_element_type=jnp.float32)
        outer = outer.reshape(cols, half_width * half_width).astype(jnp.bfloat16)
        return jnp.dot(outer, outer_mean_output_weight, preferred_element_type=jnp.float32)

    opm = lax.map(opm_row, jnp.transpose(left_proj, (1, 0, 2)))
    row_pos = row_start + jnp.arange(rows, dtype=jnp.int32)
    col_pos = col_start + jnp.arange(cols, dtype=jnp.int32)
    row_chain = lax.dynamic_slice_in_dim(residue_chain_index, row_start, rows)
    col_chain = lax.dynamic_slice_in_dim(residue_chain_index, col_start, cols)
    offset = jnp.clip(row_pos[:, None] - col_pos[None, :], -RELMAX, RELMAX) + RELMAX
    bin_index = jnp.where(row_chain[:, None] == col_chain[None, :], offset, 2 * RELMAX + 1)
    bin_count = relative_offset_table.shape[0]
    one_hot = (
        bin_index[:, :, None] == jnp.arange(bin_count, dtype=jnp.int32)[None, None, :]
    ).astype(jnp.bfloat16)
    relpos = jnp.einsum(
        "ijb,bc->ijc", one_hot, relative_offset_table, preferred_element_type=jnp.float32
    )
    stream = (
        pairwise_state.astype(jnp.float32) + relpos + opm / jnp.maximum(counts, 1.0)[:, :, None]
    )
    pair_live = row_present[:, None] * col_live[None, :]
    for turn_index in range(2):
        stream = triangle(
            stream,
            pair_live,
            triangle_projection_weight[turn_index],
            triangle_output_weight[turn_index],
            turn_index == 1,
        )
    return stream.astype(jnp.bfloat16)


def solution(mesh):
    return jax.shard_map(
        per_device,
        mesh=mesh,
        in_specs=(
            P(("grp", "wide"), "narrow", None),
            P("grp", "wide", None),
            P("grp"),
            P("grp"),
            P("grp", "wide"),
            P(),
            P(),
            P(),
            P(),
            P(),
        ),
        out_specs=P(("grp", "wide"), "narrow", None),
        check_vma=False,
    )
```

```python
import jax
import jax.numpy as jnp
from jax import lax
from jax.sharding import PartitionSpec as P

RELMAX = 32


EPSILON = 1e-05


def apply_layer_norm(values, axis_dim):
    center = values - jnp.mean(values, axis=axis_dim, keepdims=True)
    spread = jnp.mean(center * center, axis=axis_dim, keepdims=True)
    return center * lax.rsqrt(spread + EPSILON)


def gather_wide(block):
    n = lax.axis_size("wide")
    if n % 4 or n < 8:
        return lax.all_gather(block, "wide", axis=0)
    outer = n // 4
    me = lax.axis_index("wide")
    high, mid, low = me // 4, (me // 2) % 2, me % 2
    arrived = [block]
    for shift in range(1, outer):
        perm = [(w, ((w // 4 + shift) % outer) * 4 + w % 4) for w in range(n)]
        arrived.append(lax.ppermute(block, "wide", perm))
    held = jnp.zeros((outer,) + block.shape, block.dtype)
    for shift, piece in enumerate(arrived):
        held = lax.dynamic_update_index_in_dim(held, piece, (high - shift + outer) % outer, 0)
    other = lax.ppermute(held, "wide", [(w, w ^ 2) for w in range(n)])
    held = jnp.stack(
        [jnp.where(mid == 0, held, other), jnp.where(mid == 0, other, held)], axis=1
    )
    other = lax.ppermute(held, "wide", [(w, w ^ 1) for w in range(n)])
    held = jnp.stack(
        [jnp.where(low == 0, held, other), jnp.where(low == 0, other, held)], axis=2
    )
    return held.reshape((n,) + block.shape)


def chip_exchange(blocks):
    count = lax.axis_size("wide")
    groups = [list(range(core, count, 2)) for core in range(2)]
    return lax.all_to_all(blocks, "wide", 0, 0, axis_index_groups=groups, tiled=True)


def core_swap(block):
    count = lax.axis_size("wide")
    return lax.ppermute(block, "wide", [(w, w ^ 1) for w in range(count)])


def planes_by_chip(left_side, right_side, incoming):
    width, rows, cols = left_side.shape
    chips = lax.axis_size("wide") // 2
    per_chip = width // chips
    core = lax.axis_index("wide") % 2
    both = jnp.stack(
        [left_side.reshape(chips, per_chip, rows, cols), right_side.reshape(chips, per_chip, rows, cols)],
        axis=1,
    )
    both = jnp.transpose(chip_exchange(both), (1, 2, 0, 3, 4))
    if incoming:
        both = both.reshape(2, per_chip, chips * rows, cols)
        partial = jnp.einsum("cki,ckj->cij", both[0], both[1], preferred_element_type=jnp.float32)
        partial = partial.reshape(per_chip, chips, 2, rows, cols)
        mine = jnp.where(core == 0, partial[:, :, 0], partial[:, :, 1])
        theirs = jnp.where(core == 0, partial[:, :, 1], partial[:, :, 0])
        mixed = mine + core_swap(theirs)
    else:
        left = both[0].reshape(per_chip, chips * rows, cols)
        mine = both[1]
        theirs = core_swap(mine)
        right = jnp.stack(
            [jnp.where(core == 0, mine, theirs), jnp.where(core == 0, theirs, mine)], axis=2
        ).reshape(per_chip, 2 * chips * rows, cols)
        mixed = jnp.einsum("cik,cjk->cij", left, right, preferred_element_type=jnp.float32)
        mixed = mixed.reshape(per_chip, chips, rows, cols)
    mixed = jnp.transpose(mixed.astype(jnp.bfloat16), (1, 0, 2, 3))
    return chip_exchange(mixed).reshape(width, rows, cols)


def planes_by_device(left_side, right_side, incoming):
    width, rows, cols = left_side.shape
    wide_count = lax.axis_size("wide")
    core_count = lax.axis_size("narrow")
    devices = wide_count * core_count
    per_dev = width // devices
    both = jnp.stack(
        [
            left_side.reshape(devices, per_dev, rows * cols),
            right_side.reshape(devices, per_dev, rows * cols),
        ],
        axis=1,
    ).reshape(devices, 2 * per_dev, rows * cols)
    both = lax.all_to_all(both, ("wide", "narrow"), split_axis=0, concat_axis=0, tiled=True)
    both = both.reshape(wide_count, core_count, 2, per_dev, rows, cols)
    both = jnp.transpose(both, (2, 3, 0, 4, 1, 5)).reshape(
        2, per_dev, wide_count * rows, core_count * cols
    )
    form = "cki,ckj->cij" if incoming else "cik,cjk->cij"
    mixed = jnp.einsum(form, both[0], both[1], preferred_element_type=jnp.float32).astype(
        jnp.bfloat16
    )
    spread_out = mixed.reshape(per_dev, wide_count, rows, core_count, cols)
    spread_out = jnp.transpose(spread_out, (1, 3, 0, 2, 4)).reshape(
        wide_count * core_count * per_dev, rows * cols
    )
    return lax.all_to_all(
        spread_out, ("wide", "narrow"), split_axis=0, concat_axis=0, tiled=True
    ).reshape(width, rows, cols)


def triangle(stream, pair_live, proj_weight, out_weight, incoming):
    width = out_weight.shape[0]
    wide_count = lax.axis_size("wide")
    by_chip = lax.axis_size("narrow") == 1 and wide_count in (4, 8, 16)
    normed = apply_layer_norm(stream, 2).astype(jnp.bfloat16)
    blocks = [proj_weight[:, index * width : (index + 1) * width] for index in range(4)]

    def project(block):
        return jnp.einsum("ijd,dc->cij", normed, block, preferred_element_type=jnp.float32)

    left_side = (jax.nn.sigmoid(project(blocks[0])) * project(blocks[1]) * pair_live[None]).astype(
        jnp.bfloat16
    )
    right_side = (jax.nn.sigmoid(project(blocks[2])) * project(blocks[3]) * pair_live[None]).astype(
        jnp.bfloat16
    )
    gate = jax.nn.sigmoid(
        jnp.einsum(
            "ijd,dc->ijc", normed, proj_weight[:, 4 * width :], preferred_element_type=jnp.float32
        )
    )
    planes = planes_by_chip if by_chip else planes_by_device
    returned = planes(left_side, right_side, incoming)
    blended_standardize = apply_layer_norm(returned.astype(jnp.float32), 0).astype(jnp.bfloat16)
    update = jnp.einsum(
        "cij,cd->ijd", blended_standardize, out_weight, preferred_element_type=jnp.float32
    )
    return stream + gate * update


def per_device(
    pairwise_state,
    homolog_features,
    residue_chain_index,
    resolved_residue_mask,
    alignment_mask,
    relative_offset_table,
    homolog_to_sides_matrix,
    outer_mean_output_weight,
    triangle_projection_weight,
    triangle_output_weight,
):
    rows = pairwise_state.shape[0]
    cols = pairwise_state.shape[1]
    row_start = lax.axis_index("wide") * rows
    col_start = lax.axis_index("narrow") * cols
    residue_present = resolved_residue_mask.astype(jnp.float32)
    row_present = lax.dynamic_slice_in_dim(residue_present, row_start, rows)
    col_live = lax.dynamic_slice_in_dim(residue_present, col_start, cols)
    present_flags = alignment_mask.astype(jnp.float32) * row_present[None, :]
    alignment_normed = apply_layer_norm(homolog_features.astype(jnp.float32), 2).astype(
        jnp.bfloat16
    )
    projected_rows = jnp.einsum(
        "tna,ak->tnk", alignment_normed, homolog_to_sides_matrix, preferred_element_type=jnp.float32
    )
    projected_rows = (projected_rows * present_flags[:, :, None]).astype(jnp.bfloat16)
    half_width = projected_rows.shape[2] // 2
    homologs = projected_rows.shape[0]
    left_proj = projected_rows[:, :, :half_width]
    right_proj = projected_rows[:, :, half_width:]
    live_flags = present_flags.astype(jnp.bfloat16)
    packed = jnp.concatenate(
        [jnp.transpose(right_proj, (1, 0, 2)).reshape(rows, homologs * half_width), live_flags.T],
        axis=1,
    )
    gathered = gather_wide(packed).reshape(-1, packed.shape[1])
    gathered = lax.dynamic_slice_in_dim(gathered, col_start, cols, 0)
    right_mine = jnp.transpose(
        gathered[:, : homologs * half_width].reshape(cols, homologs, half_width), (1, 0, 2)
    )
    live_mine = gathered[:, homologs * half_width :].T
    counts = jnp.dot(live_flags.T, live_mine, preferred_element_type=jnp.float32)

    def opm_row(left_row):
        outer = jnp.einsum("sc,sjd->jcd", left_row, right_mine, preferred_element_type=jnp.float32)
        outer = outer.reshape(cols, half_width * half_width).astype(jnp.bfloat16)
        return jnp.dot(outer, outer_mean_output_weight, preferred_element_type=jnp.float32)

    opm = lax.map(opm_row, jnp.transpose(left_proj, (1, 0, 2)))
    row_pos = row_start + jnp.arange(rows, dtype=jnp.int32)
    col_pos = col_start + jnp.arange(cols, dtype=jnp.int32)
    row_chain = lax.dynamic_slice_in_dim(residue_chain_index, row_start, rows)
    col_chain = lax.dynamic_slice_in_dim(residue_chain_index, col_start, cols)
    offset = jnp.clip(row_pos[:, None] - col_pos[None, :], -RELMAX, RELMAX) + RELMAX
    bin_index = jnp.where(row_chain[:, None] == col_chain[None, :], offset, 2 * RELMAX + 1)
    bin_count = relative_offset_table.shape[0]
    one_hot = (
        bin_index[:, :, None] == jnp.arange(bin_count, dtype=jnp.int32)[None, None, :]
    ).astype(jnp.bfloat16)
    relpos = jnp.einsum(
        "ijb,bc->ijc", one_hot, relative_offset_table, preferred_element_type=jnp.float32
    )
    stream = (
        pairwise_state.astype(jnp.float32) + relpos + opm / jnp.maximum(counts, 1.0)[:, :, None]
    )
    pair_live = row_present[:, None] * col_live[None, :]
    for turn_index in range(2):
        stream = triangle(
            stream,
            pair_live,
            triangle_projection_weight[turn_index],
            triangle_output_weight[turn_index],
            turn_index == 1,
        )
    return stream.astype(jnp.bfloat16)


def solution(mesh):
    return jax.shard_map(
        per_device,
        mesh=mesh,
        in_specs=(
            P(("grp", "wide"), "narrow", None),
            P("grp", "wide", None),
            P("grp"),
            P("grp"),
            P("grp", "wide"),
            P(),
            P(),
            P(),
            P(),
            P(),
        ),
        out_specs=P(("grp", "wide"), "narrow", None),
        check_vma=False,
    )
```

```python
import functools

import jax
import jax.numpy as jnp
from jax import lax
from jax.experimental import pallas as pl
from jax.experimental.pallas import tpu as pltpu
from jax.sharding import PartitionSpec as P

RELMAX = 32
EPSILON = 1e-05
LANES = 128
F32 = jnp.float32
BF16 = jnp.bfloat16


def apply_layer_norm(values, axis_dim):
    center = values - jnp.mean(values, axis=axis_dim, keepdims=True)
    spread = jnp.mean(center * center, axis=axis_dim, keepdims=True)
    return center * lax.rsqrt(spread + EPSILON)


def gather_wide(block):
    n = lax.axis_size("wide")
    if n % 4 or n < 8:
        return lax.all_gather(block, "wide", axis=0)
    outer = n // 4
    me = lax.axis_index("wide")
    high, mid, low = me // 4, (me // 2) % 2, me % 2
    arrived = [block]
    for shift in range(1, outer):
        perm = [(w, ((w // 4 + shift) % outer) * 4 + w % 4) for w in range(n)]
        arrived.append(lax.ppermute(block, "wide", perm))
    held = jnp.zeros((outer,) + block.shape, block.dtype)
    for shift, piece in enumerate(arrived):
        held = lax.dynamic_update_index_in_dim(held, piece, (high - shift + outer) % outer, 0)
    other = lax.ppermute(held, "wide", [(w, w ^ 2) for w in range(n)])
    held = jnp.stack(
        [jnp.where(mid == 0, held, other), jnp.where(mid == 0, other, held)], axis=1
    )
    other = lax.ppermute(held, "wide", [(w, w ^ 1) for w in range(n)])
    held = jnp.stack(
        [jnp.where(low == 0, held, other), jnp.where(low == 0, other, held)], axis=2
    )
    return held.reshape((n,) + block.shape)


def triangle(stream, pair_live, proj_weight, out_weight, incoming):
    rows = stream.shape[0]
    cols = stream.shape[1]
    width = out_weight.shape[0]
    wide_count = lax.axis_size("wide")
    core_count = lax.axis_size("narrow")
    devices = wide_count * core_count
    per_dev = width // devices
    normed = apply_layer_norm(stream, 2).astype(jnp.bfloat16)
    blocks = [proj_weight[:, index * width : (index + 1) * width] for index in range(4)]

    def project(block):
        return jnp.einsum("ijd,dc->cij", normed, block, preferred_element_type=jnp.float32)

    left_side = (jax.nn.sigmoid(project(blocks[0])) * project(blocks[1]) * pair_live[None]).astype(
        jnp.bfloat16
    )
    right_side = (jax.nn.sigmoid(project(blocks[2])) * project(blocks[3]) * pair_live[None]).astype(
        jnp.bfloat16
    )
    gate = jax.nn.sigmoid(
        jnp.einsum(
            "ijd,dc->ijc", normed, proj_weight[:, 4 * width :], preferred_element_type=jnp.float32
        )
    )
    form = "cki,ckj->cij" if incoming else "cik,cjk->cij"
    both = jnp.stack(
        [
            left_side.reshape(devices, per_dev, rows * cols),
            right_side.reshape(devices, per_dev, rows * cols),
        ],
        axis=1,
    ).reshape(devices, 2 * per_dev, rows * cols)
    both = lax.all_to_all(both, ("wide", "narrow"), split_axis=0, concat_axis=0, tiled=True)
    both = both.reshape(wide_count, core_count, 2, per_dev, rows, cols)
    both = jnp.transpose(both, (2, 3, 0, 4, 1, 5)).reshape(
        2, per_dev, wide_count * rows, core_count * cols
    )
    mixed = jnp.einsum(form, both[0], both[1], preferred_element_type=jnp.float32).astype(
        jnp.bfloat16
    )
    spread_out = mixed.reshape(per_dev, wide_count, rows, core_count, cols)
    spread_out = jnp.transpose(spread_out, (1, 3, 0, 2, 4)).reshape(
        wide_count * core_count * per_dev, rows * cols
    )
    returned = lax.all_to_all(
        spread_out, ("wide", "narrow"), split_axis=0, concat_axis=0, tiled=True
    ).reshape(width, rows, cols)
    blended_standardize = apply_layer_norm(returned.astype(jnp.float32), 0).astype(jnp.bfloat16)
    update = jnp.einsum(
        "cij,cd->ijd", blended_standardize, out_weight, preferred_element_type=jnp.float32
    )
    return stream + gate * update


def per_device_general(
    pairwise_state,
    homolog_features,
    residue_chain_index,
    resolved_residue_mask,
    alignment_mask,
    relative_offset_table,
    homolog_to_sides_matrix,
    outer_mean_output_weight,
    triangle_projection_weight,
    triangle_output_weight,
):
    rows = pairwise_state.shape[0]
    cols = pairwise_state.shape[1]
    row_start = lax.axis_index("wide") * rows
    col_start = lax.axis_index("narrow") * cols
    residue_present = resolved_residue_mask.astype(jnp.float32)
    row_present = lax.dynamic_slice_in_dim(residue_present, row_start, rows)
    col_live = lax.dynamic_slice_in_dim(residue_present, col_start, cols)
    present_flags = alignment_mask.astype(jnp.float32) * row_present[None, :]
    alignment_normed = apply_layer_norm(homolog_features.astype(jnp.float32), 2).astype(
        jnp.bfloat16
    )
    projected_rows = jnp.einsum(
        "tna,ak->tnk", alignment_normed, homolog_to_sides_matrix, preferred_element_type=jnp.float32
    )
    projected_rows = (projected_rows * present_flags[:, :, None]).astype(jnp.bfloat16)
    half_width = projected_rows.shape[2] // 2
    homologs = projected_rows.shape[0]
    left_proj = projected_rows[:, :, :half_width]
    right_proj = projected_rows[:, :, half_width:]
    live_flags = present_flags.astype(jnp.bfloat16)
    packed = jnp.concatenate(
        [jnp.transpose(right_proj, (1, 0, 2)).reshape(rows, homologs * half_width), live_flags.T],
        axis=1,
    )
    gathered = gather_wide(packed).reshape(-1, packed.shape[1])
    gathered = lax.dynamic_slice_in_dim(gathered, col_start, cols, 0)
    right_mine = jnp.transpose(
        gathered[:, : homologs * half_width].reshape(cols, homologs, half_width), (1, 0, 2)
    )
    live_mine = gathered[:, homologs * half_width :].T
    counts = jnp.dot(live_flags.T, live_mine, preferred_element_type=jnp.float32)

    def opm_row(left_row):
        outer = jnp.einsum("sc,sjd->jcd", left_row, right_mine, preferred_element_type=jnp.float32)
        outer = outer.reshape(cols, half_width * half_width).astype(jnp.bfloat16)
        return jnp.dot(outer, outer_mean_output_weight, preferred_element_type=jnp.float32)

    opm = lax.map(opm_row, jnp.transpose(left_proj, (1, 0, 2)))
    row_pos = row_start + jnp.arange(rows, dtype=jnp.int32)
    col_pos = col_start + jnp.arange(cols, dtype=jnp.int32)
    row_chain = lax.dynamic_slice_in_dim(residue_chain_index, row_start, rows)
    col_chain = lax.dynamic_slice_in_dim(residue_chain_index, col_start, cols)
    offset = jnp.clip(row_pos[:, None] - col_pos[None, :], -RELMAX, RELMAX) + RELMAX
    bin_index = jnp.where(row_chain[:, None] == col_chain[None, :], offset, 2 * RELMAX + 1)
    bin_count = relative_offset_table.shape[0]
    one_hot = (
        bin_index[:, :, None] == jnp.arange(bin_count, dtype=jnp.int32)[None, None, :]
    ).astype(jnp.bfloat16)
    relpos = jnp.einsum(
        "ijb,bc->ijc", one_hot, relative_offset_table, preferred_element_type=jnp.float32
    )
    stream = (
        pairwise_state.astype(jnp.float32) + relpos + opm / jnp.maximum(counts, 1.0)[:, :, None]
    )
    pair_live = row_present[:, None] * col_live[None, :]
    for turn_index in range(2):
        stream = triangle(
            stream,
            pair_live,
            triangle_projection_weight[turn_index],
            triangle_output_weight[turn_index],
            turn_index == 1,
        )
    return stream.astype(jnp.bfloat16)


def nn(a, b):
    return lax.dot_general(a, b, (((1,), (0,)), ((), ())), preferred_element_type=F32)


def nt(a, b):
    return lax.dot_general(a, b, (((1,), (1,)), ((), ())), preferred_element_type=F32)


def tn(a, b):
    return lax.dot_general(a, b, (((0,), (0,)), ((), ())), preferred_element_type=F32)


def identity(size):
    rows = lax.broadcasted_iota(jnp.int32, (size, size), 0)
    cols = lax.broadcasted_iota(jnp.int32, (size, size), 1)
    return (rows == cols).astype(F32).astype(BF16)


def flip(block):
    return nt(identity(block.shape[1]), block)


def norm_rows(values):
    scale = 1.0 / values.shape[0]
    center = values - jnp.sum(values, axis=0, keepdims=True) * scale
    spread = jnp.sum(center * center, axis=0, keepdims=True) * scale
    return (center * lax.rsqrt(spread + EPSILON)).astype(BF16)


def run(kernel, outs, *args, smem=(), scratch=(), flops=10**7):
    vmem = pl.BlockSpec(memory_space=pltpu.VMEM)
    in_specs = [
        pl.BlockSpec(memory_space=pltpu.SMEM) if at in smem else vmem for at in range(len(args))
    ]
    moved = sum(a.size * a.dtype.itemsize for a in args)
    return pl.pallas_call(
        kernel,
        out_shape=[jax.ShapeDtypeStruct(shape, kind) for shape, kind in outs],
        in_specs=in_specs,
        out_specs=[vmem] * len(outs),
        scratch_shapes=[pltpu.VMEM(shape, kind) for shape, kind in scratch],
        compiler_params=pltpu.CompilerParams(vmem_limit_bytes=VMEM_LIMIT),
        cost_estimate=pl.CostEstimate(flops=flops, bytes_accessed=moved, transcendentals=0),
    )(*args)


VMEM_LIMIT = 20 * 1024 * 1024


def project_kernel(where_ref, feat_ref, weight_ref, mask_ref, present_ref, pay_ref, left_ref, live_ref, turned, packed):
    homologs, rows, _ = feat_ref.shape
    half = weight_ref.shape[1] // 2
    quarter = half // 2
    values = feat_ref[...].astype(F32).reshape(homologs * rows, feat_ref.shape[2])
    center = values - jnp.mean(values, axis=1, keepdims=True)
    spread = jnp.mean(center * center, axis=1, keepdims=True)
    normed = (center * lax.rsqrt(spread + EPSILON)).astype(BF16)
    total = homologs * rows
    out_row = lax.broadcasted_iota(jnp.int32, (total, total), 0)
    in_row = lax.broadcasted_iota(jnp.int32, (total, total), 1)
    order = in_row == (out_row & (homologs - 1)) * rows + out_row // homologs
    normed = nn(order.astype(F32).astype(BF16), normed).astype(BF16)
    seq = lax.broadcasted_iota(jnp.int32, (homologs, 2 * homologs), 0)
    lane = lax.broadcasted_iota(jnp.int32, (homologs, 2 * homologs), 1)
    twice = (seq == (lane & (homologs - 1))).astype(F32).astype(BF16)
    live = tn(mask_ref[...], twice)
    cols = present_ref.shape[1]
    here = lax.broadcasted_iota(jnp.int32, (rows, cols), 1) == (
        lax.broadcasted_iota(jnp.int32, (rows, cols), 0) + where_ref[0]
    )
    present = jnp.sum(jnp.where(here, present_ref[...].astype(F32), 0.0), axis=1, keepdims=True)
    live = live * present
    weight = flip(weight_ref[...]).astype(BF16)
    blank = jnp.zeros((homologs, normed.shape[1]), BF16)
    for row in range(rows):
        mine = normed[row * homologs : (row + 1) * homologs]
        low = nt(weight, jnp.concatenate([mine, blank], axis=0)) * live[row : row + 1]
        high = nt(weight, jnp.concatenate([blank, mine], axis=0)) * live[row : row + 1]
        left_ref[row * half : (row + 1) * half] = low[:half].astype(BF16)
        left_ref[(rows + row) * half : (rows + row + 1) * half] = high[:half].astype(BF16)
        turned[row] = low[half : half + quarter] + high[half + quarter :]
    for pair in range(quarter):
        packed[pair * rows : (pair + 1) * rows] = turned[:, pair, :]
    packed[quarter * rows : (quarter + 1) * rows] = live
    packed[(quarter + 1) * rows :] = jnp.zeros((rows, 2 * homologs), F32)
    pay_ref[...] = packed[...].astype(BF16)
    live_ref[...] = jnp.where(lax.broadcasted_iota(jnp.int32, live.shape, 1) < homologs, live, 0.0)


def prep_kernel(
    where_ref, chain_ref, chains_ref, pair_ref, table_ref, outer_ref, proj_ref, out_ref,
    base_ref, outer_t_ref, proj_t_ref, out_t_ref, table_pad, outer_pad,
):
    rows, cols, width = pair_ref.shape
    bins = table_ref.shape[0]
    table_pad[...] = jnp.zeros_like(table_pad)
    table_pad[0:bins, :] = table_ref[...].astype(F32)
    table = flip(table_pad[...].astype(BF16)).astype(BF16)
    chains = chains_ref[...]
    col = lax.broadcasted_iota(jnp.int32, (1, cols), 1)
    slot = lax.broadcasted_iota(jnp.int32, (table_pad.shape[0], cols), 0)
    for row in range(rows):
        place = where_ref[0] + row
        offset = jnp.clip(place - col, -RELMAX, RELMAX) + RELMAX
        bin_index = jnp.where(chains == chain_ref[place], offset, 2 * RELMAX + 1)
        hot = (slot == bin_index).astype(F32).astype(BF16)
        base_ref[row] = flip(pair_ref[row]) + nn(table, hot)
    half = outer_pad.shape[0]
    outer_pad[...] = outer_ref[...].astype(F32).reshape(outer_pad.shape)
    for d in range(half):
        outer_t_ref[:, d * half : (d + 1) * half] = flip(outer_pad[:, d, :].astype(BF16)).astype(BF16)
    for turn in range(2):
        proj_t_ref[turn] = tn(proj_ref[turn], identity(width)).astype(BF16)
        out_t_ref[turn] = flip(out_ref[turn]).astype(BF16)


def sides(normed, weight, live):
    width = normed.shape[0]
    made = nn(weight, normed)
    part = [made[at * width : (at + 1) * width] for at in range(5)]
    left = jax.nn.sigmoid(part[0]) * part[1] * live
    right = jax.nn.sigmoid(part[2]) * part[3] * live
    return left, right, jax.nn.sigmoid(part[4])


def outer_kernel(
    where_ref, flag_ref, own_ref, other_ref, left_ref, live_ref, base_ref, outer_t_ref, proj_ref, present_ref,
    stream_ref, gate_ref, both0, both1, both2, both3, far0, far1, far2, far3, came, outer, lefts, rights,
):
    rows, width, cols = base_ref.shape
    chip, core = where_ref[1], where_ref[2]
    per = own_ref.shape[1]
    chips = own_ref.shape[0]
    for at in range(chips):
        chip_at = chip ^ ((at % 4) * 2 + at // 4)
        came[chip_at * 2 + core] = own_ref[at].astype(F32)
        came[chip_at * 2 + (1 - core)] = other_ref[at].astype(F32)
    half = left_ref.shape[0] // (2 * rows)
    quarter = half // 2
    live_all = came[:, quarter * rows : (quarter + 1) * rows, :].reshape(cols, per_lane(came)).astype(BF16)
    counts = nt(live_ref[...].astype(BF16), live_all)
    share = 1.0 / jnp.maximum(counts, 1.0)
    left_all = left_ref[...]
    for pair in range(quarter):
        right = came[:, pair * rows : (pair + 1) * rows, :].reshape(cols, per_lane(came)).astype(BF16)
        made = nt(left_all, right).astype(BF16)
        for part in range(2):
            d = part * quarter + pair
            for row in range(rows):
                first = (part * rows + row) * half
                outer[row, d * half : (d + 1) * half, :] = made[first : first + half]
    present = present_ref[...].astype(F32)
    for row in range(rows):
        stream = base_ref[row] + nn(outer_t_ref[...], outer[row]) * share[row : row + 1]
        stream_ref[row] = stream
        live = present * flag_ref[where_ref[0] + row].astype(F32)
        left, right, gate = sides(norm_rows(stream), proj_ref[0], live)
        gate_ref[row] = gate
        lefts[:, row, :] = left
        rights[:, row, :] = right
    groups = 4
    size = width // groups
    for step, (near, far) in enumerate(((both0, far0), (both1, far1), (both2, far2), (both3, far3))):
        group = (chip & (groups - 1)) ^ step
        block = rights[pl.ds(group * size, size)].reshape(size * rows, cols).astype(BF16)
        far[...] = block
        near[size * rows :] = block
        near[0 : size * rows] = lefts[pl.ds(group * size, size)].reshape(size * rows, cols).astype(BF16)


def per_lane(ref):
    return ref.shape[-1]


def mix_rows_kernel(
    where_ref, both0, both1, both2, both3, far4, far5, far6, far7, other_ref,
    out0, out1, out2, out3, lefts, rights, mixed,
):
    chip, core = where_ref[1], where_ref[2]
    count, rows, cols = lefts.shape[1:]
    block = count * rows
    nears = (both0, both1, both2, both3)
    fars = (far4, far5, far6, far7)
    for step in range(8):
        mine = (nears[step][block:] if step < 4 else fars[step - 4][...]).astype(F32)
        rights[(chip ^ step) * 2 + core] = mine.reshape(count, rows, cols)
        rights[(chip ^ step) * 2 + (1 - core)] = other_ref[step].astype(F32).reshape(count, rows, cols)
        if step < 4:
            lefts[step] = nears[step][0:block].astype(F32).reshape(count, rows, cols)
    for c in range(count):
        left = lefts[:, c].reshape(4 * rows, cols).astype(BF16)
        right = rights[:, c].reshape(16 * rows, cols).astype(BF16)
        mixed[:, c, :] = nt(left, right)
    for step, out in enumerate((out0, out1, out2, out3)):
        out[...] = mixed[step * rows : (step + 1) * rows].reshape(block, cols).astype(BF16)


def update(came, row, stream, gate, out_weight):
    mixed = came[row]
    mixed = mixed.reshape(mixed.shape[0] * mixed.shape[1], mixed.shape[2])
    return stream + gate * nn(out_weight, norm_rows(mixed))


def between_kernel(
    where_ref, flag_ref, in0, in1, in2, in3, stream_ref, gate_ref, out_weight_ref, proj_ref, present_ref,
    next_ref, next_gate_ref, b0, b1, b2, b3, b4, b5, b6, b7, came, lefts, rights,
):
    rows, width, cols = stream_ref.shape
    chip = where_ref[1]
    groups = 4
    for step, block in enumerate((in0, in1, in2, in3)):
        came[:, (chip & (groups - 1)) ^ step] = block[...].astype(F32).reshape(rows, width // groups, cols)
    present = present_ref[...].astype(F32)
    for row in range(rows):
        stream = update(came, row, stream_ref[row], gate_ref[row], out_weight_ref[0])
        next_ref[row] = stream
        live = present * flag_ref[where_ref[0] + row].astype(F32)
        left, right, gate = sides(norm_rows(stream), proj_ref[1], live)
        next_gate_ref[row] = gate
        lefts[:, row, :] = left
        rights[:, row, :] = right
    outs = (b0, b1, b2, b3, b4, b5, b6, b7)
    size = width // len(outs)
    for step, out in enumerate(outs):
        first = (chip ^ step) * size
        out[0 : size * rows] = lefts[pl.ds(first, size)].reshape(size * rows, cols).astype(BF16)
        out[size * rows :] = rights[pl.ds(first, size)].reshape(size * rows, cols).astype(BF16)


def mix_cols_kernel(where_ref, b0, b1, b2, b3, b4, b5, b6, b7, mine_ref, theirs_ref, lefts, rights, partial):
    chip, core = where_ref[1], where_ref[2]
    chips, count, rows, cols = lefts.shape
    block = count * rows
    for step, came in enumerate((b0, b1, b2, b3, b4, b5, b6, b7)):
        lefts[step] = came[0:block].astype(F32).reshape(count, rows, cols)
        rights[step] = came[block:].astype(F32).reshape(count, rows, cols)
    for c in range(count):
        left = lefts[:, c].reshape(chips * rows, cols).astype(BF16)
        right = rights[:, c].reshape(chips * rows, cols).astype(BF16)
        partial[:, c, :] = tn(left, right)
    for step in range(chips):
        at = (chip ^ step) * 2
        mine_ref[step] = partial[pl.ds((at + core) * rows, rows)].reshape(block, cols)
        theirs_ref[step] = partial[pl.ds((at + 1 - core) * rows, rows)].reshape(block, cols)


def sum_kernel(mine_ref, got_ref, *outs):
    for step, out in enumerate(outs):
        out[...] = (mine_ref[step] + got_ref[step]).astype(BF16)


def final_kernel(
    where_ref, b0, b1, b2, b3, b4, b5, b6, b7, stream_ref, gate_ref, out_weight_ref, out_ref, came
):
    rows, width, cols = stream_ref.shape
    chip = where_ref[1]
    blocks = (b0, b1, b2, b3, b4, b5, b6, b7)
    for step, block in enumerate(blocks):
        came[:, chip ^ step] = block[...].astype(F32).reshape(rows, width // len(blocks), cols)
    for row in range(rows):
        stream = update(came, row, stream_ref[row], gate_ref[row], out_weight_ref[1])
        out_ref[row] = flip_out(stream)


def flip_out(stream):
    return nt(identity(stream.shape[1]), stream.astype(BF16)).astype(BF16)


def chip_permute(block, step):
    count = lax.axis_size("wide")
    return lax.ppermute(block, "wide", [(w, w ^ (2 * step)) for w in range(count)])


def core_permute(block):
    count = lax.axis_size("wide")
    return lax.ppermute(block, "wide", [(w, w ^ 1) for w in range(count)])


def per_device_chips(
    pairwise_state,
    homolog_features,
    residue_chain_index,
    resolved_residue_mask,
    alignment_mask,
    relative_offset_table,
    homolog_to_sides_matrix,
    outer_mean_output_weight,
    triangle_projection_weight,
    triangle_output_weight,
):
    rows, cols, width = pairwise_state.shape
    homologs = homolog_features.shape[0]
    half = homolog_to_sides_matrix.shape[1] // 2
    device = lax.axis_index("wide")
    chip, core = device // 2, device % 2
    where = jnp.stack([device * rows, chip, core]).astype(jnp.int32)
    present = resolved_residue_mask.reshape(1, cols)
    pay_rows = (half // 2 + 2) * rows
    pay, left, live = run(
        project_kernel,
        [((pay_rows, LANES), BF16), ((2 * rows * half, LANES), BF16), ((rows, LANES), F32)],
        where, homolog_features, homolog_to_sides_matrix, alignment_mask, present,
        smem=(0,),
        scratch=[((rows, half // 2, LANES), F32), ((pay_rows, LANES), F32)],
    )
    along_z = [chip_permute(pay, 2 * z) for z in (2, 3, 1)]
    base, outer_t, proj_t, out_t = run(
        prep_kernel,
        [
            ((rows, width, cols), F32),
            ((width, half * half), BF16),
            ((2, triangle_projection_weight.shape[2], width), BF16),
            ((2, width, width), BF16),
        ],
        where, residue_chain_index, residue_chain_index.reshape(1, cols), pairwise_state,
        relative_offset_table, outer_mean_output_weight, triangle_projection_weight, triangle_output_weight,
        smem=(0, 1),
        scratch=[((LANES, width), F32), ((half, half, width), F32)],
    )
    along_z = jnp.stack([pay, along_z[2], along_z[0], along_z[1]])
    own = jnp.concatenate([along_z, chip_permute(along_z, 1)], axis=0)
    other = core_permute(own)
    tall = width * rows
    made = run(
        outer_kernel,
        [((rows, width, cols), F32)] * 2
        + [((tall // 2, cols), BF16)] * 4
        + [((tall // 4, cols), BF16)] * 4,
        where, resolved_residue_mask, own, other, left, live, base, outer_t, proj_t, present,
        smem=(0, 1),
        scratch=[
            ((16, pay_rows, LANES), F32),
            ((rows, half * half, cols), BF16),
            ((width, rows, cols), F32),
            ((width, rows, cols), F32),
        ],
        flops=4 * 10**8,
    )
    stream, gate, both, far = made[0], made[1], made[2:6], made[6:10]
    far = [chip_permute(far[step], step + 4) for step in (3, 2, 1, 0)][::-1]
    near = [chip_permute(both[step], step) for step in (3, 2, 1)][::-1]
    rights = jnp.stack([b[tall // 4 :] for b in [both[0]] + near] + far)
    rights = core_permute(rights)
    mixed = run(
        mix_rows_kernel,
        [((tall // 4, cols), BF16)] * 4,
        where, both[0], *near, *far, rights,
        smem=(0,),
        scratch=[
            ((4, width // 4, rows, cols), F32),
            ((16, width // 4, rows, cols), F32),
            ((4 * rows, width // 4, cols), F32),
        ],
    )
    mixed = [mixed[0]] + [chip_permute(mixed[step], step) for step in (3, 2, 1)][::-1]
    made = run(
        between_kernel,
        [((rows, width, cols), F32)] * 2 + [((tall // 4, cols), BF16)] * 8,
        where, resolved_residue_mask, *mixed, stream, gate, out_t, proj_t, present,
        smem=(0, 1),
        scratch=[
            ((rows, 4, width // 4, cols), F32),
            ((width, rows, cols), F32),
            ((width, rows, cols), F32),
        ],
    )
    stream, gate, both = made[0], made[1], made[2:]
    came = [both[0]] + [chip_permute(both[step], step) for step in range(7, 0, -1)][::-1]
    mine, theirs = run(
        mix_cols_kernel,
        [((8, tall // 8, cols), F32)] * 2,
        where, *came,
        smem=(0,),
        scratch=[
            ((8, width // 8, rows, cols), F32),
            ((8, width // 8, rows, cols), F32),
            ((16 * rows, width // 8, cols), F32),
        ],
    )
    mixed = run(sum_kernel, [((tall // 8, cols), BF16)] * 8, mine, core_permute(theirs))
    mixed = [mixed[0]] + [chip_permute(mixed[step], step) for step in range(7, 0, -1)][::-1]
    return run(
        final_kernel,
        [((rows, cols, width), BF16)],
        where, *mixed, stream, gate, out_t,
        smem=(0,),
        scratch=[((rows, 8, width // 8, cols), F32)],
    )[0]


def fits_chips(mesh):
    return mesh.shape["narrow"] == 1 and mesh.shape["wide"] == 16


def solution(mesh):
    per_device = per_device_chips if fits_chips(mesh) else per_device_general
    return jax.shard_map(
        per_device,
        mesh=mesh,
        in_specs=(
            P(("grp", "wide"), "narrow", None),
            P("grp", "wide", None),
            P("grp"),
            P("grp"),
            P("grp", "wide"),
            P(),
            P(),
            P(),
            P(),
            P(),
        ),
        out_specs=P(("grp", "wide"), "narrow", None),
        check_vma=False,
    )
```

```python
import functools

import jax
import jax.numpy as jnp
from jax import lax
from jax.experimental import pallas as pl
from jax.experimental.pallas import tpu as pltpu
from jax.sharding import PartitionSpec as P

RELMAX = 32
EPSILON = 1e-05
LANES = 128
F32 = jnp.float32
BF16 = jnp.bfloat16


def apply_layer_norm(values, axis_dim):
    center = values - jnp.mean(values, axis=axis_dim, keepdims=True)
    spread = jnp.mean(center * center, axis=axis_dim, keepdims=True)
    return center * lax.rsqrt(spread + EPSILON)


def gather_wide(block):
    n = lax.axis_size("wide")
    if n % 4 or n < 8:
        return lax.all_gather(block, "wide", axis=0)
    outer = n // 4
    me = lax.axis_index("wide")
    high, mid, low = me // 4, (me // 2) % 2, me % 2
    arrived = [block]
    for shift in range(1, outer):
        perm = [(w, ((w // 4 + shift) % outer) * 4 + w % 4) for w in range(n)]
        arrived.append(lax.ppermute(block, "wide", perm))
    held = jnp.zeros((outer,) + block.shape, block.dtype)
    for shift, piece in enumerate(arrived):
        held = lax.dynamic_update_index_in_dim(held, piece, (high - shift + outer) % outer, 0)
    other = lax.ppermute(held, "wide", [(w, w ^ 2) for w in range(n)])
    held = jnp.stack(
        [jnp.where(mid == 0, held, other), jnp.where(mid == 0, other, held)], axis=1
    )
    other = lax.ppermute(held, "wide", [(w, w ^ 1) for w in range(n)])
    held = jnp.stack(
        [jnp.where(low == 0, held, other), jnp.where(low == 0, other, held)], axis=2
    )
    return held.reshape((n,) + block.shape)


def triangle(stream, pair_live, proj_weight, out_weight, incoming):
    rows = stream.shape[0]
    cols = stream.shape[1]
    width = out_weight.shape[0]
    wide_count = lax.axis_size("wide")
    core_count = lax.axis_size("narrow")
    devices = wide_count * core_count
    per_dev = width // devices
    normed = apply_layer_norm(stream, 2).astype(jnp.bfloat16)
    blocks = [proj_weight[:, index * width : (index + 1) * width] for index in range(4)]

    def project(block):
        return jnp.einsum("ijd,dc->cij", normed, block, preferred_element_type=jnp.float32)

    left_side = (jax.nn.sigmoid(project(blocks[0])) * project(blocks[1]) * pair_live[None]).astype(
        jnp.bfloat16
    )
    right_side = (jax.nn.sigmoid(project(blocks[2])) * project(blocks[3]) * pair_live[None]).astype(
        jnp.bfloat16
    )
    gate = jax.nn.sigmoid(
        jnp.einsum(
            "ijd,dc->ijc", normed, proj_weight[:, 4 * width :], preferred_element_type=jnp.float32
        )
    )
    form = "cki,ckj->cij" if incoming else "cik,cjk->cij"
    both = jnp.stack(
        [
            left_side.reshape(devices, per_dev, rows * cols),
            right_side.reshape(devices, per_dev, rows * cols),
        ],
        axis=1,
    ).reshape(devices, 2 * per_dev, rows * cols)
    both = lax.all_to_all(both, ("wide", "narrow"), split_axis=0, concat_axis=0, tiled=True)
    both = both.reshape(wide_count, core_count, 2, per_dev, rows, cols)
    both = jnp.transpose(both, (2, 3, 0, 4, 1, 5)).reshape(
        2, per_dev, wide_count * rows, core_count * cols
    )
    mixed = jnp.einsum(form, both[0], both[1], preferred_element_type=jnp.float32).astype(
        jnp.bfloat16
    )
    spread_out = mixed.reshape(per_dev, wide_count, rows, core_count, cols)
    spread_out = jnp.transpose(spread_out, (1, 3, 0, 2, 4)).reshape(
        wide_count * core_count * per_dev, rows * cols
    )
    returned = lax.all_to_all(
        spread_out, ("wide", "narrow"), split_axis=0, concat_axis=0, tiled=True
    ).reshape(width, rows, cols)
    blended_standardize = apply_layer_norm(returned.astype(jnp.float32), 0).astype(jnp.bfloat16)
    update = jnp.einsum(
        "cij,cd->ijd", blended_standardize, out_weight, preferred_element_type=jnp.float32
    )
    return stream + gate * update


def per_device_general(
    pairwise_state,
    homolog_features,
    residue_chain_index,
    resolved_residue_mask,
    alignment_mask,
    relative_offset_table,
    homolog_to_sides_matrix,
    outer_mean_output_weight,
    triangle_projection_weight,
    triangle_output_weight,
):
    rows = pairwise_state.shape[0]
    cols = pairwise_state.shape[1]
    row_start = lax.axis_index("wide") * rows
    col_start = lax.axis_index("narrow") * cols
    residue_present = resolved_residue_mask.astype(jnp.float32)
    row_present = lax.dynamic_slice_in_dim(residue_present, row_start, rows)
    col_live = lax.dynamic_slice_in_dim(residue_present, col_start, cols)
    present_flags = alignment_mask.astype(jnp.float32) * row_present[None, :]
    alignment_normed = apply_layer_norm(homolog_features.astype(jnp.float32), 2).astype(
        jnp.bfloat16
    )
    projected_rows = jnp.einsum(
        "tna,ak->tnk", alignment_normed, homolog_to_sides_matrix, preferred_element_type=jnp.float32
    )
    projected_rows = (projected_rows * present_flags[:, :, None]).astype(jnp.bfloat16)
    half_width = projected_rows.shape[2] // 2
    homologs = projected_rows.shape[0]
    left_proj = projected_rows[:, :, :half_width]
    right_proj = projected_rows[:, :, half_width:]
    live_flags = present_flags.astype(jnp.bfloat16)
    packed = jnp.concatenate(
        [jnp.transpose(right_proj, (1, 0, 2)).reshape(rows, homologs * half_width), live_flags.T],
        axis=1,
    )
    gathered = gather_wide(packed).reshape(-1, packed.shape[1])
    gathered = lax.dynamic_slice_in_dim(gathered, col_start, cols, 0)
    right_mine = jnp.transpose(
        gathered[:, : homologs * half_width].reshape(cols, homologs, half_width), (1, 0, 2)
    )
    live_mine = gathered[:, homologs * half_width :].T
    counts = jnp.dot(live_flags.T, live_mine, preferred_element_type=jnp.float32)

    def opm_row(left_row):
        outer = jnp.einsum("sc,sjd->jcd", left_row, right_mine, preferred_element_type=jnp.float32)
        outer = outer.reshape(cols, half_width * half_width).astype(jnp.bfloat16)
        return jnp.dot(outer, outer_mean_output_weight, preferred_element_type=jnp.float32)

    opm = lax.map(opm_row, jnp.transpose(left_proj, (1, 0, 2)))
    row_pos = row_start + jnp.arange(rows, dtype=jnp.int32)
    col_pos = col_start + jnp.arange(cols, dtype=jnp.int32)
    row_chain = lax.dynamic_slice_in_dim(residue_chain_index, row_start, rows)
    col_chain = lax.dynamic_slice_in_dim(residue_chain_index, col_start, cols)
    offset = jnp.clip(row_pos[:, None] - col_pos[None, :], -RELMAX, RELMAX) + RELMAX
    bin_index = jnp.where(row_chain[:, None] == col_chain[None, :], offset, 2 * RELMAX + 1)
    bin_count = relative_offset_table.shape[0]
    one_hot = (
        bin_index[:, :, None] == jnp.arange(bin_count, dtype=jnp.int32)[None, None, :]
    ).astype(jnp.bfloat16)
    relpos = jnp.einsum(
        "ijb,bc->ijc", one_hot, relative_offset_table, preferred_element_type=jnp.float32
    )
    stream = (
        pairwise_state.astype(jnp.float32) + relpos + opm / jnp.maximum(counts, 1.0)[:, :, None]
    )
    pair_live = row_present[:, None] * col_live[None, :]
    for turn_index in range(2):
        stream = triangle(
            stream,
            pair_live,
            triangle_projection_weight[turn_index],
            triangle_output_weight[turn_index],
            turn_index == 1,
        )
    return stream.astype(jnp.bfloat16)


def nn(a, b):
    return lax.dot_general(a, b, (((1,), (0,)), ((), ())), preferred_element_type=F32)


def nt(a, b):
    return lax.dot_general(a, b, (((1,), (1,)), ((), ())), preferred_element_type=F32)


def tn(a, b):
    return lax.dot_general(a, b, (((0,), (0,)), ((), ())), preferred_element_type=F32)


def identity(size):
    rows = lax.broadcasted_iota(jnp.int32, (size, size), 0)
    cols = lax.broadcasted_iota(jnp.int32, (size, size), 1)
    return (rows == cols).astype(F32).astype(BF16)


def flip(block):
    return nt(identity(block.shape[1]), block)


def norm_rows(values):
    scale = 1.0 / values.shape[0]
    center = values - jnp.sum(values, axis=0, keepdims=True) * scale
    spread = jnp.sum(center * center, axis=0, keepdims=True) * scale
    return (center * lax.rsqrt(spread + EPSILON)).astype(BF16)


def run(kernel, outs, *args, smem=(), hbm=(), scratch=(), flops=10**7, sems=0, limit=None):
    vmem = pl.BlockSpec(memory_space=pltpu.VMEM)
    in_specs = [
        pl.BlockSpec(memory_space=pltpu.SMEM if at in smem else pltpu.HBM if at in hbm else pltpu.VMEM)
        for at in range(len(args))
    ]
    semaphores = [pltpu.SemaphoreType.DMA((sems,))] if sems else []
    moved = sum(a.size * a.dtype.itemsize for a in args)
    return pl.pallas_call(
        kernel,
        out_shape=[jax.ShapeDtypeStruct(shape, kind) for shape, kind in outs],
        in_specs=in_specs,
        out_specs=[vmem] * len(outs),
        scratch_shapes=[pltpu.VMEM(shape, kind) for shape, kind in scratch] + semaphores,
        compiler_params=pltpu.CompilerParams(vmem_limit_bytes=limit or VMEM_LIMIT),
        cost_estimate=pl.CostEstimate(flops=flops, bytes_accessed=moved, transcendentals=0),
    )(*args)


VMEM_LIMIT = 20 * 1024 * 1024


def project_kernel(
    where_ref, feat_hbm, weight_hbm, mask_hbm, present_hbm, pay_ref, left_ref, live_ref,
    turned, packed, feat_ref, weight_ref, mask_ref, present_ref, sems,
):
    pairs = ((feat_hbm, feat_ref), (weight_hbm, weight_ref), (mask_hbm, mask_ref), (present_hbm, present_ref))
    copies = [pltpu.make_async_copy(a, b, sems.at[at]) for at, (a, b) in enumerate(pairs)]
    for copy in copies:
        copy.start()
    for copy in copies:
        copy.wait()
    homologs, rows, _ = feat_ref.shape
    half = weight_ref.shape[0] // 2
    quarter = half // 2
    values = feat_ref[...].astype(F32).reshape(homologs * rows, feat_ref.shape[2])
    center = values - jnp.mean(values, axis=1, keepdims=True)
    spread = jnp.mean(center * center, axis=1, keepdims=True)
    normed = (center * lax.rsqrt(spread + EPSILON)).astype(BF16)
    total = homologs * rows
    out_row = lax.broadcasted_iota(jnp.int32, (total, total), 0)
    in_row = lax.broadcasted_iota(jnp.int32, (total, total), 1)
    order = in_row == (out_row & (homologs - 1)) * rows + out_row // homologs
    normed = nn(order.astype(F32).astype(BF16), normed).astype(BF16)
    seq = lax.broadcasted_iota(jnp.int32, (homologs, 2 * homologs), 0)
    lane = lax.broadcasted_iota(jnp.int32, (homologs, 2 * homologs), 1)
    twice = (seq == (lane & (homologs - 1))).astype(F32).astype(BF16)
    live = nn(mask_ref[...], twice)
    cols = present_ref.shape[1]
    here = lax.broadcasted_iota(jnp.int32, (rows, cols), 1) == (
        lax.broadcasted_iota(jnp.int32, (rows, cols), 0) + where_ref[0]
    )
    present = jnp.sum(jnp.where(here, present_ref[...].astype(F32), 0.0), axis=1, keepdims=True)
    live = live * present
    weight = weight_ref[...]
    blank = jnp.zeros((homologs, normed.shape[1]), BF16)
    for row in range(rows):
        mine = normed[row * homologs : (row + 1) * homologs]
        low = nt(weight, jnp.concatenate([mine, blank], axis=0)) * live[row : row + 1]
        high = nt(weight, jnp.concatenate([blank, mine], axis=0)) * live[row : row + 1]
        left_ref[row * half : (row + 1) * half] = low[:half].astype(BF16)
        left_ref[(rows + row) * half : (rows + row + 1) * half] = high[:half].astype(BF16)
        turned[row] = low[half : half + quarter] + high[half + quarter :]
    for pair in range(quarter):
        packed[pair * rows : (pair + 1) * rows] = turned[:, pair, :]
    packed[quarter * rows : (quarter + 1) * rows] = live
    packed[(quarter + 1) * rows :] = jnp.zeros((rows, 2 * homologs), F32)
    pay_ref[...] = packed[...].astype(BF16)
    live_ref[...] = jnp.where(lax.broadcasted_iota(jnp.int32, live.shape, 1) < homologs, live, 0.0)


def prep_kernel(
    where_ref, chain_ref, chains_ref, pair_ref, table_ref, outer_ref, proj_ref, out_ref,
    base_ref, outer_t_ref, proj_t_ref, out_t_ref, table_pad, outer_pad,
):
    rows, cols, width = pair_ref.shape
    bins = table_ref.shape[0]
    table_pad[...] = jnp.zeros_like(table_pad)
    table_pad[0:bins, :] = table_ref[...].astype(F32)
    table = flip(table_pad[...].astype(BF16)).astype(BF16)
    chains = chains_ref[...]
    col = lax.broadcasted_iota(jnp.int32, (1, cols), 1)
    slot = lax.broadcasted_iota(jnp.int32, (table_pad.shape[0], cols), 0)
    for row in range(rows):
        place = where_ref[0] + row
        offset = jnp.clip(place - col, -RELMAX, RELMAX) + RELMAX
        bin_index = jnp.where(chains == chain_ref[place], offset, 2 * RELMAX + 1)
        hot = (slot == bin_index).astype(F32).astype(BF16)
        base_ref[row] = flip(pair_ref[row]) + nn(table, hot)
    half = outer_pad.shape[0]
    outer_pad[...] = outer_ref[...].astype(F32).reshape(outer_pad.shape)
    for d in range(half):
        outer_t_ref[:, d * half : (d + 1) * half] = flip(outer_pad[:, d, :].astype(BF16)).astype(BF16)
    for turn in range(2):
        proj_t_ref[turn] = tn(proj_ref[turn], identity(width)).astype(BF16)
        out_t_ref[turn] = flip(out_ref[turn]).astype(BF16)


def sides(normed, weight, live):
    width = normed.shape[0]
    made = nn(weight, normed)
    part = [made[at * width : (at + 1) * width] for at in range(5)]
    left = jax.nn.sigmoid(part[0]) * part[1] * live
    right = jax.nn.sigmoid(part[2]) * part[3] * live
    return left, right, jax.nn.sigmoid(part[4])


def outer_kernel(
    where_ref, flag_ref, own_ref, other_ref, left_ref, live_ref, base_ref, outer_t_ref, proj_ref, present_ref,
    stream_ref, gate_ref, both0, both1, both2, both3, far0, far1, far2, far3, came, outer, lefts, rights,
):
    rows, width, cols = base_ref.shape
    chip, core = where_ref[1], where_ref[2]
    per = own_ref.shape[1]
    chips = own_ref.shape[0]
    for at in range(chips):
        chip_at = chip ^ ((3 - at % 4) * 2 + at // 4)
        came[chip_at * 2 + core] = own_ref[at].astype(F32)
        came[chip_at * 2 + (1 - core)] = other_ref[at].astype(F32)
    half = left_ref.shape[0] // (2 * rows)
    quarter = half // 2
    live_all = came[:, quarter * rows : (quarter + 1) * rows, :].reshape(cols, per_lane(came)).astype(BF16)
    counts = nt(live_ref[...].astype(BF16), live_all)
    share = 1.0 / jnp.maximum(counts, 1.0)
    left_all = left_ref[...]
    for pair in range(quarter):
        right = came[:, pair * rows : (pair + 1) * rows, :].reshape(cols, per_lane(came)).astype(BF16)
        made = nt(left_all, right).astype(BF16)
        for part in range(2):
            d = part * quarter + pair
            for row in range(rows):
                first = (part * rows + row) * half
                outer[row, d * half : (d + 1) * half, :] = made[first : first + half]
    present = present_ref[...].astype(F32)
    for row in range(rows):
        stream = base_ref[row] + nn(outer_t_ref[...], outer[row]) * share[row : row + 1]
        stream_ref[row] = stream
        live = present * flag_ref[where_ref[0] + row].astype(F32)
        left, right, gate = sides(norm_rows(stream), proj_ref[0], live)
        gate_ref[row] = gate
        lefts[:, row, :] = left
        rights[:, row, :] = right
    groups = 4
    size = width // groups
    for step, (near, far) in enumerate(((both0, far0), (both1, far1), (both2, far2), (both3, far3))):
        group = (chip & (groups - 1)) ^ step
        block = rights[pl.ds(group * size, size)].reshape(size * rows, cols).astype(BF16)
        far[...] = block
        near[size * rows :] = block
        near[0 : size * rows] = lefts[pl.ds(group * size, size)].reshape(size * rows, cols).astype(BF16)


def per_lane(ref):
    return ref.shape[-1]


def mix_rows_kernel(
    where_ref, far7, far6, far5, far4, both3, both2, both1, both0, other_ref,
    out0, out1, out2, out3, lefts, rights, mixed,
):
    chip, core = where_ref[1], where_ref[2]
    count, rows, cols = lefts.shape[1:]
    block = count * rows
    nears = (both0, both1, both2, both3)
    fars = (far4, far5, far6, far7)
    for step in range(8):
        mine = (nears[step][block:] if step < 4 else fars[step - 4][...]).astype(F32)
        rights[(chip ^ step) * 2 + core] = mine.reshape(count, rows, cols)
        rights[(chip ^ step) * 2 + (1 - core)] = other_ref[7 - step].astype(F32).reshape(count, rows, cols)
        if step < 4:
            lefts[step] = nears[step][0:block].astype(F32).reshape(count, rows, cols)
    for c in range(count):
        left = lefts[:, c].reshape(4 * rows, cols).astype(BF16)
        right = rights[:, c].reshape(16 * rows, cols).astype(BF16)
        mixed[:, c, :] = nt(left, right)
    for step, out in enumerate((out0, out1, out2, out3)):
        out[...] = mixed[step * rows : (step + 1) * rows].reshape(block, cols).astype(BF16)


def update(came, row, stream, gate, out_weight):
    mixed = came[row]
    mixed = mixed.reshape(mixed.shape[0] * mixed.shape[1], mixed.shape[2])
    return stream + gate * nn(out_weight, norm_rows(mixed))


def between_kernel(
    where_ref, flag_ref, in3, in2, in1, in0, stream_ref, gate_ref, out_weight_ref, proj_ref, present_ref,
    next_ref, next_gate_ref, b0, b1, b2, b3, b4, b5, b6, b7, came, lefts, rights,
):
    rows, width, cols = stream_ref.shape
    chip = where_ref[1]
    groups = 4
    for step, block in enumerate((in0, in1, in2, in3)):
        came[:, (chip & (groups - 1)) ^ step] = block[...].astype(F32).reshape(rows, width // groups, cols)
    present = present_ref[...].astype(F32)
    for row in range(rows):
        stream = update(came, row, stream_ref[row], gate_ref[row], out_weight_ref[0])
        next_ref[row] = stream
        live = present * flag_ref[where_ref[0] + row].astype(F32)
        left, right, gate = sides(norm_rows(stream), proj_ref[1], live)
        next_gate_ref[row] = gate
        lefts[:, row, :] = left
        rights[:, row, :] = right
    outs = (b0, b1, b2, b3, b4, b5, b6, b7)
    size = width // len(outs)
    for step, out in enumerate(outs):
        first = (chip ^ step) * size
        out[0 : size * rows] = lefts[pl.ds(first, size)].reshape(size * rows, cols).astype(BF16)
        out[size * rows :] = rights[pl.ds(first, size)].reshape(size * rows, cols).astype(BF16)


def mix_cols_kernel(where_ref, b7, b6, b5, b4, b3, b2, b1, b0, mine_ref, theirs_ref, lefts, rights, partial):
    chip, core = where_ref[1], where_ref[2]
    chips, count, rows, cols = lefts.shape
    block = count * rows
    for step, came in enumerate((b0, b1, b2, b3, b4, b5, b6, b7)):
        lefts[step] = came[0:block].astype(F32).reshape(count, rows, cols)
        rights[step] = came[block:].astype(F32).reshape(count, rows, cols)
    for c in range(count):
        left = lefts[:, c].reshape(chips * rows, cols).astype(BF16)
        right = rights[:, c].reshape(chips * rows, cols).astype(BF16)
        partial[:, c, :] = tn(left, right)
    for step in range(chips):
        at = (chip ^ step) * 2
        mine_ref[step] = partial[pl.ds((at + core) * rows, rows)].reshape(block, cols)
        theirs_ref[step] = partial[pl.ds((at + 1 - core) * rows, rows)].reshape(block, cols)


def sum_kernel(mine_ref, got_ref, *outs):
    for step, out in enumerate(outs):
        out[...] = (mine_ref[step] + got_ref[step]).astype(BF16)


def final_kernel(
    where_ref, b7, b6, b5, b4, b3, b2, b1, b0, stream_ref, gate_ref, out_weight_ref, out_ref, came
):
    rows, width, cols = stream_ref.shape
    chip = where_ref[1]
    blocks = (b0, b1, b2, b3, b4, b5, b6, b7)
    for step, block in enumerate(blocks):
        came[:, chip ^ step] = block[...].astype(F32).reshape(rows, width // len(blocks), cols)
    for row in range(rows):
        stream = update(came, row, stream_ref[row], gate_ref[row], out_weight_ref[1])
        out_ref[row] = flip_out(stream)


def flip_out(stream):
    return nt(identity(stream.shape[1]), stream.astype(BF16)).astype(BF16)


def chip_permute(block, step):
    count = lax.axis_size("wide")
    return lax.ppermute(block, "wide", [(w, w ^ (2 * step)) for w in range(count)])


def core_permute(block):
    count = lax.axis_size("wide")
    return lax.ppermute(block, "wide", [(w, w ^ 1) for w in range(count)])


def per_device_chips(
    pairwise_state,
    homolog_features,
    residue_chain_index,
    resolved_residue_mask,
    alignment_mask,
    relative_offset_table,
    homolog_to_sides_matrix,
    outer_mean_output_weight,
    triangle_projection_weight,
    triangle_output_weight,
):
    rows, cols, width = pairwise_state.shape
    homologs = homolog_features.shape[0]
    half = homolog_to_sides_matrix.shape[1] // 2
    device = lax.axis_index("wide")
    chip, core = device // 2, device % 2
    where = jnp.stack([device * rows, chip, core]).astype(jnp.int32)
    present = resolved_residue_mask.reshape(1, cols)
    pay_rows = (half // 2 + 2) * rows
    pay, left, live = run(
        project_kernel,
        [((pay_rows, LANES), BF16), ((2 * rows * half, LANES), BF16), ((rows, LANES), F32)],
        where, homolog_features, homolog_to_sides_matrix.T, alignment_mask.T, present,
        smem=(0,),
        hbm=(1, 2, 3, 4),
        scratch=[
            ((rows, half // 2, LANES), F32),
            ((pay_rows, LANES), F32),
            (homolog_features.shape, BF16),
            (homolog_to_sides_matrix.shape[::-1], BF16),
            (alignment_mask.shape[::-1], BF16),
            ((1, cols), jnp.int32),
        ],
        sems=4,
        limit=60 * 1024 * 1024,
    )
    along_z = [chip_permute(pay, 2 * z) for z in (2, 3, 1)]
    base, outer_t, proj_t, out_t = run(
        prep_kernel,
        [
            ((rows, width, cols), F32),
            ((width, half * half), BF16),
            ((2, triangle_projection_weight.shape[2], width), BF16),
            ((2, width, width), BF16),
        ],
        where, residue_chain_index, residue_chain_index.reshape(1, cols), pairwise_state,
        relative_offset_table, outer_mean_output_weight, triangle_projection_weight, triangle_output_weight,
        smem=(0, 1),
        scratch=[((LANES, width), F32), ((half, half, width), F32)],
    )
    along_z = jnp.stack([along_z[1], along_z[0], along_z[2], pay])
    along_z, base, outer_t, proj_t, out_t = lax.optimization_barrier((along_z, base, outer_t, proj_t, out_t))
    own = jnp.concatenate([along_z, chip_permute(along_z, 1)], axis=0)
    other = core_permute(own)
    tall = width * rows
    made = run(
        outer_kernel,
        [((rows, width, cols), F32)] * 2
        + [((tall // 2, cols), BF16)] * 4
        + [((tall // 4, cols), BF16)] * 4,
        where, resolved_residue_mask, own, other, left, live, base, outer_t, proj_t, present,
        smem=(0, 1),
        scratch=[
            ((16, pay_rows, LANES), F32),
            ((rows, half * half, cols), BF16),
            ((width, rows, cols), F32),
            ((width, rows, cols), F32),
        ],
        flops=4 * 10**8,
    )
    stream, gate, both, far = made[0], made[1], made[2:6], made[6:10]
    far = [chip_permute(far[step], step + 4) for step in (3, 2, 1, 0)][::-1]
    near = [chip_permute(both[step], step) for step in (3, 2, 1)][::-1]
    rights = jnp.stack(far[::-1] + [b[tall // 4 :] for b in near[::-1] + [both[0]]])
    rights = core_permute(rights)
    mixed = run(
        mix_rows_kernel,
        [((tall // 4, cols), BF16)] * 4,
        where, *far[::-1], *near[::-1], both[0], rights,
        smem=(0,),
        scratch=[
            ((4, width // 4, rows, cols), F32),
            ((16, width // 4, rows, cols), F32),
            ((4 * rows, width // 4, cols), F32),
        ],
    )
    mixed = [mixed[0]] + [chip_permute(mixed[step], step) for step in (3, 2, 1)][::-1]
    made = run(
        between_kernel,
        [((rows, width, cols), F32)] * 2 + [((tall // 4, cols), BF16)] * 8,
        where, resolved_residue_mask, *mixed[::-1], stream, gate, out_t, proj_t, present,
        smem=(0, 1),
        scratch=[
            ((rows, 4, width // 4, cols), F32),
            ((width, rows, cols), F32),
            ((width, rows, cols), F32),
        ],
    )
    stream, gate, both = made[0], made[1], made[2:]
    came = [both[0]] + [chip_permute(both[step], step) for step in range(7, 0, -1)][::-1]
    mine, theirs = run(
        mix_cols_kernel,
        [((8, tall // 8, cols), F32)] * 2,
        where, *came[::-1],
        smem=(0,),
        scratch=[
            ((8, width // 8, rows, cols), F32),
            ((8, width // 8, rows, cols), F32),
            ((16 * rows, width // 8, cols), F32),
        ],
    )
    mixed = run(sum_kernel, [((tall // 8, cols), BF16)] * 8, mine, core_permute(theirs))
    mixed = [mixed[0]] + [chip_permute(mixed[step], step) for step in range(7, 0, -1)][::-1]
    return run(
        final_kernel,
        [((rows, cols, width), BF16)],
        where, *mixed[::-1], stream, gate, out_t,
        smem=(0,),
        scratch=[((rows, 8, width // 8, cols), F32)],
    )[0]


def fits_chips(mesh):
    return mesh.shape["narrow"] == 1 and mesh.shape["wide"] == 16


def solution(mesh):
    per_device = per_device_chips if fits_chips(mesh) else per_device_general
    return jax.shard_map(
        per_device,
        mesh=mesh,
        in_specs=(
            P(("grp", "wide"), "narrow", None),
            P("grp", "wide", None),
            P("grp"),
            P("grp"),
            P("grp", "wide"),
            P(),
            P(),
            P(),
            P(),
            P(),
        ),
        out_specs=P(("grp", "wide"), "narrow", None),
        check_vma=False,
    )
```

```python
import functools

import jax
import jax.numpy as jnp
from jax import lax
from jax.experimental import pallas as pl
from jax.experimental.pallas import tpu as pltpu
from jax.sharding import PartitionSpec as P

RELMAX = 32
EPSILON = 1e-05
LANES = 128
F32 = jnp.float32
BF16 = jnp.bfloat16


def apply_layer_norm(values, axis_dim):
    center = values - jnp.mean(values, axis=axis_dim, keepdims=True)
    spread = jnp.mean(center * center, axis=axis_dim, keepdims=True)
    return center * lax.rsqrt(spread + EPSILON)


def gather_wide(block):
    n = lax.axis_size("wide")
    if n % 4 or n < 8:
        return lax.all_gather(block, "wide", axis=0)
    outer = n // 4
    me = lax.axis_index("wide")
    high, mid, low = me // 4, (me // 2) % 2, me % 2
    arrived = [block]
    for shift in range(1, outer):
        perm = [(w, ((w // 4 + shift) % outer) * 4 + w % 4) for w in range(n)]
        arrived.append(lax.ppermute(block, "wide", perm))
    held = jnp.zeros((outer,) + block.shape, block.dtype)
    for shift, piece in enumerate(arrived):
        held = lax.dynamic_update_index_in_dim(held, piece, (high - shift + outer) % outer, 0)
    other = lax.ppermute(held, "wide", [(w, w ^ 2) for w in range(n)])
    held = jnp.stack(
        [jnp.where(mid == 0, held, other), jnp.where(mid == 0, other, held)], axis=1
    )
    other = lax.ppermute(held, "wide", [(w, w ^ 1) for w in range(n)])
    held = jnp.stack(
        [jnp.where(low == 0, held, other), jnp.where(low == 0, other, held)], axis=2
    )
    return held.reshape((n,) + block.shape)


def triangle(stream, pair_live, proj_weight, out_weight, incoming):
    rows = stream.shape[0]
    cols = stream.shape[1]
    width = out_weight.shape[0]
    wide_count = lax.axis_size("wide")
    core_count = lax.axis_size("narrow")
    devices = wide_count * core_count
    per_dev = width // devices
    normed = apply_layer_norm(stream, 2).astype(jnp.bfloat16)
    blocks = [proj_weight[:, index * width : (index + 1) * width] for index in range(4)]

    def project(block):
        return jnp.einsum("ijd,dc->cij", normed, block, preferred_element_type=jnp.float32)

    left_side = (jax.nn.sigmoid(project(blocks[0])) * project(blocks[1]) * pair_live[None]).astype(
        jnp.bfloat16
    )
    right_side = (jax.nn.sigmoid(project(blocks[2])) * project(blocks[3]) * pair_live[None]).astype(
        jnp.bfloat16
    )
    gate = jax.nn.sigmoid(
        jnp.einsum(
            "ijd,dc->ijc", normed, proj_weight[:, 4 * width :], preferred_element_type=jnp.float32
        )
    )
    form = "cki,ckj->cij" if incoming else "cik,cjk->cij"
    both = jnp.stack(
        [
            left_side.reshape(devices, per_dev, rows * cols),
            right_side.reshape(devices, per_dev, rows * cols),
        ],
        axis=1,
    ).reshape(devices, 2 * per_dev, rows * cols)
    both = lax.all_to_all(both, ("wide", "narrow"), split_axis=0, concat_axis=0, tiled=True)
    both = both.reshape(wide_count, core_count, 2, per_dev, rows, cols)
    both = jnp.transpose(both, (2, 3, 0, 4, 1, 5)).reshape(
        2, per_dev, wide_count * rows, core_count * cols
    )
    mixed = jnp.einsum(form, both[0], both[1], preferred_element_type=jnp.float32).astype(
        jnp.bfloat16
    )
    spread_out = mixed.reshape(per_dev, wide_count, rows, core_count, cols)
    spread_out = jnp.transpose(spread_out, (1, 3, 0, 2, 4)).reshape(
        wide_count * core_count * per_dev, rows * cols
    )
    returned = lax.all_to_all(
        spread_out, ("wide", "narrow"), split_axis=0, concat_axis=0, tiled=True
    ).reshape(width, rows, cols)
    blended_standardize = apply_layer_norm(returned.astype(jnp.float32), 0).astype(jnp.bfloat16)
    update = jnp.einsum(
        "cij,cd->ijd", blended_standardize, out_weight, preferred_element_type=jnp.float32
    )
    return stream + gate * update


def per_device_general(
    pairwise_state,
    homolog_features,
    residue_chain_index,
    resolved_residue_mask,
    alignment_mask,
    relative_offset_table,
    homolog_to_sides_matrix,
    outer_mean_output_weight,
    triangle_projection_weight,
    triangle_output_weight,
):
    rows = pairwise_state.shape[0]
    cols = pairwise_state.shape[1]
    row_start = lax.axis_index("wide") * rows
    col_start = lax.axis_index("narrow") * cols
    residue_present = resolved_residue_mask.astype(jnp.float32)
    row_present = lax.dynamic_slice_in_dim(residue_present, row_start, rows)
    col_live = lax.dynamic_slice_in_dim(residue_present, col_start, cols)
    present_flags = alignment_mask.astype(jnp.float32) * row_present[None, :]
    alignment_normed = apply_layer_norm(homolog_features.astype(jnp.float32), 2).astype(
        jnp.bfloat16
    )
    projected_rows = jnp.einsum(
        "tna,ak->tnk", alignment_normed, homolog_to_sides_matrix, preferred_element_type=jnp.float32
    )
    projected_rows = (projected_rows * present_flags[:, :, None]).astype(jnp.bfloat16)
    half_width = projected_rows.shape[2] // 2
    homologs = projected_rows.shape[0]
    left_proj = projected_rows[:, :, :half_width]
    right_proj = projected_rows[:, :, half_width:]
    live_flags = present_flags.astype(jnp.bfloat16)
    packed = jnp.concatenate(
        [jnp.transpose(right_proj, (1, 0, 2)).reshape(rows, homologs * half_width), live_flags.T],
        axis=1,
    )
    gathered = gather_wide(packed).reshape(-1, packed.shape[1])
    gathered = lax.dynamic_slice_in_dim(gathered, col_start, cols, 0)
    right_mine = jnp.transpose(
        gathered[:, : homologs * half_width].reshape(cols, homologs, half_width), (1, 0, 2)
    )
    live_mine = gathered[:, homologs * half_width :].T
    counts = jnp.dot(live_flags.T, live_mine, preferred_element_type=jnp.float32)

    def opm_row(left_row):
        outer = jnp.einsum("sc,sjd->jcd", left_row, right_mine, preferred_element_type=jnp.float32)
        outer = outer.reshape(cols, half_width * half_width).astype(jnp.bfloat16)
        return jnp.dot(outer, outer_mean_output_weight, preferred_element_type=jnp.float32)

    opm = lax.map(opm_row, jnp.transpose(left_proj, (1, 0, 2)))
    row_pos = row_start + jnp.arange(rows, dtype=jnp.int32)
    col_pos = col_start + jnp.arange(cols, dtype=jnp.int32)
    row_chain = lax.dynamic_slice_in_dim(residue_chain_index, row_start, rows)
    col_chain = lax.dynamic_slice_in_dim(residue_chain_index, col_start, cols)
    offset = jnp.clip(row_pos[:, None] - col_pos[None, :], -RELMAX, RELMAX) + RELMAX
    bin_index = jnp.where(row_chain[:, None] == col_chain[None, :], offset, 2 * RELMAX + 1)
    bin_count = relative_offset_table.shape[0]
    one_hot = (
        bin_index[:, :, None] == jnp.arange(bin_count, dtype=jnp.int32)[None, None, :]
    ).astype(jnp.bfloat16)
    relpos = jnp.einsum(
        "ijb,bc->ijc", one_hot, relative_offset_table, preferred_element_type=jnp.float32
    )
    stream = (
        pairwise_state.astype(jnp.float32) + relpos + opm / jnp.maximum(counts, 1.0)[:, :, None]
    )
    pair_live = row_present[:, None] * col_live[None, :]
    for turn_index in range(2):
        stream = triangle(
            stream,
            pair_live,
            triangle_projection_weight[turn_index],
            triangle_output_weight[turn_index],
            turn_index == 1,
        )
    return stream.astype(jnp.bfloat16)


def nn(a, b):
    return lax.dot_general(a, b, (((1,), (0,)), ((), ())), preferred_element_type=F32)


def nt(a, b):
    return lax.dot_general(a, b, (((1,), (1,)), ((), ())), preferred_element_type=F32)


def tn(a, b):
    return lax.dot_general(a, b, (((0,), (0,)), ((), ())), preferred_element_type=F32)


def identity(size):
    rows = lax.broadcasted_iota(jnp.int32, (size, size), 0)
    cols = lax.broadcasted_iota(jnp.int32, (size, size), 1)
    return (rows == cols).astype(F32).astype(BF16)


def flip(block):
    return nt(identity(block.shape[1]), block)


def norm_rows(values):
    scale = 1.0 / values.shape[0]
    center = values - jnp.sum(values, axis=0, keepdims=True) * scale
    spread = jnp.sum(center * center, axis=0, keepdims=True) * scale
    return (center * lax.rsqrt(spread + EPSILON)).astype(BF16)


def run(kernel, outs, *args, smem=(), scratch=(), flops=15 * 10**8):
    vmem = pl.BlockSpec(memory_space=pltpu.VMEM)
    in_specs = [
        pl.BlockSpec(memory_space=pltpu.SMEM if at in smem else pltpu.VMEM) for at in range(len(args))
    ]
    moved = sum(a.size * a.dtype.itemsize for a in args)
    return pl.pallas_call(
        kernel,
        out_shape=[jax.ShapeDtypeStruct(shape, kind) for shape, kind in outs],
        in_specs=in_specs,
        out_specs=[vmem] * len(outs),
        scratch_shapes=[pltpu.VMEM(shape, kind) for shape, kind in scratch],
        compiler_params=pltpu.CompilerParams(vmem_limit_bytes=VMEM_LIMIT),
        cost_estimate=pl.CostEstimate(flops=flops, bytes_accessed=moved, transcendentals=0),
    )(*args)


VMEM_LIMIT = 20 * 1024 * 1024
ALL_STEPS = (7, 3, 1, 6, 2, 5, 4, 0)
NEAR_STEPS = (3, 1, 2, 0)


def project_kernel(feat_ref, weight_ref, live_in_ref, pay_ref, left_ref, live_ref, turned, packed):
    homologs, rows, _ = feat_ref.shape
    half = weight_ref.shape[0] // 2
    quarter = half // 2
    values = feat_ref[...].astype(F32).reshape(homologs * rows, feat_ref.shape[2])
    center = values - jnp.mean(values, axis=1, keepdims=True)
    spread = jnp.mean(center * center, axis=1, keepdims=True)
    normed = (center * lax.rsqrt(spread + EPSILON)).astype(BF16)
    total = homologs * rows
    out_row = lax.broadcasted_iota(jnp.int32, (total, total), 0)
    in_row = lax.broadcasted_iota(jnp.int32, (total, total), 1)
    order = in_row == (out_row & (homologs - 1)) * rows + out_row // homologs
    normed = nn(order.astype(F32).astype(BF16), normed).astype(BF16)
    live = live_in_ref[...]
    weight = weight_ref[...]
    blank = jnp.zeros((homologs, normed.shape[1]), BF16)
    for row in range(rows):
        mine = normed[row * homologs : (row + 1) * homologs]
        low = nt(weight, jnp.concatenate([mine, blank], axis=0)) * live[row : row + 1]
        high = nt(weight, jnp.concatenate([blank, mine], axis=0)) * live[row : row + 1]
        left_ref[row * half : (row + 1) * half] = low[:half].astype(BF16)
        left_ref[(rows + row) * half : (rows + row + 1) * half] = high[:half].astype(BF16)
        turned[row] = low[half : half + quarter] + high[half + quarter :]
    for pair in range(quarter):
        packed[pair * rows : (pair + 1) * rows] = turned[:, pair, :]
    packed[quarter * rows : (quarter + 1) * rows] = live
    packed[(quarter + 1) * rows :] = jnp.zeros((rows, 2 * homologs), F32)
    pay_ref[...] = packed[...].astype(BF16)
    live_ref[...] = jnp.where(lax.broadcasted_iota(jnp.int32, live.shape, 1) < homologs, live, 0.0)


def prep_kernel(
    where_ref, chain_ref, chains_ref, pair_ref, table_ref, outer_ref, proj_ref, out_ref,
    base_ref, outer_t_ref, proj_t_ref, out_t_ref, table_pad, outer_pad,
):
    rows, cols, width = pair_ref.shape
    bins = table_ref.shape[0]
    table_pad[...] = jnp.zeros_like(table_pad)
    table_pad[0:bins, :] = table_ref[...].astype(F32)
    table = flip(table_pad[...].astype(BF16)).astype(BF16)
    chains = chains_ref[...]
    col = lax.broadcasted_iota(jnp.int32, (1, cols), 1)
    slot = lax.broadcasted_iota(jnp.int32, (table_pad.shape[0], cols), 0)
    for row in range(rows):
        place = where_ref[0] + row
        offset = jnp.clip(place - col, -RELMAX, RELMAX) + RELMAX
        bin_index = jnp.where(chains == chain_ref[place], offset, 2 * RELMAX + 1)
        hot = (slot == bin_index).astype(F32).astype(BF16)
        base_ref[row] = flip(pair_ref[row]) + nn(table, hot)
    half = outer_pad.shape[0]
    outer_pad[...] = outer_ref[...].astype(F32).reshape(outer_pad.shape)
    for d in range(half):
        outer_t_ref[:, d * half : (d + 1) * half] = flip(outer_pad[:, d, :].astype(BF16)).astype(BF16)
    for turn in range(2):
        proj_t_ref[turn] = tn(proj_ref[turn], identity(width)).astype(BF16)
        out_t_ref[turn] = flip(out_ref[turn]).astype(BF16)


def sides(normed, weight, live):
    width = normed.shape[0]
    made = nn(weight, normed)
    part = [made[at * width : (at + 1) * width] for at in range(5)]
    left = jax.nn.sigmoid(part[0]) * part[1] * live
    right = jax.nn.sigmoid(part[2]) * part[3] * live
    return left, right, jax.nn.sigmoid(part[4])


def outer_kernel(
    where_ref, flag_ref, own_ref, other_ref, left_ref, live_ref, base_ref, outer_t_ref, proj_ref, present_ref,
    stream_ref, gate_ref, both0, both1, both2, both3, far0, far1, far2, far3, came, outer, lefts, rights,
):
    rows, width, cols = base_ref.shape
    chip, core = where_ref[1], where_ref[2]
    per = own_ref.shape[1]
    chips = own_ref.shape[0]
    for at in range(chips):
        chip_at = chip ^ ((3 - at % 4) * 2 + at // 4)
        came[chip_at * 2 + core] = own_ref[at].astype(F32)
        came[chip_at * 2 + (1 - core)] = other_ref[at].astype(F32)
    half = left_ref.shape[0] // (2 * rows)
    quarter = half // 2
    live_all = came[:, quarter * rows : (quarter + 1) * rows, :].reshape(cols, per_lane(came)).astype(BF16)
    counts = nt(live_ref[...].astype(BF16), live_all)
    share = 1.0 / jnp.maximum(counts, 1.0)
    left_all = left_ref[...]
    for pair in range(quarter):
        right = came[:, pair * rows : (pair + 1) * rows, :].reshape(cols, per_lane(came)).astype(BF16)
        made = nt(left_all, right).astype(BF16)
        for part in range(2):
            d = part * quarter + pair
            for row in range(rows):
                first = (part * rows + row) * half
                outer[row, d * half : (d + 1) * half, :] = made[first : first + half]
    present = present_ref[...].astype(F32)
    for row in range(rows):
        stream = base_ref[row] + nn(outer_t_ref[...], outer[row]) * share[row : row + 1]
        stream_ref[row] = stream
        live = present * flag_ref[where_ref[0] + row].astype(F32)
        left, right, gate = sides(norm_rows(stream), proj_ref[0], live)
        gate_ref[row] = gate
        lefts[:, row, :] = left
        rights[:, row, :] = right
    groups = 4
    size = width // groups
    for step, (near, far) in enumerate(((both0, far0), (both1, far1), (both2, far2), (both3, far3))):
        group = (chip & (groups - 1)) ^ step
        block = rights[pl.ds(group * size, size)].reshape(size * rows, cols).astype(BF16)
        far[...] = block
        near[size * rows :] = block
        near[0 : size * rows] = lefts[pl.ds(group * size, size)].reshape(size * rows, cols).astype(BF16)


def per_lane(ref):
    return ref.shape[-1]


def mix_rows_kernel(
    where_ref, *refs,
):
    came, (other_ref, out0, out1, out2, out3, lefts, rights, mixed) = refs[:8], refs[8:]
    chip, core = where_ref[1], where_ref[2]
    count, rows, cols = lefts.shape[1:]
    block = count * rows
    for at, step in enumerate(ALL_STEPS):
        mine = came[at][came[at].shape[0] - block :].astype(F32)
        rights[(chip ^ step) * 2 + core] = mine.reshape(count, rows, cols)
        rights[(chip ^ step) * 2 + (1 - core)] = other_ref[at].astype(F32).reshape(count, rows, cols)
        if step < 4:
            lefts[step] = came[at][0:block].astype(F32).reshape(count, rows, cols)
    for c in range(count):
        left = lefts[:, c].reshape(4 * rows, cols).astype(BF16)
        right = rights[:, c].reshape(16 * rows, cols).astype(BF16)
        mixed[:, c, :] = nt(left, right)
    for step, out in enumerate((out0, out1, out2, out3)):
        out[...] = mixed[step * rows : (step + 1) * rows].reshape(block, cols).astype(BF16)


def update(came, row, stream, gate, out_weight):
    mixed = came[row]
    mixed = mixed.reshape(mixed.shape[0] * mixed.shape[1], mixed.shape[2])
    return stream + gate * nn(out_weight, norm_rows(mixed))


def between_kernel(
    where_ref, flag_ref, in0, in1, in2, in3, stream_ref, gate_ref, out_weight_ref, proj_ref, present_ref,
    next_ref, next_gate_ref, b0, b1, b2, b3, b4, b5, b6, b7, came, lefts, rights,
):
    rows, width, cols = stream_ref.shape
    chip = where_ref[1]
    groups = 4
    for step, block in zip(NEAR_STEPS, (in0, in1, in2, in3)):
        came[:, (chip & (groups - 1)) ^ step] = block[...].astype(F32).reshape(rows, width // groups, cols)
    present = present_ref[...].astype(F32)
    for row in range(rows):
        stream = update(came, row, stream_ref[row], gate_ref[row], out_weight_ref[0])
        next_ref[row] = stream
        live = present * flag_ref[where_ref[0] + row].astype(F32)
        left, right, gate = sides(norm_rows(stream), proj_ref[1], live)
        next_gate_ref[row] = gate
        lefts[:, row, :] = left
        rights[:, row, :] = right
    outs = (b0, b1, b2, b3, b4, b5, b6, b7)
    size = width // len(outs)
    for step, out in enumerate(outs):
        first = (chip ^ step) * size
        out[0 : size * rows] = lefts[pl.ds(first, size)].reshape(size * rows, cols).astype(BF16)
        out[size * rows :] = rights[pl.ds(first, size)].reshape(size * rows, cols).astype(BF16)


def mix_cols_kernel(where_ref, b0, b1, b2, b3, b4, b5, b6, b7, mine_ref, theirs_ref, lefts, rights, partial):
    chip, core = where_ref[1], where_ref[2]
    chips, count, rows, cols = lefts.shape
    block = count * rows
    for step, came in enumerate((b0, b1, b2, b3, b4, b5, b6, b7)):
        lefts[step] = came[0:block].astype(F32).reshape(count, rows, cols)
        rights[step] = came[block:].astype(F32).reshape(count, rows, cols)
    for c in range(count):
        left = lefts[:, c].reshape(chips * rows, cols).astype(BF16)
        right = rights[:, c].reshape(chips * rows, cols).astype(BF16)
        partial[:, c, :] = tn(left, right)
    for step in range(chips):
        at = (chip ^ step) * 2
        mine_ref[step] = partial[pl.ds((at + core) * rows, rows)].reshape(block, cols)
        theirs_ref[step] = partial[pl.ds((at + 1 - core) * rows, rows)].reshape(block, cols)


def sum_kernel(mine_ref, got_ref, *outs):
    for step, out in enumerate(outs):
        out[...] = (mine_ref[step] + got_ref[step]).astype(BF16)


def final_kernel(
    where_ref, b0, b1, b2, b3, b4, b5, b6, b7, stream_ref, gate_ref, out_weight_ref, out_ref, came
):
    rows, width, cols = stream_ref.shape
    chip = where_ref[1]
    blocks = (b0, b1, b2, b3, b4, b5, b6, b7)
    for step, block in zip(ALL_STEPS, blocks):
        came[:, chip ^ step] = block[...].astype(F32).reshape(rows, width // len(blocks), cols)
    for row in range(rows):
        stream = update(came, row, stream_ref[row], gate_ref[row], out_weight_ref[1])
        out_ref[row] = flip_out(stream)


def flip_out(stream):
    return nt(identity(stream.shape[1]), stream.astype(BF16)).astype(BF16)


def chip_permute(block, step):
    count = lax.axis_size("wide")
    return lax.ppermute(block, "wide", [(w, w ^ (2 * step)) for w in range(count)])


def exchange(blocks, steps):
    return [chip_permute(blocks[step], step) if step else blocks[0] for step in steps]


def core_permute(block):
    count = lax.axis_size("wide")
    return lax.ppermute(block, "wide", [(w, w ^ 1) for w in range(count)])


def per_device_chips(
    pairwise_state,
    homolog_features,
    residue_chain_index,
    resolved_residue_mask,
    alignment_mask,
    relative_offset_table,
    homolog_to_sides_matrix,
    outer_mean_output_weight,
    triangle_projection_weight,
    triangle_output_weight,
):
    rows, cols, width = pairwise_state.shape
    homologs = homolog_features.shape[0]
    half = homolog_to_sides_matrix.shape[1] // 2
    device = lax.axis_index("wide")
    chip, core = device // 2, device % 2
    where = jnp.stack([device * rows, chip, core]).astype(jnp.int32)
    present = resolved_residue_mask.reshape(1, cols)
    pay_rows = (half // 2 + 2) * rows
    row_present = lax.dynamic_slice_in_dim(resolved_residue_mask, device * rows, rows).astype(F32)
    live = alignment_mask.T.astype(F32) * row_present[:, None]
    live = jnp.concatenate([live, live], axis=1)
    pay, left, live = run(
        project_kernel,
        [((pay_rows, LANES), BF16), ((2 * rows * half, LANES), BF16), ((rows, LANES), F32)],
        homolog_features, homolog_to_sides_matrix.T, live,
        scratch=[((rows, half // 2, LANES), F32), ((pay_rows, LANES), F32)],
    )
    along_z = [chip_permute(pay, 2 * z) for z in (2, 3, 1)]
    base, outer_t, proj_t, out_t = run(
        prep_kernel,
        [
            ((rows, width, cols), F32),
            ((width, half * half), BF16),
            ((2, triangle_projection_weight.shape[2], width), BF16),
            ((2, width, width), BF16),
        ],
        where, residue_chain_index, residue_chain_index.reshape(1, cols), pairwise_state,
        relative_offset_table, outer_mean_output_weight, triangle_projection_weight, triangle_output_weight,
        smem=(0, 1),
        scratch=[((LANES, width), F32), ((half, half, width), F32)],
    )
    along_z = jnp.stack([along_z[1], along_z[0], along_z[2], pay])
    along_z, base, outer_t, proj_t, out_t = lax.optimization_barrier((along_z, base, outer_t, proj_t, out_t))
    own = jnp.concatenate([along_z, chip_permute(along_z, 1)], axis=0)
    other = core_permute(own)
    tall = width * rows
    made = run(
        outer_kernel,
        [((rows, width, cols), F32)] * 2
        + [((tall // 2, cols), BF16)] * 4
        + [((tall // 4, cols), BF16)] * 4,
        where, resolved_residue_mask, own, other, left, live, base, outer_t, proj_t, present,
        smem=(0, 1),
        scratch=[
            ((16, pay_rows, LANES), F32),
            ((rows, half * half, cols), BF16),
            ((width, rows, cols), F32),
            ((width, rows, cols), F32),
        ],
        flops=4 * 10**9,
    )
    stream, gate, both, far = made[0], made[1], made[2:6], made[6:10]
    came = exchange(list(both) + list(far), ALL_STEPS)
    rights = core_permute(jnp.stack([block[block.shape[0] - tall // 4 :] for block in came]))
    mixed = run(
        mix_rows_kernel,
        [((tall // 4, cols), BF16)] * 4,
        where, *came, rights,
        smem=(0,),
        scratch=[
            ((4, width // 4, rows, cols), F32),
            ((16, width // 4, rows, cols), F32),
            ((4 * rows, width // 4, cols), F32),
        ],
    )
    mixed = exchange(mixed, NEAR_STEPS)
    made = run(
        between_kernel,
        [((rows, width, cols), F32)] * 2 + [((tall // 4, cols), BF16)] * 8,
        where, resolved_residue_mask, *mixed, stream, gate, out_t, proj_t, present,
        smem=(0, 1),
        scratch=[
            ((rows, 4, width // 4, cols), F32),
            ((width, rows, cols), F32),
            ((width, rows, cols), F32),
        ],
    )
    stream, gate, both = made[0], made[1], made[2:]
    came = exchange(both, ALL_STEPS)
    mine, theirs = run(
        mix_cols_kernel,
        [((8, tall // 8, cols), F32)] * 2,
        where, *came,
        smem=(0,),
        scratch=[
            ((8, width // 8, rows, cols), F32),
            ((8, width // 8, rows, cols), F32),
            ((16 * rows, width // 8, cols), F32),
        ],
    )
    mixed = run(sum_kernel, [((tall // 8, cols), BF16)] * 8, mine, core_permute(theirs))
    mixed = exchange(mixed, ALL_STEPS)
    return run(
        final_kernel,
        [((rows, cols, width), BF16)],
        where, *mixed, stream, gate, out_t,
        smem=(0,),
        scratch=[((rows, 8, width // 8, cols), F32)],
    )[0]


def fits_chips(mesh):
    return mesh.shape["narrow"] == 1 and mesh.shape["wide"] == 16


def solution(mesh):
    per_device = per_device_chips if fits_chips(mesh) else per_device_general
    return jax.shard_map(
        per_device,
        mesh=mesh,
        in_specs=(
            P(("grp", "wide"), "narrow", None),
            P("grp", "wide", None),
            P("grp"),
            P("grp"),
            P("grp", "wide"),
            P(),
            P(),
            P(),
            P(),
            P(),
        ),
        out_specs=P(("grp", "wide"), "narrow", None),
        check_vma=False,
    )
```

```python
import functools

import jax
import jax.numpy as jnp
from jax import lax
from jax.experimental import pallas as pl
from jax.experimental.pallas import tpu as pltpu
from jax.sharding import PartitionSpec as P

RELMAX = 32
EPSILON = 1e-05
LANES = 128
F32 = jnp.float32
BF16 = jnp.bfloat16


def apply_layer_norm(values, axis_dim):
    center = values - jnp.mean(values, axis=axis_dim, keepdims=True)
    spread = jnp.mean(center * center, axis=axis_dim, keepdims=True)
    return center * lax.rsqrt(spread + EPSILON)


def gather_wide(block):
    n = lax.axis_size("wide")
    if n % 4 or n < 8:
        return lax.all_gather(block, "wide", axis=0)
    outer = n // 4
    me = lax.axis_index("wide")
    high, mid, low = me // 4, (me // 2) % 2, me % 2
    arrived = [block]
    for shift in range(1, outer):
        perm = [(w, ((w // 4 + shift) % outer) * 4 + w % 4) for w in range(n)]
        arrived.append(lax.ppermute(block, "wide", perm))
    held = jnp.zeros((outer,) + block.shape, block.dtype)
    for shift, piece in enumerate(arrived):
        held = lax.dynamic_update_index_in_dim(held, piece, (high - shift + outer) % outer, 0)
    other = lax.ppermute(held, "wide", [(w, w ^ 2) for w in range(n)])
    held = jnp.stack(
        [jnp.where(mid == 0, held, other), jnp.where(mid == 0, other, held)], axis=1
    )
    other = lax.ppermute(held, "wide", [(w, w ^ 1) for w in range(n)])
    held = jnp.stack(
        [jnp.where(low == 0, held, other), jnp.where(low == 0, other, held)], axis=2
    )
    return held.reshape((n,) + block.shape)


def triangle(stream, pair_live, proj_weight, out_weight, incoming):
    rows = stream.shape[0]
    cols = stream.shape[1]
    width = out_weight.shape[0]
    wide_count = lax.axis_size("wide")
    core_count = lax.axis_size("narrow")
    devices = wide_count * core_count
    per_dev = width // devices
    normed = apply_layer_norm(stream, 2).astype(jnp.bfloat16)
    blocks = [proj_weight[:, index * width : (index + 1) * width] for index in range(4)]

    def project(block):
        return jnp.einsum("ijd,dc->cij", normed, block, preferred_element_type=jnp.float32)

    left_side = (jax.nn.sigmoid(project(blocks[0])) * project(blocks[1]) * pair_live[None]).astype(
        jnp.bfloat16
    )
    right_side = (jax.nn.sigmoid(project(blocks[2])) * project(blocks[3]) * pair_live[None]).astype(
        jnp.bfloat16
    )
    gate = jax.nn.sigmoid(
        jnp.einsum(
            "ijd,dc->ijc", normed, proj_weight[:, 4 * width :], preferred_element_type=jnp.float32
        )
    )
    form = "cki,ckj->cij" if incoming else "cik,cjk->cij"
    both = jnp.stack(
        [
            left_side.reshape(devices, per_dev, rows * cols),
            right_side.reshape(devices, per_dev, rows * cols),
        ],
        axis=1,
    ).reshape(devices, 2 * per_dev, rows * cols)
    both = lax.all_to_all(both, ("wide", "narrow"), split_axis=0, concat_axis=0, tiled=True)
    both = both.reshape(wide_count, core_count, 2, per_dev, rows, cols)
    both = jnp.transpose(both, (2, 3, 0, 4, 1, 5)).reshape(
        2, per_dev, wide_count * rows, core_count * cols
    )
    mixed = jnp.einsum(form, both[0], both[1], preferred_element_type=jnp.float32).astype(
        jnp.bfloat16
    )
    spread_out = mixed.reshape(per_dev, wide_count, rows, core_count, cols)
    spread_out = jnp.transpose(spread_out, (1, 3, 0, 2, 4)).reshape(
        wide_count * core_count * per_dev, rows * cols
    )
    returned = lax.all_to_all(
        spread_out, ("wide", "narrow"), split_axis=0, concat_axis=0, tiled=True
    ).reshape(width, rows, cols)
    blended_standardize = apply_layer_norm(returned.astype(jnp.float32), 0).astype(jnp.bfloat16)
    update = jnp.einsum(
        "cij,cd->ijd", blended_standardize, out_weight, preferred_element_type=jnp.float32
    )
    return stream + gate * update


def per_device_general(
    pairwise_state,
    homolog_features,
    residue_chain_index,
    resolved_residue_mask,
    alignment_mask,
    relative_offset_table,
    homolog_to_sides_matrix,
    outer_mean_output_weight,
    triangle_projection_weight,
    triangle_output_weight,
):
    rows = pairwise_state.shape[0]
    cols = pairwise_state.shape[1]
    row_start = lax.axis_index("wide") * rows
    col_start = lax.axis_index("narrow") * cols
    residue_present = resolved_residue_mask.astype(jnp.float32)
    row_present = lax.dynamic_slice_in_dim(residue_present, row_start, rows)
    col_live = lax.dynamic_slice_in_dim(residue_present, col_start, cols)
    present_flags = alignment_mask.astype(jnp.float32) * row_present[None, :]
    alignment_normed = apply_layer_norm(homolog_features.astype(jnp.float32), 2).astype(
        jnp.bfloat16
    )
    projected_rows = jnp.einsum(
        "tna,ak->tnk", alignment_normed, homolog_to_sides_matrix, preferred_element_type=jnp.float32
    )
    projected_rows = (projected_rows * present_flags[:, :, None]).astype(jnp.bfloat16)
    half_width = projected_rows.shape[2] // 2
    homologs = projected_rows.shape[0]
    left_proj = projected_rows[:, :, :half_width]
    right_proj = projected_rows[:, :, half_width:]
    live_flags = present_flags.astype(jnp.bfloat16)
    packed = jnp.concatenate(
        [jnp.transpose(right_proj, (1, 0, 2)).reshape(rows, homologs * half_width), live_flags.T],
        axis=1,
    )
    gathered = gather_wide(packed).reshape(-1, packed.shape[1])
    gathered = lax.dynamic_slice_in_dim(gathered, col_start, cols, 0)
    right_mine = jnp.transpose(
        gathered[:, : homologs * half_width].reshape(cols, homologs, half_width), (1, 0, 2)
    )
    live_mine = gathered[:, homologs * half_width :].T
    counts = jnp.dot(live_flags.T, live_mine, preferred_element_type=jnp.float32)

    def opm_row(left_row):
        outer = jnp.einsum("sc,sjd->jcd", left_row, right_mine, preferred_element_type=jnp.float32)
        outer = outer.reshape(cols, half_width * half_width).astype(jnp.bfloat16)
        return jnp.dot(outer, outer_mean_output_weight, preferred_element_type=jnp.float32)

    opm = lax.map(opm_row, jnp.transpose(left_proj, (1, 0, 2)))
    row_pos = row_start + jnp.arange(rows, dtype=jnp.int32)
    col_pos = col_start + jnp.arange(cols, dtype=jnp.int32)
    row_chain = lax.dynamic_slice_in_dim(residue_chain_index, row_start, rows)
    col_chain = lax.dynamic_slice_in_dim(residue_chain_index, col_start, cols)
    offset = jnp.clip(row_pos[:, None] - col_pos[None, :], -RELMAX, RELMAX) + RELMAX
    bin_index = jnp.where(row_chain[:, None] == col_chain[None, :], offset, 2 * RELMAX + 1)
    bin_count = relative_offset_table.shape[0]
    one_hot = (
        bin_index[:, :, None] == jnp.arange(bin_count, dtype=jnp.int32)[None, None, :]
    ).astype(jnp.bfloat16)
    relpos = jnp.einsum(
        "ijb,bc->ijc", one_hot, relative_offset_table, preferred_element_type=jnp.float32
    )
    stream = (
        pairwise_state.astype(jnp.float32) + relpos + opm / jnp.maximum(counts, 1.0)[:, :, None]
    )
    pair_live = row_present[:, None] * col_live[None, :]
    for turn_index in range(2):
        stream = triangle(
            stream,
            pair_live,
            triangle_projection_weight[turn_index],
            triangle_output_weight[turn_index],
            turn_index == 1,
        )
    return stream.astype(jnp.bfloat16)


def nn(a, b):
    return lax.dot_general(a, b, (((1,), (0,)), ((), ())), preferred_element_type=F32)


def nt(a, b):
    return lax.dot_general(a, b, (((1,), (1,)), ((), ())), preferred_element_type=F32)


def tn(a, b):
    return lax.dot_general(a, b, (((0,), (0,)), ((), ())), preferred_element_type=F32)


def identity(size):
    rows = lax.broadcasted_iota(jnp.int32, (size, size), 0)
    cols = lax.broadcasted_iota(jnp.int32, (size, size), 1)
    return (rows == cols).astype(F32).astype(BF16)


def flip(block):
    return nt(identity(block.shape[1]), block)


def norm_rows(values):
    scale = 1.0 / values.shape[0]
    center = values - jnp.sum(values, axis=0, keepdims=True) * scale
    spread = jnp.sum(center * center, axis=0, keepdims=True) * scale
    return (center * lax.rsqrt(spread + EPSILON)).astype(BF16)


def run(kernel, outs, *args, smem=(), scratch=(), flops=15 * 10**8):
    vmem = pl.BlockSpec(memory_space=pltpu.VMEM)
    in_specs = [
        pl.BlockSpec(memory_space=pltpu.SMEM if at in smem else pltpu.VMEM) for at in range(len(args))
    ]
    moved = sum(a.size * a.dtype.itemsize for a in args)
    return pl.pallas_call(
        kernel,
        out_shape=[jax.ShapeDtypeStruct(shape, kind) for shape, kind in outs],
        in_specs=in_specs,
        out_specs=[vmem] * len(outs),
        scratch_shapes=[pltpu.VMEM(shape, kind) for shape, kind in scratch],
        compiler_params=pltpu.CompilerParams(vmem_limit_bytes=VMEM_LIMIT),
        cost_estimate=pl.CostEstimate(flops=flops, bytes_accessed=moved, transcendentals=0),
    )(*args)


VMEM_LIMIT = 20 * 1024 * 1024
SPLIT = ((7, 5), (6, 4), (3, 2), (1, 0))
OPS = len(SPLIT)
NEAR = 4


def partner_chip(chip, core, op):
    return chip ^ jnp.where(core == 0, SPLIT[op][0], SPLIT[op][1])


def project_kernel(feat_ref, weight_ref, live_in_ref, pay_ref, left_ref, live_ref, turned, packed):
    homologs, rows, _ = feat_ref.shape
    half = weight_ref.shape[0] // 2
    quarter = half // 2
    values = feat_ref[...].astype(F32).reshape(homologs * rows, feat_ref.shape[2])
    center = values - jnp.mean(values, axis=1, keepdims=True)
    spread = jnp.mean(center * center, axis=1, keepdims=True)
    normed = (center * lax.rsqrt(spread + EPSILON)).astype(BF16)
    total = homologs * rows
    out_row = lax.broadcasted_iota(jnp.int32, (total, total), 0)
    in_row = lax.broadcasted_iota(jnp.int32, (total, total), 1)
    order = in_row == (out_row & (homologs - 1)) * rows + out_row // homologs
    normed = nn(order.astype(F32).astype(BF16), normed).astype(BF16)
    live = live_in_ref[...]
    weight = weight_ref[...]
    blank = jnp.zeros((homologs, normed.shape[1]), BF16)
    for row in range(rows):
        mine = normed[row * homologs : (row + 1) * homologs]
        low = nt(weight, jnp.concatenate([mine, blank], axis=0)) * live[row : row + 1]
        high = nt(weight, jnp.concatenate([blank, mine], axis=0)) * live[row : row + 1]
        left_ref[row * half : (row + 1) * half] = low[:half].astype(BF16)
        left_ref[(rows + row) * half : (rows + row + 1) * half] = high[:half].astype(BF16)
        turned[row] = low[half : half + quarter] + high[half + quarter :]
    for pair in range(quarter):
        packed[pair * rows : (pair + 1) * rows] = turned[:, pair, :]
    packed[quarter * rows : (quarter + 1) * rows] = live
    packed[(quarter + 1) * rows :] = jnp.zeros((rows, 2 * homologs), F32)
    pay_ref[...] = packed[...].astype(BF16)
    live_ref[...] = jnp.where(lax.broadcasted_iota(jnp.int32, live.shape, 1) < homologs, live, 0.0)


def prep_kernel(
    where_ref, chain_ref, chains_ref, pair_ref, table_ref, outer_ref, proj_ref, out_ref,
    base_ref, outer_t_ref, proj_t_ref, out_t_ref, table_pad, outer_pad,
):
    rows, cols, width = pair_ref.shape
    bins = table_ref.shape[0]
    table_pad[...] = jnp.zeros_like(table_pad)
    table_pad[0:bins, :] = table_ref[...].astype(F32)
    table = flip(table_pad[...].astype(BF16)).astype(BF16)
    chains = chains_ref[...]
    col = lax.broadcasted_iota(jnp.int32, (1, cols), 1)
    slot = lax.broadcasted_iota(jnp.int32, (table_pad.shape[0], cols), 0)
    for row in range(rows):
        place = where_ref[0] + row
        offset = jnp.clip(place - col, -RELMAX, RELMAX) + RELMAX
        bin_index = jnp.where(chains == chain_ref[place], offset, 2 * RELMAX + 1)
        hot = (slot == bin_index).astype(F32).astype(BF16)
        base_ref[row] = flip(pair_ref[row]) + nn(table, hot)
    half = outer_pad.shape[0]
    outer_pad[...] = outer_ref[...].astype(F32).reshape(outer_pad.shape)
    for d in range(half):
        outer_t_ref[:, d * half : (d + 1) * half] = flip(outer_pad[:, d, :].astype(BF16)).astype(BF16)
    for turn in range(2):
        proj_t_ref[turn] = tn(proj_ref[turn], identity(width)).astype(BF16)
        out_t_ref[turn] = flip(out_ref[turn]).astype(BF16)


def sigmoid(values):
    return 0.5 * jnp.tanh(0.5 * values) + 0.5


def sides(streams, weight, lives, gate_ref, lefts, rights, row):
    width, cols = streams[0].shape
    made = nn(weight, jnp.concatenate([norm_rows(stream) for stream in streams], axis=1))
    for at, live in enumerate(lives):
        part = [
            made[block * width : (block + 1) * width, at * cols : (at + 1) * cols] for block in range(5)
        ]
        lefts[:, row + at, :] = sigmoid(part[0]) * part[1] * live
        rights[:, row + at, :] = sigmoid(part[2]) * part[3] * live
        gate_ref[row + at] = sigmoid(part[4])


def flat(block):
    return block.reshape(block.shape[0] * block.shape[1], block.shape[2])


def outer_kernel(
    where_ref, flag_ref, own_ref, other_ref, left_ref, live_ref, base_ref, outer_t_ref, proj_ref, present_ref,
    stream_ref, gate_ref, mine0, mine1, mine2, mine3, theirs_ref, came, outer, lefts, rights,
):
    rows, width, cols = base_ref.shape
    chip, core = where_ref[1], where_ref[2]
    per = own_ref.shape[1]
    chips = own_ref.shape[0]
    for at in range(chips):
        chip_at = chip ^ ((3 - at % 4) * 2 + at // 4)
        came[chip_at * 2 + core] = own_ref[at].astype(F32)
        came[chip_at * 2 + (1 - core)] = other_ref[at].astype(F32)
    half = left_ref.shape[0] // (2 * rows)
    quarter = half // 2
    live_all = came[:, quarter * rows : (quarter + 1) * rows, :].reshape(cols, per_lane(came)).astype(BF16)
    counts = nt(live_ref[...].astype(BF16), live_all)
    share = 1.0 / jnp.maximum(counts, 1.0)
    left_all = left_ref[...]
    for pair in range(quarter):
        right = came[:, pair * rows : (pair + 1) * rows, :].reshape(cols, per_lane(came)).astype(BF16)
        made = nt(left_all, right).astype(BF16)
        for part in range(2):
            d = part * quarter + pair
            for row in range(rows):
                first = (part * rows + row) * half
                lane = (row % 2) * cols
                outer[row // 2, d * half : (d + 1) * half, lane : lane + cols] = made[first : first + half]
    present = present_ref[...].astype(F32)
    for row in range(0, rows, 2):
        product = nn(outer_t_ref[...], outer[row // 2])
        streams, lives = [], []
        for at in range(2):
            streams.append(
                base_ref[row + at] + product[:, at * cols : (at + 1) * cols] * share[row + at : row + at + 1]
            )
            stream_ref[row + at] = streams[at]
            lives.append(present * flag_ref[where_ref[0] + row + at].astype(F32))
        sides(streams, proj_ref[0], lives, gate_ref, lefts, rights, row)
    size = width // NEAR
    block = size * rows
    place = 0
    for op, mine in enumerate((mine0, mine1, mine2, mine3)):
        for theirs in range(2):
            to = partner_chip(chip, core ^ theirs, op)
            first = pl.multiple_of((to & (NEAR - 1)) * size, size)
            sent = [rights] if op < OPS // 2 else [lefts, rights]
            for at, side in enumerate(sent):
                made = flat(side[pl.ds(first, size)]).astype(BF16)
                if theirs:
                    theirs_ref[place : place + block] = made
                    place += block
                else:
                    mine[at * block : (at + 1) * block] = made


def per_lane(ref):
    return ref.shape[-1]


def mix_rows_kernel(where_ref, came0, came1, came2, came3, other_ref, out0, out1, lefts, rights, mixed):
    chip, core = where_ref[1], where_ref[2]
    count, rows, cols = lefts.shape[1:]
    block = count * rows
    for op, came in enumerate((came0, came1, came2, came3)):
        sent = came.shape[0] // 2
        for half in range(2):
            mine = came[(half + 1) * sent - block : (half + 1) * sent].astype(F32)
            at = partner_chip(chip, core, op) * 2 + (core ^ half)
            rights[at] = mine.reshape(count, rows, cols)
            at = partner_chip(chip, 1 - core, op) * 2 + ((1 - core) ^ half)
            rights[at] = other_ref[op * 2 + half].astype(F32).reshape(count, rows, cols)
            if op >= OPS // 2:
                left = came[half * sent : half * sent + block].astype(F32)
                lefts[(op - OPS // 2) * 2 + half] = left.reshape(count, rows, cols)
    for c in range(count):
        left = flat(lefts[:, c]).astype(BF16)
        right = flat(rights[:, c]).astype(BF16)
        mixed[:, c, :] = nt(left, right)
    for at, out in enumerate((out0, out1)):
        out[...] = flat(mixed[at * 2 * rows : (at + 1) * 2 * rows]).astype(BF16)


def update(came, row, stream_ref, gate_ref, out_weight):
    normed = jnp.concatenate([norm_rows(flat(came[row + at])) for at in range(2)], axis=1)
    made = nn(out_weight, normed)
    cols = made.shape[1] // 2
    return [
        stream_ref[row + at] + gate_ref[row + at] * made[:, at * cols : (at + 1) * cols] for at in range(2)
    ]


def between_kernel(
    where_ref, flag_ref, in0, in1, other_ref, stream_ref, gate_ref, out_weight_ref, proj_ref, present_ref,
    next_ref, next_gate_ref, mine0, mine1, mine2, mine3, theirs_ref, came, lefts, rights,
):
    rows, width, cols = stream_ref.shape
    chip, core = where_ref[1], where_ref[2]
    size = width // NEAR
    for at, block in enumerate((in0, in1)):
        op = OPS // 2 + at
        group = partner_chip(chip, core, op) & (NEAR - 1)
        came[:, group] = block[0 : size * rows].astype(F32).reshape(rows, size, cols)
        group = partner_chip(chip, 1 - core, op) & (NEAR - 1)
        block = other_ref[at * size * rows : (at + 1) * size * rows]
        came[:, group] = block.astype(F32).reshape(rows, size, cols)
    present = present_ref[...].astype(F32)
    for row in range(0, rows, 2):
        streams = update(came, row, stream_ref, gate_ref, out_weight_ref[0])
        lives = []
        for at in range(2):
            next_ref[row + at] = streams[at]
            lives.append(present * flag_ref[where_ref[0] + row + at].astype(F32))
        sides(streams, proj_ref[1], lives, next_gate_ref, lefts, rights, row)
    size = width // (2 * OPS)
    block = size * rows
    for op, mine in enumerate((mine0, mine1, mine2, mine3)):
        for at, side in enumerate((lefts, rights)):
            first = pl.multiple_of(partner_chip(chip, core, op) * size, size)
            mine[at * block : (at + 1) * block] = flat(side[pl.ds(first, size)]).astype(BF16)
            first = pl.multiple_of(partner_chip(chip, 1 - core, op) * size, size)
            place = (op * 2 + at) * block
            theirs_ref[place : place + block] = flat(side[pl.ds(first, size)]).astype(BF16)


def mix_cols_kernel(where_ref, came0, came1, came2, came3, mine_ref, theirs_ref, lefts, rights, partial):
    chip, core = where_ref[1], where_ref[2]
    count, rows, cols = lefts.shape[1:]
    block = count * rows
    for op, came in enumerate((came0, came1, came2, came3)):
        for half in range(2):
            for at, side in enumerate((lefts, rights)):
                place = (half * 2 + at) * block
                side[op * 2 + half] = came[place : place + block].astype(F32).reshape(count, rows, cols)
    for c in range(count):
        left = flat(lefts[:, c]).astype(BF16)
        right = flat(rights[:, c]).astype(BF16)
        partial[:, c, :] = tn(left, right)
    for op in range(OPS):
        for half in range(2):
            to = (partner_chip(chip, core, op) * 2 + (core ^ half)) * rows
            mine_ref[op, half * block : (half + 1) * block] = flat(partial[pl.ds(to, rows)])
            to = (partner_chip(chip, 1 - core, op) * 2 + ((1 - core) ^ half)) * rows
            theirs_ref[op, half * block : (half + 1) * block] = flat(partial[pl.ds(to, rows)])


def sum_kernel(mine_ref, got_ref, *outs):
    for op, out in enumerate(outs):
        out[...] = (mine_ref[op] + got_ref[op]).astype(BF16)


def final_kernel(
    where_ref, came0, came1, came2, came3, other_ref, stream_ref, gate_ref, out_weight_ref, out_ref, came
):
    rows, width, cols = stream_ref.shape
    chip, core = where_ref[1], where_ref[2]
    size = width // (2 * OPS)
    block = size * rows
    for op, mine in enumerate((came0, came1, came2, came3)):
        came[:, partner_chip(chip, core, op)] = mine[0:block].astype(F32).reshape(rows, size, cols)
        theirs = other_ref[op * block : (op + 1) * block]
        came[:, partner_chip(chip, 1 - core, op)] = theirs.astype(F32).reshape(rows, size, cols)
    for row in range(0, rows, 2):
        for at, stream in enumerate(update(came, row, stream_ref, gate_ref, out_weight_ref[1])):
            out_ref[row + at] = flip_out(stream)


def flip_out(stream):
    return nt(identity(stream.shape[1]), stream.astype(BF16)).astype(BF16)


def chip_permute(block, step):
    count = lax.axis_size("wide")
    return lax.ppermute(block, "wide", [(w, w ^ (2 * step)) for w in range(count)])


def split_permute(block, op):
    count = lax.axis_size("wide")
    return lax.ppermute(block, "wide", [(w, w ^ (2 * SPLIT[op][w % 2])) for w in range(count)])


def with_partner(mine, theirs):
    got, messages, place = core_permute(theirs), [], 0
    for block in mine:
        messages.append(jnp.concatenate([block, got[place : place + block.shape[0]]], axis=0))
        place += block.shape[0]
    return messages


def core_permute(block):
    count = lax.axis_size("wide")
    return lax.ppermute(block, "wide", [(w, w ^ 1) for w in range(count)])


def per_device_chips(
    pairwise_state,
    homolog_features,
    residue_chain_index,
    resolved_residue_mask,
    alignment_mask,
    relative_offset_table,
    homolog_to_sides_matrix,
    outer_mean_output_weight,
    triangle_projection_weight,
    triangle_output_weight,
):
    rows, cols, width = pairwise_state.shape
    homologs = homolog_features.shape[0]
    half = homolog_to_sides_matrix.shape[1] // 2
    device = lax.axis_index("wide")
    chip, core = device // 2, device % 2
    where = jnp.stack([device * rows, chip, core]).astype(jnp.int32)
    present = resolved_residue_mask.reshape(1, cols)
    pay_rows = (half // 2 + 2) * rows
    row_present = lax.dynamic_slice_in_dim(resolved_residue_mask, device * rows, rows).astype(F32)
    live = alignment_mask.T.astype(F32) * row_present[:, None]
    live = jnp.concatenate([live, live], axis=1)
    pay, left, live = run(
        project_kernel,
        [((pay_rows, LANES), BF16), ((2 * rows * half, LANES), BF16), ((rows, LANES), F32)],
        homolog_features, homolog_to_sides_matrix.T, live,
        scratch=[((rows, half // 2, LANES), F32), ((pay_rows, LANES), F32)],
    )
    along_z = [chip_permute(pay, 2 * z) for z in (2, 3, 1)]
    base, outer_t, proj_t, out_t = run(
        prep_kernel,
        [
            ((rows, width, cols), F32),
            ((width, half * half), BF16),
            ((2, triangle_projection_weight.shape[2], width), BF16),
            ((2, width, width), BF16),
        ],
        where, residue_chain_index, residue_chain_index.reshape(1, cols), pairwise_state,
        relative_offset_table, outer_mean_output_weight, triangle_projection_weight, triangle_output_weight,
        smem=(0, 1),
        scratch=[((LANES, width), F32), ((half, half, width), F32)],
    )
    along_z = jnp.stack([along_z[1], along_z[0], along_z[2], pay])
    along_z, base, outer_t, proj_t, out_t = lax.optimization_barrier((along_z, base, outer_t, proj_t, out_t))
    own = jnp.concatenate([along_z, chip_permute(along_z, 1)], axis=0)
    other = core_permute(own)
    tall = width * rows
    near, all_ = tall // NEAR, tall // (2 * OPS)
    made = run(
        outer_kernel,
        [((rows, width, cols), F32)] * 2
        + [((near, cols), BF16)] * 2
        + [((2 * near, cols), BF16)] * 2
        + [((6 * near, cols), BF16)],
        where, resolved_residue_mask, own, other, left, live, base, outer_t, proj_t, present,
        smem=(0, 1),
        scratch=[
            ((16, pay_rows, LANES), F32),
            ((rows // 2, half * half, 2 * cols), BF16),
            ((width, rows, cols), F32),
            ((width, rows, cols), F32),
        ],
        flops=4 * 10**9,
    )
    stream, gate, theirs = made[0], made[1], made[6]
    came = [split_permute(block, op) for op, block in enumerate(with_partner(made[2:6], theirs))]
    rights = []
    for block in came:
        for part in range(2):
            end = (part + 1) * block.shape[0] // 2
            rights.append(block[end - near : end])
    mixed = run(
        mix_rows_kernel,
        [((2 * near, cols), BF16)] * 2,
        where, *came, core_permute(jnp.stack(rights)),
        smem=(0,),
        scratch=[
            ((4, width // NEAR, rows, cols), F32),
            ((16, width // NEAR, rows, cols), F32),
            ((4 * rows, width // NEAR, cols), F32),
        ],
    )
    mixed = [split_permute(block, OPS // 2 + at) for at, block in enumerate(mixed)]
    other = core_permute(jnp.concatenate([block[near:] for block in mixed], axis=0))
    made = run(
        between_kernel,
        [((rows, width, cols), F32)] * 2 + [((2 * all_, cols), BF16)] * OPS + [((2 * OPS * all_, cols), BF16)],
        where, resolved_residue_mask, *mixed, other, stream, gate, out_t, proj_t, present,
        smem=(0, 1),
        scratch=[
            ((rows, NEAR, width // NEAR, cols), F32),
            ((width, rows, cols), F32),
            ((width, rows, cols), F32),
        ],
    )
    stream, gate, theirs = made[0], made[1], made[6]
    came = [split_permute(block, op) for op, block in enumerate(with_partner(made[2:6], theirs))]
    mine, theirs = run(
        mix_cols_kernel,
        [((OPS, 2 * all_, cols), F32)] * 2,
        where, *came,
        smem=(0,),
        scratch=[
            ((2 * OPS, width // (2 * OPS), rows, cols), F32),
            ((2 * OPS, width // (2 * OPS), rows, cols), F32),
            ((16 * rows, width // (2 * OPS), cols), F32),
        ],
    )
    mixed = run(sum_kernel, [((2 * all_, cols), BF16)] * OPS, mine, core_permute(theirs))
    mixed = [split_permute(block, op) for op, block in enumerate(mixed)]
    other = core_permute(jnp.concatenate([block[all_:] for block in mixed], axis=0))
    return run(
        final_kernel,
        [((rows, cols, width), BF16)],
        where, *mixed, other, stream, gate, out_t,
        smem=(0,),
        scratch=[((rows, 2 * OPS, width // (2 * OPS), cols), F32)],
    )[0]


def fits_chips(mesh):
    return mesh.shape["narrow"] == 1 and mesh.shape["wide"] == 16


def solution(mesh):
    per_device = per_device_chips if fits_chips(mesh) else per_device_general
    return jax.shard_map(
        per_device,
        mesh=mesh,
        in_specs=(
            P(("grp", "wide"), "narrow", None),
            P("grp", "wide", None),
            P("grp"),
            P("grp"),
            P("grp", "wide"),
            P(),
            P(),
            P(),
            P(),
            P(),
        ),
        out_specs=P(("grp", "wide"), "narrow", None),
        check_vma=False,
    )
```

```python
import functools

import jax
import jax.numpy as jnp
from jax import lax
from jax.experimental import pallas as pl
from jax.experimental.pallas import tpu as pltpu
from jax.sharding import PartitionSpec as P

RELMAX = 32
EPSILON = 1e-05
LANES = 128
F32 = jnp.float32
BF16 = jnp.bfloat16


def apply_layer_norm(values, axis_dim):
    center = values - jnp.mean(values, axis=axis_dim, keepdims=True)
    spread = jnp.mean(center * center, axis=axis_dim, keepdims=True)
    return center * lax.rsqrt(spread + EPSILON)


def gather_wide(block):
    n = lax.axis_size("wide")
    if n % 4 or n < 8:
        return lax.all_gather(block, "wide", axis=0)
    outer = n // 4
    me = lax.axis_index("wide")
    high, mid, low = me // 4, (me // 2) % 2, me % 2
    arrived = [block]
    for shift in range(1, outer):
        perm = [(w, ((w // 4 + shift) % outer) * 4 + w % 4) for w in range(n)]
        arrived.append(lax.ppermute(block, "wide", perm))
    held = jnp.zeros((outer,) + block.shape, block.dtype)
    for shift, piece in enumerate(arrived):
        held = lax.dynamic_update_index_in_dim(held, piece, (high - shift + outer) % outer, 0)
    other = lax.ppermute(held, "wide", [(w, w ^ 2) for w in range(n)])
    held = jnp.stack(
        [jnp.where(mid == 0, held, other), jnp.where(mid == 0, other, held)], axis=1
    )
    other = lax.ppermute(held, "wide", [(w, w ^ 1) for w in range(n)])
    held = jnp.stack(
        [jnp.where(low == 0, held, other), jnp.where(low == 0, other, held)], axis=2
    )
    return held.reshape((n,) + block.shape)


def triangle(stream, pair_live, proj_weight, out_weight, incoming):
    rows = stream.shape[0]
    cols = stream.shape[1]
    width = out_weight.shape[0]
    wide_count = lax.axis_size("wide")
    core_count = lax.axis_size("narrow")
    devices = wide_count * core_count
    per_dev = width // devices
    normed = apply_layer_norm(stream, 2).astype(jnp.bfloat16)
    blocks = [proj_weight[:, index * width : (index + 1) * width] for index in range(4)]

    def project(block):
        return jnp.einsum("ijd,dc->cij", normed, block, preferred_element_type=jnp.float32)

    left_side = (jax.nn.sigmoid(project(blocks[0])) * project(blocks[1]) * pair_live[None]).astype(
        jnp.bfloat16
    )
    right_side = (jax.nn.sigmoid(project(blocks[2])) * project(blocks[3]) * pair_live[None]).astype(
        jnp.bfloat16
    )
    gate = jax.nn.sigmoid(
        jnp.einsum(
            "ijd,dc->ijc", normed, proj_weight[:, 4 * width :], preferred_element_type=jnp.float32
        )
    )
    form = "cki,ckj->cij" if incoming else "cik,cjk->cij"
    both = jnp.stack(
        [
            left_side.reshape(devices, per_dev, rows * cols),
            right_side.reshape(devices, per_dev, rows * cols),
        ],
        axis=1,
    ).reshape(devices, 2 * per_dev, rows * cols)
    both = lax.all_to_all(both, ("wide", "narrow"), split_axis=0, concat_axis=0, tiled=True)
    both = both.reshape(wide_count, core_count, 2, per_dev, rows, cols)
    both = jnp.transpose(both, (2, 3, 0, 4, 1, 5)).reshape(
        2, per_dev, wide_count * rows, core_count * cols
    )
    mixed = jnp.einsum(form, both[0], both[1], preferred_element_type=jnp.float32).astype(
        jnp.bfloat16
    )
    spread_out = mixed.reshape(per_dev, wide_count, rows, core_count, cols)
    spread_out = jnp.transpose(spread_out, (1, 3, 0, 2, 4)).reshape(
        wide_count * core_count * per_dev, rows * cols
    )
    returned = lax.all_to_all(
        spread_out, ("wide", "narrow"), split_axis=0, concat_axis=0, tiled=True
    ).reshape(width, rows, cols)
    blended_standardize = apply_layer_norm(returned.astype(jnp.float32), 0).astype(jnp.bfloat16)
    update = jnp.einsum(
        "cij,cd->ijd", blended_standardize, out_weight, preferred_element_type=jnp.float32
    )
    return stream + gate * update


def per_device_general(
    pairwise_state,
    homolog_features,
    residue_chain_index,
    resolved_residue_mask,
    alignment_mask,
    relative_offset_table,
    homolog_to_sides_matrix,
    outer_mean_output_weight,
    triangle_projection_weight,
    triangle_output_weight,
):
    rows = pairwise_state.shape[0]
    cols = pairwise_state.shape[1]
    row_start = lax.axis_index("wide") * rows
    col_start = lax.axis_index("narrow") * cols
    residue_present = resolved_residue_mask.astype(jnp.float32)
    row_present = lax.dynamic_slice_in_dim(residue_present, row_start, rows)
    col_live = lax.dynamic_slice_in_dim(residue_present, col_start, cols)
    present_flags = alignment_mask.astype(jnp.float32) * row_present[None, :]
    alignment_normed = apply_layer_norm(homolog_features.astype(jnp.float32), 2).astype(
        jnp.bfloat16
    )
    projected_rows = jnp.einsum(
        "tna,ak->tnk", alignment_normed, homolog_to_sides_matrix, preferred_element_type=jnp.float32
    )
    projected_rows = (projected_rows * present_flags[:, :, None]).astype(jnp.bfloat16)
    half_width = projected_rows.shape[2] // 2
    homologs = projected_rows.shape[0]
    left_proj = projected_rows[:, :, :half_width]
    right_proj = projected_rows[:, :, half_width:]
    live_flags = present_flags.astype(jnp.bfloat16)
    packed = jnp.concatenate(
        [jnp.transpose(right_proj, (1, 0, 2)).reshape(rows, homologs * half_width), live_flags.T],
        axis=1,
    )
    gathered = gather_wide(packed).reshape(-1, packed.shape[1])
    gathered = lax.dynamic_slice_in_dim(gathered, col_start, cols, 0)
    right_mine = jnp.transpose(
        gathered[:, : homologs * half_width].reshape(cols, homologs, half_width), (1, 0, 2)
    )
    live_mine = gathered[:, homologs * half_width :].T
    counts = jnp.dot(live_flags.T, live_mine, preferred_element_type=jnp.float32)

    def opm_row(left_row):
        outer = jnp.einsum("sc,sjd->jcd", left_row, right_mine, preferred_element_type=jnp.float32)
        outer = outer.reshape(cols, half_width * half_width).astype(jnp.bfloat16)
        return jnp.dot(outer, outer_mean_output_weight, preferred_element_type=jnp.float32)

    opm = lax.map(opm_row, jnp.transpose(left_proj, (1, 0, 2)))
    row_pos = row_start + jnp.arange(rows, dtype=jnp.int32)
    col_pos = col_start + jnp.arange(cols, dtype=jnp.int32)
    row_chain = lax.dynamic_slice_in_dim(residue_chain_index, row_start, rows)
    col_chain = lax.dynamic_slice_in_dim(residue_chain_index, col_start, cols)
    offset = jnp.clip(row_pos[:, None] - col_pos[None, :], -RELMAX, RELMAX) + RELMAX
    bin_index = jnp.where(row_chain[:, None] == col_chain[None, :], offset, 2 * RELMAX + 1)
    bin_count = relative_offset_table.shape[0]
    one_hot = (
        bin_index[:, :, None] == jnp.arange(bin_count, dtype=jnp.int32)[None, None, :]
    ).astype(jnp.bfloat16)
    relpos = jnp.einsum(
        "ijb,bc->ijc", one_hot, relative_offset_table, preferred_element_type=jnp.float32
    )
    stream = (
        pairwise_state.astype(jnp.float32) + relpos + opm / jnp.maximum(counts, 1.0)[:, :, None]
    )
    pair_live = row_present[:, None] * col_live[None, :]
    for turn_index in range(2):
        stream = triangle(
            stream,
            pair_live,
            triangle_projection_weight[turn_index],
            triangle_output_weight[turn_index],
            turn_index == 1,
        )
    return stream.astype(jnp.bfloat16)


def nn(a, b):
    return lax.dot_general(a, b, (((1,), (0,)), ((), ())), preferred_element_type=F32)


def nt(a, b):
    return lax.dot_general(a, b, (((1,), (1,)), ((), ())), preferred_element_type=F32)


def tn(a, b):
    return lax.dot_general(a, b, (((0,), (0,)), ((), ())), preferred_element_type=F32)


def identity(size):
    rows = lax.broadcasted_iota(jnp.int32, (size, size), 0)
    cols = lax.broadcasted_iota(jnp.int32, (size, size), 1)
    return (rows == cols).astype(F32).astype(BF16)


def flip(block):
    return nt(identity(block.shape[1]), block)


def norm_rows(values):
    scale = 1.0 / values.shape[0]
    center = values - jnp.sum(values, axis=0, keepdims=True) * scale
    spread = jnp.sum(center * center, axis=0, keepdims=True) * scale
    return (center * lax.rsqrt(spread + EPSILON)).astype(BF16)


def run(kernel, outs, *args, smem=(), scratch=(), flops=15 * 10**8):
    vmem = pl.BlockSpec(memory_space=pltpu.VMEM)
    in_specs = [
        pl.BlockSpec(memory_space=pltpu.SMEM if at in smem else pltpu.VMEM) for at in range(len(args))
    ]
    moved = sum(a.size * a.dtype.itemsize for a in args)
    return pl.pallas_call(
        kernel,
        out_shape=[jax.ShapeDtypeStruct(shape, kind) for shape, kind in outs],
        in_specs=in_specs,
        out_specs=[vmem] * len(outs),
        scratch_shapes=[pltpu.VMEM(shape, kind) for shape, kind in scratch],
        compiler_params=pltpu.CompilerParams(vmem_limit_bytes=VMEM_LIMIT),
        cost_estimate=pl.CostEstimate(flops=flops, bytes_accessed=moved, transcendentals=0),
    )(*args)


VMEM_LIMIT = 20 * 1024 * 1024
SPLIT = ((7, 5), (6, 4), (3, 2), (1, 0))
OPS = len(SPLIT)
NEAR = 4
NEAR_STEPS = (3, 2, 1, 0)


def partner_chip(chip, core, op):
    return chip ^ jnp.where(core == 0, SPLIT[op][0], SPLIT[op][1])


def project_kernel(feat_ref, weight_ref, live_in_ref, pay_ref, left_ref, live_ref, turned, packed):
    homologs, rows, _ = feat_ref.shape
    half = weight_ref.shape[0] // 2
    quarter = half // 2
    values = feat_ref[...].reshape(homologs * rows, feat_ref.shape[2])
    center = values - jnp.mean(values, axis=1, keepdims=True)
    spread = jnp.mean(center * center, axis=1, keepdims=True)
    normed = (center * lax.rsqrt(spread + EPSILON)).astype(BF16)
    total = homologs * rows
    out_row = lax.broadcasted_iota(jnp.int32, (total, total), 0)
    in_row = lax.broadcasted_iota(jnp.int32, (total, total), 1)
    order = in_row == (out_row & (homologs - 1)) * rows + out_row // homologs
    normed = nn(order.astype(F32).astype(BF16), normed).astype(BF16)
    live = live_in_ref[...]
    weight = weight_ref[...]
    blank = jnp.zeros((homologs, normed.shape[1]), BF16)
    for row in range(rows):
        mine = normed[row * homologs : (row + 1) * homologs]
        low = nt(weight, jnp.concatenate([mine, blank], axis=0)) * live[row : row + 1]
        high = nt(weight, jnp.concatenate([blank, mine], axis=0)) * live[row : row + 1]
        left_ref[row * half : (row + 1) * half] = low[:half].astype(BF16)
        left_ref[(rows + row) * half : (rows + row + 1) * half] = high[:half].astype(BF16)
        turned[row] = low[half : half + quarter] + high[half + quarter :]
    for pair in range(quarter):
        packed[pair * rows : (pair + 1) * rows] = turned[:, pair, :]
    packed[quarter * rows : (quarter + 1) * rows] = live
    packed[(quarter + 1) * rows :] = jnp.zeros((rows, 2 * homologs), F32)
    pay_ref[...] = packed[...].astype(BF16)
    live_ref[...] = jnp.where(lax.broadcasted_iota(jnp.int32, live.shape, 1) < homologs, live, 0.0)


def prep_kernel(
    where_ref, chain_ref, chains_ref, pair_ref, table_ref, outer_ref, proj_ref, out_ref,
    base_ref, outer_t_ref, proj_t_ref, out_t_ref, table_pad, outer_pad,
):
    rows, cols, width = pair_ref.shape
    bins = table_ref.shape[0]
    table_pad[...] = jnp.zeros_like(table_pad)
    table_pad[0:bins, :] = table_ref[...].astype(F32)
    table = flip(table_pad[...].astype(BF16)).astype(BF16)
    chains = chains_ref[...]
    col = lax.broadcasted_iota(jnp.int32, (1, cols), 1)
    slot = lax.broadcasted_iota(jnp.int32, (table_pad.shape[0], cols), 0)
    for row in range(rows):
        place = where_ref[0] + row
        offset = jnp.clip(place - col, -RELMAX, RELMAX) + RELMAX
        bin_index = jnp.where(chains == chain_ref[place], offset, 2 * RELMAX + 1)
        hot = (slot == bin_index).astype(F32).astype(BF16)
        base_ref[row] = flip(pair_ref[row]) + nn(table, hot)
    half = outer_pad.shape[0]
    outer_pad[...] = outer_ref[...].astype(F32).reshape(outer_pad.shape)
    for d in range(half):
        outer_t_ref[:, d * half : (d + 1) * half] = flip(outer_pad[:, d, :].astype(BF16)).astype(BF16)
    for turn in range(2):
        proj_t_ref[turn] = tn(proj_ref[turn], identity(width)).astype(BF16)
        out_t_ref[turn] = flip(out_ref[turn]).astype(BF16)


def sigmoid(values):
    return 0.5 * jnp.tanh(0.5 * values) + 0.5


def sides(streams, weight, lives, gate_ref, lefts, rights, row):
    width, cols = streams[0].shape
    made = nn(weight, jnp.concatenate([norm_rows(stream) for stream in streams], axis=1))
    for at, live in enumerate(lives):
        part = [
            made[block * width : (block + 1) * width, at * cols : (at + 1) * cols] for block in range(5)
        ]
        lefts[:, row + at, :] = sigmoid(part[0]) * part[1] * live
        rights[:, row + at, :] = sigmoid(part[2]) * part[3] * live
        gate_ref[row + at] = sigmoid(part[4])


def flat(block):
    return block.reshape(block.shape[0] * block.shape[1], block.shape[2])


def outer_kernel(
    where_ref, flag_ref, own_ref, other_ref, left_ref, live_ref, base_ref, outer_t_ref, proj_ref, present_ref,
    stream_ref, gate_ref, far0, far1, theirs_ref, near0, near1, near2, near3, came, outer, lefts, rights,
):
    rows, width, cols = base_ref.shape
    chip, core = where_ref[1], where_ref[2]
    per = own_ref.shape[1]
    chips = own_ref.shape[0]
    for at in range(chips):
        chip_at = chip ^ (at % 2 * 4 + at // 2 % 2 * 2 + at // 4)
        came[chip_at * 2 + core] = own_ref[at].astype(F32)
        came[chip_at * 2 + (1 - core)] = other_ref[at].astype(F32)
    half = left_ref.shape[0] // (2 * rows)
    quarter = half // 2
    live_all = came[:, quarter * rows : (quarter + 1) * rows, :].reshape(cols, per_lane(came)).astype(BF16)
    counts = nt(live_ref[...].astype(BF16), live_all)
    share = 1.0 / jnp.maximum(counts, 1.0)
    left_all = left_ref[...]
    for pair in range(quarter):
        right = came[:, pair * rows : (pair + 1) * rows, :].reshape(cols, per_lane(came)).astype(BF16)
        made = nt(left_all, right).astype(BF16)
        for part in range(2):
            d = part * quarter + pair
            for row in range(rows):
                first = (part * rows + row) * half
                lane = (row % 2) * cols
                outer[row // 2, d * half : (d + 1) * half, lane : lane + cols] = made[first : first + half]
    present = present_ref[...].astype(F32)
    for row in range(0, rows, 2):
        product = nn(outer_t_ref[...], outer[row // 2])
        streams, lives = [], []
        for at in range(2):
            streams.append(
                base_ref[row + at] + product[:, at * cols : (at + 1) * cols] * share[row + at : row + at + 1]
            )
            stream_ref[row + at] = streams[at]
            lives.append(present * flag_ref[where_ref[0] + row + at].astype(F32))
        sides(streams, proj_ref[0], lives, gate_ref, lefts, rights, row)
    size = width // NEAR
    block = size * rows

    def group(side, to):
        first = pl.multiple_of((to & (NEAR - 1)) * size, size)
        return flat(side[pl.ds(first, size)]).astype(BF16)

    for op, far in enumerate((far0, far1)):
        far[...] = group(rights, partner_chip(chip, core, op))
        theirs_ref[op * block : (op + 1) * block] = group(rights, partner_chip(chip, 1 - core, op))
    for step, near in enumerate((near0, near1, near2, near3)):
        near[0:block] = group(lefts, chip ^ step)
        near[block:] = group(rights, chip ^ step)


def per_lane(ref):
    return ref.shape[-1]


def mix_rows_kernel(
    where_ref, near0, near1, near2, near3, far0, far1, other_ref,
    out0, out1, out2, out3, lefts, rights, mixed,
):
    chip, core = where_ref[1], where_ref[2]
    count, rows, cols = lefts.shape[1:]
    block = count * rows
    for at, (step, near) in enumerate(zip(NEAR_STEPS, (near0, near1, near2, near3))):
        lefts[step] = near[0:block].astype(F32).reshape(count, rows, cols)
        rights[(chip ^ step) * 2 + core] = near[block:].astype(F32).reshape(count, rows, cols)
        theirs = other_ref[at * block : (at + 1) * block]
        rights[(chip ^ step) * 2 + (1 - core)] = theirs.astype(F32).reshape(count, rows, cols)
    for op, far in enumerate((far0, far1)):
        for half in range(2):
            at = partner_chip(chip, core, op) * 2 + (core ^ half)
            rights[at] = far[half * block : (half + 1) * block].astype(F32).reshape(count, rows, cols)
            at = partner_chip(chip, 1 - core, op) * 2 + ((1 - core) ^ half)
            place = (NEAR + op * 2 + half) * block
            rights[at] = other_ref[place : place + block].astype(F32).reshape(count, rows, cols)
    for c in range(count):
        left = flat(lefts[:, c]).astype(BF16)
        right = flat(rights[:, c]).astype(BF16)
        mixed[:, c, :] = nt(left, right)
    for step, out in enumerate((out0, out1, out2, out3)):
        out[...] = flat(mixed[step * rows : (step + 1) * rows]).astype(BF16)


def pick_kernel(*refs):
    blocks, out_ref = refs[:-1], refs[-1]
    for at, block in enumerate(blocks):
        half = block.shape[0] // 2
        out_ref[at * half : (at + 1) * half] = block[half:]


def update(came, row, stream_ref, gate_ref, out_weight):
    normed = jnp.concatenate([norm_rows(flat(came[row + at])) for at in range(2)], axis=1)
    made = nn(out_weight, normed)
    cols = made.shape[1] // 2
    return [
        stream_ref[row + at] + gate_ref[row + at] * made[:, at * cols : (at + 1) * cols] for at in range(2)
    ]


def between_kernel(
    where_ref, flag_ref, in0, in1, in2, in3, stream_ref, gate_ref, out_weight_ref, proj_ref, present_ref,
    next_ref, next_gate_ref, mine0, mine1, mine2, mine3, theirs_ref, came, lefts, rights,
):
    rows, width, cols = stream_ref.shape
    chip, core = where_ref[1], where_ref[2]
    size = width // NEAR
    for step, block in zip(NEAR_STEPS, (in0, in1, in2, in3)):
        came[:, (chip ^ step) & (NEAR - 1)] = block[...].astype(F32).reshape(rows, size, cols)
    present = present_ref[...].astype(F32)
    for row in range(0, rows, 2):
        streams = update(came, row, stream_ref, gate_ref, out_weight_ref[0])
        lives = []
        for at in range(2):
            next_ref[row + at] = streams[at]
            lives.append(present * flag_ref[where_ref[0] + row + at].astype(F32))
        sides(streams, proj_ref[1], lives, next_gate_ref, lefts, rights, row)
    size = width // (2 * OPS)
    block = size * rows
    for op, mine in enumerate((mine0, mine1, mine2, mine3)):
        for at, side in enumerate((lefts, rights)):
            first = pl.multiple_of(partner_chip(chip, core, op) * size, size)
            mine[at * block : (at + 1) * block] = flat(side[pl.ds(first, size)]).astype(BF16)
            first = pl.multiple_of(partner_chip(chip, 1 - core, op) * size, size)
            place = (op * 2 + at) * block
            theirs_ref[place : place + block] = flat(side[pl.ds(first, size)]).astype(BF16)


def mix_cols_kernel(where_ref, came0, came1, came2, came3, mine_ref, theirs_ref, lefts, rights, partial):
    chip, core = where_ref[1], where_ref[2]
    count, rows, cols = lefts.shape[1:]
    block = count * rows
    for op, came in enumerate((came0, came1, came2, came3)):
        for half in range(2):
            for at, side in enumerate((lefts, rights)):
                place = (half * 2 + at) * block
                side[op * 2 + half] = came[place : place + block].astype(F32).reshape(count, rows, cols)
    for c in range(count):
        left = flat(lefts[:, c]).astype(BF16)
        right = flat(rights[:, c]).astype(BF16)
        partial[:, c, :] = tn(left, right)
    for op in range(OPS):
        for half in range(2):
            to = (partner_chip(chip, core, op) * 2 + (core ^ half)) * rows
            mine_ref[op, half * block : (half + 1) * block] = flat(partial[pl.ds(to, rows)])
            to = (partner_chip(chip, 1 - core, op) * 2 + ((1 - core) ^ half)) * rows
            theirs_ref[op, half * block : (half + 1) * block] = flat(partial[pl.ds(to, rows)])


def sum_kernel(mine_ref, got_ref, *outs):
    for op, out in enumerate(outs):
        out[...] = (mine_ref[op] + got_ref[op]).astype(BF16)


def final_kernel(
    where_ref, came0, came1, came2, came3, other_ref, stream_ref, gate_ref, out_weight_ref, out_ref, came
):
    rows, width, cols = stream_ref.shape
    chip, core = where_ref[1], where_ref[2]
    size = width // (2 * OPS)
    block = size * rows
    for op, mine in enumerate((came0, came1, came2, came3)):
        came[:, partner_chip(chip, core, op)] = mine[0:block].astype(F32).reshape(rows, size, cols)
        theirs = other_ref[op * block : (op + 1) * block]
        came[:, partner_chip(chip, 1 - core, op)] = theirs.astype(F32).reshape(rows, size, cols)
    for row in range(0, rows, 2):
        for at, stream in enumerate(update(came, row, stream_ref, gate_ref, out_weight_ref[1])):
            out_ref[row + at] = flip_out(stream)


def flip_out(stream):
    return nt(identity(stream.shape[1]), stream.astype(BF16)).astype(BF16)


def chip_permute(block, step):
    count = lax.axis_size("wide")
    return lax.ppermute(block, "wide", [(w, w ^ (2 * step)) for w in range(count)])


def exchange(blocks, steps):
    return [chip_permute(blocks[step], step) if step else blocks[0] for step in steps]


def split_permute(block, op):
    count = lax.axis_size("wide")
    return lax.ppermute(block, "wide", [(w, w ^ (2 * SPLIT[op][w % 2])) for w in range(count)])


def with_partner(mine, theirs):
    got, messages, place = core_permute(theirs), [], 0
    for block in mine:
        messages.append(jnp.concatenate([block, got[place : place + block.shape[0]]], axis=0))
        place += block.shape[0]
    return messages


def core_permute(block):
    count = lax.axis_size("wide")
    return lax.ppermute(block, "wide", [(w, w ^ 1) for w in range(count)])


def per_device_chips(
    pairwise_state,
    homolog_features,
    residue_chain_index,
    resolved_residue_mask,
    alignment_mask,
    relative_offset_table,
    homolog_to_sides_matrix,
    outer_mean_output_weight,
    triangle_projection_weight,
    triangle_output_weight,
):
    rows, cols, width = pairwise_state.shape
    homologs = homolog_features.shape[0]
    half = homolog_to_sides_matrix.shape[1] // 2
    device = lax.axis_index("wide")
    chip, core = device // 2, device % 2
    where = jnp.stack([device * rows, chip, core]).astype(jnp.int32)
    present = resolved_residue_mask.reshape(1, cols)
    pay_rows = (half // 2 + 2) * rows
    row_present = lax.dynamic_slice_in_dim(resolved_residue_mask, device * rows, rows).astype(F32)
    live = alignment_mask.T.astype(F32) * row_present[:, None]
    live = jnp.concatenate([live, live], axis=1)
    pay, left, live = run(
        project_kernel,
        [((pay_rows, LANES), BF16), ((2 * rows * half, LANES), BF16), ((rows, LANES), F32)],
        homolog_features.astype(F32), homolog_to_sides_matrix.T, live,
        scratch=[((rows, half // 2, LANES), F32), ((pay_rows, LANES), F32)],
    )
    far_z = chip_permute(pay, 4)
    base, outer_t, proj_t, out_t = run(
        prep_kernel,
        [
            ((rows, width, cols), F32),
            ((width, half * half), BF16),
            ((2, triangle_projection_weight.shape[2], width), BF16),
            ((2, width, width), BF16),
        ],
        where, residue_chain_index, residue_chain_index.reshape(1, cols), pairwise_state,
        relative_offset_table, outer_mean_output_weight, triangle_projection_weight, triangle_output_weight,
        smem=(0, 1),
        scratch=[((LANES, width), F32), ((half, half, width), F32)],
    )
    along_z = jnp.stack([pay, far_z])
    along_z, base, outer_t, proj_t, out_t = lax.optimization_barrier((along_z, base, outer_t, proj_t, out_t))
    along_z = jnp.concatenate([along_z, chip_permute(along_z, 2)], axis=0)
    own = jnp.concatenate([along_z, chip_permute(along_z, 1)], axis=0)
    other = core_permute(own)
    tall = width * rows
    near, all_ = tall // NEAR, tall // (2 * OPS)
    made = run(
        outer_kernel,
        [((rows, width, cols), F32)] * 2
        + [((near, cols), BF16)] * 2
        + [((2 * near, cols), BF16)] * (1 + NEAR),
        where, resolved_residue_mask, own, other, left, live, base, outer_t, proj_t, present,
        smem=(0, 1),
        scratch=[
            ((16, pay_rows, LANES), F32),
            ((rows // 2, half * half, 2 * cols), BF16),
            ((width, rows, cols), F32),
            ((width, rows, cols), F32),
        ],
        flops=4 * 10**9,
    )
    stream, gate = made[0], made[1]
    came = exchange(made[5:9], NEAR_STEPS)
    far = [split_permute(block, op) for op, block in enumerate(with_partner(made[2:4], made[4]))]
    rights = jnp.concatenate([block[near:] for block in came] + far, axis=0)
    mixed = run(
        mix_rows_kernel,
        [((near, cols), BF16)] * NEAR,
        where, *came, *far, core_permute(rights),
        smem=(0,),
        scratch=[
            ((NEAR, width // NEAR, rows, cols), F32),
            ((16, width // NEAR, rows, cols), F32),
            ((NEAR * rows, width // NEAR, cols), F32),
        ],
    )
    mixed = exchange(mixed, NEAR_STEPS)
    made = run(
        between_kernel,
        [((rows, width, cols), F32)] * 2 + [((2 * all_, cols), BF16)] * OPS + [((2 * OPS * all_, cols), BF16)],
        where, resolved_residue_mask, *mixed, stream, gate, out_t, proj_t, present,
        smem=(0, 1),
        scratch=[
            ((rows, NEAR, width // NEAR, cols), F32),
            ((width, rows, cols), F32),
            ((width, rows, cols), F32),
        ],
    )
    stream, gate, theirs = made[0], made[1], made[6]
    came = [split_permute(block, op) for op, block in enumerate(with_partner(made[2:6], theirs))]
    mine, theirs = run(
        mix_cols_kernel,
        [((OPS, 2 * all_, cols), F32)] * 2,
        where, *came,
        smem=(0,),
        scratch=[
            ((2 * OPS, width // (2 * OPS), rows, cols), F32),
            ((2 * OPS, width // (2 * OPS), rows, cols), F32),
            ((16 * rows, width // (2 * OPS), cols), F32),
        ],
    )
    mixed = run(sum_kernel, [((2 * all_, cols), BF16)] * OPS, mine, core_permute(theirs))
    mixed = [split_permute(block, op) for op, block in enumerate(mixed)]
    other = core_permute(run(pick_kernel, [((OPS * all_, cols), BF16)], *mixed)[0])
    return run(
        final_kernel,
        [((rows, cols, width), BF16)],
        where, *mixed, other, stream, gate, out_t,
        smem=(0,),
        scratch=[((rows, 2 * OPS, width // (2 * OPS), cols), F32)],
    )[0]


def fits_chips(mesh):
    return mesh.shape["narrow"] == 1 and mesh.shape["wide"] == 16


def solution(mesh):
    per_device = per_device_chips if fits_chips(mesh) else per_device_general
    return jax.shard_map(
        per_device,
        mesh=mesh,
        in_specs=(
            P(("grp", "wide"), "narrow", None),
            P("grp", "wide", None),
            P("grp"),
            P("grp"),
            P("grp", "wide"),
            P(),
            P(),
            P(),
            P(),
            P(),
        ),
        out_specs=P(("grp", "wide"), "narrow", None),
        check_vma=False,
    )
```

```python
import functools

import jax
import jax.numpy as jnp
from jax import lax
from jax.experimental import pallas as pl
from jax.experimental.pallas import tpu as pltpu
from jax.sharding import PartitionSpec as P

RELMAX = 32
EPSILON = 1e-05
LANES = 128
F32 = jnp.float32
BF16 = jnp.bfloat16


def apply_layer_norm(values, axis_dim):
    center = values - jnp.mean(values, axis=axis_dim, keepdims=True)
    spread = jnp.mean(center * center, axis=axis_dim, keepdims=True)
    return center * lax.rsqrt(spread + EPSILON)


def gather_wide(block):
    n = lax.axis_size("wide")
    if n % 4 or n < 8:
        return lax.all_gather(block, "wide", axis=0)
    outer = n // 4
    me = lax.axis_index("wide")
    high, mid, low = me // 4, (me // 2) % 2, me % 2
    arrived = [block]
    for shift in range(1, outer):
        perm = [(w, ((w // 4 + shift) % outer) * 4 + w % 4) for w in range(n)]
        arrived.append(lax.ppermute(block, "wide", perm))
    held = jnp.zeros((outer,) + block.shape, block.dtype)
    for shift, piece in enumerate(arrived):
        held = lax.dynamic_update_index_in_dim(held, piece, (high - shift + outer) % outer, 0)
    other = lax.ppermute(held, "wide", [(w, w ^ 2) for w in range(n)])
    held = jnp.stack(
        [jnp.where(mid == 0, held, other), jnp.where(mid == 0, other, held)], axis=1
    )
    other = lax.ppermute(held, "wide", [(w, w ^ 1) for w in range(n)])
    held = jnp.stack(
        [jnp.where(low == 0, held, other), jnp.where(low == 0, other, held)], axis=2
    )
    return held.reshape((n,) + block.shape)


def triangle(stream, pair_live, proj_weight, out_weight, incoming):
    rows = stream.shape[0]
    cols = stream.shape[1]
    width = out_weight.shape[0]
    wide_count = lax.axis_size("wide")
    core_count = lax.axis_size("narrow")
    devices = wide_count * core_count
    per_dev = width // devices
    normed = apply_layer_norm(stream, 2).astype(jnp.bfloat16)
    blocks = [proj_weight[:, index * width : (index + 1) * width] for index in range(4)]

    def project(block):
        return jnp.einsum("ijd,dc->cij", normed, block, preferred_element_type=jnp.float32)

    left_side = (jax.nn.sigmoid(project(blocks[0])) * project(blocks[1]) * pair_live[None]).astype(
        jnp.bfloat16
    )
    right_side = (jax.nn.sigmoid(project(blocks[2])) * project(blocks[3]) * pair_live[None]).astype(
        jnp.bfloat16
    )
    gate = jax.nn.sigmoid(
        jnp.einsum(
            "ijd,dc->ijc", normed, proj_weight[:, 4 * width :], preferred_element_type=jnp.float32
        )
    )
    form = "cki,ckj->cij" if incoming else "cik,cjk->cij"
    both = jnp.stack(
        [
            left_side.reshape(devices, per_dev, rows * cols),
            right_side.reshape(devices, per_dev, rows * cols),
        ],
        axis=1,
    ).reshape(devices, 2 * per_dev, rows * cols)
    both = lax.all_to_all(both, ("wide", "narrow"), split_axis=0, concat_axis=0, tiled=True)
    both = both.reshape(wide_count, core_count, 2, per_dev, rows, cols)
    both = jnp.transpose(both, (2, 3, 0, 4, 1, 5)).reshape(
        2, per_dev, wide_count * rows, core_count * cols
    )
    mixed = jnp.einsum(form, both[0], both[1], preferred_element_type=jnp.float32).astype(
        jnp.bfloat16
    )
    spread_out = mixed.reshape(per_dev, wide_count, rows, core_count, cols)
    spread_out = jnp.transpose(spread_out, (1, 3, 0, 2, 4)).reshape(
        wide_count * core_count * per_dev, rows * cols
    )
    returned = lax.all_to_all(
        spread_out, ("wide", "narrow"), split_axis=0, concat_axis=0, tiled=True
    ).reshape(width, rows, cols)
    blended_standardize = apply_layer_norm(returned.astype(jnp.float32), 0).astype(jnp.bfloat16)
    update = jnp.einsum(
        "cij,cd->ijd", blended_standardize, out_weight, preferred_element_type=jnp.float32
    )
    return stream + gate * update


def per_device_general(
    pairwise_state,
    homolog_features,
    residue_chain_index,
    resolved_residue_mask,
    alignment_mask,
    relative_offset_table,
    homolog_to_sides_matrix,
    outer_mean_output_weight,
    triangle_projection_weight,
    triangle_output_weight,
):
    rows = pairwise_state.shape[0]
    cols = pairwise_state.shape[1]
    row_start = lax.axis_index("wide") * rows
    col_start = lax.axis_index("narrow") * cols
    residue_present = resolved_residue_mask.astype(jnp.float32)
    row_present = lax.dynamic_slice_in_dim(residue_present, row_start, rows)
    col_live = lax.dynamic_slice_in_dim(residue_present, col_start, cols)
    present_flags = alignment_mask.astype(jnp.float32) * row_present[None, :]
    alignment_normed = apply_layer_norm(homolog_features.astype(jnp.float32), 2).astype(
        jnp.bfloat16
    )
    projected_rows = jnp.einsum(
        "tna,ak->tnk", alignment_normed, homolog_to_sides_matrix, preferred_element_type=jnp.float32
    )
    projected_rows = (projected_rows * present_flags[:, :, None]).astype(jnp.bfloat16)
    half_width = projected_rows.shape[2] // 2
    homologs = projected_rows.shape[0]
    left_proj = projected_rows[:, :, :half_width]
    right_proj = projected_rows[:, :, half_width:]
    live_flags = present_flags.astype(jnp.bfloat16)
    packed = jnp.concatenate(
        [jnp.transpose(right_proj, (1, 0, 2)).reshape(rows, homologs * half_width), live_flags.T],
        axis=1,
    )
    gathered = gather_wide(packed).reshape(-1, packed.shape[1])
    gathered = lax.dynamic_slice_in_dim(gathered, col_start, cols, 0)
    right_mine = jnp.transpose(
        gathered[:, : homologs * half_width].reshape(cols, homologs, half_width), (1, 0, 2)
    )
    live_mine = gathered[:, homologs * half_width :].T
    counts = jnp.dot(live_flags.T, live_mine, preferred_element_type=jnp.float32)

    def opm_row(left_row):
        outer = jnp.einsum("sc,sjd->jcd", left_row, right_mine, preferred_element_type=jnp.float32)
        outer = outer.reshape(cols, half_width * half_width).astype(jnp.bfloat16)
        return jnp.dot(outer, outer_mean_output_weight, preferred_element_type=jnp.float32)

    opm = lax.map(opm_row, jnp.transpose(left_proj, (1, 0, 2)))
    row_pos = row_start + jnp.arange(rows, dtype=jnp.int32)
    col_pos = col_start + jnp.arange(cols, dtype=jnp.int32)
    row_chain = lax.dynamic_slice_in_dim(residue_chain_index, row_start, rows)
    col_chain = lax.dynamic_slice_in_dim(residue_chain_index, col_start, cols)
    offset = jnp.clip(row_pos[:, None] - col_pos[None, :], -RELMAX, RELMAX) + RELMAX
    bin_index = jnp.where(row_chain[:, None] == col_chain[None, :], offset, 2 * RELMAX + 1)
    bin_count = relative_offset_table.shape[0]
    one_hot = (
        bin_index[:, :, None] == jnp.arange(bin_count, dtype=jnp.int32)[None, None, :]
    ).astype(jnp.bfloat16)
    relpos = jnp.einsum(
        "ijb,bc->ijc", one_hot, relative_offset_table, preferred_element_type=jnp.float32
    )
    stream = (
        pairwise_state.astype(jnp.float32) + relpos + opm / jnp.maximum(counts, 1.0)[:, :, None]
    )
    pair_live = row_present[:, None] * col_live[None, :]
    for turn_index in range(2):
        stream = triangle(
            stream,
            pair_live,
            triangle_projection_weight[turn_index],
            triangle_output_weight[turn_index],
            turn_index == 1,
        )
    return stream.astype(jnp.bfloat16)


def nn(a, b):
    return lax.dot_general(a, b, (((1,), (0,)), ((), ())), preferred_element_type=F32)


def nt(a, b):
    return lax.dot_general(a, b, (((1,), (1,)), ((), ())), preferred_element_type=F32)


def tn(a, b):
    return lax.dot_general(a, b, (((0,), (0,)), ((), ())), preferred_element_type=F32)


def identity(size):
    rows = lax.broadcasted_iota(jnp.int32, (size, size), 0)
    cols = lax.broadcasted_iota(jnp.int32, (size, size), 1)
    return (rows == cols).astype(F32).astype(BF16)


def flip(block):
    return nt(identity(block.shape[1]), block)


def norm_rows(values):
    scale = 1.0 / values.shape[0]
    center = values - jnp.sum(values, axis=0, keepdims=True) * scale
    spread = jnp.sum(center * center, axis=0, keepdims=True) * scale
    return (center * lax.rsqrt(spread + EPSILON)).astype(BF16)


def run(kernel, outs, *args, smem=(), scratch=(), flops=15 * 10**8):
    vmem = pl.BlockSpec(memory_space=pltpu.VMEM)
    in_specs = [
        pl.BlockSpec(memory_space=pltpu.SMEM if at in smem else pltpu.VMEM) for at in range(len(args))
    ]
    moved = sum(a.size * a.dtype.itemsize for a in args)
    return pl.pallas_call(
        kernel,
        out_shape=[jax.ShapeDtypeStruct(shape, kind) for shape, kind in outs],
        in_specs=in_specs,
        out_specs=[vmem] * len(outs),
        scratch_shapes=[pltpu.VMEM(shape, kind) for shape, kind in scratch],
        compiler_params=pltpu.CompilerParams(vmem_limit_bytes=VMEM_LIMIT),
        cost_estimate=pl.CostEstimate(flops=flops, bytes_accessed=moved, transcendentals=0),
    )(*args)


VMEM_LIMIT = 20 * 1024 * 1024
SPLIT = ((7, 3), (2, 6), (5, 1), (0, 4))
FAR_SPLIT = ((7, 5), (6, 4))
OPS = len(SPLIT)
NEAR = 4
NEAR_STEPS = (3, 2, 1, 0)


def partner_chip(chip, core, op, split=SPLIT):
    return chip ^ jnp.where(core == 0, split[op][0], split[op][1])


def project_kernel(feat_ref, weight_ref, live_in_ref, pay_ref, left_ref, live_ref, turned, packed):
    homologs, rows, _ = feat_ref.shape
    half = weight_ref.shape[0] // 2
    quarter = half // 2
    values = feat_ref[...].reshape(homologs * rows, feat_ref.shape[2])
    center = values - jnp.mean(values, axis=1, keepdims=True)
    spread = jnp.mean(center * center, axis=1, keepdims=True)
    normed = (center * lax.rsqrt(spread + EPSILON)).astype(BF16)
    total = homologs * rows
    out_row = lax.broadcasted_iota(jnp.int32, (total, total), 0)
    in_row = lax.broadcasted_iota(jnp.int32, (total, total), 1)
    order = in_row == (out_row & (homologs - 1)) * rows + out_row // homologs
    normed = nn(order.astype(F32).astype(BF16), normed).astype(BF16)
    live = live_in_ref[...]
    weight = weight_ref[...]
    blank = jnp.zeros((homologs, normed.shape[1]), BF16)
    for row in range(rows):
        mine = normed[row * homologs : (row + 1) * homologs]
        low = nt(weight, jnp.concatenate([mine, blank], axis=0)) * live[row : row + 1]
        high = nt(weight, jnp.concatenate([blank, mine], axis=0)) * live[row : row + 1]
        left_ref[row * half : (row + 1) * half] = low[:half].astype(BF16)
        left_ref[(rows + row) * half : (rows + row + 1) * half] = high[:half].astype(BF16)
        turned[row] = low[half : half + quarter] + high[half + quarter :]
    for pair in range(quarter):
        packed[pair * rows : (pair + 1) * rows] = turned[:, pair, :]
    packed[quarter * rows : (quarter + 1) * rows] = live
    packed[(quarter + 1) * rows :] = jnp.zeros((rows, 2 * homologs), F32)
    pay_ref[...] = packed[...].astype(BF16)
    live_ref[...] = jnp.where(lax.broadcasted_iota(jnp.int32, live.shape, 1) < homologs, live, 0.0)


def prep_kernel(
    where_ref, chain_ref, chains_ref, pair_ref, table_ref, outer_ref, proj_ref, out_ref,
    base_ref, outer_t_ref, proj_t_ref, out_t_ref, table_pad, outer_pad,
):
    rows, cols, width = pair_ref.shape
    bins = table_ref.shape[0]
    table_pad[...] = jnp.zeros_like(table_pad)
    table_pad[0:bins, :] = table_ref[...].astype(F32)
    table = flip(table_pad[...].astype(BF16)).astype(BF16)
    chains = chains_ref[...]
    col = lax.broadcasted_iota(jnp.int32, (1, cols), 1)
    slot = lax.broadcasted_iota(jnp.int32, (table_pad.shape[0], cols), 0)
    for row in range(rows):
        place = where_ref[0] + row
        offset = jnp.clip(place - col, -RELMAX, RELMAX) + RELMAX
        bin_index = jnp.where(chains == chain_ref[place], offset, 2 * RELMAX + 1)
        hot = (slot == bin_index).astype(F32).astype(BF16)
        base_ref[row] = flip(pair_ref[row]) + nn(table, hot)
    half = outer_pad.shape[0]
    outer_pad[...] = outer_ref[...].astype(F32).reshape(outer_pad.shape)
    for d in range(half):
        outer_t_ref[:, d * half : (d + 1) * half] = flip(outer_pad[:, d, :].astype(BF16)).astype(BF16)
    for turn in range(2):
        proj_t_ref[turn] = tn(proj_ref[turn], identity(width)).astype(BF16)
        out_t_ref[turn] = flip(out_ref[turn]).astype(BF16)


def sigmoid(values):
    return 0.5 * jnp.tanh(0.5 * values) + 0.5


def sides(streams, weight, lives, gate_ref, lefts, rights, row):
    width, cols = streams[0].shape
    made = nn(weight, jnp.concatenate([norm_rows(stream) for stream in streams], axis=1))
    for at, live in enumerate(lives):
        part = [
            made[block * width : (block + 1) * width, at * cols : (at + 1) * cols] for block in range(5)
        ]
        lefts[:, row + at, :] = sigmoid(part[0]) * part[1] * live
        rights[:, row + at, :] = sigmoid(part[2]) * part[3] * live
        gate_ref[row + at] = sigmoid(part[4])


def flat(block):
    return block.reshape(block.shape[0] * block.shape[1], block.shape[2])


def outer_kernel(
    where_ref, flag_ref, own_ref, other_ref, left_ref, live_ref, base_ref, outer_t_ref, proj_ref, present_ref,
    stream_ref, gate_ref, far0, far1, theirs_ref, near0, near1, near2, near3, came, outer, lefts, rights,
):
    rows, width, cols = base_ref.shape
    chip, core = where_ref[1], where_ref[2]
    per = own_ref.shape[1]
    chips = own_ref.shape[0]
    for at in range(chips):
        chip_at = chip ^ (at % 2 * 4 + at // 2 % 2 * 2 + at // 4)
        came[chip_at * 2 + core] = own_ref[at].astype(F32)
        came[chip_at * 2 + (1 - core)] = other_ref[at].astype(F32)
    half = left_ref.shape[0] // (2 * rows)
    quarter = half // 2
    live_all = came[:, quarter * rows : (quarter + 1) * rows, :].reshape(cols, per_lane(came)).astype(BF16)
    counts = nt(live_ref[...].astype(BF16), live_all)
    share = 1.0 / jnp.maximum(counts, 1.0)
    left_all = left_ref[...]
    for pair in range(quarter):
        right = came[:, pair * rows : (pair + 1) * rows, :].reshape(cols, per_lane(came)).astype(BF16)
        made = nt(left_all, right).astype(BF16)
        for part in range(2):
            d = part * quarter + pair
            for row in range(rows):
                first = (part * rows + row) * half
                lane = (row % 2) * cols
                outer[row // 2, d * half : (d + 1) * half, lane : lane + cols] = made[first : first + half]
    present = present_ref[...].astype(F32)
    for row in range(0, rows, 2):
        product = nn(outer_t_ref[...], outer[row // 2])
        streams, lives = [], []
        for at in range(2):
            streams.append(
                base_ref[row + at] + product[:, at * cols : (at + 1) * cols] * share[row + at : row + at + 1]
            )
            stream_ref[row + at] = streams[at]
            lives.append(present * flag_ref[where_ref[0] + row + at].astype(F32))
        sides(streams, proj_ref[0], lives, gate_ref, lefts, rights, row)
    size = width // NEAR
    block = size * rows

    def group(side, to):
        first = pl.multiple_of((to & (NEAR - 1)) * size, size)
        return flat(side[pl.ds(first, size)]).astype(BF16)

    for op, far in enumerate((far0, far1)):
        far[...] = group(rights, partner_chip(chip, core, op, FAR_SPLIT))
        theirs_ref[op * block : (op + 1) * block] = group(rights, partner_chip(chip, 1 - core, op, FAR_SPLIT))
    for step, near in enumerate((near0, near1, near2, near3)):
        near[0:block] = group(lefts, chip ^ step)
        near[block:] = group(rights, chip ^ step)


def per_lane(ref):
    return ref.shape[-1]


def mix_rows_kernel(
    where_ref, near0, near1, near2, near3, far0, far1, other_ref,
    out0, out1, out2, out3, lefts, rights, mixed,
):
    chip, core = where_ref[1], where_ref[2]
    count, rows, cols = lefts.shape[1:]
    block = count * rows
    for at, (step, near) in enumerate(zip(NEAR_STEPS, (near0, near1, near2, near3))):
        lefts[step] = near[0:block].astype(F32).reshape(count, rows, cols)
        rights[(chip ^ step) * 2 + core] = near[block:].astype(F32).reshape(count, rows, cols)
        theirs = other_ref[at * block : (at + 1) * block]
        rights[(chip ^ step) * 2 + (1 - core)] = theirs.astype(F32).reshape(count, rows, cols)
    for op, far in enumerate((far0, far1)):
        for half in range(2):
            at = partner_chip(chip, core, op, FAR_SPLIT) * 2 + (core ^ half)
            rights[at] = far[half * block : (half + 1) * block].astype(F32).reshape(count, rows, cols)
            at = partner_chip(chip, 1 - core, op, FAR_SPLIT) * 2 + ((1 - core) ^ half)
            place = (NEAR + op * 2 + half) * block
            rights[at] = other_ref[place : place + block].astype(F32).reshape(count, rows, cols)
    for c in range(count):
        left = flat(lefts[:, c]).astype(BF16)
        right = flat(rights[:, c]).astype(BF16)
        mixed[:, c, :] = nt(left, right)
    for step, out in enumerate((out0, out1, out2, out3)):
        out[...] = flat(mixed[step * rows : (step + 1) * rows]).astype(BF16)


def pick_kernel(*refs):
    blocks, out_ref = refs[:-1], refs[-1]
    for at, block in enumerate(blocks):
        half = block.shape[0] // 2
        out_ref[at * half : (at + 1) * half] = block[half:]


def update(came, row, stream_ref, gate_ref, out_weight):
    normed = jnp.concatenate([norm_rows(flat(came[row + at])) for at in range(2)], axis=1)
    made = nn(out_weight, normed)
    cols = made.shape[1] // 2
    return [
        stream_ref[row + at] + gate_ref[row + at] * made[:, at * cols : (at + 1) * cols] for at in range(2)
    ]


def between_kernel(
    where_ref, flag_ref, in0, in1, in2, in3, stream_ref, gate_ref, out_weight_ref, proj_ref, present_ref,
    next_ref, next_gate_ref, mine0, mine1, mine2, mine3, theirs_ref, came, lefts, rights,
):
    rows, width, cols = stream_ref.shape
    chip, core = where_ref[1], where_ref[2]
    size = width // NEAR
    for step, block in zip(NEAR_STEPS, (in0, in1, in2, in3)):
        came[:, (chip ^ step) & (NEAR - 1)] = block[...].astype(F32).reshape(rows, size, cols)
    present = present_ref[...].astype(F32)
    for row in range(0, rows, 2):
        streams = update(came, row, stream_ref, gate_ref, out_weight_ref[0])
        lives = []
        for at in range(2):
            next_ref[row + at] = streams[at]
            lives.append(present * flag_ref[where_ref[0] + row + at].astype(F32))
        sides(streams, proj_ref[1], lives, next_gate_ref, lefts, rights, row)
    size = width // (2 * OPS)
    block = size * rows
    for op, mine in enumerate((mine0, mine1, mine2, mine3)):
        for at, side in enumerate((lefts, rights)):
            first = pl.multiple_of(partner_chip(chip, core, op) * size, size)
            mine[at * block : (at + 1) * block] = flat(side[pl.ds(first, size)]).astype(BF16)
            first = pl.multiple_of(partner_chip(chip, 1 - core, op) * size, size)
            place = (op * 2 + at) * block
            theirs_ref[place : place + block] = flat(side[pl.ds(first, size)]).astype(BF16)


def mix_cols_kernel(where_ref, came0, came1, came2, came3, mine_ref, theirs_ref, lefts, rights, partial):
    chip, core = where_ref[1], where_ref[2]
    count, rows, cols = lefts.shape[1:]
    block = count * rows
    for op, came in enumerate((came0, came1, came2, came3)):
        for half in range(2):
            for at, side in enumerate((lefts, rights)):
                place = (half * 2 + at) * block
                side[op * 2 + half] = came[place : place + block].astype(F32).reshape(count, rows, cols)
    for c in range(count):
        left = flat(lefts[:, c]).astype(BF16)
        right = flat(rights[:, c]).astype(BF16)
        partial[:, c, :] = tn(left, right)
    for op in range(OPS):
        for half in range(2):
            to = (partner_chip(chip, core, op) * 2 + (core ^ half)) * rows
            mine_ref[op, half * block : (half + 1) * block] = flat(partial[pl.ds(to, rows)])
            to = (partner_chip(chip, 1 - core, op) * 2 + ((1 - core) ^ half)) * rows
            theirs_ref[op, half * block : (half + 1) * block] = flat(partial[pl.ds(to, rows)])


def sum_kernel(mine_ref, got_ref, *outs):
    for op, out in enumerate(outs):
        out[...] = (mine_ref[op] + got_ref[op]).astype(BF16)


def final_kernel(
    where_ref, came0, came1, came2, came3, other_ref, stream_ref, gate_ref, out_weight_ref, out_ref, came
):
    rows, width, cols = stream_ref.shape
    chip, core = where_ref[1], where_ref[2]
    size = width // (2 * OPS)
    block = size * rows
    for op, mine in enumerate((came0, came1, came2, came3)):
        came[:, partner_chip(chip, core, op)] = mine[0:block].astype(F32).reshape(rows, size, cols)
        theirs = other_ref[op * block : (op + 1) * block]
        came[:, partner_chip(chip, 1 - core, op)] = theirs.astype(F32).reshape(rows, size, cols)
    for row in range(0, rows, 2):
        for at, stream in enumerate(update(came, row, stream_ref, gate_ref, out_weight_ref[1])):
            out_ref[row + at] = flip_out(stream)


def flip_out(stream):
    return nt(identity(stream.shape[1]), stream.astype(BF16)).astype(BF16)


def chip_permute(block, step):
    count = lax.axis_size("wide")
    return lax.ppermute(block, "wide", [(w, w ^ (2 * step)) for w in range(count)])


def exchange(blocks, steps):
    return [chip_permute(blocks[step], step) if step else blocks[0] for step in steps]


def split_permute(block, steps):
    count = lax.axis_size("wide")
    return lax.ppermute(block, "wide", [(w, w ^ (2 * steps[w % 2])) for w in range(count)])


def split_exchange(blocks, split=SPLIT):
    return [split_permute(block, steps) for block, steps in zip(blocks, split)]


def with_partner(mine, theirs):
    got, messages, place = core_permute(theirs), [], 0
    for block in mine:
        messages.append(jnp.concatenate([block, got[place : place + block.shape[0]]], axis=0))
        place += block.shape[0]
    return messages


def core_permute(block):
    count = lax.axis_size("wide")
    return lax.ppermute(block, "wide", [(w, w ^ 1) for w in range(count)])


def per_device_chips(
    pairwise_state,
    homolog_features,
    residue_chain_index,
    resolved_residue_mask,
    alignment_mask,
    relative_offset_table,
    homolog_to_sides_matrix,
    outer_mean_output_weight,
    triangle_projection_weight,
    triangle_output_weight,
):
    rows, cols, width = pairwise_state.shape
    homologs = homolog_features.shape[0]
    half = homolog_to_sides_matrix.shape[1] // 2
    device = lax.axis_index("wide")
    chip, core = device // 2, device % 2
    where = jnp.stack([device * rows, chip, core]).astype(jnp.int32)
    present = resolved_residue_mask.reshape(1, cols)
    pay_rows = (half // 2 + 2) * rows
    row_present = lax.dynamic_slice_in_dim(resolved_residue_mask, device * rows, rows).astype(F32)
    live = alignment_mask.T.astype(F32) * row_present[:, None]
    live = jnp.concatenate([live, live], axis=1)
    pay, left, live = run(
        project_kernel,
        [((pay_rows, LANES), BF16), ((2 * rows * half, LANES), BF16), ((rows, LANES), F32)],
        homolog_features.astype(F32), homolog_to_sides_matrix.T, live,
        scratch=[((rows, half // 2, LANES), F32), ((pay_rows, LANES), F32)],
    )
    far_z = chip_permute(pay, 4)
    base, outer_t, proj_t, out_t = run(
        prep_kernel,
        [
            ((rows, width, cols), F32),
            ((width, half * half), BF16),
            ((2, triangle_projection_weight.shape[2], width), BF16),
            ((2, width, width), BF16),
        ],
        where, residue_chain_index, residue_chain_index.reshape(1, cols), pairwise_state,
        relative_offset_table, outer_mean_output_weight, triangle_projection_weight, triangle_output_weight,
        smem=(0, 1),
        scratch=[((LANES, width), F32), ((half, half, width), F32)],
    )
    along_z = jnp.stack([pay, far_z])
    along_z, base, outer_t, proj_t, out_t = lax.optimization_barrier((along_z, base, outer_t, proj_t, out_t))
    along_z = jnp.concatenate([along_z, chip_permute(along_z, 2)], axis=0)
    own = jnp.concatenate([along_z, chip_permute(along_z, 1)], axis=0)
    other = core_permute(own)
    tall = width * rows
    near, all_ = tall // NEAR, tall // (2 * OPS)
    made = run(
        outer_kernel,
        [((rows, width, cols), F32)] * 2
        + [((near, cols), BF16)] * 2
        + [((2 * near, cols), BF16)] * (1 + NEAR),
        where, resolved_residue_mask, own, other, left, live, base, outer_t, proj_t, present,
        smem=(0, 1),
        scratch=[
            ((16, pay_rows, LANES), F32),
            ((rows // 2, half * half, 2 * cols), BF16),
            ((width, rows, cols), F32),
            ((width, rows, cols), F32),
        ],
        flops=4 * 10**9,
    )
    stream, gate = made[0], made[1]
    came = exchange(made[5:9], NEAR_STEPS)
    far = split_exchange(with_partner(made[2:4], made[4]), FAR_SPLIT)
    rights = jnp.concatenate([block[near:] for block in came] + far, axis=0)
    mixed = run(
        mix_rows_kernel,
        [((near, cols), BF16)] * NEAR,
        where, *came, *far, core_permute(rights),
        smem=(0,),
        scratch=[
            ((NEAR, width // NEAR, rows, cols), F32),
            ((16, width // NEAR, rows, cols), F32),
            ((NEAR * rows, width // NEAR, cols), F32),
        ],
    )
    mixed = exchange(mixed, NEAR_STEPS)
    made = run(
        between_kernel,
        [((rows, width, cols), F32)] * 2 + [((2 * all_, cols), BF16)] * OPS + [((2 * OPS * all_, cols), BF16)],
        where, resolved_residue_mask, *mixed, stream, gate, out_t, proj_t, present,
        smem=(0, 1),
        scratch=[
            ((rows, NEAR, width // NEAR, cols), F32),
            ((width, rows, cols), F32),
            ((width, rows, cols), F32),
        ],
    )
    stream, gate, theirs = made[0], made[1], made[6]
    came = split_exchange(with_partner(made[2:6], theirs))
    mine, theirs = run(
        mix_cols_kernel,
        [((OPS, 2 * all_, cols), F32)] * 2,
        where, *came,
        smem=(0,),
        scratch=[
            ((2 * OPS, width // (2 * OPS), rows, cols), F32),
            ((2 * OPS, width // (2 * OPS), rows, cols), F32),
            ((16 * rows, width // (2 * OPS), cols), F32),
        ],
    )
    mixed = run(sum_kernel, [((2 * all_, cols), BF16)] * OPS, mine, core_permute(theirs))
    mixed = split_exchange(mixed)
    other = core_permute(run(pick_kernel, [((OPS * all_, cols), BF16)], *mixed)[0])
    return run(
        final_kernel,
        [((rows, cols, width), BF16)],
        where, *mixed, other, stream, gate, out_t,
        smem=(0,),
        scratch=[((rows, 2 * OPS, width // (2 * OPS), cols), F32)],
    )[0]


def fits_chips(mesh):
    return mesh.shape["narrow"] == 1 and mesh.shape["wide"] == 16


def solution(mesh):
    per_device = per_device_chips if fits_chips(mesh) else per_device_general
    return jax.shard_map(
        per_device,
        mesh=mesh,
        in_specs=(
            P(("grp", "wide"), "narrow", None),
            P("grp", "wide", None),
            P("grp"),
            P("grp"),
            P("grp", "wide"),
            P(),
            P(),
            P(),
            P(),
            P(),
        ),
        out_specs=P(("grp", "wide"), "narrow", None),
        check_vma=False,
    )
```

```python
import functools

import jax
import jax.numpy as jnp
from jax import lax
from jax.experimental import pallas as pl
from jax.experimental.pallas import tpu as pltpu
from jax.sharding import PartitionSpec as P

RELMAX = 32
EPSILON = 1e-05
LANES = 128
F32 = jnp.float32
BF16 = jnp.bfloat16


def apply_layer_norm(values, axis_dim):
    center = values - jnp.mean(values, axis=axis_dim, keepdims=True)
    spread = jnp.mean(center * center, axis=axis_dim, keepdims=True)
    return center * lax.rsqrt(spread + EPSILON)


def gather_wide(block):
    n = lax.axis_size("wide")
    if n % 4 or n < 8:
        return lax.all_gather(block, "wide", axis=0)
    outer = n // 4
    me = lax.axis_index("wide")
    high, mid, low = me // 4, (me // 2) % 2, me % 2
    arrived = [block]
    for shift in range(1, outer):
        perm = [(w, ((w // 4 + shift) % outer) * 4 + w % 4) for w in range(n)]
        arrived.append(lax.ppermute(block, "wide", perm))
    held = jnp.zeros((outer,) + block.shape, block.dtype)
    for shift, piece in enumerate(arrived):
        held = lax.dynamic_update_index_in_dim(held, piece, (high - shift + outer) % outer, 0)
    other = lax.ppermute(held, "wide", [(w, w ^ 2) for w in range(n)])
    held = jnp.stack(
        [jnp.where(mid == 0, held, other), jnp.where(mid == 0, other, held)], axis=1
    )
    other = lax.ppermute(held, "wide", [(w, w ^ 1) for w in range(n)])
    held = jnp.stack(
        [jnp.where(low == 0, held, other), jnp.where(low == 0, other, held)], axis=2
    )
    return held.reshape((n,) + block.shape)


def triangle(stream, pair_live, proj_weight, out_weight, incoming):
    rows = stream.shape[0]
    cols = stream.shape[1]
    width = out_weight.shape[0]
    wide_count = lax.axis_size("wide")
    core_count = lax.axis_size("narrow")
    devices = wide_count * core_count
    per_dev = width // devices
    normed = apply_layer_norm(stream, 2).astype(jnp.bfloat16)
    blocks = [proj_weight[:, index * width : (index + 1) * width] for index in range(4)]

    def project(block):
        return jnp.einsum("ijd,dc->cij", normed, block, preferred_element_type=jnp.float32)

    left_side = (jax.nn.sigmoid(project(blocks[0])) * project(blocks[1]) * pair_live[None]).astype(
        jnp.bfloat16
    )
    right_side = (jax.nn.sigmoid(project(blocks[2])) * project(blocks[3]) * pair_live[None]).astype(
        jnp.bfloat16
    )
    gate = jax.nn.sigmoid(
        jnp.einsum(
            "ijd,dc->ijc", normed, proj_weight[:, 4 * width :], preferred_element_type=jnp.float32
        )
    )
    form = "cki,ckj->cij" if incoming else "cik,cjk->cij"
    both = jnp.stack(
        [
            left_side.reshape(devices, per_dev, rows * cols),
            right_side.reshape(devices, per_dev, rows * cols),
        ],
        axis=1,
    ).reshape(devices, 2 * per_dev, rows * cols)
    both = lax.all_to_all(both, ("wide", "narrow"), split_axis=0, concat_axis=0, tiled=True)
    both = both.reshape(wide_count, core_count, 2, per_dev, rows, cols)
    both = jnp.transpose(both, (2, 3, 0, 4, 1, 5)).reshape(
        2, per_dev, wide_count * rows, core_count * cols
    )
    mixed = jnp.einsum(form, both[0], both[1], preferred_element_type=jnp.float32).astype(
        jnp.bfloat16
    )
    spread_out = mixed.reshape(per_dev, wide_count, rows, core_count, cols)
    spread_out = jnp.transpose(spread_out, (1, 3, 0, 2, 4)).reshape(
        wide_count * core_count * per_dev, rows * cols
    )
    returned = lax.all_to_all(
        spread_out, ("wide", "narrow"), split_axis=0, concat_axis=0, tiled=True
    ).reshape(width, rows, cols)
    blended_standardize = apply_layer_norm(returned.astype(jnp.float32), 0).astype(jnp.bfloat16)
    update = jnp.einsum(
        "cij,cd->ijd", blended_standardize, out_weight, preferred_element_type=jnp.float32
    )
    return stream + gate * update


def per_device_general(
    pairwise_state,
    homolog_features,
    residue_chain_index,
    resolved_residue_mask,
    alignment_mask,
    relative_offset_table,
    homolog_to_sides_matrix,
    outer_mean_output_weight,
    triangle_projection_weight,
    triangle_output_weight,
):
    rows = pairwise_state.shape[0]
    cols = pairwise_state.shape[1]
    row_start = lax.axis_index("wide") * rows
    col_start = lax.axis_index("narrow") * cols
    residue_present = resolved_residue_mask.astype(jnp.float32)
    row_present = lax.dynamic_slice_in_dim(residue_present, row_start, rows)
    col_live = lax.dynamic_slice_in_dim(residue_present, col_start, cols)
    present_flags = alignment_mask.astype(jnp.float32) * row_present[None, :]
    alignment_normed = apply_layer_norm(homolog_features.astype(jnp.float32), 2).astype(
        jnp.bfloat16
    )
    projected_rows = jnp.einsum(
        "tna,ak->tnk", alignment_normed, homolog_to_sides_matrix, preferred_element_type=jnp.float32
    )
    projected_rows = (projected_rows * present_flags[:, :, None]).astype(jnp.bfloat16)
    half_width = projected_rows.shape[2] // 2
    homologs = projected_rows.shape[0]
    left_proj = projected_rows[:, :, :half_width]
    right_proj = projected_rows[:, :, half_width:]
    live_flags = present_flags.astype(jnp.bfloat16)
    packed = jnp.concatenate(
        [jnp.transpose(right_proj, (1, 0, 2)).reshape(rows, homologs * half_width), live_flags.T],
        axis=1,
    )
    gathered = gather_wide(packed).reshape(-1, packed.shape[1])
    gathered = lax.dynamic_slice_in_dim(gathered, col_start, cols, 0)
    right_mine = jnp.transpose(
        gathered[:, : homologs * half_width].reshape(cols, homologs, half_width), (1, 0, 2)
    )
    live_mine = gathered[:, homologs * half_width :].T
    counts = jnp.dot(live_flags.T, live_mine, preferred_element_type=jnp.float32)

    def opm_row(left_row):
        outer = jnp.einsum("sc,sjd->jcd", left_row, right_mine, preferred_element_type=jnp.float32)
        outer = outer.reshape(cols, half_width * half_width).astype(jnp.bfloat16)
        return jnp.dot(outer, outer_mean_output_weight, preferred_element_type=jnp.float32)

    opm = lax.map(opm_row, jnp.transpose(left_proj, (1, 0, 2)))
    row_pos = row_start + jnp.arange(rows, dtype=jnp.int32)
    col_pos = col_start + jnp.arange(cols, dtype=jnp.int32)
    row_chain = lax.dynamic_slice_in_dim(residue_chain_index, row_start, rows)
    col_chain = lax.dynamic_slice_in_dim(residue_chain_index, col_start, cols)
    offset = jnp.clip(row_pos[:, None] - col_pos[None, :], -RELMAX, RELMAX) + RELMAX
    bin_index = jnp.where(row_chain[:, None] == col_chain[None, :], offset, 2 * RELMAX + 1)
    bin_count = relative_offset_table.shape[0]
    one_hot = (
        bin_index[:, :, None] == jnp.arange(bin_count, dtype=jnp.int32)[None, None, :]
    ).astype(jnp.bfloat16)
    relpos = jnp.einsum(
        "ijb,bc->ijc", one_hot, relative_offset_table, preferred_element_type=jnp.float32
    )
    stream = (
        pairwise_state.astype(jnp.float32) + relpos + opm / jnp.maximum(counts, 1.0)[:, :, None]
    )
    pair_live = row_present[:, None] * col_live[None, :]
    for turn_index in range(2):
        stream = triangle(
            stream,
            pair_live,
            triangle_projection_weight[turn_index],
            triangle_output_weight[turn_index],
            turn_index == 1,
        )
    return stream.astype(jnp.bfloat16)


def nn(a, b):
    return lax.dot_general(a, b, (((1,), (0,)), ((), ())), preferred_element_type=F32)


def nt(a, b):
    return lax.dot_general(a, b, (((1,), (1,)), ((), ())), preferred_element_type=F32)


def tn(a, b):
    return lax.dot_general(a, b, (((0,), (0,)), ((), ())), preferred_element_type=F32)


def identity(size):
    rows = lax.broadcasted_iota(jnp.int32, (size, size), 0)
    cols = lax.broadcasted_iota(jnp.int32, (size, size), 1)
    return (rows == cols).astype(F32).astype(BF16)


def flip(block):
    return nt(identity(block.shape[1]), block)


def norm_rows(values):
    scale = 1.0 / values.shape[0]
    center = values - jnp.sum(values, axis=0, keepdims=True) * scale
    spread = jnp.sum(center * center, axis=0, keepdims=True) * scale
    return (center * lax.rsqrt(spread + EPSILON)).astype(BF16)


def run(kernel, outs, *args, smem=(), scratch=(), flops=15 * 10**8):
    vmem = pl.BlockSpec(memory_space=pltpu.VMEM)
    in_specs = [
        pl.BlockSpec(memory_space=pltpu.SMEM if at in smem else pltpu.VMEM) for at in range(len(args))
    ]
    moved = sum(a.size * a.dtype.itemsize for a in args)
    return pl.pallas_call(
        kernel,
        out_shape=[jax.ShapeDtypeStruct(shape, kind) for shape, kind in outs],
        in_specs=in_specs,
        out_specs=[vmem] * len(outs),
        scratch_shapes=[pltpu.VMEM(shape, kind) for shape, kind in scratch],
        compiler_params=pltpu.CompilerParams(vmem_limit_bytes=VMEM_LIMIT),
        cost_estimate=pl.CostEstimate(flops=flops, bytes_accessed=moved, transcendentals=0),
    )(*args)


VMEM_LIMIT = 20 * 1024 * 1024
SPLIT = ((7, 5), (6, 4), (3, 2), (1, 0))
FAR_SPLIT = SPLIT[:2]
SMALL_SPLIT = ((7, 3), (2, 6), (5, 1), (0, 4))
SMALL_NEAR = ((3, 1), (1, 2), (2, 3), (0, 0))
OPS = len(SPLIT)
NEAR = 4
NEAR_STEPS = (3, 2, 1, 0)


def partner_chip(chip, core, op, split=SPLIT):
    return chip ^ jnp.where(core == 0, split[op][0], split[op][1])


def project_kernel(feat_ref, weight_ref, live_in_ref, pay_ref, left_ref, live_ref, turned, packed):
    homologs, rows, _ = feat_ref.shape
    half = weight_ref.shape[0] // 2
    quarter = half // 2
    values = feat_ref[...].reshape(homologs * rows, feat_ref.shape[2])
    center = values - jnp.mean(values, axis=1, keepdims=True)
    spread = jnp.mean(center * center, axis=1, keepdims=True)
    normed = (center * lax.rsqrt(spread + EPSILON)).astype(BF16)
    total = homologs * rows
    out_row = lax.broadcasted_iota(jnp.int32, (total, total), 0)
    in_row = lax.broadcasted_iota(jnp.int32, (total, total), 1)
    order = in_row == (out_row & (homologs - 1)) * rows + out_row // homologs
    normed = nn(order.astype(F32).astype(BF16), normed).astype(BF16)
    live = live_in_ref[...]
    weight = weight_ref[...]
    blank = jnp.zeros((homologs, normed.shape[1]), BF16)
    for row in range(rows):
        mine = normed[row * homologs : (row + 1) * homologs]
        low = nt(weight, jnp.concatenate([mine, blank], axis=0)) * live[row : row + 1]
        high = nt(weight, jnp.concatenate([blank, mine], axis=0)) * live[row : row + 1]
        left_ref[row * half : (row + 1) * half] = low[:half].astype(BF16)
        left_ref[(rows + row) * half : (rows + row + 1) * half] = high[:half].astype(BF16)
        turned[row] = low[half : half + quarter] + high[half + quarter :]
    for pair in range(quarter):
        packed[pair * rows : (pair + 1) * rows] = turned[:, pair, :]
    packed[quarter * rows : (quarter + 1) * rows] = live
    packed[(quarter + 1) * rows :] = jnp.zeros((rows, 2 * homologs), F32)
    pay_ref[...] = packed[...].astype(BF16)
    live_ref[...] = jnp.where(lax.broadcasted_iota(jnp.int32, live.shape, 1) < homologs, live, 0.0)


def prep_kernel(
    where_ref, chain_ref, chains_ref, pair_ref, table_ref, outer_ref, proj_ref, out_ref,
    base_ref, outer_t_ref, proj_t_ref, out_t_ref, table_pad, outer_pad,
):
    rows, cols, width = pair_ref.shape
    bins = table_ref.shape[0]
    table_pad[...] = jnp.zeros_like(table_pad)
    table_pad[0:bins, :] = table_ref[...].astype(F32)
    table = flip(table_pad[...].astype(BF16)).astype(BF16)
    chains = chains_ref[...]
    col = lax.broadcasted_iota(jnp.int32, (1, cols), 1)
    slot = lax.broadcasted_iota(jnp.int32, (table_pad.shape[0], cols), 0)
    for row in range(rows):
        place = where_ref[0] + row
        offset = jnp.clip(place - col, -RELMAX, RELMAX) + RELMAX
        bin_index = jnp.where(chains == chain_ref[place], offset, 2 * RELMAX + 1)
        hot = (slot == bin_index).astype(F32).astype(BF16)
        base_ref[row] = flip(pair_ref[row]) + nn(table, hot)
    half = outer_pad.shape[0]
    outer_pad[...] = outer_ref[...].astype(F32).reshape(outer_pad.shape)
    for d in range(half):
        outer_t_ref[:, d * half : (d + 1) * half] = flip(outer_pad[:, d, :].astype(BF16)).astype(BF16)
    for turn in range(2):
        proj_t_ref[turn] = tn(proj_ref[turn], identity(width)).astype(BF16)
        out_t_ref[turn] = flip(out_ref[turn]).astype(BF16)


def sigmoid(values):
    return 0.5 * jnp.tanh(0.5 * values) + 0.5


def sides(streams, weight, lives, gate_ref, lefts, rights, row):
    width, cols = streams[0].shape
    made = nn(weight, jnp.concatenate([norm_rows(stream) for stream in streams], axis=1))
    for at, live in enumerate(lives):
        part = [
            made[block * width : (block + 1) * width, at * cols : (at + 1) * cols] for block in range(5)
        ]
        lefts[:, row + at, :] = sigmoid(part[0]) * part[1] * live
        rights[:, row + at, :] = sigmoid(part[2]) * part[3] * live
        gate_ref[row + at] = sigmoid(part[4])


def flat(block):
    return block.reshape(block.shape[0] * block.shape[1], block.shape[2])


def outer_kernel(
    where_ref, flag_ref, own_ref, other_ref, left_ref, live_ref, base_ref, outer_t_ref, proj_ref, present_ref,
    stream_ref, gate_ref, far0, far1, theirs_ref, near0, near1, near2, near3, came, outer, lefts, rights,
):
    rows, width, cols = base_ref.shape
    chip, core = where_ref[1], where_ref[2]
    per = own_ref.shape[1]
    chips = own_ref.shape[0]
    for at in range(chips):
        chip_at = chip ^ (at % 2 * 4 + at // 2 % 2 * 2 + at // 4)
        came[chip_at * 2 + core] = own_ref[at].astype(F32)
        came[chip_at * 2 + (1 - core)] = other_ref[at].astype(F32)
    half = left_ref.shape[0] // (2 * rows)
    quarter = half // 2
    live_all = came[:, quarter * rows : (quarter + 1) * rows, :].reshape(cols, per_lane(came)).astype(BF16)
    counts = nt(live_ref[...].astype(BF16), live_all)
    share = 1.0 / jnp.maximum(counts, 1.0)
    left_all = left_ref[...]
    for pair in range(quarter):
        right = came[:, pair * rows : (pair + 1) * rows, :].reshape(cols, per_lane(came)).astype(BF16)
        made = nt(left_all, right).astype(BF16)
        for part in range(2):
            d = part * quarter + pair
            for row in range(rows):
                first = (part * rows + row) * half
                lane = (row % 2) * cols
                outer[row // 2, d * half : (d + 1) * half, lane : lane + cols] = made[first : first + half]
    present = present_ref[...].astype(F32)
    for row in range(0, rows, 2):
        product = nn(outer_t_ref[...], outer[row // 2])
        streams, lives = [], []
        for at in range(2):
            streams.append(
                base_ref[row + at] + product[:, at * cols : (at + 1) * cols] * share[row + at : row + at + 1]
            )
            stream_ref[row + at] = streams[at]
            lives.append(present * flag_ref[where_ref[0] + row + at].astype(F32))
        sides(streams, proj_ref[0], lives, gate_ref, lefts, rights, row)
    size = width // NEAR
    block = size * rows

    def group(side, to):
        first = pl.multiple_of((to & (NEAR - 1)) * size, size)
        return flat(side[pl.ds(first, size)]).astype(BF16)

    for op, far in enumerate((far0, far1)):
        far[...] = group(rights, partner_chip(chip, core, op, FAR_SPLIT))
        theirs_ref[op * block : (op + 1) * block] = group(rights, partner_chip(chip, 1 - core, op, FAR_SPLIT))
    for step, near in enumerate((near0, near1, near2, near3)):
        near[0:block] = group(lefts, chip ^ step)
        near[block:] = group(rights, chip ^ step)


def per_lane(ref):
    return ref.shape[-1]


def mix_rows_kernel(
    where_ref, near0, near1, near2, near3, far0, far1, other_ref,
    out0, out1, out2, out3, lefts, rights, mixed,
):
    chip, core = where_ref[1], where_ref[2]
    count, rows, cols = lefts.shape[1:]
    block = count * rows
    for at, (step, near) in enumerate(zip(NEAR_STEPS, (near0, near1, near2, near3))):
        lefts[step] = near[0:block].astype(F32).reshape(count, rows, cols)
        rights[(chip ^ step) * 2 + core] = near[block:].astype(F32).reshape(count, rows, cols)
        theirs = other_ref[at * block : (at + 1) * block]
        rights[(chip ^ step) * 2 + (1 - core)] = theirs.astype(F32).reshape(count, rows, cols)
    for op, far in enumerate((far0, far1)):
        for half in range(2):
            at = partner_chip(chip, core, op, FAR_SPLIT) * 2 + (core ^ half)
            rights[at] = far[half * block : (half + 1) * block].astype(F32).reshape(count, rows, cols)
            at = partner_chip(chip, 1 - core, op, FAR_SPLIT) * 2 + ((1 - core) ^ half)
            place = (NEAR + op * 2 + half) * block
            rights[at] = other_ref[place : place + block].astype(F32).reshape(count, rows, cols)
    for c in range(count):
        left = flat(lefts[:, c]).astype(BF16)
        right = flat(rights[:, c]).astype(BF16)
        mixed[:, c, :] = nt(left, right)
    for op, out in enumerate((out0, out1, out2, out3)):
        first = pl.multiple_of(partner_chip(0, core, op, SMALL_NEAR) * rows, rows)
        out[...] = flat(mixed[pl.ds(first, rows)]).astype(BF16)


def pick_kernel(*refs):
    blocks, out_ref = refs[:-1], refs[-1]
    for at, block in enumerate(blocks):
        half = block.shape[0] // 2
        out_ref[at * half : (at + 1) * half] = block[half:]


def update(came, row, stream_ref, gate_ref, out_weight):
    normed = jnp.concatenate([norm_rows(flat(came[row + at])) for at in range(2)], axis=1)
    made = nn(out_weight, normed)
    cols = made.shape[1] // 2
    return [
        stream_ref[row + at] + gate_ref[row + at] * made[:, at * cols : (at + 1) * cols] for at in range(2)
    ]


def between_kernel(
    where_ref, flag_ref, in0, in1, in2, in3, stream_ref, gate_ref, out_weight_ref, proj_ref, present_ref,
    next_ref, next_gate_ref, mine0, mine1, mine2, mine3, theirs_ref, came, lefts, rights,
):
    rows, width, cols = stream_ref.shape
    chip, core = where_ref[1], where_ref[2]
    size = width // NEAR
    for op, block in enumerate((in0, in1, in2, in3)):
        came[:, partner_chip(chip, core, op, SMALL_NEAR) & (NEAR - 1)] = block[...].astype(F32).reshape(rows, size, cols)
    present = present_ref[...].astype(F32)
    for row in range(0, rows, 2):
        streams = update(came, row, stream_ref, gate_ref, out_weight_ref[0])
        lives = []
        for at in range(2):
            next_ref[row + at] = streams[at]
            lives.append(present * flag_ref[where_ref[0] + row + at].astype(F32))
        sides(streams, proj_ref[1], lives, next_gate_ref, lefts, rights, row)
    size = width // (2 * OPS)
    block = size * rows
    for op, mine in enumerate((mine0, mine1, mine2, mine3)):
        for at, side in enumerate((lefts, rights)):
            first = pl.multiple_of(partner_chip(chip, core, op) * size, size)
            mine[at * block : (at + 1) * block] = flat(side[pl.ds(first, size)]).astype(BF16)
            first = pl.multiple_of(partner_chip(chip, 1 - core, op) * size, size)
            place = (op * 2 + at) * block
            theirs_ref[place : place + block] = flat(side[pl.ds(first, size)]).astype(BF16)


def mix_cols_kernel(where_ref, came0, came1, came2, came3, mine_ref, theirs_ref, lefts, rights, partial):
    chip, core = where_ref[1], where_ref[2]
    count, rows, cols = lefts.shape[1:]
    block = count * rows
    for op, came in enumerate((came0, came1, came2, came3)):
        for half in range(2):
            for at, side in enumerate((lefts, rights)):
                place = (half * 2 + at) * block
                side[op * 2 + half] = came[place : place + block].astype(F32).reshape(count, rows, cols)
    for c in range(count):
        left = flat(lefts[:, c]).astype(BF16)
        right = flat(rights[:, c]).astype(BF16)
        partial[:, c, :] = tn(left, right)
    for op in range(OPS):
        for half in range(2):
            to = (partner_chip(chip, core, op, SMALL_SPLIT) * 2 + (core ^ half)) * rows
            mine_ref[op, half * block : (half + 1) * block] = flat(partial[pl.ds(to, rows)])
            to = (partner_chip(chip, 1 - core, op, SMALL_SPLIT) * 2 + ((1 - core) ^ half)) * rows
            theirs_ref[op, half * block : (half + 1) * block] = flat(partial[pl.ds(to, rows)])


def sum_kernel(mine_ref, got_ref, *outs):
    for op, out in enumerate(outs):
        out[...] = (mine_ref[op] + got_ref[op]).astype(BF16)


def final_kernel(
    where_ref, came0, came1, came2, came3, other_ref, stream_ref, gate_ref, out_weight_ref, out_ref, came
):
    rows, width, cols = stream_ref.shape
    chip, core = where_ref[1], where_ref[2]
    size = width // (2 * OPS)
    block = size * rows
    for op, mine in enumerate((came0, came1, came2, came3)):
        came[:, partner_chip(chip, core, op, SMALL_SPLIT)] = mine[0:block].astype(F32).reshape(rows, size, cols)
        theirs = other_ref[op * block : (op + 1) * block]
        came[:, partner_chip(chip, 1 - core, op, SMALL_SPLIT)] = theirs.astype(F32).reshape(rows, size, cols)
    for row in range(0, rows, 2):
        for at, stream in enumerate(update(came, row, stream_ref, gate_ref, out_weight_ref[1])):
            out_ref[row + at] = flip_out(stream)


def flip_out(stream):
    return nt(identity(stream.shape[1]), stream.astype(BF16)).astype(BF16)


def chip_permute(block, step):
    count = lax.axis_size("wide")
    return lax.ppermute(block, "wide", [(w, w ^ (2 * step)) for w in range(count)])


def exchange(blocks, steps):
    return [chip_permute(blocks[step], step) if step else blocks[0] for step in steps]


def split_permute(block, steps):
    count = lax.axis_size("wide")
    return lax.ppermute(block, "wide", [(w, w ^ (2 * steps[w % 2])) for w in range(count)])


def split_exchange(blocks, split=SPLIT):
    return [split_permute(block, steps) for block, steps in zip(blocks, split)]


def with_partner(mine, theirs):
    got, messages, place = core_permute(theirs), [], 0
    for block in mine:
        messages.append(jnp.concatenate([block, got[place : place + block.shape[0]]], axis=0))
        place += block.shape[0]
    return messages


def core_permute(block):
    count = lax.axis_size("wide")
    return lax.ppermute(block, "wide", [(w, w ^ 1) for w in range(count)])


def per_device_chips(
    pairwise_state,
    homolog_features,
    residue_chain_index,
    resolved_residue_mask,
    alignment_mask,
    relative_offset_table,
    homolog_to_sides_matrix,
    outer_mean_output_weight,
    triangle_projection_weight,
    triangle_output_weight,
):
    rows, cols, width = pairwise_state.shape
    homologs = homolog_features.shape[0]
    half = homolog_to_sides_matrix.shape[1] // 2
    device = lax.axis_index("wide")
    chip, core = device // 2, device % 2
    where = jnp.stack([device * rows, chip, core]).astype(jnp.int32)
    present = resolved_residue_mask.reshape(1, cols)
    pay_rows = (half // 2 + 2) * rows
    row_present = lax.dynamic_slice_in_dim(resolved_residue_mask, device * rows, rows).astype(F32)
    live = alignment_mask.T.astype(F32) * row_present[:, None]
    live = jnp.concatenate([live, live], axis=1)
    pay, left, live = run(
        project_kernel,
        [((pay_rows, LANES), BF16), ((2 * rows * half, LANES), BF16), ((rows, LANES), F32)],
        homolog_features.astype(F32), homolog_to_sides_matrix.T, live,
        scratch=[((rows, half // 2, LANES), F32), ((pay_rows, LANES), F32)],
    )
    far_z = chip_permute(pay, 4)
    base, outer_t, proj_t, out_t = run(
        prep_kernel,
        [
            ((rows, width, cols), F32),
            ((width, half * half), BF16),
            ((2, triangle_projection_weight.shape[2], width), BF16),
            ((2, width, width), BF16),
        ],
        where, residue_chain_index, residue_chain_index.reshape(1, cols), pairwise_state,
        relative_offset_table, outer_mean_output_weight, triangle_projection_weight, triangle_output_weight,
        smem=(0, 1),
        scratch=[((LANES, width), F32), ((half, half, width), F32)],
    )
    along_z = jnp.stack([pay, far_z])
    along_z, base, outer_t, proj_t, out_t = lax.optimization_barrier((along_z, base, outer_t, proj_t, out_t))
    along_z = jnp.concatenate([along_z, chip_permute(along_z, 2)], axis=0)
    own = jnp.concatenate([along_z, chip_permute(along_z, 1)], axis=0)
    other = core_permute(own)
    tall = width * rows
    near, all_ = tall // NEAR, tall // (2 * OPS)
    made = run(
        outer_kernel,
        [((rows, width, cols), F32)] * 2
        + [((near, cols), BF16)] * 2
        + [((2 * near, cols), BF16)] * (1 + NEAR),
        where, resolved_residue_mask, own, other, left, live, base, outer_t, proj_t, present,
        smem=(0, 1),
        scratch=[
            ((16, pay_rows, LANES), F32),
            ((rows // 2, half * half, 2 * cols), BF16),
            ((width, rows, cols), F32),
            ((width, rows, cols), F32),
        ],
        flops=4 * 10**9,
    )
    stream, gate = made[0], made[1]
    came = exchange(made[5:9], NEAR_STEPS)
    far = split_exchange(with_partner(made[2:4], made[4]), FAR_SPLIT)
    rights = jnp.concatenate([block[near:] for block in came] + far, axis=0)
    mixed = run(
        mix_rows_kernel,
        [((near, cols), BF16)] * NEAR,
        where, *came, *far, core_permute(rights),
        smem=(0,),
        scratch=[
            ((NEAR, width // NEAR, rows, cols), F32),
            ((16, width // NEAR, rows, cols), F32),
            ((NEAR * rows, width // NEAR, cols), F32),
        ],
    )
    mixed = split_exchange(mixed[: NEAR - 1], SMALL_NEAR) + [mixed[NEAR - 1]]
    made = run(
        between_kernel,
        [((rows, width, cols), F32)] * 2 + [((2 * all_, cols), BF16)] * OPS + [((2 * OPS * all_, cols), BF16)],
        where, resolved_residue_mask, *mixed, stream, gate, out_t, proj_t, present,
        smem=(0, 1),
        scratch=[
            ((rows, NEAR, width // NEAR, cols), F32),
            ((width, rows, cols), F32),
            ((width, rows, cols), F32),
        ],
    )
    stream, gate, theirs = made[0], made[1], made[6]
    came = split_exchange(with_partner(made[2:6], theirs))
    mine, theirs = run(
        mix_cols_kernel,
        [((OPS, 2 * all_, cols), F32)] * 2,
        where, *came,
        smem=(0,),
        scratch=[
            ((2 * OPS, width // (2 * OPS), rows, cols), F32),
            ((2 * OPS, width // (2 * OPS), rows, cols), F32),
            ((16 * rows, width // (2 * OPS), cols), F32),
        ],
    )
    mixed = run(sum_kernel, [((2 * all_, cols), BF16)] * OPS, mine, core_permute(theirs))
    mixed = split_exchange(mixed, SMALL_SPLIT)
    other = core_permute(run(pick_kernel, [((OPS * all_, cols), BF16)], *mixed)[0])
    return run(
        final_kernel,
        [((rows, cols, width), BF16)],
        where, *mixed, other, stream, gate, out_t,
        smem=(0,),
        scratch=[((rows, 2 * OPS, width // (2 * OPS), cols), F32)],
    )[0]


def fits_chips(mesh):
    return mesh.shape["narrow"] == 1 and mesh.shape["wide"] == 16


def solution(mesh):
    per_device = per_device_chips if fits_chips(mesh) else per_device_general
    return jax.shard_map(
        per_device,
        mesh=mesh,
        in_specs=(
            P(("grp", "wide"), "narrow", None),
            P("grp", "wide", None),
            P("grp"),
            P("grp"),
            P("grp", "wide"),
            P(),
            P(),
            P(),
            P(),
            P(),
        ),
        out_specs=P(("grp", "wide"), "narrow", None),
        check_vma=False,
    )
```

```python
import functools

import jax
import jax.numpy as jnp
from jax import lax
from jax.experimental import pallas as pl
from jax.experimental.pallas import tpu as pltpu
from jax.sharding import PartitionSpec as P

RELMAX = 32
EPSILON = 1e-05
LANES = 128
F32 = jnp.float32
BF16 = jnp.bfloat16


def apply_layer_norm(values, axis_dim):
    center = values - jnp.mean(values, axis=axis_dim, keepdims=True)
    spread = jnp.mean(center * center, axis=axis_dim, keepdims=True)
    return center * lax.rsqrt(spread + EPSILON)


def gather_wide(block):
    n = lax.axis_size("wide")
    if n % 4 or n < 8:
        return lax.all_gather(block, "wide", axis=0)
    outer = n // 4
    me = lax.axis_index("wide")
    high, mid, low = me // 4, (me // 2) % 2, me % 2
    arrived = [block]
    for shift in range(1, outer):
        perm = [(w, ((w // 4 + shift) % outer) * 4 + w % 4) for w in range(n)]
        arrived.append(lax.ppermute(block, "wide", perm))
    held = jnp.zeros((outer,) + block.shape, block.dtype)
    for shift, piece in enumerate(arrived):
        held = lax.dynamic_update_index_in_dim(held, piece, (high - shift + outer) % outer, 0)
    other = lax.ppermute(held, "wide", [(w, w ^ 2) for w in range(n)])
    held = jnp.stack(
        [jnp.where(mid == 0, held, other), jnp.where(mid == 0, other, held)], axis=1
    )
    other = lax.ppermute(held, "wide", [(w, w ^ 1) for w in range(n)])
    held = jnp.stack(
        [jnp.where(low == 0, held, other), jnp.where(low == 0, other, held)], axis=2
    )
    return held.reshape((n,) + block.shape)


def triangle(stream, pair_live, proj_weight, out_weight, incoming):
    rows = stream.shape[0]
    cols = stream.shape[1]
    width = out_weight.shape[0]
    wide_count = lax.axis_size("wide")
    core_count = lax.axis_size("narrow")
    devices = wide_count * core_count
    per_dev = width // devices
    normed = apply_layer_norm(stream, 2).astype(jnp.bfloat16)
    blocks = [proj_weight[:, index * width : (index + 1) * width] for index in range(4)]

    def project(block):
        return jnp.einsum("ijd,dc->cij", normed, block, preferred_element_type=jnp.float32)

    left_side = (jax.nn.sigmoid(project(blocks[0])) * project(blocks[1]) * pair_live[None]).astype(
        jnp.bfloat16
    )
    right_side = (jax.nn.sigmoid(project(blocks[2])) * project(blocks[3]) * pair_live[None]).astype(
        jnp.bfloat16
    )
    gate = jax.nn.sigmoid(
        jnp.einsum(
            "ijd,dc->ijc", normed, proj_weight[:, 4 * width :], preferred_element_type=jnp.float32
        )
    )
    form = "cki,ckj->cij" if incoming else "cik,cjk->cij"
    both = jnp.stack(
        [
            left_side.reshape(devices, per_dev, rows * cols),
            right_side.reshape(devices, per_dev, rows * cols),
        ],
        axis=1,
    ).reshape(devices, 2 * per_dev, rows * cols)
    both = lax.all_to_all(both, ("wide", "narrow"), split_axis=0, concat_axis=0, tiled=True)
    both = both.reshape(wide_count, core_count, 2, per_dev, rows, cols)
    both = jnp.transpose(both, (2, 3, 0, 4, 1, 5)).reshape(
        2, per_dev, wide_count * rows, core_count * cols
    )
    mixed = jnp.einsum(form, both[0], both[1], preferred_element_type=jnp.float32).astype(
        jnp.bfloat16
    )
    spread_out = mixed.reshape(per_dev, wide_count, rows, core_count, cols)
    spread_out = jnp.transpose(spread_out, (1, 3, 0, 2, 4)).reshape(
        wide_count * core_count * per_dev, rows * cols
    )
    returned = lax.all_to_all(
        spread_out, ("wide", "narrow"), split_axis=0, concat_axis=0, tiled=True
    ).reshape(width, rows, cols)
    blended_standardize = apply_layer_norm(returned.astype(jnp.float32), 0).astype(jnp.bfloat16)
    update = jnp.einsum(
        "cij,cd->ijd", blended_standardize, out_weight, preferred_element_type=jnp.float32
    )
    return stream + gate * update


def per_device_general(
    pairwise_state,
    homolog_features,
    residue_chain_index,
    resolved_residue_mask,
    alignment_mask,
    relative_offset_table,
    homolog_to_sides_matrix,
    outer_mean_output_weight,
    triangle_projection_weight,
    triangle_output_weight,
):
    rows = pairwise_state.shape[0]
    cols = pairwise_state.shape[1]
    row_start = lax.axis_index("wide") * rows
    col_start = lax.axis_index("narrow") * cols
    residue_present = resolved_residue_mask.astype(jnp.float32)
    row_present = lax.dynamic_slice_in_dim(residue_present, row_start, rows)
    col_live = lax.dynamic_slice_in_dim(residue_present, col_start, cols)
    present_flags = alignment_mask.astype(jnp.float32) * row_present[None, :]
    alignment_normed = apply_layer_norm(homolog_features.astype(jnp.float32), 2).astype(
        jnp.bfloat16
    )
    projected_rows = jnp.einsum(
        "tna,ak->tnk", alignment_normed, homolog_to_sides_matrix, preferred_element_type=jnp.float32
    )
    projected_rows = (projected_rows * present_flags[:, :, None]).astype(jnp.bfloat16)
    half_width = projected_rows.shape[2] // 2
    homologs = projected_rows.shape[0]
    left_proj = projected_rows[:, :, :half_width]
    right_proj = projected_rows[:, :, half_width:]
    live_flags = present_flags.astype(jnp.bfloat16)
    packed = jnp.concatenate(
        [jnp.transpose(right_proj, (1, 0, 2)).reshape(rows, homologs * half_width), live_flags.T],
        axis=1,
    )
    gathered = gather_wide(packed).reshape(-1, packed.shape[1])
    gathered = lax.dynamic_slice_in_dim(gathered, col_start, cols, 0)
    right_mine = jnp.transpose(
        gathered[:, : homologs * half_width].reshape(cols, homologs, half_width), (1, 0, 2)
    )
    live_mine = gathered[:, homologs * half_width :].T
    counts = jnp.dot(live_flags.T, live_mine, preferred_element_type=jnp.float32)

    def opm_row(left_row):
        outer = jnp.einsum("sc,sjd->jcd", left_row, right_mine, preferred_element_type=jnp.float32)
        outer = outer.reshape(cols, half_width * half_width).astype(jnp.bfloat16)
        return jnp.dot(outer, outer_mean_output_weight, preferred_element_type=jnp.float32)

    opm = lax.map(opm_row, jnp.transpose(left_proj, (1, 0, 2)))
    row_pos = row_start + jnp.arange(rows, dtype=jnp.int32)
    col_pos = col_start + jnp.arange(cols, dtype=jnp.int32)
    row_chain = lax.dynamic_slice_in_dim(residue_chain_index, row_start, rows)
    col_chain = lax.dynamic_slice_in_dim(residue_chain_index, col_start, cols)
    offset = jnp.clip(row_pos[:, None] - col_pos[None, :], -RELMAX, RELMAX) + RELMAX
    bin_index = jnp.where(row_chain[:, None] == col_chain[None, :], offset, 2 * RELMAX + 1)
    bin_count = relative_offset_table.shape[0]
    one_hot = (
        bin_index[:, :, None] == jnp.arange(bin_count, dtype=jnp.int32)[None, None, :]
    ).astype(jnp.bfloat16)
    relpos = jnp.einsum(
        "ijb,bc->ijc", one_hot, relative_offset_table, preferred_element_type=jnp.float32
    )
    stream = (
        pairwise_state.astype(jnp.float32) + relpos + opm / jnp.maximum(counts, 1.0)[:, :, None]
    )
    pair_live = row_present[:, None] * col_live[None, :]
    for turn_index in range(2):
        stream = triangle(
            stream,
            pair_live,
            triangle_projection_weight[turn_index],
            triangle_output_weight[turn_index],
            turn_index == 1,
        )
    return stream.astype(jnp.bfloat16)


def nn(a, b):
    return lax.dot_general(a, b, (((1,), (0,)), ((), ())), preferred_element_type=F32)


def nt(a, b):
    return lax.dot_general(a, b, (((1,), (1,)), ((), ())), preferred_element_type=F32)


def tn(a, b):
    return lax.dot_general(a, b, (((0,), (0,)), ((), ())), preferred_element_type=F32)


def identity(size):
    rows = lax.broadcasted_iota(jnp.int32, (size, size), 0)
    cols = lax.broadcasted_iota(jnp.int32, (size, size), 1)
    return (rows == cols).astype(F32).astype(BF16)


def flip(block):
    return nt(identity(block.shape[1]), block)


def norm_rows(values):
    scale = 1.0 / values.shape[0]
    center = values - jnp.sum(values, axis=0, keepdims=True) * scale
    spread = jnp.sum(center * center, axis=0, keepdims=True) * scale
    return (center * lax.rsqrt(spread + EPSILON)).astype(BF16)


def run(kernel, outs, *args, smem=(), scratch=(), flops=15 * 10**8):
    vmem = pl.BlockSpec(memory_space=pltpu.VMEM)
    in_specs = [
        pl.BlockSpec(memory_space=pltpu.SMEM if at in smem else pltpu.VMEM) for at in range(len(args))
    ]
    moved = sum(a.size * a.dtype.itemsize for a in args)
    return pl.pallas_call(
        kernel,
        out_shape=[jax.ShapeDtypeStruct(shape, kind) for shape, kind in outs],
        in_specs=in_specs,
        out_specs=[vmem] * len(outs),
        scratch_shapes=[pltpu.VMEM(shape, kind) for shape, kind in scratch],
        compiler_params=pltpu.CompilerParams(vmem_limit_bytes=VMEM_LIMIT),
        cost_estimate=pl.CostEstimate(flops=flops, bytes_accessed=moved, transcendentals=0),
    )(*args)


VMEM_LIMIT = 20 * 1024 * 1024
SPLIT = ((7, 5), (6, 4), (3, 2), (1, 0))
FAR_SPLIT = SPLIT[:2]
SMALL_SPLIT = ((7, 3), (2, 6), (5, 1), (0, 4))
OPS = len(SPLIT)
NEAR = 4
NEAR_STEPS = (3, 2, 1, 0)


def partner_chip(chip, core, op, split=SPLIT):
    return chip ^ jnp.where(core == 0, split[op][0], split[op][1])


def project_kernel(feat_ref, weight_ref, live_in_ref, pay_ref, left_ref, live_ref, turned, packed):
    homologs, rows, _ = feat_ref.shape
    half = weight_ref.shape[0] // 2
    quarter = half // 2
    values = feat_ref[...].reshape(homologs * rows, feat_ref.shape[2])
    center = values - jnp.mean(values, axis=1, keepdims=True)
    spread = jnp.mean(center * center, axis=1, keepdims=True)
    normed = (center * lax.rsqrt(spread + EPSILON)).astype(BF16)
    total = homologs * rows
    out_row = lax.broadcasted_iota(jnp.int32, (total, total), 0)
    in_row = lax.broadcasted_iota(jnp.int32, (total, total), 1)
    order = in_row == (out_row & (homologs - 1)) * rows + out_row // homologs
    normed = nn(order.astype(F32).astype(BF16), normed).astype(BF16)
    live = live_in_ref[...]
    weight = weight_ref[...]
    blank = jnp.zeros((homologs, normed.shape[1]), BF16)
    for row in range(rows):
        mine = normed[row * homologs : (row + 1) * homologs]
        low = nt(weight, jnp.concatenate([mine, blank], axis=0)) * live[row : row + 1]
        high = nt(weight, jnp.concatenate([blank, mine], axis=0)) * live[row : row + 1]
        left_ref[row * half : (row + 1) * half] = low[:half].astype(BF16)
        left_ref[(rows + row) * half : (rows + row + 1) * half] = high[:half].astype(BF16)
        turned[row * quarter : (row + 1) * quarter] = low[half : half + quarter] + high[half + quarter :]
    for pair in range(quarter):
        packed[pair * rows : (pair + 1) * rows] = turned[pl.ds(pair, rows, stride=quarter), :]
    packed[quarter * rows : (quarter + 1) * rows] = live
    packed[(quarter + 1) * rows :] = jnp.zeros((rows, 2 * homologs), F32)
    pay_ref[...] = packed[...].astype(BF16)
    live_ref[...] = jnp.where(lax.broadcasted_iota(jnp.int32, live.shape, 1) < homologs, live, 0.0)


def prep_kernel(
    where_ref, chain_ref, chains_ref, pair_ref, table_ref, outer_ref, proj_ref, out_ref,
    base_ref, outer_t_ref, proj_t_ref, out_t_ref, table_pad, outer_pad,
):
    rows, cols, width = pair_ref.shape
    bins = table_ref.shape[0]
    table_pad[...] = jnp.zeros_like(table_pad)
    table_pad[0:bins, :] = table_ref[...].astype(F32)
    table = flip(table_pad[...].astype(BF16)).astype(BF16)
    chains = chains_ref[...]
    col = lax.broadcasted_iota(jnp.int32, (1, cols), 1)
    slot = lax.broadcasted_iota(jnp.int32, (table_pad.shape[0], cols), 0)
    for row in range(rows):
        place = where_ref[0] + row
        offset = jnp.clip(place - col, -RELMAX, RELMAX) + RELMAX
        bin_index = jnp.where(chains == chain_ref[place], offset, 2 * RELMAX + 1)
        hot = (slot == bin_index).astype(F32).astype(BF16)
        base_ref[row] = flip(pair_ref[row]) + nn(table, hot)
    half = round(outer_pad.shape[0] ** 0.5)
    outer_pad[...] = outer_ref[...].astype(F32)
    for d in range(half):
        outer_t_ref[:, d * half : (d + 1) * half] = flip(outer_pad[pl.ds(d, half, stride=half), :].astype(BF16)).astype(BF16)
    for turn in range(2):
        proj_t_ref[turn] = tn(proj_ref[turn], identity(width)).astype(BF16)
        out_t_ref[turn] = flip(out_ref[turn]).astype(BF16)


def sigmoid(values):
    return 0.5 * jnp.tanh(0.5 * values) + 0.5


def sides(streams, weight, lives, gate_ref, lefts, rights, row):
    width, cols = streams[0].shape
    rows = lefts.shape[0] // width
    made = nn(weight, jnp.concatenate([norm_rows(stream) for stream in streams], axis=1))
    for at, live in enumerate(lives):
        part = [
            made[block * width : (block + 1) * width, at * cols : (at + 1) * cols] for block in range(5)
        ]
        lefts[pl.ds(row + at, width, stride=rows), :] = sigmoid(part[0]) * part[1] * live
        rights[pl.ds(row + at, width, stride=rows), :] = sigmoid(part[2]) * part[3] * live
        gate_ref[row + at] = sigmoid(part[4])


def flat(block):
    return block.reshape(block.shape[0] * block.shape[1], block.shape[2])


def outer_kernel(
    where_ref, flag_ref, own_ref, other_ref, left_ref, live_ref, base_ref, outer_t_ref, proj_ref, present_ref,
    stream_ref, gate_ref, far0, far1, theirs_ref, near0, near1, near2, near3, came, outer, lefts, rights,
):
    rows, width, cols = base_ref.shape
    chip, core = where_ref[1], where_ref[2]
    per = own_ref.shape[1]
    chips = own_ref.shape[0]
    for at in range(chips):
        chip_at = chip ^ (at % 2 * 4 + at // 2 % 2 * 2 + at // 4)
        came[chip_at * 2 + core] = own_ref[at].astype(F32)
        came[chip_at * 2 + (1 - core)] = other_ref[at].astype(F32)
    half = left_ref.shape[0] // (2 * rows)
    quarter = half // 2
    live_all = came[:, quarter * rows : (quarter + 1) * rows, :].reshape(cols, per_lane(came)).astype(BF16)
    counts = nt(live_ref[...].astype(BF16), live_all)
    share = 1.0 / jnp.maximum(counts, 1.0)
    left_all = left_ref[...]
    for pair in range(quarter):
        right = came[:, pair * rows : (pair + 1) * rows, :].reshape(cols, per_lane(came)).astype(BF16)
        made = nt(left_all, right).astype(BF16)
        for part in range(2):
            d = part * quarter + pair
            for row in range(rows):
                first = (part * rows + row) * half
                lane = (row % 2) * cols
                outer[row // 2, d * half : (d + 1) * half, lane : lane + cols] = made[first : first + half]
    present = present_ref[...].astype(F32)
    for row in range(0, rows, 2):
        product = nn(outer_t_ref[...], outer[row // 2])
        streams, lives = [], []
        for at in range(2):
            streams.append(
                base_ref[row + at] + product[:, at * cols : (at + 1) * cols] * share[row + at : row + at + 1]
            )
            stream_ref[row + at] = streams[at]
            lives.append(present * flag_ref[where_ref[0] + row + at].astype(F32))
        sides(streams, proj_ref[0], lives, gate_ref, lefts, rights, row)
    size = width // NEAR
    block = size * rows

    def group(side, to):
        first = pl.multiple_of((to & (NEAR - 1)) * block, block)
        return side[pl.ds(first, block), :].astype(BF16)

    for op, far in enumerate((far0, far1)):
        far[...] = group(rights, partner_chip(chip, core, op, FAR_SPLIT))
        theirs_ref[op * block : (op + 1) * block] = group(rights, partner_chip(chip, 1 - core, op, FAR_SPLIT))
    for step, near in enumerate((near0, near1, near2, near3)):
        near[0:block] = group(lefts, chip ^ step)
        near[block:] = group(rights, chip ^ step)


def per_lane(ref):
    return ref.shape[-1]


def mix_rows_kernel(
    where_ref, near0, near1, near2, near3, far0, far1, other_ref,
    out0, out1, out2, out3, lefts, rights, mixed,
):
    chip, core = where_ref[1], where_ref[2]
    count, rows, cols = lefts.shape[1:]
    block = count * rows
    for at, (step, near) in enumerate(zip(NEAR_STEPS, (near0, near1, near2, near3))):
        lefts[step] = near[0:block].astype(F32).reshape(count, rows, cols)
        rights[(chip ^ step) * 2 + core] = near[block:].astype(F32).reshape(count, rows, cols)
        theirs = other_ref[at * block : (at + 1) * block]
        rights[(chip ^ step) * 2 + (1 - core)] = theirs.astype(F32).reshape(count, rows, cols)
    for op, far in enumerate((far0, far1)):
        for half in range(2):
            at = partner_chip(chip, core, op, FAR_SPLIT) * 2 + (core ^ half)
            rights[at] = far[half * block : (half + 1) * block].astype(F32).reshape(count, rows, cols)
            at = partner_chip(chip, 1 - core, op, FAR_SPLIT) * 2 + ((1 - core) ^ half)
            place = (NEAR + op * 2 + half) * block
            rights[at] = other_ref[place : place + block].astype(F32).reshape(count, rows, cols)
    for c in range(count):
        left = flat(lefts[:, c]).astype(BF16)
        right = flat(rights[:, c]).astype(BF16)
        mixed[pl.ds(c, NEAR * rows, stride=count), :] = nt(left, right)
    for step, out in enumerate((out0, out1, out2, out3)):
        out[...] = mixed[step * block : (step + 1) * block].astype(BF16)


def pick_kernel(*refs):
    blocks, out_ref = refs[:-1], refs[-1]
    for at, block in enumerate(blocks):
        half = block.shape[0] // 2
        out_ref[at * half : (at + 1) * half] = block[half:]


def update(came, row, stream_ref, gate_ref, out_weight):
    normed = jnp.concatenate([norm_rows(flat(came[row + at])) for at in range(2)], axis=1)
    made = nn(out_weight, normed)
    cols = made.shape[1] // 2
    return [
        stream_ref[row + at] + gate_ref[row + at] * made[:, at * cols : (at + 1) * cols] for at in range(2)
    ]


def between_kernel(
    where_ref, flag_ref, in0, in1, in2, in3, stream_ref, gate_ref, out_weight_ref, proj_ref, present_ref,
    next_ref, next_gate_ref, mine0, mine1, mine2, mine3, theirs_ref, came, lefts, rights,
):
    rows, width, cols = stream_ref.shape
    chip, core = where_ref[1], where_ref[2]
    size = width // NEAR
    for step, block in zip(NEAR_STEPS, (in0, in1, in2, in3)):
        came[:, (chip ^ step) & (NEAR - 1)] = block[...].astype(F32).reshape(rows, size, cols)
    present = present_ref[...].astype(F32)
    for row in range(0, rows, 2):
        streams = update(came, row, stream_ref, gate_ref, out_weight_ref[0])
        lives = []
        for at in range(2):
            next_ref[row + at] = streams[at]
            lives.append(present * flag_ref[where_ref[0] + row + at].astype(F32))
        sides(streams, proj_ref[1], lives, next_gate_ref, lefts, rights, row)
    block = width // (2 * OPS) * rows
    for op, mine in enumerate((mine0, mine1, mine2, mine3)):
        for at, side in enumerate((lefts, rights)):
            first = pl.multiple_of(partner_chip(chip, core, op) * block, block)
            mine[at * block : (at + 1) * block] = side[pl.ds(first, block), :].astype(BF16)
            first = pl.multiple_of(partner_chip(chip, 1 - core, op) * block, block)
            place = (op * 2 + at) * block
            theirs_ref[place : place + block] = side[pl.ds(first, block), :].astype(BF16)


def mix_cols_kernel(where_ref, came0, came1, came2, came3, mine_ref, theirs_ref, lefts, rights, partial):
    chip, core = where_ref[1], where_ref[2]
    count, rows, cols = lefts.shape[1:]
    block = count * rows
    for op, came in enumerate((came0, came1, came2, came3)):
        for half in range(2):
            for at, side in enumerate((lefts, rights)):
                place = (half * 2 + at) * block
                side[op * 2 + half] = came[place : place + block].astype(F32).reshape(count, rows, cols)
    for c in range(count):
        left = flat(lefts[:, c]).astype(BF16)
        right = flat(rights[:, c]).astype(BF16)
        partial[pl.ds(c, partial.shape[0] // count, stride=count), :] = tn(left, right)
    for op in range(OPS):
        for half in range(2):
            to = pl.multiple_of((partner_chip(chip, core, op, SMALL_SPLIT) * 2 + (core ^ half)) * block, block)
            mine_ref[op, half * block : (half + 1) * block] = partial[pl.ds(to, block), :]
            to = partner_chip(chip, 1 - core, op, SMALL_SPLIT) * 2 + ((1 - core) ^ half)
            to = pl.multiple_of(to * block, block)
            theirs_ref[op, half * block : (half + 1) * block] = partial[pl.ds(to, block), :]


def sum_kernel(mine_ref, got_ref, *outs):
    for op, out in enumerate(outs):
        out[...] = (mine_ref[op] + got_ref[op]).astype(BF16)


def final_kernel(
    where_ref, came0, came1, came2, came3, other_ref, stream_ref, gate_ref, out_weight_ref, out_ref, came
):
    rows, width, cols = stream_ref.shape
    chip, core = where_ref[1], where_ref[2]
    size = width // (2 * OPS)
    block = size * rows
    for op, mine in enumerate((came0, came1, came2, came3)):
        came[:, partner_chip(chip, core, op, SMALL_SPLIT)] = mine[0:block].astype(F32).reshape(rows, size, cols)
        theirs = other_ref[op * block : (op + 1) * block]
        came[:, partner_chip(chip, 1 - core, op, SMALL_SPLIT)] = theirs.astype(F32).reshape(rows, size, cols)
    for row in range(0, rows, 2):
        for at, stream in enumerate(update(came, row, stream_ref, gate_ref, out_weight_ref[1])):
            out_ref[row + at] = flip_out(stream)


def flip_out(stream):
    return nt(identity(stream.shape[1]), stream.astype(BF16)).astype(BF16)


def chip_permute(block, step):
    count = lax.axis_size("wide")
    return lax.ppermute(block, "wide", [(w, w ^ (2 * step)) for w in range(count)])


def exchange(blocks, steps):
    return [chip_permute(blocks[step], step) if step else blocks[0] for step in steps]


def split_permute(block, steps):
    count = lax.axis_size("wide")
    return lax.ppermute(block, "wide", [(w, w ^ (2 * steps[w % 2])) for w in range(count)])


def split_exchange(blocks, split=SPLIT):
    return [split_permute(block, steps) for block, steps in zip(blocks, split)]


def with_partner(mine, theirs):
    got, messages, place = core_permute(theirs), [], 0
    for block in mine:
        messages.append(jnp.concatenate([block, got[place : place + block.shape[0]]], axis=0))
        place += block.shape[0]
    return messages


def core_permute(block):
    count = lax.axis_size("wide")
    return lax.ppermute(block, "wide", [(w, w ^ 1) for w in range(count)])


def per_device_chips(
    pairwise_state,
    homolog_features,
    residue_chain_index,
    resolved_residue_mask,
    alignment_mask,
    relative_offset_table,
    homolog_to_sides_matrix,
    outer_mean_output_weight,
    triangle_projection_weight,
    triangle_output_weight,
):
    rows, cols, width = pairwise_state.shape
    homologs = homolog_features.shape[0]
    half = homolog_to_sides_matrix.shape[1] // 2
    device = lax.axis_index("wide")
    chip, core = device // 2, device % 2
    where = jnp.stack([device * rows, chip, core]).astype(jnp.int32)
    present = resolved_residue_mask.reshape(1, cols)
    pay_rows = (half // 2 + 2) * rows
    row_present = lax.dynamic_slice_in_dim(resolved_residue_mask, device * rows, rows).astype(F32)
    live = alignment_mask.T.astype(F32) * row_present[:, None]
    live = jnp.concatenate([live, live], axis=1)
    pay, left, live = run(
        project_kernel,
        [((pay_rows, LANES), BF16), ((2 * rows * half, LANES), BF16), ((rows, LANES), F32)],
        homolog_features.astype(F32), homolog_to_sides_matrix.T, live,
        scratch=[((rows * half // 2, LANES), F32), ((pay_rows, LANES), F32)],
    )
    far_z = chip_permute(pay, 4)
    base, outer_t, proj_t, out_t = run(
        prep_kernel,
        [
            ((rows, width, cols), F32),
            ((width, half * half), BF16),
            ((2, triangle_projection_weight.shape[2], width), BF16),
            ((2, width, width), BF16),
        ],
        where, residue_chain_index, residue_chain_index.reshape(1, cols), pairwise_state,
        relative_offset_table, outer_mean_output_weight, triangle_projection_weight, triangle_output_weight,
        smem=(0, 1),
        scratch=[((LANES, width), F32), ((half * half, width), F32)],
    )
    along_z = jnp.stack([pay, far_z])
    along_z, base, outer_t, proj_t, out_t = lax.optimization_barrier((along_z, base, outer_t, proj_t, out_t))
    along_z = jnp.concatenate([along_z, chip_permute(along_z, 2)], axis=0)
    own = jnp.concatenate([along_z, chip_permute(along_z, 1)], axis=0)
    other = core_permute(own)
    tall = width * rows
    near, all_ = tall // NEAR, tall // (2 * OPS)
    made = run(
        outer_kernel,
        [((rows, width, cols), F32)] * 2
        + [((near, cols), BF16)] * 2
        + [((2 * near, cols), BF16)] * (1 + NEAR),
        where, resolved_residue_mask, own, other, left, live, base, outer_t, proj_t, present,
        smem=(0, 1),
        scratch=[
            ((16, pay_rows, LANES), F32),
            ((rows // 2, half * half, 2 * cols), BF16),
            ((tall, cols), F32),
            ((tall, cols), F32),
        ],
        flops=4 * 10**9,
    )
    stream, gate = made[0], made[1]
    came = exchange(made[5:9], NEAR_STEPS)
    far = split_exchange(with_partner(made[2:4], made[4]), FAR_SPLIT)
    rights = jnp.concatenate([block[near:] for block in came] + far, axis=0)
    mixed = run(
        mix_rows_kernel,
        [((near, cols), BF16)] * NEAR,
        where, *came, *far, core_permute(rights),
        smem=(0,),
        scratch=[
            ((NEAR, width // NEAR, rows, cols), F32),
            ((16, width // NEAR, rows, cols), F32),
            ((tall, cols), F32),
        ],
    )
    mixed = exchange(mixed, NEAR_STEPS)
    made = run(
        between_kernel,
        [((rows, width, cols), F32)] * 2 + [((2 * all_, cols), BF16)] * OPS + [((2 * OPS * all_, cols), BF16)],
        where, resolved_residue_mask, *mixed, stream, gate, out_t, proj_t, present,
        smem=(0, 1),
        scratch=[
            ((rows, NEAR, width // NEAR, cols), F32),
            ((tall, cols), F32),
            ((tall, cols), F32),
        ],
    )
    stream, gate, theirs = made[0], made[1], made[6]
    came = split_exchange(with_partner(made[2:6], theirs))
    mine, theirs = run(
        mix_cols_kernel,
        [((OPS, 2 * all_, cols), F32)] * 2,
        where, *came,
        smem=(0,),
        scratch=[
            ((2 * OPS, width // (2 * OPS), rows, cols), F32),
            ((2 * OPS, width // (2 * OPS), rows, cols), F32),
            ((2 * tall, cols), F32),
        ],
    )
    mixed = run(sum_kernel, [((2 * all_, cols), BF16)] * OPS, mine, core_permute(theirs))
    mixed = split_exchange(mixed, SMALL_SPLIT)
    other = core_permute(run(pick_kernel, [((OPS * all_, cols), BF16)], *mixed)[0])
    return run(
        final_kernel,
        [((rows, cols, width), BF16)],
        where, *mixed, other, stream, gate, out_t,
        smem=(0,),
        scratch=[((rows, 2 * OPS, width // (2 * OPS), cols), F32)],
    )[0]


def fits_chips(mesh):
    return mesh.shape["narrow"] == 1 and mesh.shape["wide"] == 16


def solution(mesh):
    per_device = per_device_chips if fits_chips(mesh) else per_device_general
    return jax.shard_map(
        per_device,
        mesh=mesh,
        in_specs=(
            P(("grp", "wide"), "narrow", None),
            P("grp", "wide", None),
            P("grp"),
            P("grp"),
            P("grp", "wide"),
            P(),
            P(),
            P(),
            P(),
            P(),
        ),
        out_specs=P(("grp", "wide"), "narrow", None),
        check_vma=False,
    )
```

```python
import functools

import jax
import jax.numpy as jnp
from jax import lax
from jax.experimental import pallas as pl
from jax.experimental.pallas import tpu as pltpu
from jax.sharding import PartitionSpec as P

RELMAX = 32
EPSILON = 1e-05
LANES = 128
F32 = jnp.float32
BF16 = jnp.bfloat16


def apply_layer_norm(values, axis_dim):
    center = values - jnp.mean(values, axis=axis_dim, keepdims=True)
    spread = jnp.mean(center * center, axis=axis_dim, keepdims=True)
    return center * lax.rsqrt(spread + EPSILON)


def gather_wide(block):
    n = lax.axis_size("wide")
    if n % 4 or n < 8:
        return lax.all_gather(block, "wide", axis=0)
    outer = n // 4
    me = lax.axis_index("wide")
    high, mid, low = me // 4, (me // 2) % 2, me % 2
    arrived = [block]
    for shift in range(1, outer):
        perm = [(w, ((w // 4 + shift) % outer) * 4 + w % 4) for w in range(n)]
        arrived.append(lax.ppermute(block, "wide", perm))
    held = jnp.zeros((outer,) + block.shape, block.dtype)
    for shift, piece in enumerate(arrived):
        held = lax.dynamic_update_index_in_dim(held, piece, (high - shift + outer) % outer, 0)
    other = lax.ppermute(held, "wide", [(w, w ^ 2) for w in range(n)])
    held = jnp.stack(
        [jnp.where(mid == 0, held, other), jnp.where(mid == 0, other, held)], axis=1
    )
    other = lax.ppermute(held, "wide", [(w, w ^ 1) for w in range(n)])
    held = jnp.stack(
        [jnp.where(low == 0, held, other), jnp.where(low == 0, other, held)], axis=2
    )
    return held.reshape((n,) + block.shape)


def triangle(stream, pair_live, proj_weight, out_weight, incoming):
    rows = stream.shape[0]
    cols = stream.shape[1]
    width = out_weight.shape[0]
    wide_count = lax.axis_size("wide")
    core_count = lax.axis_size("narrow")
    devices = wide_count * core_count
    per_dev = width // devices
    normed = apply_layer_norm(stream, 2).astype(jnp.bfloat16)
    blocks = [proj_weight[:, index * width : (index + 1) * width] for index in range(4)]

    def project(block):
        return jnp.einsum("ijd,dc->cij", normed, block, preferred_element_type=jnp.float32)

    left_side = (jax.nn.sigmoid(project(blocks[0])) * project(blocks[1]) * pair_live[None]).astype(
        jnp.bfloat16
    )
    right_side = (jax.nn.sigmoid(project(blocks[2])) * project(blocks[3]) * pair_live[None]).astype(
        jnp.bfloat16
    )
    gate = jax.nn.sigmoid(
        jnp.einsum(
            "ijd,dc->ijc", normed, proj_weight[:, 4 * width :], preferred_element_type=jnp.float32
        )
    )
    form = "cki,ckj->cij" if incoming else "cik,cjk->cij"
    both = jnp.stack(
        [
            left_side.reshape(devices, per_dev, rows * cols),
            right_side.reshape(devices, per_dev, rows * cols),
        ],
        axis=1,
    ).reshape(devices, 2 * per_dev, rows * cols)
    both = lax.all_to_all(both, ("wide", "narrow"), split_axis=0, concat_axis=0, tiled=True)
    both = both.reshape(wide_count, core_count, 2, per_dev, rows, cols)
    both = jnp.transpose(both, (2, 3, 0, 4, 1, 5)).reshape(
        2, per_dev, wide_count * rows, core_count * cols
    )
    mixed = jnp.einsum(form, both[0], both[1], preferred_element_type=jnp.float32).astype(
        jnp.bfloat16
    )
    spread_out = mixed.reshape(per_dev, wide_count, rows, core_count, cols)
    spread_out = jnp.transpose(spread_out, (1, 3, 0, 2, 4)).reshape(
        wide_count * core_count * per_dev, rows * cols
    )
    returned = lax.all_to_all(
        spread_out, ("wide", "narrow"), split_axis=0, concat_axis=0, tiled=True
    ).reshape(width, rows, cols)
    blended_standardize = apply_layer_norm(returned.astype(jnp.float32), 0).astype(jnp.bfloat16)
    update = jnp.einsum(
        "cij,cd->ijd", blended_standardize, out_weight, preferred_element_type=jnp.float32
    )
    return stream + gate * update


def per_device_general(
    pairwise_state,
    homolog_features,
    residue_chain_index,
    resolved_residue_mask,
    alignment_mask,
    relative_offset_table,
    homolog_to_sides_matrix,
    outer_mean_output_weight,
    triangle_projection_weight,
    triangle_output_weight,
):
    rows = pairwise_state.shape[0]
    cols = pairwise_state.shape[1]
    row_start = lax.axis_index("wide") * rows
    col_start = lax.axis_index("narrow") * cols
    residue_present = resolved_residue_mask.astype(jnp.float32)
    row_present = lax.dynamic_slice_in_dim(residue_present, row_start, rows)
    col_live = lax.dynamic_slice_in_dim(residue_present, col_start, cols)
    present_flags = alignment_mask.astype(jnp.float32) * row_present[None, :]
    alignment_normed = apply_layer_norm(homolog_features.astype(jnp.float32), 2).astype(
        jnp.bfloat16
    )
    projected_rows = jnp.einsum(
        "tna,ak->tnk", alignment_normed, homolog_to_sides_matrix, preferred_element_type=jnp.float32
    )
    projected_rows = (projected_rows * present_flags[:, :, None]).astype(jnp.bfloat16)
    half_width = projected_rows.shape[2] // 2
    homologs = projected_rows.shape[0]
    left_proj = projected_rows[:, :, :half_width]
    right_proj = projected_rows[:, :, half_width:]
    live_flags = present_flags.astype(jnp.bfloat16)
    packed = jnp.concatenate(
        [jnp.transpose(right_proj, (1, 0, 2)).reshape(rows, homologs * half_width), live_flags.T],
        axis=1,
    )
    gathered = gather_wide(packed).reshape(-1, packed.shape[1])
    gathered = lax.dynamic_slice_in_dim(gathered, col_start, cols, 0)
    right_mine = jnp.transpose(
        gathered[:, : homologs * half_width].reshape(cols, homologs, half_width), (1, 0, 2)
    )
    live_mine = gathered[:, homologs * half_width :].T
    counts = jnp.dot(live_flags.T, live_mine, preferred_element_type=jnp.float32)

    def opm_row(left_row):
        outer = jnp.einsum("sc,sjd->jcd", left_row, right_mine, preferred_element_type=jnp.float32)
        outer = outer.reshape(cols, half_width * half_width).astype(jnp.bfloat16)
        return jnp.dot(outer, outer_mean_output_weight, preferred_element_type=jnp.float32)

    opm = lax.map(opm_row, jnp.transpose(left_proj, (1, 0, 2)))
    row_pos = row_start + jnp.arange(rows, dtype=jnp.int32)
    col_pos = col_start + jnp.arange(cols, dtype=jnp.int32)
    row_chain = lax.dynamic_slice_in_dim(residue_chain_index, row_start, rows)
    col_chain = lax.dynamic_slice_in_dim(residue_chain_index, col_start, cols)
    offset = jnp.clip(row_pos[:, None] - col_pos[None, :], -RELMAX, RELMAX) + RELMAX
    bin_index = jnp.where(row_chain[:, None] == col_chain[None, :], offset, 2 * RELMAX + 1)
    bin_count = relative_offset_table.shape[0]
    one_hot = (
        bin_index[:, :, None] == jnp.arange(bin_count, dtype=jnp.int32)[None, None, :]
    ).astype(jnp.bfloat16)
    relpos = jnp.einsum(
        "ijb,bc->ijc", one_hot, relative_offset_table, preferred_element_type=jnp.float32
    )
    stream = (
        pairwise_state.astype(jnp.float32) + relpos + opm / jnp.maximum(counts, 1.0)[:, :, None]
    )
    pair_live = row_present[:, None] * col_live[None, :]
    for turn_index in range(2):
        stream = triangle(
            stream,
            pair_live,
            triangle_projection_weight[turn_index],
            triangle_output_weight[turn_index],
            turn_index == 1,
        )
    return stream.astype(jnp.bfloat16)


def nn(a, b):
    return lax.dot_general(a, b, (((1,), (0,)), ((), ())), preferred_element_type=F32)


def nt(a, b):
    return lax.dot_general(a, b, (((1,), (1,)), ((), ())), preferred_element_type=F32)


def tn(a, b):
    return lax.dot_general(a, b, (((0,), (0,)), ((), ())), preferred_element_type=F32)


def identity(size):
    rows = lax.broadcasted_iota(jnp.int32, (size, size), 0)
    cols = lax.broadcasted_iota(jnp.int32, (size, size), 1)
    return (rows == cols).astype(F32).astype(BF16)


def flip(block):
    return nt(identity(block.shape[1]), block)


def norm_rows(values):
    scale = 1.0 / values.shape[0]
    center = values - jnp.sum(values, axis=0, keepdims=True) * scale
    spread = jnp.sum(center * center, axis=0, keepdims=True) * scale
    return (center * lax.rsqrt(spread + EPSILON)).astype(BF16)


def run(kernel, outs, *args, smem=(), scratch=(), flops=15 * 10**8):
    vmem = pl.BlockSpec(memory_space=pltpu.VMEM)
    in_specs = [
        pl.BlockSpec(memory_space=pltpu.SMEM if at in smem else pltpu.VMEM) for at in range(len(args))
    ]
    moved = sum(a.size * a.dtype.itemsize for a in args)
    return pl.pallas_call(
        kernel,
        out_shape=[jax.ShapeDtypeStruct(shape, kind) for shape, kind in outs],
        in_specs=in_specs,
        out_specs=[vmem] * len(outs),
        scratch_shapes=[pltpu.VMEM(shape, kind) for shape, kind in scratch],
        compiler_params=pltpu.CompilerParams(vmem_limit_bytes=VMEM_LIMIT),
        cost_estimate=pl.CostEstimate(flops=flops, bytes_accessed=moved, transcendentals=0),
    )(*args)


VMEM_LIMIT = 20 * 1024 * 1024
SPLIT = ((7, 5), (6, 4), (3, 2), (1, 0))
FAR_SPLIT = SPLIT[:2]
SMALL_SPLIT = ((7, 3), (2, 6), (5, 1), (0, 4))
OPS = len(SPLIT)
NEAR = 4
NEAR_STEPS = (3, 2, 1, 0)


def partner_chip(chip, core, op, split=SPLIT):
    return chip ^ jnp.where(core == 0, split[op][0], split[op][1])


def project_kernel(feat_ref, weight_ref, live_in_ref, pay_ref, left_ref, live_ref, turned, packed):
    homologs, rows, _ = feat_ref.shape
    half = weight_ref.shape[0] // 2
    quarter = half // 2
    values = feat_ref[...].reshape(homologs * rows, feat_ref.shape[2])
    center = values - jnp.mean(values, axis=1, keepdims=True)
    spread = jnp.mean(center * center, axis=1, keepdims=True)
    normed = (center * lax.rsqrt(spread + EPSILON)).astype(BF16)
    total = homologs * rows
    out_row = lax.broadcasted_iota(jnp.int32, (total, total), 0)
    in_row = lax.broadcasted_iota(jnp.int32, (total, total), 1)
    order = in_row == (out_row & (homologs - 1)) * rows + out_row // homologs
    normed = nn(order.astype(F32).astype(BF16), normed).astype(BF16)
    live = live_in_ref[...]
    weight = weight_ref[...]
    blank = jnp.zeros((homologs, normed.shape[1]), BF16)
    for row in range(rows):
        mine = normed[row * homologs : (row + 1) * homologs]
        low = nt(weight, jnp.concatenate([mine, blank], axis=0)) * live[row : row + 1]
        high = nt(weight, jnp.concatenate([blank, mine], axis=0)) * live[row : row + 1]
        left_ref[row * half : (row + 1) * half] = low[:half].astype(BF16)
        left_ref[(rows + row) * half : (rows + row + 1) * half] = high[:half].astype(BF16)
        turned[row * quarter : (row + 1) * quarter] = low[half : half + quarter] + high[half + quarter :]
    for pair in range(quarter):
        packed[pair * rows : (pair + 1) * rows] = turned[pl.ds(pair, rows, stride=quarter), :]
    packed[quarter * rows : (quarter + 1) * rows] = live
    packed[(quarter + 1) * rows :] = jnp.zeros((rows, 2 * homologs), F32)
    pay_ref[...] = packed[...].astype(BF16)
    live_ref[...] = jnp.where(lax.broadcasted_iota(jnp.int32, live.shape, 1) < homologs, live, 0.0)


def prep_kernel(
    where_ref, chain_ref, chains_ref, pair_ref, table_ref, outer_ref, proj_ref, out_ref,
    base_ref, outer_t_ref, proj_t_ref, out_t_ref, table_pad, outer_pad,
):
    rows, cols, width = pair_ref.shape
    bins = table_ref.shape[0]
    table_pad[...] = jnp.zeros_like(table_pad)
    table_pad[0:bins, :] = table_ref[...].astype(F32)
    table = flip(table_pad[...].astype(BF16)).astype(BF16)
    chains = chains_ref[...]
    col = lax.broadcasted_iota(jnp.int32, (1, cols), 1)
    slot = lax.broadcasted_iota(jnp.int32, (table_pad.shape[0], cols), 0)
    for row in range(rows):
        place = where_ref[0] + row
        offset = jnp.clip(place - col, -RELMAX, RELMAX) + RELMAX
        bin_index = jnp.where(chains == chain_ref[place], offset, 2 * RELMAX + 1)
        hot = (slot == bin_index).astype(F32).astype(BF16)
        base_ref[row] = flip(pair_ref[row]) + nn(table, hot)
    half = round(outer_pad.shape[0] ** 0.5)
    outer_pad[...] = outer_ref[...].astype(F32)
    for d in range(half):
        outer_t_ref[:, d * half : (d + 1) * half] = flip(outer_pad[pl.ds(d, half, stride=half), :].astype(BF16)).astype(BF16)
    for turn in range(2):
        proj_t_ref[turn] = tn(proj_ref[turn], identity(width)).astype(BF16)
        out_t_ref[turn] = flip(out_ref[turn]).astype(BF16)


def sigmoid(values):
    return 0.5 * jnp.tanh(0.5 * values) + 0.5


def sides(streams, weight, lives, gate_ref, lefts, rights, row):
    width, cols = streams[0].shape
    rows = lefts.shape[0] // width
    made = nn(weight, jnp.concatenate([norm_rows(stream) for stream in streams], axis=1))
    for at, live in enumerate(lives):
        part = [
            made[block * width : (block + 1) * width, at * cols : (at + 1) * cols] for block in range(5)
        ]
        lefts[pl.ds(row + at, width, stride=rows), :] = sigmoid(part[0]) * part[1] * live
        rights[pl.ds(row + at, width, stride=rows), :] = sigmoid(part[2]) * part[3] * live
        gate_ref[row + at] = sigmoid(part[4])


def flat(block):
    return block.reshape(block.shape[0] * block.shape[1], block.shape[2])


def outer_kernel(
    where_ref, flag_ref, own_ref, other_ref, left_ref, live_ref, base_ref, outer_t_ref, proj_ref, present_ref,
    stream_ref, gate_ref, far0, far1, theirs_ref, near0, near1, near2, near3, came, outer, lefts, rights,
):
    rows, width, cols = base_ref.shape
    chip, core = where_ref[1], where_ref[2]
    per = own_ref.shape[1]
    chips = own_ref.shape[0]
    for at in range(chips):
        chip_at = chip ^ (at % 2 * 4 + at // 2 % 2 * 2 + at // 4)
        came[chip_at * 2 + core] = own_ref[at].astype(F32)
        came[chip_at * 2 + (1 - core)] = other_ref[at].astype(F32)
    half = left_ref.shape[0] // (2 * rows)
    quarter = half // 2
    live_all = came[:, quarter * rows : (quarter + 1) * rows, :].reshape(cols, per_lane(came)).astype(BF16)
    counts = nt(live_ref[...].astype(BF16), live_all)
    share = 1.0 / jnp.maximum(counts, 1.0)
    left_all = left_ref[...]
    for pair in range(quarter):
        right = came[:, pair * rows : (pair + 1) * rows, :].reshape(cols, per_lane(came)).astype(BF16)
        made = nt(left_all, right).astype(BF16)
        for part in range(2):
            d = part * quarter + pair
            for row in range(rows):
                first = (part * rows + row) * half
                lane = (row % 2) * cols
                outer[row // 2, d * half : (d + 1) * half, lane : lane + cols] = made[first : first + half]
    present = present_ref[...].astype(F32)
    for row in range(0, rows, 2):
        product = nn(outer_t_ref[...], outer[row // 2])
        streams, lives = [], []
        for at in range(2):
            streams.append(
                base_ref[row + at] + product[:, at * cols : (at + 1) * cols] * share[row + at : row + at + 1]
            )
            stream_ref[row + at] = streams[at]
            lives.append(present * flag_ref[where_ref[0] + row + at].astype(F32))
        sides(streams, proj_ref[0], lives, gate_ref, lefts, rights, row)
    size = width // NEAR
    block = size * rows

    def group(side, to):
        first = pl.multiple_of((to & (NEAR - 1)) * block, block)
        return side[pl.ds(first, block), :].astype(BF16)

    for op, far in enumerate((far0, far1)):
        far[...] = group(rights, partner_chip(chip, core, op, FAR_SPLIT))
        theirs_ref[op * block : (op + 1) * block] = group(rights, partner_chip(chip, 1 - core, op, FAR_SPLIT))
    for step, near in enumerate((near0, near1, near2, near3)):
        near[0:block] = group(lefts, chip ^ step)
        near[block:] = group(rights, chip ^ step)


def per_lane(ref):
    return ref.shape[-1]


def mix_rows_kernel(
    where_ref, near0, near1, near2, near3, far0, far1, other_ref,
    out0, out1, out2, out3, lefts, rights, mixed,
):
    chip, core = where_ref[1], where_ref[2]
    count, rows, cols = lefts.shape[1:]
    block = count * rows
    for at, (step, near) in enumerate(zip(NEAR_STEPS, (near0, near1, near2, near3))):
        lefts[step] = near[0:block].astype(F32).reshape(count, rows, cols)
        rights[(chip ^ step) * 2 + core] = near[block:].astype(F32).reshape(count, rows, cols)
        theirs = other_ref[at * block : (at + 1) * block]
        rights[(chip ^ step) * 2 + (1 - core)] = theirs.astype(F32).reshape(count, rows, cols)
    for op, far in enumerate((far0, far1)):
        for half in range(2):
            at = partner_chip(chip, core, op, FAR_SPLIT) * 2 + (core ^ half)
            rights[at] = far[half * block : (half + 1) * block].astype(F32).reshape(count, rows, cols)
            at = partner_chip(chip, 1 - core, op, FAR_SPLIT) * 2 + ((1 - core) ^ half)
            place = (NEAR + op * 2 + half) * block
            rights[at] = other_ref[place : place + block].astype(F32).reshape(count, rows, cols)
    for c in range(count):
        left = flat(lefts[:, c]).astype(BF16)
        right = flat(rights[:, c]).astype(BF16)
        mixed[pl.ds(c, NEAR * rows, stride=count), :] = nt(left, right)
    for step, out in enumerate((out0, out1, out2, out3)):
        out[...] = mixed[step * block : (step + 1) * block].astype(BF16)


def pick_kernel(*refs):
    blocks, out_ref = refs[:-1], refs[-1]
    for at, block in enumerate(blocks):
        half = block.shape[0] // 2
        out_ref[at * half : (at + 1) * half] = block[half:]


def update(came, row, stream_ref, gate_ref, out_weight):
    normed = jnp.concatenate([norm_rows(flat(came[row + at])) for at in range(2)], axis=1)
    made = nn(out_weight, normed)
    cols = made.shape[1] // 2
    return [
        stream_ref[row + at] + gate_ref[row + at] * made[:, at * cols : (at + 1) * cols] for at in range(2)
    ]


def between_kernel(
    where_ref, flag_ref, in0, in1, in2, in3, stream_ref, gate_ref, out_weight_ref, proj_ref, present_ref,
    next_ref, next_gate_ref, mine0, mine1, mine2, mine3, theirs_ref, came, lefts, rights,
):
    rows, width, cols = stream_ref.shape
    chip, core = where_ref[1], where_ref[2]
    size = width // NEAR
    for step, block in zip(NEAR_STEPS, (in0, in1, in2, in3)):
        came[:, (chip ^ step) & (NEAR - 1)] = block[...].astype(F32).reshape(rows, size, cols)
    present = present_ref[...].astype(F32)
    for row in range(0, rows, 2):
        streams = update(came, row, stream_ref, gate_ref, out_weight_ref[0])
        lives = []
        for at in range(2):
            next_ref[row + at] = streams[at]
            lives.append(present * flag_ref[where_ref[0] + row + at].astype(F32))
        sides(streams, proj_ref[1], lives, next_gate_ref, lefts, rights, row)
    block = width // (2 * OPS) * rows
    for op, mine in enumerate((mine0, mine1, mine2, mine3)):
        for at, side in enumerate((lefts, rights)):
            first = pl.multiple_of(partner_chip(chip, core, op) * block, block)
            mine[at * block : (at + 1) * block] = side[pl.ds(first, block), :].astype(BF16)
            first = pl.multiple_of(partner_chip(chip, 1 - core, op) * block, block)
            place = (op * 2 + at) * block
            theirs_ref[place : place + block] = side[pl.ds(first, block), :].astype(BF16)


def mix_cols_kernel(where_ref, came0, came1, came2, came3, mine_ref, theirs_ref, lefts, rights, partial):
    chip, core = where_ref[1], where_ref[2]
    count, rows, cols = lefts.shape[1:]
    block = count * rows
    for op, came in enumerate((came0, came1, came2, came3)):
        for half in range(2):
            for at, side in enumerate((lefts, rights)):
                place = (half * 2 + at) * block
                side[op * 2 + half] = came[place : place + block].astype(F32).reshape(count, rows, cols)
    for c in range(count):
        left = flat(lefts[:, c]).astype(BF16)
        right = flat(rights[:, c]).astype(BF16)
        partial[pl.ds(c, partial.shape[0] // count, stride=count), :] = tn(left, right)
    for op in range(OPS):
        for half in range(2):
            to = pl.multiple_of((partner_chip(chip, core, op, SMALL_SPLIT) * 2 + (core ^ half)) * block, block)
            mine_ref[op, half * block : (half + 1) * block] = partial[pl.ds(to, block), :]
            to = partner_chip(chip, 1 - core, op, SMALL_SPLIT) * 2 + ((1 - core) ^ half)
            to = pl.multiple_of(to * block, block)
            theirs_ref[op, half * block : (half + 1) * block] = partial[pl.ds(to, block), :].astype(BF16)


def sum_kernel(mine_ref, got_ref, *outs):
    for op, out in enumerate(outs):
        out[...] = (mine_ref[op] + got_ref[op].astype(F32)).astype(BF16)


def final_kernel(
    where_ref, came0, came1, came2, came3, other_ref, stream_ref, gate_ref, out_weight_ref, out_ref, came
):
    rows, width, cols = stream_ref.shape
    chip, core = where_ref[1], where_ref[2]
    size = width // (2 * OPS)
    block = size * rows
    for op, mine in enumerate((came0, came1, came2, came3)):
        came[:, partner_chip(chip, core, op, SMALL_SPLIT)] = mine[0:block].astype(F32).reshape(rows, size, cols)
        theirs = other_ref[op * block : (op + 1) * block]
        came[:, partner_chip(chip, 1 - core, op, SMALL_SPLIT)] = theirs.astype(F32).reshape(rows, size, cols)
    for row in range(0, rows, 2):
        for at, stream in enumerate(update(came, row, stream_ref, gate_ref, out_weight_ref[1])):
            out_ref[row + at] = flip_out(stream)


def flip_out(stream):
    return nt(identity(stream.shape[1]), stream.astype(BF16)).astype(BF16)


def chip_permute(block, step):
    count = lax.axis_size("wide")
    return lax.ppermute(block, "wide", [(w, w ^ (2 * step)) for w in range(count)])


def exchange(blocks, steps):
    return [chip_permute(blocks[step], step) if step else blocks[0] for step in steps]


def split_permute(block, steps):
    count = lax.axis_size("wide")
    return lax.ppermute(block, "wide", [(w, w ^ (2 * steps[w % 2])) for w in range(count)])


def split_exchange(blocks, split=SPLIT):
    return [split_permute(block, steps) for block, steps in zip(blocks, split)]


def with_partner(mine, theirs):
    got, messages, place = core_permute(theirs), [], 0
    for block in mine:
        messages.append(jnp.concatenate([block, got[place : place + block.shape[0]]], axis=0))
        place += block.shape[0]
    return messages


def core_permute(block):
    count = lax.axis_size("wide")
    return lax.ppermute(block, "wide", [(w, w ^ 1) for w in range(count)])


def per_device_chips(
    pairwise_state,
    homolog_features,
    residue_chain_index,
    resolved_residue_mask,
    alignment_mask,
    relative_offset_table,
    homolog_to_sides_matrix,
    outer_mean_output_weight,
    triangle_projection_weight,
    triangle_output_weight,
):
    rows, cols, width = pairwise_state.shape
    homologs = homolog_features.shape[0]
    half = homolog_to_sides_matrix.shape[1] // 2
    device = lax.axis_index("wide")
    chip, core = device // 2, device % 2
    where = jnp.stack([device * rows, chip, core]).astype(jnp.int32)
    present = resolved_residue_mask.reshape(1, cols)
    pay_rows = (half // 2 + 2) * rows
    row_present = lax.dynamic_slice_in_dim(resolved_residue_mask, device * rows, rows).astype(F32)
    live = alignment_mask.T.astype(F32) * row_present[:, None]
    live = jnp.concatenate([live, live], axis=1)
    pay, left, live = run(
        project_kernel,
        [((pay_rows, LANES), BF16), ((2 * rows * half, LANES), BF16), ((rows, LANES), F32)],
        homolog_features.astype(F32), homolog_to_sides_matrix.T, live,
        scratch=[((rows * half // 2, LANES), F32), ((pay_rows, LANES), F32)],
    )
    far_z = chip_permute(pay, 4)
    base, outer_t, proj_t, out_t = run(
        prep_kernel,
        [
            ((rows, width, cols), F32),
            ((width, half * half), BF16),
            ((2, triangle_projection_weight.shape[2], width), BF16),
            ((2, width, width), BF16),
        ],
        where, residue_chain_index, residue_chain_index.reshape(1, cols), pairwise_state,
        relative_offset_table, outer_mean_output_weight, triangle_projection_weight, triangle_output_weight,
        smem=(0, 1),
        scratch=[((LANES, width), F32), ((half * half, width), F32)],
    )
    along_z = jnp.stack([pay, far_z])
    along_z = jnp.concatenate([along_z, chip_permute(along_z, 2)], axis=0)
    own = jnp.concatenate([along_z, chip_permute(along_z, 1)], axis=0)
    own, base, outer_t, proj_t, out_t = lax.optimization_barrier((own, base, outer_t, proj_t, out_t))
    other = core_permute(own)
    tall = width * rows
    near, all_ = tall // NEAR, tall // (2 * OPS)
    made = run(
        outer_kernel,
        [((rows, width, cols), F32)] * 2
        + [((near, cols), BF16)] * 2
        + [((2 * near, cols), BF16)] * (1 + NEAR),
        where, resolved_residue_mask, own, other, left, live, base, outer_t, proj_t, present,
        smem=(0, 1),
        scratch=[
            ((16, pay_rows, LANES), F32),
            ((rows // 2, half * half, 2 * cols), BF16),
            ((tall, cols), F32),
            ((tall, cols), F32),
        ],
        flops=4 * 10**9,
    )
    stream, gate = made[0], made[1]
    came = exchange(made[5:9], NEAR_STEPS)
    far = split_exchange(with_partner(made[2:4], made[4]), FAR_SPLIT)
    rights = jnp.concatenate([block[near:] for block in came] + far, axis=0)
    mixed = run(
        mix_rows_kernel,
        [((near, cols), BF16)] * NEAR,
        where, *came, *far, core_permute(rights),
        smem=(0,),
        scratch=[
            ((NEAR, width // NEAR, rows, cols), F32),
            ((16, width // NEAR, rows, cols), F32),
            ((tall, cols), F32),
        ],
    )
    mixed = exchange(mixed, NEAR_STEPS)
    made = run(
        between_kernel,
        [((rows, width, cols), F32)] * 2 + [((2 * all_, cols), BF16)] * OPS + [((2 * OPS * all_, cols), BF16)],
        where, resolved_residue_mask, *mixed, stream, gate, out_t, proj_t, present,
        smem=(0, 1),
        scratch=[
            ((rows, NEAR, width // NEAR, cols), F32),
            ((tall, cols), F32),
            ((tall, cols), F32),
        ],
    )
    stream, gate, theirs = made[0], made[1], made[6]
    came = split_exchange(with_partner(made[2:6], theirs))
    mine, theirs = run(
        mix_cols_kernel,
        [((OPS, 2 * all_, cols), F32), ((OPS, 2 * all_, cols), BF16)],
        where, *came,
        smem=(0,),
        scratch=[
            ((2 * OPS, width // (2 * OPS), rows, cols), F32),
            ((2 * OPS, width // (2 * OPS), rows, cols), F32),
            ((2 * tall, cols), F32),
        ],
    )
    mixed = run(sum_kernel, [((2 * all_, cols), BF16)] * OPS, mine, core_permute(theirs))
    mixed = split_exchange(mixed, SMALL_SPLIT)
    other = core_permute(run(pick_kernel, [((OPS * all_, cols), BF16)], *mixed)[0])
    return run(
        final_kernel,
        [((rows, cols, width), BF16)],
        where, *mixed, other, stream, gate, out_t,
        smem=(0,),
        scratch=[((rows, 2 * OPS, width // (2 * OPS), cols), F32)],
    )[0]


def fits_chips(mesh):
    return mesh.shape["narrow"] == 1 and mesh.shape["wide"] == 16


def solution(mesh):
    per_device = per_device_chips if fits_chips(mesh) else per_device_general
    return jax.shard_map(
        per_device,
        mesh=mesh,
        in_specs=(
            P(("grp", "wide"), "narrow", None),
            P("grp", "wide", None),
            P("grp"),
            P("grp"),
            P("grp", "wide"),
            P(),
            P(),
            P(),
            P(),
            P(),
        ),
        out_specs=P(("grp", "wide"), "narrow", None),
        check_vma=False,
    )
```

```python
import functools

import jax
import jax.numpy as jnp
from jax import lax
from jax.experimental import pallas as pl
from jax.experimental.pallas import tpu as pltpu
from jax.sharding import PartitionSpec as P

RELMAX = 32
EPSILON = 1e-05
LANES = 128
F32 = jnp.float32
BF16 = jnp.bfloat16


def apply_layer_norm(values, axis_dim):
    center = values - jnp.mean(values, axis=axis_dim, keepdims=True)
    spread = jnp.mean(center * center, axis=axis_dim, keepdims=True)
    return center * lax.rsqrt(spread + EPSILON)


def gather_wide(block):
    n = lax.axis_size("wide")
    if n % 4 or n < 8:
        return lax.all_gather(block, "wide", axis=0)
    outer = n // 4
    me = lax.axis_index("wide")
    high, mid, low = me // 4, (me // 2) % 2, me % 2
    arrived = [block]
    for shift in range(1, outer):
        perm = [(w, ((w // 4 + shift) % outer) * 4 + w % 4) for w in range(n)]
        arrived.append(lax.ppermute(block, "wide", perm))
    held = jnp.zeros((outer,) + block.shape, block.dtype)
    for shift, piece in enumerate(arrived):
        held = lax.dynamic_update_index_in_dim(held, piece, (high - shift + outer) % outer, 0)
    other = lax.ppermute(held, "wide", [(w, w ^ 2) for w in range(n)])
    held = jnp.stack(
        [jnp.where(mid == 0, held, other), jnp.where(mid == 0, other, held)], axis=1
    )
    other = lax.ppermute(held, "wide", [(w, w ^ 1) for w in range(n)])
    held = jnp.stack(
        [jnp.where(low == 0, held, other), jnp.where(low == 0, other, held)], axis=2
    )
    return held.reshape((n,) + block.shape)


def triangle(stream, pair_live, proj_weight, out_weight, incoming):
    rows = stream.shape[0]
    cols = stream.shape[1]
    width = out_weight.shape[0]
    wide_count = lax.axis_size("wide")
    core_count = lax.axis_size("narrow")
    devices = wide_count * core_count
    per_dev = width // devices
    normed = apply_layer_norm(stream, 2).astype(jnp.bfloat16)
    blocks = [proj_weight[:, index * width : (index + 1) * width] for index in range(4)]

    def project(block):
        return jnp.einsum("ijd,dc->cij", normed, block, preferred_element_type=jnp.float32)

    left_side = (jax.nn.sigmoid(project(blocks[0])) * project(blocks[1]) * pair_live[None]).astype(
        jnp.bfloat16
    )
    right_side = (jax.nn.sigmoid(project(blocks[2])) * project(blocks[3]) * pair_live[None]).astype(
        jnp.bfloat16
    )
    gate = jax.nn.sigmoid(
        jnp.einsum(
            "ijd,dc->ijc", normed, proj_weight[:, 4 * width :], preferred_element_type=jnp.float32
        )
    )
    form = "cki,ckj->cij" if incoming else "cik,cjk->cij"
    both = jnp.stack(
        [
            left_side.reshape(devices, per_dev, rows * cols),
            right_side.reshape(devices, per_dev, rows * cols),
        ],
        axis=1,
    ).reshape(devices, 2 * per_dev, rows * cols)
    both = lax.all_to_all(both, ("wide", "narrow"), split_axis=0, concat_axis=0, tiled=True)
    both = both.reshape(wide_count, core_count, 2, per_dev, rows, cols)
    both = jnp.transpose(both, (2, 3, 0, 4, 1, 5)).reshape(
        2, per_dev, wide_count * rows, core_count * cols
    )
    mixed = jnp.einsum(form, both[0], both[1], preferred_element_type=jnp.float32).astype(
        jnp.bfloat16
    )
    spread_out = mixed.reshape(per_dev, wide_count, rows, core_count, cols)
    spread_out = jnp.transpose(spread_out, (1, 3, 0, 2, 4)).reshape(
        wide_count * core_count * per_dev, rows * cols
    )
    returned = lax.all_to_all(
        spread_out, ("wide", "narrow"), split_axis=0, concat_axis=0, tiled=True
    ).reshape(width, rows, cols)
    blended_standardize = apply_layer_norm(returned.astype(jnp.float32), 0).astype(jnp.bfloat16)
    update = jnp.einsum(
        "cij,cd->ijd", blended_standardize, out_weight, preferred_element_type=jnp.float32
    )
    return stream + gate * update


def per_device_general(
    pairwise_state,
    homolog_features,
    residue_chain_index,
    resolved_residue_mask,
    alignment_mask,
    relative_offset_table,
    homolog_to_sides_matrix,
    outer_mean_output_weight,
    triangle_projection_weight,
    triangle_output_weight,
):
    rows = pairwise_state.shape[0]
    cols = pairwise_state.shape[1]
    row_start = lax.axis_index("wide") * rows
    col_start = lax.axis_index("narrow") * cols
    residue_present = resolved_residue_mask.astype(jnp.float32)
    row_present = lax.dynamic_slice_in_dim(residue_present, row_start, rows)
    col_live = lax.dynamic_slice_in_dim(residue_present, col_start, cols)
    present_flags = alignment_mask.astype(jnp.float32) * row_present[None, :]
    alignment_normed = apply_layer_norm(homolog_features.astype(jnp.float32), 2).astype(
        jnp.bfloat16
    )
    projected_rows = jnp.einsum(
        "tna,ak->tnk", alignment_normed, homolog_to_sides_matrix, preferred_element_type=jnp.float32
    )
    projected_rows = (projected_rows * present_flags[:, :, None]).astype(jnp.bfloat16)
    half_width = projected_rows.shape[2] // 2
    homologs = projected_rows.shape[0]
    left_proj = projected_rows[:, :, :half_width]
    right_proj = projected_rows[:, :, half_width:]
    live_flags = present_flags.astype(jnp.bfloat16)
    packed = jnp.concatenate(
        [jnp.transpose(right_proj, (1, 0, 2)).reshape(rows, homologs * half_width), live_flags.T],
        axis=1,
    )
    gathered = gather_wide(packed).reshape(-1, packed.shape[1])
    gathered = lax.dynamic_slice_in_dim(gathered, col_start, cols, 0)
    right_mine = jnp.transpose(
        gathered[:, : homologs * half_width].reshape(cols, homologs, half_width), (1, 0, 2)
    )
    live_mine = gathered[:, homologs * half_width :].T
    counts = jnp.dot(live_flags.T, live_mine, preferred_element_type=jnp.float32)

    def opm_row(left_row):
        outer = jnp.einsum("sc,sjd->jcd", left_row, right_mine, preferred_element_type=jnp.float32)
        outer = outer.reshape(cols, half_width * half_width).astype(jnp.bfloat16)
        return jnp.dot(outer, outer_mean_output_weight, preferred_element_type=jnp.float32)

    opm = lax.map(opm_row, jnp.transpose(left_proj, (1, 0, 2)))
    row_pos = row_start + jnp.arange(rows, dtype=jnp.int32)
    col_pos = col_start + jnp.arange(cols, dtype=jnp.int32)
    row_chain = lax.dynamic_slice_in_dim(residue_chain_index, row_start, rows)
    col_chain = lax.dynamic_slice_in_dim(residue_chain_index, col_start, cols)
    offset = jnp.clip(row_pos[:, None] - col_pos[None, :], -RELMAX, RELMAX) + RELMAX
    bin_index = jnp.where(row_chain[:, None] == col_chain[None, :], offset, 2 * RELMAX + 1)
    bin_count = relative_offset_table.shape[0]
    one_hot = (
        bin_index[:, :, None] == jnp.arange(bin_count, dtype=jnp.int32)[None, None, :]
    ).astype(jnp.bfloat16)
    relpos = jnp.einsum(
        "ijb,bc->ijc", one_hot, relative_offset_table, preferred_element_type=jnp.float32
    )
    stream = (
        pairwise_state.astype(jnp.float32) + relpos + opm / jnp.maximum(counts, 1.0)[:, :, None]
    )
    pair_live = row_present[:, None] * col_live[None, :]
    for turn_index in range(2):
        stream = triangle(
            stream,
            pair_live,
            triangle_projection_weight[turn_index],
            triangle_output_weight[turn_index],
            turn_index == 1,
        )
    return stream.astype(jnp.bfloat16)


def nn(a, b):
    return lax.dot_general(a, b, (((1,), (0,)), ((), ())), preferred_element_type=F32)


def nt(a, b):
    return lax.dot_general(a, b, (((1,), (1,)), ((), ())), preferred_element_type=F32)


def tn(a, b):
    return lax.dot_general(a, b, (((0,), (0,)), ((), ())), preferred_element_type=F32)


def identity(size):
    rows = lax.broadcasted_iota(jnp.int32, (size, size), 0)
    cols = lax.broadcasted_iota(jnp.int32, (size, size), 1)
    return (rows == cols).astype(F32).astype(BF16)


def flip(block):
    return nt(identity(block.shape[1]), block)


def norm_rows(values):
    scale = 1.0 / values.shape[0]
    center = values - jnp.sum(values, axis=0, keepdims=True) * scale
    spread = jnp.sum(center * center, axis=0, keepdims=True) * scale
    return (center * lax.rsqrt(spread + EPSILON)).astype(BF16)


def run(kernel, outs, *args, smem=(), scratch=(), flops=15 * 10**8):
    vmem = pl.BlockSpec(memory_space=pltpu.VMEM)
    in_specs = [
        pl.BlockSpec(memory_space=pltpu.SMEM if at in smem else pltpu.VMEM) for at in range(len(args))
    ]
    moved = sum(a.size * a.dtype.itemsize for a in args)
    return pl.pallas_call(
        kernel,
        out_shape=[jax.ShapeDtypeStruct(shape, kind) for shape, kind in outs],
        in_specs=in_specs,
        out_specs=[vmem] * len(outs),
        scratch_shapes=[pltpu.VMEM(shape, kind) for shape, kind in scratch],
        compiler_params=pltpu.CompilerParams(vmem_limit_bytes=VMEM_LIMIT),
        cost_estimate=pl.CostEstimate(flops=flops, bytes_accessed=moved, transcendentals=0),
    )(*args)


VMEM_LIMIT = 20 * 1024 * 1024
SPLIT = ((7, 5), (6, 4), (3, 2), (1, 0))
FAR_SPLIT = SPLIT[:2]
SMALL_SPLIT = ((7, 3), (2, 6), (5, 1), (0, 4))
OPS = len(SPLIT)
NEAR = 4
NEAR_STEPS = (3, 2, 1, 0)


def partner_chip(chip, core, op, split=SPLIT):
    return chip ^ jnp.where(core == 0, split[op][0], split[op][1])


def project_kernel(
    where_ref, feat_ref, weight_ref, mask_ref, present_ref, pay_ref, left_ref, live_ref, turned, packed
):
    homologs, rows, _ = feat_ref.shape
    half = weight_ref.shape[0] // 2
    quarter = half // 2
    values = feat_ref[...].reshape(homologs * rows, feat_ref.shape[2])
    center = values - jnp.mean(values, axis=1, keepdims=True)
    spread = jnp.mean(center * center, axis=1, keepdims=True)
    normed = (center * lax.rsqrt(spread + EPSILON)).astype(BF16)
    total = homologs * rows
    out_row = lax.broadcasted_iota(jnp.int32, (total, total), 0)
    in_row = lax.broadcasted_iota(jnp.int32, (total, total), 1)
    order = in_row == (out_row & (homologs - 1)) * rows + out_row // homologs
    normed = nn(order.astype(F32).astype(BF16), normed).astype(BF16)
    seq = lax.broadcasted_iota(jnp.int32, (homologs, 2 * homologs), 0)
    lane = lax.broadcasted_iota(jnp.int32, (homologs, 2 * homologs), 1)
    twice = (seq == (lane & (homologs - 1))).astype(F32).astype(BF16)
    cols = present_ref.shape[1]
    here = lax.broadcasted_iota(jnp.int32, (rows, cols), 1) == (
        lax.broadcasted_iota(jnp.int32, (rows, cols), 0) + where_ref[0]
    )
    present = jnp.sum(jnp.where(here, present_ref[...].astype(F32), 0.0), axis=1, keepdims=True)
    live = nn(mask_ref[...], twice) * present
    weight = weight_ref[...]
    blank = jnp.zeros((homologs, normed.shape[1]), BF16)
    for row in range(rows):
        mine = normed[row * homologs : (row + 1) * homologs]
        low = nt(weight, jnp.concatenate([mine, blank], axis=0)) * live[row : row + 1]
        high = nt(weight, jnp.concatenate([blank, mine], axis=0)) * live[row : row + 1]
        left_ref[row * half : (row + 1) * half] = low[:half].astype(BF16)
        left_ref[(rows + row) * half : (rows + row + 1) * half] = high[:half].astype(BF16)
        turned[row * quarter : (row + 1) * quarter] = low[half : half + quarter] + high[half + quarter :]
    for pair in range(quarter):
        packed[pair * rows : (pair + 1) * rows] = turned[pl.ds(pair, rows, stride=quarter), :]
    packed[quarter * rows : (quarter + 1) * rows] = live
    packed[(quarter + 1) * rows :] = jnp.zeros((rows, 2 * homologs), F32)
    pay_ref[...] = packed[...].astype(BF16)
    live_ref[...] = jnp.where(lax.broadcasted_iota(jnp.int32, live.shape, 1) < homologs, live, 0.0)


def prep_kernel(
    where_ref, chain_ref, chains_ref, pair_ref, table_ref, outer_ref, proj_ref, out_ref,
    base_ref, outer_t_ref, proj_t_ref, out_t_ref, table_pad, outer_pad,
):
    rows, cols, width = pair_ref.shape
    bins = table_ref.shape[0]
    table_pad[...] = jnp.zeros_like(table_pad)
    table_pad[0:bins, :] = table_ref[...].astype(F32)
    table = flip(table_pad[...].astype(BF16)).astype(BF16)
    chains = chains_ref[...]
    col = lax.broadcasted_iota(jnp.int32, (1, cols), 1)
    slot = lax.broadcasted_iota(jnp.int32, (table_pad.shape[0], cols), 0)
    for row in range(rows):
        place = where_ref[0] + row
        offset = jnp.clip(place - col, -RELMAX, RELMAX) + RELMAX
        bin_index = jnp.where(chains == chain_ref[place], offset, 2 * RELMAX + 1)
        hot = (slot == bin_index).astype(F32).astype(BF16)
        base_ref[row] = flip(pair_ref[row]) + nn(table, hot)
    half = round(outer_pad.shape[0] ** 0.5)
    outer_pad[...] = outer_ref[...].astype(F32)
    for d in range(half):
        outer_t_ref[:, d * half : (d + 1) * half] = flip(outer_pad[pl.ds(d, half, stride=half), :].astype(BF16)).astype(BF16)
    for turn in range(2):
        proj_t_ref[turn] = tn(proj_ref[turn], identity(width)).astype(BF16)
        out_t_ref[turn] = flip(out_ref[turn]).astype(BF16)


def sigmoid(values):
    return 0.5 * jnp.tanh(0.5 * values) + 0.5


def sides(streams, weight, lives, gate_ref, lefts, rights, row):
    width, cols = streams[0].shape
    rows = lefts.shape[0] // width
    made = nn(weight, jnp.concatenate([norm_rows(stream) for stream in streams], axis=1))
    for at, live in enumerate(lives):
        part = [
            made[block * width : (block + 1) * width, at * cols : (at + 1) * cols] for block in range(5)
        ]
        lefts[pl.ds(row + at, width, stride=rows), :] = sigmoid(part[0]) * part[1] * live
        rights[pl.ds(row + at, width, stride=rows), :] = sigmoid(part[2]) * part[3] * live
        gate_ref[row + at] = sigmoid(part[4])


def flat(block):
    return block.reshape(block.shape[0] * block.shape[1], block.shape[2])


def outer_kernel(
    where_ref, flag_ref, own_ref, other_ref, left_ref, live_ref, base_ref, outer_t_ref, proj_ref, present_ref,
    stream_ref, gate_ref, far0, far1, theirs_ref, near0, near1, near2, near3, came, outer, lefts, rights,
):
    rows, width, cols = base_ref.shape
    chip, core = where_ref[1], where_ref[2]
    per = own_ref.shape[1]
    chips = own_ref.shape[0]
    for at in range(chips):
        chip_at = chip ^ (at % 2 * 4 + at // 2 % 2 * 2 + at // 4)
        came[chip_at * 2 + core] = own_ref[at].astype(F32)
        came[chip_at * 2 + (1 - core)] = other_ref[at].astype(F32)
    half = left_ref.shape[0] // (2 * rows)
    quarter = half // 2
    live_all = came[:, quarter * rows : (quarter + 1) * rows, :].reshape(cols, per_lane(came)).astype(BF16)
    counts = nt(live_ref[...].astype(BF16), live_all)
    share = 1.0 / jnp.maximum(counts, 1.0)
    left_all = left_ref[...]
    for pair in range(quarter):
        right = came[:, pair * rows : (pair + 1) * rows, :].reshape(cols, per_lane(came)).astype(BF16)
        made = nt(left_all, right).astype(BF16)
        for part in range(2):
            d = part * quarter + pair
            for row in range(rows):
                first = (part * rows + row) * half
                lane = (row % 2) * cols
                outer[row // 2, d * half : (d + 1) * half, lane : lane + cols] = made[first : first + half]
    present = present_ref[...].astype(F32)
    for row in range(0, rows, 2):
        product = nn(outer_t_ref[...], outer[row // 2])
        streams, lives = [], []
        for at in range(2):
            streams.append(
                base_ref[row + at] + product[:, at * cols : (at + 1) * cols] * share[row + at : row + at + 1]
            )
            stream_ref[row + at] = streams[at]
            lives.append(present * flag_ref[where_ref[0] + row + at].astype(F32))
        sides(streams, proj_ref[0], lives, gate_ref, lefts, rights, row)
    size = width // NEAR
    block = size * rows

    def group(side, to):
        first = pl.multiple_of((to & (NEAR - 1)) * block, block)
        return side[pl.ds(first, block), :].astype(BF16)

    for op, far in enumerate((far0, far1)):
        far[...] = group(rights, partner_chip(chip, core, op, FAR_SPLIT))
        theirs_ref[op * block : (op + 1) * block] = group(rights, partner_chip(chip, 1 - core, op, FAR_SPLIT))
    for step, near in enumerate((near0, near1, near2, near3)):
        near[0:block] = group(lefts, chip ^ step)
        near[block:] = group(rights, chip ^ step)


def per_lane(ref):
    return ref.shape[-1]


def mix_rows_kernel(
    where_ref, near3, far0, near2, near1, near0, far1, other_ref, out0, out1, out2, out3, lefts, rights, mixed
):
    chip, core = where_ref[1], where_ref[2]
    count, rows, cols = lefts.shape[1:]
    block = count * rows
    place = 0
    for step, near in ((3, near3), (None, far0), (2, near2), (1, near1), (0, near0), (None, far1)):
        if step is None:
            op = 0 if near is far0 else 1
            for half in range(2):
                at = partner_chip(chip, core, op, FAR_SPLIT) * 2 + (core ^ half)
                rights[at] = near[half * block : (half + 1) * block].astype(F32).reshape(count, rows, cols)
                at = partner_chip(chip, 1 - core, op, FAR_SPLIT) * 2 + ((1 - core) ^ half)
                rights[at] = other_ref[place : place + block].astype(F32).reshape(count, rows, cols)
                place += block
        else:
            lefts[step] = near[0:block].astype(F32).reshape(count, rows, cols)
            rights[(chip ^ step) * 2 + core] = near[block:].astype(F32).reshape(count, rows, cols)
            theirs = other_ref[place : place + block]
            rights[(chip ^ step) * 2 + (1 - core)] = theirs.astype(F32).reshape(count, rows, cols)
            place += block
    for c in range(count):
        left = flat(lefts[:, c]).astype(BF16)
        right = flat(rights[:, c]).astype(BF16)
        mixed[pl.ds(c, NEAR * rows, stride=count), :] = nt(left, right)
    for step, out in enumerate((out0, out1, out2, out3)):
        out[...] = mixed[step * block : (step + 1) * block].astype(BF16)


def pick_kernel(*refs):
    blocks, out_ref = refs[:-1], refs[-1]
    for at, block in enumerate(blocks):
        half = block.shape[0] // 2
        out_ref[at * half : (at + 1) * half] = block[half:]


def update(came, row, stream_ref, gate_ref, out_weight):
    normed = jnp.concatenate([norm_rows(flat(came[row + at])) for at in range(2)], axis=1)
    made = nn(out_weight, normed)
    cols = made.shape[1] // 2
    return [
        stream_ref[row + at] + gate_ref[row + at] * made[:, at * cols : (at + 1) * cols] for at in range(2)
    ]


def between_kernel(
    where_ref, flag_ref, in0, in1, in2, in3, stream_ref, gate_ref, out_weight_ref, proj_ref, present_ref,
    next_ref, next_gate_ref, mine0, mine1, mine2, mine3, theirs_ref, came, lefts, rights,
):
    rows, width, cols = stream_ref.shape
    chip, core = where_ref[1], where_ref[2]
    size = width // NEAR
    for step, block in zip(NEAR_STEPS, (in0, in1, in2, in3)):
        came[:, (chip ^ step) & (NEAR - 1)] = block[...].astype(F32).reshape(rows, size, cols)
    present = present_ref[...].astype(F32)
    for row in range(0, rows, 2):
        streams = update(came, row, stream_ref, gate_ref, out_weight_ref[0])
        lives = []
        for at in range(2):
            next_ref[row + at] = streams[at]
            lives.append(present * flag_ref[where_ref[0] + row + at].astype(F32))
        sides(streams, proj_ref[1], lives, next_gate_ref, lefts, rights, row)
    block = width // (2 * OPS) * rows
    for op, mine in enumerate((mine0, mine1, mine2, mine3)):
        for at, side in enumerate((lefts, rights)):
            first = pl.multiple_of(partner_chip(chip, core, op) * block, block)
            mine[at * block : (at + 1) * block] = side[pl.ds(first, block), :].astype(BF16)
            first = pl.multiple_of(partner_chip(chip, 1 - core, op) * block, block)
            place = (op * 2 + at) * block
            theirs_ref[place : place + block] = side[pl.ds(first, block), :].astype(BF16)


def mix_cols_kernel(where_ref, came0, came1, came2, came3, mine_ref, theirs_ref, lefts, rights, partial):
    chip, core = where_ref[1], where_ref[2]
    count, rows, cols = lefts.shape[1:]
    block = count * rows
    for op, came in enumerate((came0, came1, came2, came3)):
        for half in range(2):
            for at, side in enumerate((lefts, rights)):
                place = (half * 2 + at) * block
                side[op * 2 + half] = came[place : place + block].astype(F32).reshape(count, rows, cols)
    for c in range(count):
        left = flat(lefts[:, c]).astype(BF16)
        right = flat(rights[:, c]).astype(BF16)
        partial[pl.ds(c, partial.shape[0] // count, stride=count), :] = tn(left, right)
    for op in range(OPS):
        for half in range(2):
            to = pl.multiple_of((partner_chip(chip, core, op, SMALL_SPLIT) * 2 + (core ^ half)) * block, block)
            mine_ref[op, half * block : (half + 1) * block] = partial[pl.ds(to, block), :]
            to = partner_chip(chip, 1 - core, op, SMALL_SPLIT) * 2 + ((1 - core) ^ half)
            to = pl.multiple_of(to * block, block)
            theirs_ref[op, half * block : (half + 1) * block] = partial[pl.ds(to, block), :].astype(BF16)


def sum_kernel(mine_ref, got_ref, *outs):
    for op, out in enumerate(outs):
        out[...] = (mine_ref[op] + got_ref[op].astype(F32)).astype(BF16)


def final_kernel(
    where_ref, came0, came1, came2, came3, other_ref, stream_ref, gate_ref, out_weight_ref, out_ref, came
):
    rows, width, cols = stream_ref.shape
    chip, core = where_ref[1], where_ref[2]
    size = width // (2 * OPS)
    block = size * rows
    for op, mine in enumerate((came0, came1, came2, came3)):
        came[:, partner_chip(chip, core, op, SMALL_SPLIT)] = mine[0:block].astype(F32).reshape(rows, size, cols)
        theirs = other_ref[op * block : (op + 1) * block]
        came[:, partner_chip(chip, 1 - core, op, SMALL_SPLIT)] = theirs.astype(F32).reshape(rows, size, cols)
    for row in range(0, rows, 2):
        for at, stream in enumerate(update(came, row, stream_ref, gate_ref, out_weight_ref[1])):
            out_ref[row + at] = flip_out(stream)


def flip_out(stream):
    return nt(identity(stream.shape[1]), stream.astype(BF16)).astype(BF16)


def chip_permute(block, step):
    count = lax.axis_size("wide")
    return lax.ppermute(block, "wide", [(w, w ^ (2 * step)) for w in range(count)])


def exchange(blocks, steps):
    return [chip_permute(blocks[step], step) if step else blocks[0] for step in steps]


def split_permute(block, steps):
    count = lax.axis_size("wide")
    return lax.ppermute(block, "wide", [(w, w ^ (2 * steps[w % 2])) for w in range(count)])


def split_exchange(blocks, split=SPLIT):
    return [split_permute(block, steps) for block, steps in zip(blocks, split)]


def with_partner(mine, theirs):
    got, messages, place = core_permute(theirs), [], 0
    for block in mine:
        messages.append(jnp.concatenate([block, got[place : place + block.shape[0]]], axis=0))
        place += block.shape[0]
    return messages


def core_permute(block):
    count = lax.axis_size("wide")
    return lax.ppermute(block, "wide", [(w, w ^ 1) for w in range(count)])


def per_device_chips(
    pairwise_state,
    homolog_features,
    residue_chain_index,
    resolved_residue_mask,
    alignment_mask,
    relative_offset_table,
    homolog_to_sides_matrix,
    outer_mean_output_weight,
    triangle_projection_weight,
    triangle_output_weight,
):
    rows, cols, width = pairwise_state.shape
    homologs = homolog_features.shape[0]
    half = homolog_to_sides_matrix.shape[1] // 2
    device = lax.axis_index("wide")
    chip, core = device // 2, device % 2
    where = jnp.stack([device * rows, chip, core]).astype(jnp.int32)
    present = resolved_residue_mask.reshape(1, cols)
    pay_rows = (half // 2 + 2) * rows
    pay, left, live = run(
        project_kernel,
        [((pay_rows, LANES), BF16), ((2 * rows * half, LANES), BF16), ((rows, LANES), F32)],
        where, homolog_features.astype(F32), homolog_to_sides_matrix.T, alignment_mask.T, present,
        smem=(0,),
        scratch=[((rows * half // 2, LANES), F32), ((pay_rows, LANES), F32)],
    )
    far_z = chip_permute(pay, 4)
    base, outer_t, proj_t, out_t = run(
        prep_kernel,
        [
            ((rows, width, cols), F32),
            ((width, half * half), BF16),
            ((2, triangle_projection_weight.shape[2], width), BF16),
            ((2, width, width), BF16),
        ],
        where, residue_chain_index, residue_chain_index.reshape(1, cols), pairwise_state,
        relative_offset_table, outer_mean_output_weight, triangle_projection_weight, triangle_output_weight,
        smem=(0, 1),
        scratch=[((LANES, width), F32), ((half * half, width), F32)],
    )
    along_z = jnp.stack([pay, far_z])
    along_z = jnp.concatenate([along_z, chip_permute(along_z, 2)], axis=0)
    own = jnp.concatenate([along_z, chip_permute(along_z, 1)], axis=0)
    own, base, outer_t, proj_t, out_t = lax.optimization_barrier((own, base, outer_t, proj_t, out_t))
    other = core_permute(own)
    tall = width * rows
    near, all_ = tall // NEAR, tall // (2 * OPS)
    made = run(
        outer_kernel,
        [((rows, width, cols), F32)] * 2
        + [((near, cols), BF16)] * 2
        + [((2 * near, cols), BF16)] * (1 + NEAR),
        where, resolved_residue_mask, own, other, left, live, base, outer_t, proj_t, present,
        smem=(0, 1),
        scratch=[
            ((16, pay_rows, LANES), F32),
            ((rows // 2, half * half, 2 * cols), BF16),
            ((tall, cols), F32),
            ((tall, cols), F32),
        ],
        flops=4 * 10**9,
    )
    stream, gate = made[0], made[1]
    first = chip_permute(made[8], 3)
    far, later = lax.optimization_barrier((with_partner(made[2:4], made[4]), list(made[5:8])))
    far = split_exchange(far, FAR_SPLIT)
    came = [first] + exchange(later, NEAR_STEPS[1:])
    came = [came[0], far[0], came[1], came[2], came[3], far[1]]
    rights = [block if at in (1, 5) else block[near:] for at, block in enumerate(came)]
    rights = jnp.concatenate(rights, axis=0)
    mixed = run(
        mix_rows_kernel,
        [((near, cols), BF16)] * NEAR,
        where, *came, core_permute(rights),
        smem=(0,),
        scratch=[
            ((NEAR, width // NEAR, rows, cols), F32),
            ((16, width // NEAR, rows, cols), F32),
            ((tall, cols), F32),
        ],
    )
    mixed = exchange(mixed, NEAR_STEPS)
    made = run(
        between_kernel,
        [((rows, width, cols), F32)] * 2 + [((2 * all_, cols), BF16)] * OPS + [((2 * OPS * all_, cols), BF16)],
        where, resolved_residue_mask, *mixed, stream, gate, out_t, proj_t, present,
        smem=(0, 1),
        scratch=[
            ((rows, NEAR, width // NEAR, cols), F32),
            ((tall, cols), F32),
            ((tall, cols), F32),
        ],
    )
    stream, gate, theirs = made[0], made[1], made[6]
    came = split_exchange(with_partner(made[2:6], theirs))
    mine, theirs = run(
        mix_cols_kernel,
        [((OPS, 2 * all_, cols), F32), ((OPS, 2 * all_, cols), BF16)],
        where, *came,
        smem=(0,),
        scratch=[
            ((2 * OPS, width // (2 * OPS), rows, cols), F32),
            ((2 * OPS, width // (2 * OPS), rows, cols), F32),
            ((2 * tall, cols), F32),
        ],
    )
    mixed = run(sum_kernel, [((2 * all_, cols), BF16)] * OPS, mine, core_permute(theirs))
    mixed = split_exchange(mixed, SMALL_SPLIT)
    other = core_permute(run(pick_kernel, [((OPS * all_, cols), BF16)], *mixed)[0])
    return run(
        final_kernel,
        [((rows, cols, width), BF16)],
        where, *mixed, other, stream, gate, out_t,
        smem=(0,),
        scratch=[((rows, 2 * OPS, width // (2 * OPS), cols), F32)],
    )[0]


def fits_chips(mesh):
    return mesh.shape["narrow"] == 1 and mesh.shape["wide"] == 16


def solution(mesh):
    per_device = per_device_chips if fits_chips(mesh) else per_device_general
    return jax.shard_map(
        per_device,
        mesh=mesh,
        in_specs=(
            P(("grp", "wide"), "narrow", None),
            P("grp", "wide", None),
            P("grp"),
            P("grp"),
            P("grp", "wide"),
            P(),
            P(),
            P(),
            P(),
            P(),
        ),
        out_specs=P(("grp", "wide"), "narrow", None),
        check_vma=False,
    )
```

```python
import functools

import jax
import jax.numpy as jnp
from jax import lax
from jax.experimental import pallas as pl
from jax.experimental.pallas import tpu as pltpu
from jax.sharding import PartitionSpec as P

RELMAX = 32
EPSILON = 1e-05
LANES = 128
F32 = jnp.float32
BF16 = jnp.bfloat16


def apply_layer_norm(values, axis_dim):
    center = values - jnp.mean(values, axis=axis_dim, keepdims=True)
    spread = jnp.mean(center * center, axis=axis_dim, keepdims=True)
    return center * lax.rsqrt(spread + EPSILON)


def gather_wide(block):
    n = lax.axis_size("wide")
    if n % 4 or n < 8:
        return lax.all_gather(block, "wide", axis=0)
    outer = n // 4
    me = lax.axis_index("wide")
    high, mid, low = me // 4, (me // 2) % 2, me % 2
    arrived = [block]
    for shift in range(1, outer):
        perm = [(w, ((w // 4 + shift) % outer) * 4 + w % 4) for w in range(n)]
        arrived.append(lax.ppermute(block, "wide", perm))
    held = jnp.zeros((outer,) + block.shape, block.dtype)
    for shift, piece in enumerate(arrived):
        held = lax.dynamic_update_index_in_dim(held, piece, (high - shift + outer) % outer, 0)
    other = lax.ppermute(held, "wide", [(w, w ^ 2) for w in range(n)])
    held = jnp.stack(
        [jnp.where(mid == 0, held, other), jnp.where(mid == 0, other, held)], axis=1
    )
    other = lax.ppermute(held, "wide", [(w, w ^ 1) for w in range(n)])
    held = jnp.stack(
        [jnp.where(low == 0, held, other), jnp.where(low == 0, other, held)], axis=2
    )
    return held.reshape((n,) + block.shape)


def triangle(stream, pair_live, proj_weight, out_weight, incoming):
    rows = stream.shape[0]
    cols = stream.shape[1]
    width = out_weight.shape[0]
    wide_count = lax.axis_size("wide")
    core_count = lax.axis_size("narrow")
    devices = wide_count * core_count
    per_dev = width // devices
    normed = apply_layer_norm(stream, 2).astype(jnp.bfloat16)
    blocks = [proj_weight[:, index * width : (index + 1) * width] for index in range(4)]

    def project(block):
        return jnp.einsum("ijd,dc->cij", normed, block, preferred_element_type=jnp.float32)

    left_side = (jax.nn.sigmoid(project(blocks[0])) * project(blocks[1]) * pair_live[None]).astype(
        jnp.bfloat16
    )
    right_side = (jax.nn.sigmoid(project(blocks[2])) * project(blocks[3]) * pair_live[None]).astype(
        jnp.bfloat16
    )
    gate = jax.nn.sigmoid(
        jnp.einsum(
            "ijd,dc->ijc", normed, proj_weight[:, 4 * width :], preferred_element_type=jnp.float32
        )
    )
    form = "cki,ckj->cij" if incoming else "cik,cjk->cij"
    both = jnp.stack(
        [
            left_side.reshape(devices, per_dev, rows * cols),
            right_side.reshape(devices, per_dev, rows * cols),
        ],
        axis=1,
    ).reshape(devices, 2 * per_dev, rows * cols)
    both = lax.all_to_all(both, ("wide", "narrow"), split_axis=0, concat_axis=0, tiled=True)
    both = both.reshape(wide_count, core_count, 2, per_dev, rows, cols)
    both = jnp.transpose(both, (2, 3, 0, 4, 1, 5)).reshape(
        2, per_dev, wide_count * rows, core_count * cols
    )
    mixed = jnp.einsum(form, both[0], both[1], preferred_element_type=jnp.float32).astype(
        jnp.bfloat16
    )
    spread_out = mixed.reshape(per_dev, wide_count, rows, core_count, cols)
    spread_out = jnp.transpose(spread_out, (1, 3, 0, 2, 4)).reshape(
        wide_count * core_count * per_dev, rows * cols
    )
    returned = lax.all_to_all(
        spread_out, ("wide", "narrow"), split_axis=0, concat_axis=0, tiled=True
    ).reshape(width, rows, cols)
    blended_standardize = apply_layer_norm(returned.astype(jnp.float32), 0).astype(jnp.bfloat16)
    update = jnp.einsum(
        "cij,cd->ijd", blended_standardize, out_weight, preferred_element_type=jnp.float32
    )
    return stream + gate * update


def per_device_general(
    pairwise_state,
    homolog_features,
    residue_chain_index,
    resolved_residue_mask,
    alignment_mask,
    relative_offset_table,
    homolog_to_sides_matrix,
    outer_mean_output_weight,
    triangle_projection_weight,
    triangle_output_weight,
):
    rows = pairwise_state.shape[0]
    cols = pairwise_state.shape[1]
    row_start = lax.axis_index("wide") * rows
    col_start = lax.axis_index("narrow") * cols
    residue_present = resolved_residue_mask.astype(jnp.float32)
    row_present = lax.dynamic_slice_in_dim(residue_present, row_start, rows)
    col_live = lax.dynamic_slice_in_dim(residue_present, col_start, cols)
    present_flags = alignment_mask.astype(jnp.float32) * row_present[None, :]
    alignment_normed = apply_layer_norm(homolog_features.astype(jnp.float32), 2).astype(
        jnp.bfloat16
    )
    projected_rows = jnp.einsum(
        "tna,ak->tnk", alignment_normed, homolog_to_sides_matrix, preferred_element_type=jnp.float32
    )
    projected_rows = (projected_rows * present_flags[:, :, None]).astype(jnp.bfloat16)
    half_width = projected_rows.shape[2] // 2
    homologs = projected_rows.shape[0]
    left_proj = projected_rows[:, :, :half_width]
    right_proj = projected_rows[:, :, half_width:]
    live_flags = present_flags.astype(jnp.bfloat16)
    packed = jnp.concatenate(
        [jnp.transpose(right_proj, (1, 0, 2)).reshape(rows, homologs * half_width), live_flags.T],
        axis=1,
    )
    gathered = gather_wide(packed).reshape(-1, packed.shape[1])
    gathered = lax.dynamic_slice_in_dim(gathered, col_start, cols, 0)
    right_mine = jnp.transpose(
        gathered[:, : homologs * half_width].reshape(cols, homologs, half_width), (1, 0, 2)
    )
    live_mine = gathered[:, homologs * half_width :].T
    counts = jnp.dot(live_flags.T, live_mine, preferred_element_type=jnp.float32)

    def opm_row(left_row):
        outer = jnp.einsum("sc,sjd->jcd", left_row, right_mine, preferred_element_type=jnp.float32)
        outer = outer.reshape(cols, half_width * half_width).astype(jnp.bfloat16)
        return jnp.dot(outer, outer_mean_output_weight, preferred_element_type=jnp.float32)

    opm = lax.map(opm_row, jnp.transpose(left_proj, (1, 0, 2)))
    row_pos = row_start + jnp.arange(rows, dtype=jnp.int32)
    col_pos = col_start + jnp.arange(cols, dtype=jnp.int32)
    row_chain = lax.dynamic_slice_in_dim(residue_chain_index, row_start, rows)
    col_chain = lax.dynamic_slice_in_dim(residue_chain_index, col_start, cols)
    offset = jnp.clip(row_pos[:, None] - col_pos[None, :], -RELMAX, RELMAX) + RELMAX
    bin_index = jnp.where(row_chain[:, None] == col_chain[None, :], offset, 2 * RELMAX + 1)
    bin_count = relative_offset_table.shape[0]
    one_hot = (
        bin_index[:, :, None] == jnp.arange(bin_count, dtype=jnp.int32)[None, None, :]
    ).astype(jnp.bfloat16)
    relpos = jnp.einsum(
        "ijb,bc->ijc", one_hot, relative_offset_table, preferred_element_type=jnp.float32
    )
    stream = (
        pairwise_state.astype(jnp.float32) + relpos + opm / jnp.maximum(counts, 1.0)[:, :, None]
    )
    pair_live = row_present[:, None] * col_live[None, :]
    for turn_index in range(2):
        stream = triangle(
            stream,
            pair_live,
            triangle_projection_weight[turn_index],
            triangle_output_weight[turn_index],
            turn_index == 1,
        )
    return stream.astype(jnp.bfloat16)


def nn(a, b):
    return lax.dot_general(a, b, (((1,), (0,)), ((), ())), preferred_element_type=F32)


def nt(a, b):
    return lax.dot_general(a, b, (((1,), (1,)), ((), ())), preferred_element_type=F32)


def tn(a, b):
    return lax.dot_general(a, b, (((0,), (0,)), ((), ())), preferred_element_type=F32)


def identity(size):
    rows = lax.broadcasted_iota(jnp.int32, (size, size), 0)
    cols = lax.broadcasted_iota(jnp.int32, (size, size), 1)
    return (rows == cols).astype(F32).astype(BF16)


def flip(block):
    return nt(identity(block.shape[1]), block)


def norm_rows(values):
    scale = 1.0 / values.shape[0]
    center = values - jnp.sum(values, axis=0, keepdims=True) * scale
    spread = jnp.sum(center * center, axis=0, keepdims=True) * scale
    return (center * lax.rsqrt(spread + EPSILON)).astype(BF16)


def run(kernel, outs, *args, smem=(), scratch=(), flops=15 * 10**8):
    vmem = pl.BlockSpec(memory_space=pltpu.VMEM)
    in_specs = [
        pl.BlockSpec(memory_space=pltpu.SMEM if at in smem else pltpu.VMEM) for at in range(len(args))
    ]
    moved = sum(a.size * a.dtype.itemsize for a in args)
    return pl.pallas_call(
        kernel,
        out_shape=[jax.ShapeDtypeStruct(shape, kind) for shape, kind in outs],
        in_specs=in_specs,
        out_specs=[vmem] * len(outs),
        scratch_shapes=[pltpu.VMEM(shape, kind) for shape, kind in scratch],
        compiler_params=pltpu.CompilerParams(vmem_limit_bytes=VMEM_LIMIT),
        cost_estimate=pl.CostEstimate(flops=flops, bytes_accessed=moved, transcendentals=0),
    )(*args)


VMEM_LIMIT = 20 * 1024 * 1024
SPLIT = ((7, 5), (6, 4), (3, 2), (1, 0))
FAR_SPLIT = SPLIT[:2]
SMALL_SPLIT = ((7, 3), (2, 6), (5, 1), (0, 4))
OPS = len(SPLIT)
NEAR = 4
NEAR_STEPS = (3, 2, 1, 0)


def partner_chip(chip, core, op, split=SPLIT):
    return chip ^ jnp.where(core == 0, split[op][0], split[op][1])


def project_kernel(feat_ref, weight_ref, live_in_ref, pay_ref, left_ref, live_ref, turned, packed):
    homologs, rows, _ = feat_ref.shape
    half = weight_ref.shape[0] // 2
    quarter = half // 2
    values = feat_ref[...].reshape(homologs * rows, feat_ref.shape[2])
    center = values - jnp.mean(values, axis=1, keepdims=True)
    spread = jnp.mean(center * center, axis=1, keepdims=True)
    normed = (center * lax.rsqrt(spread + EPSILON)).astype(BF16)
    total = homologs * rows
    out_row = lax.broadcasted_iota(jnp.int32, (total, total), 0)
    in_row = lax.broadcasted_iota(jnp.int32, (total, total), 1)
    order = in_row == (out_row & (homologs - 1)) * rows + out_row // homologs
    normed = nn(order.astype(F32).astype(BF16), normed).astype(BF16)
    live = live_in_ref[...]
    weight = weight_ref[...]
    blank = jnp.zeros((homologs, normed.shape[1]), BF16)
    for row in range(rows):
        mine = normed[row * homologs : (row + 1) * homologs]
        low = nt(weight, jnp.concatenate([mine, blank], axis=0)) * live[row : row + 1]
        high = nt(weight, jnp.concatenate([blank, mine], axis=0)) * live[row : row + 1]
        left_ref[row * half : (row + 1) * half] = low[:half].astype(BF16)
        left_ref[(rows + row) * half : (rows + row + 1) * half] = high[:half].astype(BF16)
        turned[row * quarter : (row + 1) * quarter] = low[half : half + quarter] + high[half + quarter :]
    for pair in range(quarter):
        packed[pair * rows : (pair + 1) * rows] = turned[pl.ds(pair, rows, stride=quarter), :]
    packed[quarter * rows : (quarter + 1) * rows] = live
    packed[(quarter + 1) * rows :] = jnp.zeros((rows, 2 * homologs), F32)
    pay_ref[...] = packed[...].astype(BF16)
    live_ref[...] = jnp.where(lax.broadcasted_iota(jnp.int32, live.shape, 1) < homologs, live, 0.0)


def prep_kernel(
    where_ref, chain_ref, chains_ref, pair_ref, table_ref, outer_ref, proj_ref, out_ref,
    base_ref, outer_t_ref, proj_t_ref, out_t_ref, table_pad, outer_pad,
):
    rows, cols, width = pair_ref.shape
    bins = table_ref.shape[0]
    table_pad[...] = jnp.zeros_like(table_pad)
    table_pad[0:bins, :] = table_ref[...].astype(F32)
    table = flip(table_pad[...].astype(BF16)).astype(BF16)
    chains = chains_ref[...]
    col = lax.broadcasted_iota(jnp.int32, (1, cols), 1)
    slot = lax.broadcasted_iota(jnp.int32, (table_pad.shape[0], cols), 0)
    for row in range(rows):
        place = where_ref[0] + row
        offset = jnp.clip(place - col, -RELMAX, RELMAX) + RELMAX
        bin_index = jnp.where(chains == chain_ref[place], offset, 2 * RELMAX + 1)
        hot = (slot == bin_index).astype(F32).astype(BF16)
        base_ref[row] = flip(pair_ref[row]) + nn(table, hot)
    half = round(outer_pad.shape[0] ** 0.5)
    outer_pad[...] = outer_ref[...].astype(F32)
    for d in range(half):
        outer_t_ref[:, d * half : (d + 1) * half] = flip(outer_pad[pl.ds(d, half, stride=half), :].astype(BF16)).astype(BF16)
    for turn in range(2):
        proj_t_ref[turn] = tn(proj_ref[turn], identity(width)).astype(BF16)
        out_t_ref[turn] = flip(out_ref[turn]).astype(BF16)


def sigmoid(values):
    return 0.5 * jnp.tanh(0.5 * values) + 0.5


def sides(streams, weight, lives, gate_ref, lefts, rights, row):
    width, cols = streams[0].shape
    rows = lefts.shape[0] // width
    made = nn(weight, jnp.concatenate([norm_rows(stream) for stream in streams], axis=1))
    for at, live in enumerate(lives):
        part = [
            made[block * width : (block + 1) * width, at * cols : (at + 1) * cols] for block in range(5)
        ]
        lefts[pl.ds(row + at, width, stride=rows), :] = sigmoid(part[0]) * part[1] * live
        rights[pl.ds(row + at, width, stride=rows), :] = sigmoid(part[2]) * part[3] * live
        gate_ref[row + at] = sigmoid(part[4])


def flat(block):
    return block.reshape(block.shape[0] * block.shape[1], block.shape[2])


def outer_kernel(
    where_ref, flag_ref, own_ref, other_ref, left_ref, live_ref, base_ref, outer_t_ref, proj_ref, present_ref,
    stream_ref, gate_ref, far0, far1, theirs_ref, near0, near1, near2, near3, came, outer, lefts, rights,
):
    rows, width, cols = base_ref.shape
    chip, core = where_ref[1], where_ref[2]
    per = own_ref.shape[1]
    chips = own_ref.shape[0]
    for at in range(chips):
        chip_at = chip ^ (at % 2 * 4 + at // 2 % 2 * 2 + at // 4)
        came[chip_at * 2 + core] = own_ref[at].astype(F32)
        came[chip_at * 2 + (1 - core)] = other_ref[at].astype(F32)
    half = left_ref.shape[0] // (2 * rows)
    quarter = half // 2
    live_all = came[:, quarter * rows : (quarter + 1) * rows, :].reshape(cols, per_lane(came)).astype(BF16)
    counts = nt(live_ref[...].astype(BF16), live_all)
    share = 1.0 / jnp.maximum(counts, 1.0)
    left_all = left_ref[...]
    for pair in range(quarter):
        right = came[:, pair * rows : (pair + 1) * rows, :].reshape(cols, per_lane(came)).astype(BF16)
        made = nt(left_all, right).astype(BF16)
        for part in range(2):
            d = part * quarter + pair
            for row in range(rows):
                first = (part * rows + row) * half
                lane = (row % 2) * cols
                outer[row // 2, d * half : (d + 1) * half, lane : lane + cols] = made[first : first + half]
    present = present_ref[...].astype(F32)
    for row in range(0, rows, 2):
        product = nn(outer_t_ref[...], outer[row // 2])
        streams, lives = [], []
        for at in range(2):
            streams.append(
                base_ref[row + at] + product[:, at * cols : (at + 1) * cols] * share[row + at : row + at + 1]
            )
            stream_ref[row + at] = streams[at]
            lives.append(present * flag_ref[where_ref[0] + row + at].astype(F32))
        sides(streams, proj_ref[0], lives, gate_ref, lefts, rights, row)
    size = width // NEAR
    block = size * rows

    def group(side, to):
        first = pl.multiple_of((to & (NEAR - 1)) * block, block)
        return side[pl.ds(first, block), :].astype(BF16)

    for op, far in enumerate((far0, far1)):
        far[...] = group(rights, partner_chip(chip, core, op, FAR_SPLIT))
        theirs_ref[op * block : (op + 1) * block] = group(rights, partner_chip(chip, 1 - core, op, FAR_SPLIT))
    for step, near in enumerate((near0, near1, near2, near3)):
        near[0:block] = group(lefts, chip ^ step)
        near[block:] = group(rights, chip ^ step)


def per_lane(ref):
    return ref.shape[-1]


def mix_rows_kernel(
    where_ref, near3, far0, far1, near2, near1, near0, other_ref, out0, out1, out2, out3, lefts, rights, mixed
):
    chip, core = where_ref[1], where_ref[2]
    count, rows, cols = lefts.shape[1:]
    block = count * rows
    place = 0
    for step, near in ((3, near3), (None, far0), (None, far1), (2, near2), (1, near1), (0, near0)):
        if step is None:
            op = 0 if near is far0 else 1
            for half in range(2):
                at = partner_chip(chip, core, op, FAR_SPLIT) * 2 + (core ^ half)
                rights[at] = near[half * block : (half + 1) * block].astype(F32).reshape(count, rows, cols)
                at = partner_chip(chip, 1 - core, op, FAR_SPLIT) * 2 + ((1 - core) ^ half)
                rights[at] = other_ref[place : place + block].astype(F32).reshape(count, rows, cols)
                place += block
        else:
            lefts[step] = near[0:block].astype(F32).reshape(count, rows, cols)
            rights[(chip ^ step) * 2 + core] = near[block:].astype(F32).reshape(count, rows, cols)
            theirs = other_ref[place : place + block]
            rights[(chip ^ step) * 2 + (1 - core)] = theirs.astype(F32).reshape(count, rows, cols)
            place += block
    for c in range(count):
        left = flat(lefts[:, c]).astype(BF16)
        right = flat(rights[:, c]).astype(BF16)
        mixed[pl.ds(c, NEAR * rows, stride=count), :] = nt(left, right)
    for step, out in enumerate((out0, out1, out2, out3)):
        out[...] = mixed[step * block : (step + 1) * block].astype(BF16)


def pick_kernel(*refs):
    blocks, out_ref = refs[:-1], refs[-1]
    for at, block in enumerate(blocks):
        half = block.shape[0] // 2
        out_ref[at * half : (at + 1) * half] = block[half:]


def update(came, row, stream_ref, gate_ref, out_weight):
    normed = jnp.concatenate([norm_rows(flat(came[row + at])) for at in range(2)], axis=1)
    made = nn(out_weight, normed)
    cols = made.shape[1] // 2
    return [
        stream_ref[row + at] + gate_ref[row + at] * made[:, at * cols : (at + 1) * cols] for at in range(2)
    ]


def between_kernel(
    where_ref, flag_ref, in0, in1, in2, in3, stream_ref, gate_ref, out_weight_ref, proj_ref, present_ref,
    next_ref, next_gate_ref, mine0, mine1, mine2, mine3, theirs_ref, came, lefts, rights,
):
    rows, width, cols = stream_ref.shape
    chip, core = where_ref[1], where_ref[2]
    size = width // NEAR
    for step, block in zip(NEAR_STEPS, (in0, in1, in2, in3)):
        came[:, (chip ^ step) & (NEAR - 1)] = block[...].astype(F32).reshape(rows, size, cols)
    present = present_ref[...].astype(F32)
    for row in range(0, rows, 2):
        streams = update(came, row, stream_ref, gate_ref, out_weight_ref[0])
        lives = []
        for at in range(2):
            next_ref[row + at] = streams[at]
            lives.append(present * flag_ref[where_ref[0] + row + at].astype(F32))
        sides(streams, proj_ref[1], lives, next_gate_ref, lefts, rights, row)
    block = width // (2 * OPS) * rows
    for op, mine in enumerate((mine0, mine1, mine2, mine3)):
        for at, side in enumerate((lefts, rights)):
            first = pl.multiple_of(partner_chip(chip, core, op) * block, block)
            mine[at * block : (at + 1) * block] = side[pl.ds(first, block), :].astype(BF16)
            first = pl.multiple_of(partner_chip(chip, 1 - core, op) * block, block)
            place = (op * 2 + at) * block
            theirs_ref[place : place + block] = side[pl.ds(first, block), :].astype(BF16)


def mix_cols_kernel(where_ref, came0, came1, came2, came3, mine_ref, theirs_ref, lefts, rights, partial):
    chip, core = where_ref[1], where_ref[2]
    count, rows, cols = lefts.shape[1:]
    block = count * rows
    for op, came in enumerate((came0, came1, came2, came3)):
        for half in range(2):
            for at, side in enumerate((lefts, rights)):
                place = (half * 2 + at) * block
                side[op * 2 + half] = came[place : place + block].astype(F32).reshape(count, rows, cols)
    for c in range(count):
        left = flat(lefts[:, c]).astype(BF16)
        right = flat(rights[:, c]).astype(BF16)
        partial[pl.ds(c, partial.shape[0] // count, stride=count), :] = tn(left, right)
    for op in range(OPS):
        for half in range(2):
            to = pl.multiple_of((partner_chip(chip, core, op, SMALL_SPLIT) * 2 + (core ^ half)) * block, block)
            mine_ref[op, half * block : (half + 1) * block] = partial[pl.ds(to, block), :]
            to = partner_chip(chip, 1 - core, op, SMALL_SPLIT) * 2 + ((1 - core) ^ half)
            to = pl.multiple_of(to * block, block)
            theirs_ref[op, half * block : (half + 1) * block] = partial[pl.ds(to, block), :].astype(BF16)


def sum_kernel(mine_ref, got_ref, *outs):
    for op, out in enumerate(outs):
        out[...] = (mine_ref[op] + got_ref[op].astype(F32)).astype(BF16)


def final_kernel(
    where_ref, came0, came1, came2, came3, other_ref, stream_ref, gate_ref, out_weight_ref, out_ref, came
):
    rows, width, cols = stream_ref.shape
    chip, core = where_ref[1], where_ref[2]
    size = width // (2 * OPS)
    block = size * rows
    for op, mine in enumerate((came0, came1, came2, came3)):
        came[:, partner_chip(chip, core, op, SMALL_SPLIT)] = mine[0:block].astype(F32).reshape(rows, size, cols)
        theirs = other_ref[op * block : (op + 1) * block]
        came[:, partner_chip(chip, 1 - core, op, SMALL_SPLIT)] = theirs.astype(F32).reshape(rows, size, cols)
    for row in range(0, rows, 2):
        for at, stream in enumerate(update(came, row, stream_ref, gate_ref, out_weight_ref[1])):
            out_ref[row + at] = flip_out(stream)


def flip_out(stream):
    return nt(identity(stream.shape[1]), stream.astype(BF16)).astype(BF16)


def chip_permute(block, step):
    count = lax.axis_size("wide")
    return lax.ppermute(block, "wide", [(w, w ^ (2 * step)) for w in range(count)])


def exchange(blocks, steps):
    return [chip_permute(blocks[step], step) if step else blocks[0] for step in steps]


def split_permute(block, steps):
    count = lax.axis_size("wide")
    return lax.ppermute(block, "wide", [(w, w ^ (2 * steps[w % 2])) for w in range(count)])


def split_exchange(blocks, split=SPLIT):
    return [split_permute(block, steps) for block, steps in zip(blocks, split)]


def with_partner(mine, theirs):
    got, messages, place = core_permute(theirs), [], 0
    for block in mine:
        messages.append(jnp.concatenate([block, got[place : place + block.shape[0]]], axis=0))
        place += block.shape[0]
    return messages


def core_permute(block):
    count = lax.axis_size("wide")
    return lax.ppermute(block, "wide", [(w, w ^ 1) for w in range(count)])


def per_device_chips(
    pairwise_state,
    homolog_features,
    residue_chain_index,
    resolved_residue_mask,
    alignment_mask,
    relative_offset_table,
    homolog_to_sides_matrix,
    outer_mean_output_weight,
    triangle_projection_weight,
    triangle_output_weight,
):
    rows, cols, width = pairwise_state.shape
    homologs = homolog_features.shape[0]
    half = homolog_to_sides_matrix.shape[1] // 2
    device = lax.axis_index("wide")
    chip, core = device // 2, device % 2
    where = jnp.stack([device * rows, chip, core]).astype(jnp.int32)
    present = resolved_residue_mask.reshape(1, cols)
    pay_rows = (half // 2 + 2) * rows
    row_present = lax.dynamic_slice_in_dim(resolved_residue_mask, device * rows, rows).astype(F32)
    live = alignment_mask.T.astype(F32) * row_present[:, None]
    live = jnp.concatenate([live, live], axis=1)
    pay, left, live = run(
        project_kernel,
        [((pay_rows, LANES), BF16), ((2 * rows * half, LANES), BF16), ((rows, LANES), F32)],
        homolog_features.astype(F32), homolog_to_sides_matrix.T, live,
        scratch=[((rows * half // 2, LANES), F32), ((pay_rows, LANES), F32)],
    )
    far_z = chip_permute(pay, 4)
    base, outer_t, proj_t, out_t = run(
        prep_kernel,
        [
            ((rows, width, cols), F32),
            ((width, half * half), BF16),
            ((2, triangle_projection_weight.shape[2], width), BF16),
            ((2, width, width), BF16),
        ],
        where, residue_chain_index, residue_chain_index.reshape(1, cols), pairwise_state,
        relative_offset_table, outer_mean_output_weight, triangle_projection_weight, triangle_output_weight,
        smem=(0, 1),
        scratch=[((LANES, width), F32), ((half * half, width), F32)],
    )
    along_z = jnp.stack([pay, far_z])
    along_z = jnp.concatenate([along_z, chip_permute(along_z, 2)], axis=0)
    own = jnp.concatenate([along_z, chip_permute(along_z, 1)], axis=0)
    own, base, outer_t, proj_t, out_t = lax.optimization_barrier((own, base, outer_t, proj_t, out_t))
    other = core_permute(own)
    tall = width * rows
    near, all_ = tall // NEAR, tall // (2 * OPS)
    made = run(
        outer_kernel,
        [((rows, width, cols), F32)] * 2
        + [((near, cols), BF16)] * 2
        + [((2 * near, cols), BF16)] * (1 + NEAR),
        where, resolved_residue_mask, own, other, left, live, base, outer_t, proj_t, present,
        smem=(0, 1),
        scratch=[
            ((16, pay_rows, LANES), F32),
            ((rows // 2, half * half, 2 * cols), BF16),
            ((tall, cols), F32),
            ((tall, cols), F32),
        ],
        flops=4 * 10**9,
    )
    stream, gate = made[0], made[1]
    first = chip_permute(made[8], 3)
    far, later = lax.optimization_barrier((with_partner(made[2:4], made[4]), list(made[5:8])))
    far = split_exchange(far, FAR_SPLIT)
    came = [first] + exchange(later, NEAR_STEPS[1:])
    came = [came[0], far[0], far[1], came[1], came[2], came[3]]
    rights = [block if at in (1, 2) else block[near:] for at, block in enumerate(came)]
    rights = jnp.concatenate(rights, axis=0)
    mixed = run(
        mix_rows_kernel,
        [((near, cols), BF16)] * NEAR,
        where, *came, core_permute(rights),
        smem=(0,),
        scratch=[
            ((NEAR, width // NEAR, rows, cols), F32),
            ((16, width // NEAR, rows, cols), F32),
            ((tall, cols), F32),
        ],
    )
    mixed = exchange(mixed, NEAR_STEPS)
    made = run(
        between_kernel,
        [((rows, width, cols), F32)] * 2 + [((2 * all_, cols), BF16)] * OPS + [((2 * OPS * all_, cols), BF16)],
        where, resolved_residue_mask, *mixed, stream, gate, out_t, proj_t, present,
        smem=(0, 1),
        scratch=[
            ((rows, NEAR, width // NEAR, cols), F32),
            ((tall, cols), F32),
            ((tall, cols), F32),
        ],
    )
    stream, gate, theirs = made[0], made[1], made[6]
    came = split_exchange(with_partner(made[2:6], theirs))
    mine, theirs = run(
        mix_cols_kernel,
        [((OPS, 2 * all_, cols), F32), ((OPS, 2 * all_, cols), BF16)],
        where, *came,
        smem=(0,),
        scratch=[
            ((2 * OPS, width // (2 * OPS), rows, cols), F32),
            ((2 * OPS, width // (2 * OPS), rows, cols), F32),
            ((2 * tall, cols), F32),
        ],
    )
    mixed = run(sum_kernel, [((2 * all_, cols), BF16)] * OPS, mine, core_permute(theirs))
    mixed = split_exchange(mixed, SMALL_SPLIT)
    other = core_permute(run(pick_kernel, [((OPS * all_, cols), BF16)], *mixed)[0])
    return run(
        final_kernel,
        [((rows, cols, width), BF16)],
        where, *mixed, other, stream, gate, out_t,
        smem=(0,),
        scratch=[((rows, 2 * OPS, width // (2 * OPS), cols), F32)],
    )[0]


def fits_chips(mesh):
    return mesh.shape["narrow"] == 1 and mesh.shape["wide"] == 16


def solution(mesh):
    per_device = per_device_chips if fits_chips(mesh) else per_device_general
    return jax.shard_map(
        per_device,
        mesh=mesh,
        in_specs=(
            P(("grp", "wide"), "narrow", None),
            P("grp", "wide", None),
            P("grp"),
            P("grp"),
            P("grp", "wide"),
            P(),
            P(),
            P(),
            P(),
            P(),
        ),
        out_specs=P(("grp", "wide"), "narrow", None),
        check_vma=False,
    )
```

```python
import functools

import jax
import jax.numpy as jnp
from jax import lax
from jax.experimental import pallas as pl
from jax.experimental.pallas import tpu as pltpu
from jax.sharding import PartitionSpec as P

RELMAX = 32
EPSILON = 1e-05
LANES = 128
F32 = jnp.float32
BF16 = jnp.bfloat16


def apply_layer_norm(values, axis_dim):
    center = values - jnp.mean(values, axis=axis_dim, keepdims=True)
    spread = jnp.mean(center * center, axis=axis_dim, keepdims=True)
    return center * lax.rsqrt(spread + EPSILON)


def gather_wide(block):
    n = lax.axis_size("wide")
    if n % 4 or n < 8:
        return lax.all_gather(block, "wide", axis=0)
    outer = n // 4
    me = lax.axis_index("wide")
    high, mid, low = me // 4, (me // 2) % 2, me % 2
    arrived = [block]
    for shift in range(1, outer):
        perm = [(w, ((w // 4 + shift) % outer) * 4 + w % 4) for w in range(n)]
        arrived.append(lax.ppermute(block, "wide", perm))
    held = jnp.zeros((outer,) + block.shape, block.dtype)
    for shift, piece in enumerate(arrived):
        held = lax.dynamic_update_index_in_dim(held, piece, (high - shift + outer) % outer, 0)
    other = lax.ppermute(held, "wide", [(w, w ^ 2) for w in range(n)])
    held = jnp.stack(
        [jnp.where(mid == 0, held, other), jnp.where(mid == 0, other, held)], axis=1
    )
    other = lax.ppermute(held, "wide", [(w, w ^ 1) for w in range(n)])
    held = jnp.stack(
        [jnp.where(low == 0, held, other), jnp.where(low == 0, other, held)], axis=2
    )
    return held.reshape((n,) + block.shape)


def triangle(stream, pair_live, proj_weight, out_weight, incoming):
    rows = stream.shape[0]
    cols = stream.shape[1]
    width = out_weight.shape[0]
    wide_count = lax.axis_size("wide")
    core_count = lax.axis_size("narrow")
    devices = wide_count * core_count
    per_dev = width // devices
    normed = apply_layer_norm(stream, 2).astype(jnp.bfloat16)
    blocks = [proj_weight[:, index * width : (index + 1) * width] for index in range(4)]

    def project(block):
        return jnp.einsum("ijd,dc->cij", normed, block, preferred_element_type=jnp.float32)

    left_side = (jax.nn.sigmoid(project(blocks[0])) * project(blocks[1]) * pair_live[None]).astype(
        jnp.bfloat16
    )
    right_side = (jax.nn.sigmoid(project(blocks[2])) * project(blocks[3]) * pair_live[None]).astype(
        jnp.bfloat16
    )
    gate = jax.nn.sigmoid(
        jnp.einsum(
            "ijd,dc->ijc", normed, proj_weight[:, 4 * width :], preferred_element_type=jnp.float32
        )
    )
    form = "cki,ckj->cij" if incoming else "cik,cjk->cij"
    both = jnp.stack(
        [
            left_side.reshape(devices, per_dev, rows * cols),
            right_side.reshape(devices, per_dev, rows * cols),
        ],
        axis=1,
    ).reshape(devices, 2 * per_dev, rows * cols)
    both = lax.all_to_all(both, ("wide", "narrow"), split_axis=0, concat_axis=0, tiled=True)
    both = both.reshape(wide_count, core_count, 2, per_dev, rows, cols)
    both = jnp.transpose(both, (2, 3, 0, 4, 1, 5)).reshape(
        2, per_dev, wide_count * rows, core_count * cols
    )
    mixed = jnp.einsum(form, both[0], both[1], preferred_element_type=jnp.float32).astype(
        jnp.bfloat16
    )
    spread_out = mixed.reshape(per_dev, wide_count, rows, core_count, cols)
    spread_out = jnp.transpose(spread_out, (1, 3, 0, 2, 4)).reshape(
        wide_count * core_count * per_dev, rows * cols
    )
    returned = lax.all_to_all(
        spread_out, ("wide", "narrow"), split_axis=0, concat_axis=0, tiled=True
    ).reshape(width, rows, cols)
    blended_standardize = apply_layer_norm(returned.astype(jnp.float32), 0).astype(jnp.bfloat16)
    update = jnp.einsum(
        "cij,cd->ijd", blended_standardize, out_weight, preferred_element_type=jnp.float32
    )
    return stream + gate * update


def per_device_general(
    pairwise_state,
    homolog_features,
    residue_chain_index,
    resolved_residue_mask,
    alignment_mask,
    relative_offset_table,
    homolog_to_sides_matrix,
    outer_mean_output_weight,
    triangle_projection_weight,
    triangle_output_weight,
):
    rows = pairwise_state.shape[0]
    cols = pairwise_state.shape[1]
    row_start = lax.axis_index("wide") * rows
    col_start = lax.axis_index("narrow") * cols
    residue_present = resolved_residue_mask.astype(jnp.float32)
    row_present = lax.dynamic_slice_in_dim(residue_present, row_start, rows)
    col_live = lax.dynamic_slice_in_dim(residue_present, col_start, cols)
    present_flags = alignment_mask.astype(jnp.float32) * row_present[None, :]
    alignment_normed = apply_layer_norm(homolog_features.astype(jnp.float32), 2).astype(
        jnp.bfloat16
    )
    projected_rows = jnp.einsum(
        "tna,ak->tnk", alignment_normed, homolog_to_sides_matrix, preferred_element_type=jnp.float32
    )
    projected_rows = (projected_rows * present_flags[:, :, None]).astype(jnp.bfloat16)
    half_width = projected_rows.shape[2] // 2
    homologs = projected_rows.shape[0]
    left_proj = projected_rows[:, :, :half_width]
    right_proj = projected_rows[:, :, half_width:]
    live_flags = present_flags.astype(jnp.bfloat16)
    packed = jnp.concatenate(
        [jnp.transpose(right_proj, (1, 0, 2)).reshape(rows, homologs * half_width), live_flags.T],
        axis=1,
    )
    gathered = gather_wide(packed).reshape(-1, packed.shape[1])
    gathered = lax.dynamic_slice_in_dim(gathered, col_start, cols, 0)
    right_mine = jnp.transpose(
        gathered[:, : homologs * half_width].reshape(cols, homologs, half_width), (1, 0, 2)
    )
    live_mine = gathered[:, homologs * half_width :].T
    counts = jnp.dot(live_flags.T, live_mine, preferred_element_type=jnp.float32)

    def opm_row(left_row):
        outer = jnp.einsum("sc,sjd->jcd", left_row, right_mine, preferred_element_type=jnp.float32)
        outer = outer.reshape(cols, half_width * half_width).astype(jnp.bfloat16)
        return jnp.dot(outer, outer_mean_output_weight, preferred_element_type=jnp.float32)

    opm = lax.map(opm_row, jnp.transpose(left_proj, (1, 0, 2)))
    row_pos = row_start + jnp.arange(rows, dtype=jnp.int32)
    col_pos = col_start + jnp.arange(cols, dtype=jnp.int32)
    row_chain = lax.dynamic_slice_in_dim(residue_chain_index, row_start, rows)
    col_chain = lax.dynamic_slice_in_dim(residue_chain_index, col_start, cols)
    offset = jnp.clip(row_pos[:, None] - col_pos[None, :], -RELMAX, RELMAX) + RELMAX
    bin_index = jnp.where(row_chain[:, None] == col_chain[None, :], offset, 2 * RELMAX + 1)
    bin_count = relative_offset_table.shape[0]
    one_hot = (
        bin_index[:, :, None] == jnp.arange(bin_count, dtype=jnp.int32)[None, None, :]
    ).astype(jnp.bfloat16)
    relpos = jnp.einsum(
        "ijb,bc->ijc", one_hot, relative_offset_table, preferred_element_type=jnp.float32
    )
    stream = (
        pairwise_state.astype(jnp.float32) + relpos + opm / jnp.maximum(counts, 1.0)[:, :, None]
    )
    pair_live = row_present[:, None] * col_live[None, :]
    for turn_index in range(2):
        stream = triangle(
            stream,
            pair_live,
            triangle_projection_weight[turn_index],
            triangle_output_weight[turn_index],
            turn_index == 1,
        )
    return stream.astype(jnp.bfloat16)


def nn(a, b):
    return lax.dot_general(a, b, (((1,), (0,)), ((), ())), preferred_element_type=F32)


def nt(a, b):
    return lax.dot_general(a, b, (((1,), (1,)), ((), ())), preferred_element_type=F32)


def tn(a, b):
    return lax.dot_general(a, b, (((0,), (0,)), ((), ())), preferred_element_type=F32)


def identity(size):
    rows = lax.broadcasted_iota(jnp.int32, (size, size), 0)
    cols = lax.broadcasted_iota(jnp.int32, (size, size), 1)
    return (rows == cols).astype(F32).astype(BF16)


def flip(block):
    return nt(identity(block.shape[1]), block)


def norm_rows(values):
    scale = 1.0 / values.shape[0]
    center = values - jnp.sum(values, axis=0, keepdims=True) * scale
    spread = jnp.sum(center * center, axis=0, keepdims=True) * scale
    return (center * lax.rsqrt(spread + EPSILON)).astype(BF16)


def run(kernel, outs, *args, smem=(), scratch=(), flops=15 * 10**8):
    vmem = pl.BlockSpec(memory_space=pltpu.VMEM)
    in_specs = [
        pl.BlockSpec(memory_space=pltpu.SMEM if at in smem else pltpu.VMEM) for at in range(len(args))
    ]
    moved = sum(a.size * a.dtype.itemsize for a in args)
    return pl.pallas_call(
        kernel,
        out_shape=[jax.ShapeDtypeStruct(shape, kind) for shape, kind in outs],
        in_specs=in_specs,
        out_specs=[vmem] * len(outs),
        scratch_shapes=[pltpu.VMEM(shape, kind) for shape, kind in scratch],
        compiler_params=pltpu.CompilerParams(vmem_limit_bytes=VMEM_LIMIT),
        cost_estimate=pl.CostEstimate(flops=flops, bytes_accessed=moved, transcendentals=0),
    )(*args)


VMEM_LIMIT = 20 * 1024 * 1024
SPLIT = ((3, 2), (7, 5), (6, 4), (1, 0))
FAR_SPLIT = SPLIT[1:3]
SMALL_SPLIT = ((7, 3), (2, 6), (5, 1), (0, 4))
OPS = len(SPLIT)
NEAR = 4
NEAR_STEPS = (3, 2, 1, 0)


def partner_chip(chip, core, op, split=SPLIT):
    return chip ^ jnp.where(core == 0, split[op][0], split[op][1])


def project_kernel(feat_ref, weight_ref, live_in_ref, pay_ref, left_ref, live_ref, turned, packed):
    homologs, rows, _ = feat_ref.shape
    half = weight_ref.shape[0] // 2
    quarter = half // 2
    values = feat_ref[...].reshape(homologs * rows, feat_ref.shape[2])
    center = values - jnp.mean(values, axis=1, keepdims=True)
    spread = jnp.mean(center * center, axis=1, keepdims=True)
    normed = (center * lax.rsqrt(spread + EPSILON)).astype(BF16)
    total = homologs * rows
    out_row = lax.broadcasted_iota(jnp.int32, (total, total), 0)
    in_row = lax.broadcasted_iota(jnp.int32, (total, total), 1)
    order = in_row == (out_row & (homologs - 1)) * rows + out_row // homologs
    normed = nn(order.astype(F32).astype(BF16), normed).astype(BF16)
    live = live_in_ref[...]
    weight = weight_ref[...]
    blank = jnp.zeros((homologs, normed.shape[1]), BF16)
    for row in range(rows):
        mine = normed[row * homologs : (row + 1) * homologs]
        low = nt(weight, jnp.concatenate([mine, blank], axis=0)) * live[row : row + 1]
        high = nt(weight, jnp.concatenate([blank, mine], axis=0)) * live[row : row + 1]
        left_ref[row * half : (row + 1) * half] = low[:half].astype(BF16)
        left_ref[(rows + row) * half : (rows + row + 1) * half] = high[:half].astype(BF16)
        turned[row * quarter : (row + 1) * quarter] = low[half : half + quarter] + high[half + quarter :]
    for pair in range(quarter):
        packed[pair * rows : (pair + 1) * rows] = turned[pl.ds(pair, rows, stride=quarter), :]
    packed[quarter * rows : (quarter + 1) * rows] = live
    packed[(quarter + 1) * rows :] = jnp.zeros((rows, 2 * homologs), F32)
    pay_ref[...] = packed[...].astype(BF16)
    live_ref[...] = jnp.where(lax.broadcasted_iota(jnp.int32, live.shape, 1) < homologs, live, 0.0)


def prep_kernel(
    where_ref, chain_ref, chains_ref, pair_ref, table_ref, outer_ref, proj_ref, out_ref,
    base_ref, outer_t_ref, proj_t_ref, out_t_ref, table_pad, outer_pad,
):
    rows, cols, width = pair_ref.shape
    bins = table_ref.shape[0]
    table_pad[...] = jnp.zeros_like(table_pad)
    table_pad[0:bins, :] = table_ref[...].astype(F32)
    table = flip(table_pad[...].astype(BF16)).astype(BF16)
    chains = chains_ref[...]
    col = lax.broadcasted_iota(jnp.int32, (1, cols), 1)
    slot = lax.broadcasted_iota(jnp.int32, (table_pad.shape[0], cols), 0)
    for row in range(rows):
        place = where_ref[0] + row
        offset = jnp.clip(place - col, -RELMAX, RELMAX) + RELMAX
        bin_index = jnp.where(chains == chain_ref[place], offset, 2 * RELMAX + 1)
        hot = (slot == bin_index).astype(F32).astype(BF16)
        base_ref[row] = flip(pair_ref[row]) + nn(table, hot)
    half = round(outer_pad.shape[0] ** 0.5)
    outer_pad[...] = outer_ref[...].astype(F32)
    for d in range(half):
        outer_t_ref[:, d * half : (d + 1) * half] = flip(outer_pad[pl.ds(d, half, stride=half), :].astype(BF16)).astype(BF16)
    for turn in range(2):
        proj_t_ref[turn] = tn(proj_ref[turn], identity(width)).astype(BF16)
        out_t_ref[turn] = flip(out_ref[turn]).astype(BF16)


def sigmoid(values):
    return 0.5 * jnp.tanh(0.5 * values) + 0.5


def sides(streams, weight, lives, gate_ref, lefts, rights, row):
    width, cols = streams[0].shape
    rows = lefts.shape[0] // width
    made = nn(weight, jnp.concatenate([norm_rows(stream) for stream in streams], axis=1))
    for at, live in enumerate(lives):
        part = [
            made[block * width : (block + 1) * width, at * cols : (at + 1) * cols] for block in range(5)
        ]
        lefts[pl.ds(row + at, width, stride=rows), :] = sigmoid(part[0]) * part[1] * live
        rights[pl.ds(row + at, width, stride=rows), :] = sigmoid(part[2]) * part[3] * live
        gate_ref[row + at] = sigmoid(part[4])


def flat(block):
    return block.reshape(block.shape[0] * block.shape[1], block.shape[2])


def outer_kernel(
    where_ref, flag_ref, own_ref, other_ref, left_ref, live_ref, base_ref, outer_t_ref, proj_ref, present_ref,
    stream_ref, gate_ref, far0, far1, theirs_ref, near0, near1, near2, near3, came, outer, lefts, rights,
):
    rows, width, cols = base_ref.shape
    chip, core = where_ref[1], where_ref[2]
    per = own_ref.shape[1]
    chips = own_ref.shape[0]
    for at in range(chips):
        chip_at = chip ^ (at % 2 * 4 + at // 2 % 2 * 2 + at // 4)
        came[chip_at * 2 + core] = own_ref[at].astype(F32)
        came[chip_at * 2 + (1 - core)] = other_ref[at].astype(F32)
    half = left_ref.shape[0] // (2 * rows)
    quarter = half // 2
    live_all = came[:, quarter * rows : (quarter + 1) * rows, :].reshape(cols, per_lane(came)).astype(BF16)
    counts = nt(live_ref[...].astype(BF16), live_all)
    share = 1.0 / jnp.maximum(counts, 1.0)
    left_all = left_ref[...]
    for pair in range(quarter):
        right = came[:, pair * rows : (pair + 1) * rows, :].reshape(cols, per_lane(came)).astype(BF16)
        made = nt(left_all, right).astype(BF16)
        for part in range(2):
            d = part * quarter + pair
            for row in range(rows):
                first = (part * rows + row) * half
                lane = (row % 2) * cols
                outer[row // 2, d * half : (d + 1) * half, lane : lane + cols] = made[first : first + half]
    present = present_ref[...].astype(F32)
    for row in range(0, rows, 2):
        product = nn(outer_t_ref[...], outer[row // 2])
        streams, lives = [], []
        for at in range(2):
            streams.append(
                base_ref[row + at] + product[:, at * cols : (at + 1) * cols] * share[row + at : row + at + 1]
            )
            stream_ref[row + at] = streams[at]
            lives.append(present * flag_ref[where_ref[0] + row + at].astype(F32))
        sides(streams, proj_ref[0], lives, gate_ref, lefts, rights, row)
    size = width // NEAR
    block = size * rows

    def group(side, to):
        first = pl.multiple_of((to & (NEAR - 1)) * block, block)
        return side[pl.ds(first, block), :].astype(BF16)

    for op, far in enumerate((far0, far1)):
        far[...] = group(rights, partner_chip(chip, core, op, FAR_SPLIT))
        theirs_ref[op * block : (op + 1) * block] = group(rights, partner_chip(chip, 1 - core, op, FAR_SPLIT))
    for step, near in enumerate((near0, near1, near2, near3)):
        near[0:block] = group(lefts, chip ^ step)
        near[block:] = group(rights, chip ^ step)


def per_lane(ref):
    return ref.shape[-1]


def mix_rows_kernel(
    where_ref, near3, far0, far1, near2, near1, near0, other_ref, out0, out1, out2, out3, lefts, rights, mixed
):
    chip, core = where_ref[1], where_ref[2]
    count, rows, cols = lefts.shape[1:]
    block = count * rows
    place = 0
    for step, near in ((3, near3), (None, far0), (None, far1), (2, near2), (1, near1), (0, near0)):
        if step is None:
            op = 0 if near is far0 else 1
            for half in range(2):
                at = partner_chip(chip, core, op, FAR_SPLIT) * 2 + (core ^ half)
                rights[at] = near[half * block : (half + 1) * block].astype(F32).reshape(count, rows, cols)
                at = partner_chip(chip, 1 - core, op, FAR_SPLIT) * 2 + ((1 - core) ^ half)
                rights[at] = other_ref[place : place + block].astype(F32).reshape(count, rows, cols)
                place += block
        else:
            lefts[step] = near[0:block].astype(F32).reshape(count, rows, cols)
            rights[(chip ^ step) * 2 + core] = near[block:].astype(F32).reshape(count, rows, cols)
            theirs = other_ref[place : place + block]
            rights[(chip ^ step) * 2 + (1 - core)] = theirs.astype(F32).reshape(count, rows, cols)
            place += block
    for c in range(count):
        left = flat(lefts[:, c]).astype(BF16)
        right = flat(rights[:, c]).astype(BF16)
        mixed[pl.ds(c, NEAR * rows, stride=count), :] = nt(left, right)
    for step, out in enumerate((out0, out1, out2, out3)):
        out[...] = mixed[step * block : (step + 1) * block].astype(BF16)


def pick_kernel(*refs):
    blocks, out_ref = refs[:-1], refs[-1]
    for at, block in enumerate(blocks):
        half = block.shape[0] // 2
        out_ref[at * half : (at + 1) * half] = block[half:]


def update(came, row, stream_ref, gate_ref, out_weight):
    normed = jnp.concatenate([norm_rows(flat(came[row + at])) for at in range(2)], axis=1)
    made = nn(out_weight, normed)
    cols = made.shape[1] // 2
    return [
        stream_ref[row + at] + gate_ref[row + at] * made[:, at * cols : (at + 1) * cols] for at in range(2)
    ]


def between_kernel(
    where_ref, flag_ref, in0, in1, in2, in3, stream_ref, gate_ref, out_weight_ref, proj_ref, present_ref,
    next_ref, next_gate_ref, mine0, mine1, mine2, mine3, theirs_ref, came, lefts, rights,
):
    rows, width, cols = stream_ref.shape
    chip, core = where_ref[1], where_ref[2]
    size = width // NEAR
    for step, block in zip(NEAR_STEPS, (in0, in1, in2, in3)):
        came[:, (chip ^ step) & (NEAR - 1)] = block[...].astype(F32).reshape(rows, size, cols)
    present = present_ref[...].astype(F32)
    for row in range(0, rows, 2):
        streams = update(came, row, stream_ref, gate_ref, out_weight_ref[0])
        lives = []
        for at in range(2):
            next_ref[row + at] = streams[at]
            lives.append(present * flag_ref[where_ref[0] + row + at].astype(F32))
        sides(streams, proj_ref[1], lives, next_gate_ref, lefts, rights, row)
    block = width // (2 * OPS) * rows
    for op, mine in enumerate((mine0, mine1, mine2, mine3)):
        for at, side in enumerate((lefts, rights)):
            first = pl.multiple_of(partner_chip(chip, core, op) * block, block)
            mine[at * block : (at + 1) * block] = side[pl.ds(first, block), :].astype(BF16)
            first = pl.multiple_of(partner_chip(chip, 1 - core, op) * block, block)
            place = (op * 2 + at) * block
            theirs_ref[place : place + block] = side[pl.ds(first, block), :].astype(BF16)


def mix_cols_kernel(where_ref, came0, came1, came2, came3, mine_ref, theirs_ref, lefts, rights, partial):
    chip, core = where_ref[1], where_ref[2]
    count, rows, cols = lefts.shape[1:]
    block = count * rows
    for op, came in enumerate((came0, came1, came2, came3)):
        for half in range(2):
            for at, side in enumerate((lefts, rights)):
                place = (half * 2 + at) * block
                side[op * 2 + half] = came[place : place + block].astype(F32).reshape(count, rows, cols)
    for c in range(count):
        left = flat(lefts[:, c]).astype(BF16)
        right = flat(rights[:, c]).astype(BF16)
        partial[pl.ds(c, partial.shape[0] // count, stride=count), :] = tn(left, right)
    for op in range(OPS):
        for half in range(2):
            to = pl.multiple_of((partner_chip(chip, core, op, SMALL_SPLIT) * 2 + (core ^ half)) * block, block)
            mine_ref[op, half * block : (half + 1) * block] = partial[pl.ds(to, block), :]
            to = partner_chip(chip, 1 - core, op, SMALL_SPLIT) * 2 + ((1 - core) ^ half)
            to = pl.multiple_of(to * block, block)
            theirs_ref[op, half * block : (half + 1) * block] = partial[pl.ds(to, block), :].astype(BF16)


def sum_kernel(mine_ref, got_ref, *outs):
    for op, out in enumerate(outs):
        out[...] = (mine_ref[op] + got_ref[op].astype(F32)).astype(BF16)


def final_kernel(
    where_ref, came0, came1, came2, came3, other_ref, stream_ref, gate_ref, out_weight_ref, out_ref, came
):
    rows, width, cols = stream_ref.shape
    chip, core = where_ref[1], where_ref[2]
    size = width // (2 * OPS)
    block = size * rows
    for op, mine in enumerate((came0, came1, came2, came3)):
        came[:, partner_chip(chip, core, op, SMALL_SPLIT)] = mine[0:block].astype(F32).reshape(rows, size, cols)
        theirs = other_ref[op * block : (op + 1) * block]
        came[:, partner_chip(chip, 1 - core, op, SMALL_SPLIT)] = theirs.astype(F32).reshape(rows, size, cols)
    for row in range(0, rows, 2):
        for at, stream in enumerate(update(came, row, stream_ref, gate_ref, out_weight_ref[1])):
            out_ref[row + at] = flip_out(stream)


def flip_out(stream):
    return nt(identity(stream.shape[1]), stream.astype(BF16)).astype(BF16)


def chip_permute(block, step):
    count = lax.axis_size("wide")
    return lax.ppermute(block, "wide", [(w, w ^ (2 * step)) for w in range(count)])


def exchange(blocks, steps):
    return [chip_permute(blocks[step], step) if step else blocks[0] for step in steps]


def split_permute(block, steps):
    count = lax.axis_size("wide")
    return lax.ppermute(block, "wide", [(w, w ^ (2 * steps[w % 2])) for w in range(count)])


def split_exchange(blocks, split=SPLIT):
    return [split_permute(block, steps) for block, steps in zip(blocks, split)]


def with_partner(mine, theirs):
    got, messages, place = core_permute(theirs), [], 0
    for block in mine:
        messages.append(jnp.concatenate([block, got[place : place + block.shape[0]]], axis=0))
        place += block.shape[0]
    return messages


def core_permute(block):
    count = lax.axis_size("wide")
    return lax.ppermute(block, "wide", [(w, w ^ 1) for w in range(count)])


def per_device_chips(
    pairwise_state,
    homolog_features,
    residue_chain_index,
    resolved_residue_mask,
    alignment_mask,
    relative_offset_table,
    homolog_to_sides_matrix,
    outer_mean_output_weight,
    triangle_projection_weight,
    triangle_output_weight,
):
    rows, cols, width = pairwise_state.shape
    homologs = homolog_features.shape[0]
    half = homolog_to_sides_matrix.shape[1] // 2
    device = lax.axis_index("wide")
    chip, core = device // 2, device % 2
    where = jnp.stack([device * rows, chip, core]).astype(jnp.int32)
    present = resolved_residue_mask.reshape(1, cols)
    pay_rows = (half // 2 + 2) * rows
    row_present = lax.dynamic_slice_in_dim(resolved_residue_mask, device * rows, rows).astype(F32)
    live = alignment_mask.T.astype(F32) * row_present[:, None]
    live = jnp.concatenate([live, live], axis=1)
    pay, left, live = run(
        project_kernel,
        [((pay_rows, LANES), BF16), ((2 * rows * half, LANES), BF16), ((rows, LANES), F32)],
        homolog_features.astype(F32), homolog_to_sides_matrix.T, live,
        scratch=[((rows * half // 2, LANES), F32), ((pay_rows, LANES), F32)],
    )
    far_z = chip_permute(pay, 4)
    base, outer_t, proj_t, out_t = run(
        prep_kernel,
        [
            ((rows, width, cols), F32),
            ((width, half * half), BF16),
            ((2, triangle_projection_weight.shape[2], width), BF16),
            ((2, width, width), BF16),
        ],
        where, residue_chain_index, residue_chain_index.reshape(1, cols), pairwise_state,
        relative_offset_table, outer_mean_output_weight, triangle_projection_weight, triangle_output_weight,
        smem=(0, 1),
        scratch=[((LANES, width), F32), ((half * half, width), F32)],
    )
    along_z = jnp.stack([pay, far_z])
    along_z = jnp.concatenate([along_z, chip_permute(along_z, 2)], axis=0)
    own = jnp.concatenate([along_z, chip_permute(along_z, 1)], axis=0)
    own, base, outer_t, proj_t, out_t = lax.optimization_barrier((own, base, outer_t, proj_t, out_t))
    other = core_permute(own)
    tall = width * rows
    near, all_ = tall // NEAR, tall // (2 * OPS)
    made = run(
        outer_kernel,
        [((rows, width, cols), F32)] * 2
        + [((near, cols), BF16)] * 2
        + [((2 * near, cols), BF16)] * (1 + NEAR),
        where, resolved_residue_mask, own, other, left, live, base, outer_t, proj_t, present,
        smem=(0, 1),
        scratch=[
            ((16, pay_rows, LANES), F32),
            ((rows // 2, half * half, 2 * cols), BF16),
            ((tall, cols), F32),
            ((tall, cols), F32),
        ],
        flops=4 * 10**9,
    )
    stream, gate = made[0], made[1]
    first = chip_permute(made[8], 3)
    far, later = lax.optimization_barrier((with_partner(made[2:4], made[4]), list(made[5:8])))
    far = split_exchange(far, FAR_SPLIT)
    came = [first] + exchange(later, NEAR_STEPS[1:])
    came = [came[0], far[0], far[1], came[1], came[2], came[3]]
    rights = [block if at in (1, 2) else block[near:] for at, block in enumerate(came)]
    rights = jnp.concatenate(rights, axis=0)
    mixed = run(
        mix_rows_kernel,
        [((near, cols), BF16)] * NEAR,
        where, *came, core_permute(rights),
        smem=(0,),
        scratch=[
            ((NEAR, width // NEAR, rows, cols), F32),
            ((16, width // NEAR, rows, cols), F32),
            ((tall, cols), F32),
        ],
    )
    mixed = exchange(mixed, NEAR_STEPS)
    made = run(
        between_kernel,
        [((rows, width, cols), F32)] * 2 + [((2 * all_, cols), BF16)] * OPS + [((2 * OPS * all_, cols), BF16)],
        where, resolved_residue_mask, *mixed, stream, gate, out_t, proj_t, present,
        smem=(0, 1),
        scratch=[
            ((rows, NEAR, width // NEAR, cols), F32),
            ((tall, cols), F32),
            ((tall, cols), F32),
        ],
    )
    stream, gate, theirs = made[0], made[1], made[6]
    came = split_exchange(with_partner(made[2:6], theirs))
    mine, theirs = run(
        mix_cols_kernel,
        [((OPS, 2 * all_, cols), F32), ((OPS, 2 * all_, cols), BF16)],
        where, *came,
        smem=(0,),
        scratch=[
            ((2 * OPS, width // (2 * OPS), rows, cols), F32),
            ((2 * OPS, width // (2 * OPS), rows, cols), F32),
            ((2 * tall, cols), F32),
        ],
    )
    mixed = run(sum_kernel, [((2 * all_, cols), BF16)] * OPS, mine, core_permute(theirs))
    mixed = split_exchange(mixed, SMALL_SPLIT)
    other = core_permute(run(pick_kernel, [((OPS * all_, cols), BF16)], *mixed)[0])
    return run(
        final_kernel,
        [((rows, cols, width), BF16)],
        where, *mixed, other, stream, gate, out_t,
        smem=(0,),
        scratch=[((rows, 2 * OPS, width // (2 * OPS), cols), F32)],
    )[0]


def fits_chips(mesh):
    return mesh.shape["narrow"] == 1 and mesh.shape["wide"] == 16


def solution(mesh):
    per_device = per_device_chips if fits_chips(mesh) else per_device_general
    return jax.shard_map(
        per_device,
        mesh=mesh,
        in_specs=(
            P(("grp", "wide"), "narrow", None),
            P("grp", "wide", None),
            P("grp"),
            P("grp"),
            P("grp", "wide"),
            P(),
            P(),
            P(),
            P(),
            P(),
        ),
        out_specs=P(("grp", "wide"), "narrow", None),
        check_vma=False,
    )
```

```python
import functools

import jax
import jax.numpy as jnp
from jax import lax
from jax.experimental import pallas as pl
from jax.experimental.pallas import tpu as pltpu
from jax.sharding import PartitionSpec as P

RELMAX = 32
EPSILON = 1e-05
LANES = 128
F32 = jnp.float32
BF16 = jnp.bfloat16


def apply_layer_norm(values, axis_dim):
    center = values - jnp.mean(values, axis=axis_dim, keepdims=True)
    spread = jnp.mean(center * center, axis=axis_dim, keepdims=True)
    return center * lax.rsqrt(spread + EPSILON)


def gather_wide(block):
    n = lax.axis_size("wide")
    if n % 4 or n < 8:
        return lax.all_gather(block, "wide", axis=0)
    outer = n // 4
    me = lax.axis_index("wide")
    high, mid, low = me // 4, (me // 2) % 2, me % 2
    arrived = [block]
    for shift in range(1, outer):
        perm = [(w, ((w // 4 + shift) % outer) * 4 + w % 4) for w in range(n)]
        arrived.append(lax.ppermute(block, "wide", perm))
    held = jnp.zeros((outer,) + block.shape, block.dtype)
    for shift, piece in enumerate(arrived):
        held = lax.dynamic_update_index_in_dim(held, piece, (high - shift + outer) % outer, 0)
    other = lax.ppermute(held, "wide", [(w, w ^ 2) for w in range(n)])
    held = jnp.stack(
        [jnp.where(mid == 0, held, other), jnp.where(mid == 0, other, held)], axis=1
    )
    other = lax.ppermute(held, "wide", [(w, w ^ 1) for w in range(n)])
    held = jnp.stack(
        [jnp.where(low == 0, held, other), jnp.where(low == 0, other, held)], axis=2
    )
    return held.reshape((n,) + block.shape)


def triangle(stream, pair_live, proj_weight, out_weight, incoming):
    rows = stream.shape[0]
    cols = stream.shape[1]
    width = out_weight.shape[0]
    wide_count = lax.axis_size("wide")
    core_count = lax.axis_size("narrow")
    devices = wide_count * core_count
    per_dev = width // devices
    normed = apply_layer_norm(stream, 2).astype(jnp.bfloat16)
    blocks = [proj_weight[:, index * width : (index + 1) * width] for index in range(4)]

    def project(block):
        return jnp.einsum("ijd,dc->cij", normed, block, preferred_element_type=jnp.float32)

    left_side = (jax.nn.sigmoid(project(blocks[0])) * project(blocks[1]) * pair_live[None]).astype(
        jnp.bfloat16
    )
    right_side = (jax.nn.sigmoid(project(blocks[2])) * project(blocks[3]) * pair_live[None]).astype(
        jnp.bfloat16
    )
    gate = jax.nn.sigmoid(
        jnp.einsum(
            "ijd,dc->ijc", normed, proj_weight[:, 4 * width :], preferred_element_type=jnp.float32
        )
    )
    form = "cki,ckj->cij" if incoming else "cik,cjk->cij"
    both = jnp.stack(
        [
            left_side.reshape(devices, per_dev, rows * cols),
            right_side.reshape(devices, per_dev, rows * cols),
        ],
        axis=1,
    ).reshape(devices, 2 * per_dev, rows * cols)
    both = lax.all_to_all(both, ("wide", "narrow"), split_axis=0, concat_axis=0, tiled=True)
    both = both.reshape(wide_count, core_count, 2, per_dev, rows, cols)
    both = jnp.transpose(both, (2, 3, 0, 4, 1, 5)).reshape(
        2, per_dev, wide_count * rows, core_count * cols
    )
    mixed = jnp.einsum(form, both[0], both[1], preferred_element_type=jnp.float32).astype(
        jnp.bfloat16
    )
    spread_out = mixed.reshape(per_dev, wide_count, rows, core_count, cols)
    spread_out = jnp.transpose(spread_out, (1, 3, 0, 2, 4)).reshape(
        wide_count * core_count * per_dev, rows * cols
    )
    returned = lax.all_to_all(
        spread_out, ("wide", "narrow"), split_axis=0, concat_axis=0, tiled=True
    ).reshape(width, rows, cols)
    blended_standardize = apply_layer_norm(returned.astype(jnp.float32), 0).astype(jnp.bfloat16)
    update = jnp.einsum(
        "cij,cd->ijd", blended_standardize, out_weight, preferred_element_type=jnp.float32
    )
    return stream + gate * update


def per_device_general(
    pairwise_state,
    homolog_features,
    residue_chain_index,
    resolved_residue_mask,
    alignment_mask,
    relative_offset_table,
    homolog_to_sides_matrix,
    outer_mean_output_weight,
    triangle_projection_weight,
    triangle_output_weight,
):
    rows = pairwise_state.shape[0]
    cols = pairwise_state.shape[1]
    row_start = lax.axis_index("wide") * rows
    col_start = lax.axis_index("narrow") * cols
    residue_present = resolved_residue_mask.astype(jnp.float32)
    row_present = lax.dynamic_slice_in_dim(residue_present, row_start, rows)
    col_live = lax.dynamic_slice_in_dim(residue_present, col_start, cols)
    present_flags = alignment_mask.astype(jnp.float32) * row_present[None, :]
    alignment_normed = apply_layer_norm(homolog_features.astype(jnp.float32), 2).astype(
        jnp.bfloat16
    )
    projected_rows = jnp.einsum(
        "tna,ak->tnk", alignment_normed, homolog_to_sides_matrix, preferred_element_type=jnp.float32
    )
    projected_rows = (projected_rows * present_flags[:, :, None]).astype(jnp.bfloat16)
    half_width = projected_rows.shape[2] // 2
    homologs = projected_rows.shape[0]
    left_proj = projected_rows[:, :, :half_width]
    right_proj = projected_rows[:, :, half_width:]
    live_flags = present_flags.astype(jnp.bfloat16)
    packed = jnp.concatenate(
        [jnp.transpose(right_proj, (1, 0, 2)).reshape(rows, homologs * half_width), live_flags.T],
        axis=1,
    )
    gathered = gather_wide(packed).reshape(-1, packed.shape[1])
    gathered = lax.dynamic_slice_in_dim(gathered, col_start, cols, 0)
    right_mine = jnp.transpose(
        gathered[:, : homologs * half_width].reshape(cols, homologs, half_width), (1, 0, 2)
    )
    live_mine = gathered[:, homologs * half_width :].T
    counts = jnp.dot(live_flags.T, live_mine, preferred_element_type=jnp.float32)

    def opm_row(left_row):
        outer = jnp.einsum("sc,sjd->jcd", left_row, right_mine, preferred_element_type=jnp.float32)
        outer = outer.reshape(cols, half_width * half_width).astype(jnp.bfloat16)
        return jnp.dot(outer, outer_mean_output_weight, preferred_element_type=jnp.float32)

    opm = lax.map(opm_row, jnp.transpose(left_proj, (1, 0, 2)))
    row_pos = row_start + jnp.arange(rows, dtype=jnp.int32)
    col_pos = col_start + jnp.arange(cols, dtype=jnp.int32)
    row_chain = lax.dynamic_slice_in_dim(residue_chain_index, row_start, rows)
    col_chain = lax.dynamic_slice_in_dim(residue_chain_index, col_start, cols)
    offset = jnp.clip(row_pos[:, None] - col_pos[None, :], -RELMAX, RELMAX) + RELMAX
    bin_index = jnp.where(row_chain[:, None] == col_chain[None, :], offset, 2 * RELMAX + 1)
    bin_count = relative_offset_table.shape[0]
    one_hot = (
        bin_index[:, :, None] == jnp.arange(bin_count, dtype=jnp.int32)[None, None, :]
    ).astype(jnp.bfloat16)
    relpos = jnp.einsum(
        "ijb,bc->ijc", one_hot, relative_offset_table, preferred_element_type=jnp.float32
    )
    stream = (
        pairwise_state.astype(jnp.float32) + relpos + opm / jnp.maximum(counts, 1.0)[:, :, None]
    )
    pair_live = row_present[:, None] * col_live[None, :]
    for turn_index in range(2):
        stream = triangle(
            stream,
            pair_live,
            triangle_projection_weight[turn_index],
            triangle_output_weight[turn_index],
            turn_index == 1,
        )
    return stream.astype(jnp.bfloat16)


def nn(a, b):
    return lax.dot_general(a, b, (((1,), (0,)), ((), ())), preferred_element_type=F32)


def nt(a, b):
    return lax.dot_general(a, b, (((1,), (1,)), ((), ())), preferred_element_type=F32)


def tn(a, b):
    return lax.dot_general(a, b, (((0,), (0,)), ((), ())), preferred_element_type=F32)


def identity(size):
    rows = lax.broadcasted_iota(jnp.int32, (size, size), 0)
    cols = lax.broadcasted_iota(jnp.int32, (size, size), 1)
    return (rows == cols).astype(F32).astype(BF16)


def flip(block):
    return nt(identity(block.shape[1]), block)


def norm_rows(values):
    scale = 1.0 / values.shape[0]
    center = values - jnp.sum(values, axis=0, keepdims=True) * scale
    spread = jnp.sum(center * center, axis=0, keepdims=True) * scale
    return (center * lax.rsqrt(spread + EPSILON)).astype(BF16)


def run(kernel, outs, *args, smem=(), scratch=(), flops=15 * 10**8):
    vmem = pl.BlockSpec(memory_space=pltpu.VMEM)
    in_specs = [
        pl.BlockSpec(memory_space=pltpu.SMEM if at in smem else pltpu.VMEM) for at in range(len(args))
    ]
    moved = sum(a.size * a.dtype.itemsize for a in args)
    return pl.pallas_call(
        kernel,
        out_shape=[jax.ShapeDtypeStruct(shape, kind) for shape, kind in outs],
        in_specs=in_specs,
        out_specs=[vmem] * len(outs),
        scratch_shapes=[pltpu.VMEM(shape, kind) for shape, kind in scratch],
        compiler_params=pltpu.CompilerParams(vmem_limit_bytes=VMEM_LIMIT),
        cost_estimate=pl.CostEstimate(flops=flops, bytes_accessed=moved, transcendentals=0),
    )(*args)


VMEM_LIMIT = 20 * 1024 * 1024
SPLIT = ((7, 5), (6, 4), (3, 2), (1, 0))
FAR_SPLIT = SPLIT[:2]
SMALL_SPLIT = ((7, 3), (2, 6), (5, 1), (0, 4))
OPS = len(SPLIT)
NEAR = 4
NEAR_STEPS = (3, 2, 1, 0)


def partner_chip(chip, core, op, split=SPLIT):
    return chip ^ jnp.where(core == 0, split[op][0], split[op][1])


def project_kernel(feat_ref, weight_ref, live_in_ref, pay_ref, left_ref, live_ref, turned, packed):
    homologs, rows, _ = feat_ref.shape
    half = weight_ref.shape[0] // 2
    quarter = half // 2
    values = feat_ref[...].reshape(homologs * rows, feat_ref.shape[2])
    center = values - jnp.mean(values, axis=1, keepdims=True)
    spread = jnp.mean(center * center, axis=1, keepdims=True)
    normed = (center * lax.rsqrt(spread + EPSILON)).astype(BF16)
    total = homologs * rows
    out_row = lax.broadcasted_iota(jnp.int32, (total, total), 0)
    in_row = lax.broadcasted_iota(jnp.int32, (total, total), 1)
    order = in_row == (out_row & (homologs - 1)) * rows + out_row // homologs
    normed = nn(order.astype(F32).astype(BF16), normed).astype(BF16)
    live = live_in_ref[...]
    weight = weight_ref[...]
    blank = jnp.zeros((homologs, normed.shape[1]), BF16)
    for row in range(rows):
        mine = normed[row * homologs : (row + 1) * homologs]
        low = nt(weight, jnp.concatenate([mine, blank], axis=0)) * live[row : row + 1]
        high = nt(weight, jnp.concatenate([blank, mine], axis=0)) * live[row : row + 1]
        left_ref[row * half : (row + 1) * half] = low[:half].astype(BF16)
        left_ref[(rows + row) * half : (rows + row + 1) * half] = high[:half].astype(BF16)
        turned[row * quarter : (row + 1) * quarter] = low[half : half + quarter] + high[half + quarter :]
    for pair in range(quarter):
        packed[pair * rows : (pair + 1) * rows] = turned[pl.ds(pair, rows, stride=quarter), :]
    packed[quarter * rows : (quarter + 1) * rows] = live
    packed[(quarter + 1) * rows :] = jnp.zeros((rows, 2 * homologs), F32)
    pay_ref[...] = packed[...].astype(BF16)
    live_ref[...] = jnp.where(lax.broadcasted_iota(jnp.int32, live.shape, 1) < homologs, live, 0.0)


def prep_kernel(
    where_ref, chain_ref, chains_ref, pair_ref, table_ref, outer_ref, proj_ref, out_ref,
    base_ref, outer_t_ref, proj_t_ref, out_t_ref, table_pad, outer_pad,
):
    rows, cols, width = pair_ref.shape
    bins = table_ref.shape[0]
    table_pad[...] = jnp.zeros_like(table_pad)
    table_pad[0:bins, :] = table_ref[...].astype(F32)
    table = flip(table_pad[...].astype(BF16)).astype(BF16)
    chains = chains_ref[...]
    col = lax.broadcasted_iota(jnp.int32, (1, cols), 1)
    slot = lax.broadcasted_iota(jnp.int32, (table_pad.shape[0], cols), 0)
    for row in range(rows):
        place = where_ref[0] + row
        offset = jnp.clip(place - col, -RELMAX, RELMAX) + RELMAX
        bin_index = jnp.where(chains == chain_ref[place], offset, 2 * RELMAX + 1)
        hot = (slot == bin_index).astype(F32).astype(BF16)
        base_ref[row] = flip(pair_ref[row]) + nn(table, hot)
    half = round(outer_pad.shape[0] ** 0.5)
    outer_pad[...] = outer_ref[...].astype(F32)
    for d in range(half):
        outer_t_ref[:, d * half : (d + 1) * half] = flip(outer_pad[pl.ds(d, half, stride=half), :].astype(BF16)).astype(BF16)
    for turn in range(2):
        proj_t_ref[turn] = tn(proj_ref[turn], identity(width)).astype(BF16)
        out_t_ref[turn] = flip(out_ref[turn]).astype(BF16)


def sigmoid(values):
    return 0.5 * jnp.tanh(0.5 * values) + 0.5


def sides(streams, weight, lives, gate_ref, lefts, rights, row):
    width, cols = streams[0].shape
    rows = lefts.shape[0] // width
    made = nn(weight, jnp.concatenate([norm_rows(stream) for stream in streams], axis=1))
    for at, live in enumerate(lives):
        part = [
            made[block * width : (block + 1) * width, at * cols : (at + 1) * cols] for block in range(5)
        ]
        lefts[pl.ds(row + at, width, stride=rows), :] = sigmoid(part[0]) * part[1] * live
        rights[pl.ds(row + at, width, stride=rows), :] = sigmoid(part[2]) * part[3] * live
        gate_ref[row + at] = sigmoid(part[4])


def flat(block):
    return block.reshape(block.shape[0] * block.shape[1], block.shape[2])


def outer_kernel(
    where_ref, flag_ref, own_ref, other_ref, left_ref, live_ref, base_ref, outer_t_ref, proj_ref, present_ref,
    stream_ref, gate_ref, far0, far1, theirs_ref, near0, near1, near2, near3, came, outer, lefts, rights,
):
    rows, width, cols = base_ref.shape
    chip, core = where_ref[1], where_ref[2]
    per = own_ref.shape[1]
    chips = own_ref.shape[0]
    for at in range(chips):
        chip_at = chip ^ (at % 2 * 4 + at // 2 % 2 * 2 + at // 4)
        came[chip_at * 2 + core] = own_ref[at].astype(F32)
        came[chip_at * 2 + (1 - core)] = other_ref[at].astype(F32)
    half = left_ref.shape[0] // (2 * rows)
    quarter = half // 2
    live_all = came[:, quarter * rows : (quarter + 1) * rows, :].reshape(cols, per_lane(came)).astype(BF16)
    counts = nt(live_ref[...].astype(BF16), live_all)
    share = 1.0 / jnp.maximum(counts, 1.0)
    left_all = left_ref[...]
    for pair in range(quarter):
        right = came[:, pair * rows : (pair + 1) * rows, :].reshape(cols, per_lane(came)).astype(BF16)
        made = nt(left_all, right).astype(BF16)
        for part in range(2):
            d = part * quarter + pair
            for row in range(rows):
                first = (part * rows + row) * half
                lane = (row % 2) * cols
                outer[row // 2, d * half : (d + 1) * half, lane : lane + cols] = made[first : first + half]
    present = present_ref[...].astype(F32)
    for row in range(0, rows, 2):
        product = nn(outer_t_ref[...], outer[row // 2])
        streams, lives = [], []
        for at in range(2):
            streams.append(
                base_ref[row + at] + product[:, at * cols : (at + 1) * cols] * share[row + at : row + at + 1]
            )
            stream_ref[row + at] = streams[at]
            lives.append(present * flag_ref[where_ref[0] + row + at].astype(F32))
        sides(streams, proj_ref[0], lives, gate_ref, lefts, rights, row)
    size = width // NEAR
    block = size * rows

    def group(side, to):
        first = pl.multiple_of((to & (NEAR - 1)) * block, block)
        return side[pl.ds(first, block), :].astype(BF16)

    for op, far in enumerate((far0, far1)):
        far[...] = group(rights, partner_chip(chip, core, op, FAR_SPLIT))
        theirs_ref[op * block : (op + 1) * block] = group(rights, partner_chip(chip, 1 - core, op, FAR_SPLIT))
    for step, near in enumerate((near0, near1, near2, near3)):
        near[0:block] = group(lefts, chip ^ step)
        near[block:] = group(rights, chip ^ step)


def per_lane(ref):
    return ref.shape[-1]


def mix_rows_kernel(
    where_ref, near1, far0, far1, near3, near2, near0, other_ref, out0, out1, out2, out3, lefts, rights, mixed
):
    chip, core = where_ref[1], where_ref[2]
    count, rows, cols = lefts.shape[1:]
    block = count * rows
    place = 0
    for step, near in ((1, near1), (None, far0), (None, far1), (3, near3), (2, near2), (0, near0)):
        if step is None:
            op = 0 if near is far0 else 1
            for half in range(2):
                at = partner_chip(chip, core, op, FAR_SPLIT) * 2 + (core ^ half)
                rights[at] = near[half * block : (half + 1) * block].astype(F32).reshape(count, rows, cols)
                at = partner_chip(chip, 1 - core, op, FAR_SPLIT) * 2 + ((1 - core) ^ half)
                rights[at] = other_ref[place : place + block].astype(F32).reshape(count, rows, cols)
                place += block
        else:
            lefts[step] = near[0:block].astype(F32).reshape(count, rows, cols)
            rights[(chip ^ step) * 2 + core] = near[block:].astype(F32).reshape(count, rows, cols)
            theirs = other_ref[place : place + block]
            rights[(chip ^ step) * 2 + (1 - core)] = theirs.astype(F32).reshape(count, rows, cols)
            place += block
    for c in range(count):
        left = flat(lefts[:, c]).astype(BF16)
        right = flat(rights[:, c]).astype(BF16)
        mixed[pl.ds(c, NEAR * rows, stride=count), :] = nt(left, right)
    for step, out in enumerate((out0, out1, out2, out3)):
        out[...] = mixed[step * block : (step + 1) * block].astype(BF16)


def pick_kernel(*refs):
    blocks, out_ref = refs[:-1], refs[-1]
    for at, block in enumerate(blocks):
        half = block.shape[0] // 2
        out_ref[at * half : (at + 1) * half] = block[half:]


def update(came, row, stream_ref, gate_ref, out_weight):
    normed = jnp.concatenate([norm_rows(flat(came[row + at])) for at in range(2)], axis=1)
    made = nn(out_weight, normed)
    cols = made.shape[1] // 2
    return [
        stream_ref[row + at] + gate_ref[row + at] * made[:, at * cols : (at + 1) * cols] for at in range(2)
    ]


def between_kernel(
    where_ref, flag_ref, in0, in1, in2, in3, stream_ref, gate_ref, out_weight_ref, proj_ref, present_ref,
    next_ref, next_gate_ref, mine0, mine1, mine2, mine3, theirs_ref, came, lefts, rights,
):
    rows, width, cols = stream_ref.shape
    chip, core = where_ref[1], where_ref[2]
    size = width // NEAR
    for step, block in zip(NEAR_STEPS, (in0, in1, in2, in3)):
        came[:, (chip ^ step) & (NEAR - 1)] = block[...].astype(F32).reshape(rows, size, cols)
    present = present_ref[...].astype(F32)
    for row in range(0, rows, 2):
        streams = update(came, row, stream_ref, gate_ref, out_weight_ref[0])
        lives = []
        for at in range(2):
            next_ref[row + at] = streams[at]
            lives.append(present * flag_ref[where_ref[0] + row + at].astype(F32))
        sides(streams, proj_ref[1], lives, next_gate_ref, lefts, rights, row)
    block = width // (2 * OPS) * rows
    for op, mine in enumerate((mine0, mine1, mine2, mine3)):
        for at, side in enumerate((lefts, rights)):
            first = pl.multiple_of(partner_chip(chip, core, op) * block, block)
            mine[at * block : (at + 1) * block] = side[pl.ds(first, block), :].astype(BF16)
            first = pl.multiple_of(partner_chip(chip, 1 - core, op) * block, block)
            place = (op * 2 + at) * block
            theirs_ref[place : place + block] = side[pl.ds(first, block), :].astype(BF16)


def mix_cols_kernel(where_ref, came0, came1, came2, came3, mine_ref, theirs_ref, lefts, rights, partial):
    chip, core = where_ref[1], where_ref[2]
    count, rows, cols = lefts.shape[1:]
    block = count * rows
    for op, came in enumerate((came0, came1, came2, came3)):
        for half in range(2):
            for at, side in enumerate((lefts, rights)):
                place = (half * 2 + at) * block
                side[op * 2 + half] = came[place : place + block].astype(F32).reshape(count, rows, cols)
    for c in range(count):
        left = flat(lefts[:, c]).astype(BF16)
        right = flat(rights[:, c]).astype(BF16)
        partial[pl.ds(c, partial.shape[0] // count, stride=count), :] = tn(left, right)
    for op in range(OPS):
        for half in range(2):
            to = pl.multiple_of((partner_chip(chip, core, op, SMALL_SPLIT) * 2 + (core ^ half)) * block, block)
            mine_ref[op, half * block : (half + 1) * block] = partial[pl.ds(to, block), :]
            to = partner_chip(chip, 1 - core, op, SMALL_SPLIT) * 2 + ((1 - core) ^ half)
            to = pl.multiple_of(to * block, block)
            theirs_ref[op, half * block : (half + 1) * block] = partial[pl.ds(to, block), :].astype(BF16)


def sum_kernel(mine_ref, got_ref, *outs):
    for op, out in enumerate(outs):
        out[...] = (mine_ref[op] + got_ref[op].astype(F32)).astype(BF16)


def final_kernel(
    where_ref, came0, came1, came2, came3, other_ref, stream_ref, gate_ref, out_weight_ref, out_ref, came
):
    rows, width, cols = stream_ref.shape
    chip, core = where_ref[1], where_ref[2]
    size = width // (2 * OPS)
    block = size * rows
    for op, mine in enumerate((came0, came1, came2, came3)):
        came[:, partner_chip(chip, core, op, SMALL_SPLIT)] = mine[0:block].astype(F32).reshape(rows, size, cols)
        theirs = other_ref[op * block : (op + 1) * block]
        came[:, partner_chip(chip, 1 - core, op, SMALL_SPLIT)] = theirs.astype(F32).reshape(rows, size, cols)
    for row in range(0, rows, 2):
        for at, stream in enumerate(update(came, row, stream_ref, gate_ref, out_weight_ref[1])):
            out_ref[row + at] = flip_out(stream)


def flip_out(stream):
    return nt(identity(stream.shape[1]), stream.astype(BF16)).astype(BF16)


def chip_permute(block, step):
    count = lax.axis_size("wide")
    return lax.ppermute(block, "wide", [(w, w ^ (2 * step)) for w in range(count)])


def exchange(blocks, steps):
    return [chip_permute(blocks[step], step) if step else blocks[0] for step in steps]


def split_permute(block, steps):
    count = lax.axis_size("wide")
    return lax.ppermute(block, "wide", [(w, w ^ (2 * steps[w % 2])) for w in range(count)])


def split_exchange(blocks, split=SPLIT):
    return [split_permute(block, steps) for block, steps in zip(blocks, split)]


def with_partner(mine, theirs):
    got, messages, place = core_permute(theirs), [], 0
    for block in mine:
        messages.append(jnp.concatenate([block, got[place : place + block.shape[0]]], axis=0))
        place += block.shape[0]
    return messages


def core_permute(block):
    count = lax.axis_size("wide")
    return lax.ppermute(block, "wide", [(w, w ^ 1) for w in range(count)])


def per_device_chips(
    pairwise_state,
    homolog_features,
    residue_chain_index,
    resolved_residue_mask,
    alignment_mask,
    relative_offset_table,
    homolog_to_sides_matrix,
    outer_mean_output_weight,
    triangle_projection_weight,
    triangle_output_weight,
):
    rows, cols, width = pairwise_state.shape
    homologs = homolog_features.shape[0]
    half = homolog_to_sides_matrix.shape[1] // 2
    device = lax.axis_index("wide")
    chip, core = device // 2, device % 2
    where = jnp.stack([device * rows, chip, core]).astype(jnp.int32)
    present = resolved_residue_mask.reshape(1, cols)
    pay_rows = (half // 2 + 2) * rows
    row_present = lax.dynamic_slice_in_dim(resolved_residue_mask, device * rows, rows).astype(F32)
    live = alignment_mask.T.astype(F32) * row_present[:, None]
    live = jnp.concatenate([live, live], axis=1)
    pay, left, live = run(
        project_kernel,
        [((pay_rows, LANES), BF16), ((2 * rows * half, LANES), BF16), ((rows, LANES), F32)],
        homolog_features.astype(F32), homolog_to_sides_matrix.T, live,
        scratch=[((rows * half // 2, LANES), F32), ((pay_rows, LANES), F32)],
    )
    far_z = chip_permute(pay, 4)
    base, outer_t, proj_t, out_t = run(
        prep_kernel,
        [
            ((rows, width, cols), F32),
            ((width, half * half), BF16),
            ((2, triangle_projection_weight.shape[2], width), BF16),
            ((2, width, width), BF16),
        ],
        where, residue_chain_index, residue_chain_index.reshape(1, cols), pairwise_state,
        relative_offset_table, outer_mean_output_weight, triangle_projection_weight, triangle_output_weight,
        smem=(0, 1),
        scratch=[((LANES, width), F32), ((half * half, width), F32)],
    )
    along_z = jnp.stack([pay, far_z])
    along_z = jnp.concatenate([along_z, chip_permute(along_z, 2)], axis=0)
    own = jnp.concatenate([along_z, chip_permute(along_z, 1)], axis=0)
    own, base, outer_t, proj_t, out_t = lax.optimization_barrier((own, base, outer_t, proj_t, out_t))
    other = core_permute(own)
    tall = width * rows
    near, all_ = tall // NEAR, tall // (2 * OPS)
    made = run(
        outer_kernel,
        [((rows, width, cols), F32)] * 2
        + [((near, cols), BF16)] * 2
        + [((2 * near, cols), BF16)] * (1 + NEAR),
        where, resolved_residue_mask, own, other, left, live, base, outer_t, proj_t, present,
        smem=(0, 1),
        scratch=[
            ((16, pay_rows, LANES), F32),
            ((rows // 2, half * half, 2 * cols), BF16),
            ((tall, cols), F32),
            ((tall, cols), F32),
        ],
        flops=4 * 10**9,
    )
    stream, gate = made[0], made[1]
    first = chip_permute(made[6], 1)
    far, later = lax.optimization_barrier((with_partner(made[2:4], made[4]), [made[5], made[7], made[8]]))
    far = split_exchange(far, FAR_SPLIT)
    came = [first, chip_permute(later[2], 3), chip_permute(later[1], 2), later[0]]
    came = [came[0], far[0], far[1], came[1], came[2], came[3]]
    rights = [block if at in (1, 2) else block[near:] for at, block in enumerate(came)]
    rights = jnp.concatenate(rights, axis=0)
    mixed = run(
        mix_rows_kernel,
        [((near, cols), BF16)] * NEAR,
        where, *came, core_permute(rights),
        smem=(0,),
        scratch=[
            ((NEAR, width // NEAR, rows, cols), F32),
            ((16, width // NEAR, rows, cols), F32),
            ((tall, cols), F32),
        ],
    )
    mixed = exchange(mixed, NEAR_STEPS)
    made = run(
        between_kernel,
        [((rows, width, cols), F32)] * 2 + [((2 * all_, cols), BF16)] * OPS + [((2 * OPS * all_, cols), BF16)],
        where, resolved_residue_mask, *mixed, stream, gate, out_t, proj_t, present,
        smem=(0, 1),
        scratch=[
            ((rows, NEAR, width // NEAR, cols), F32),
            ((tall, cols), F32),
            ((tall, cols), F32),
        ],
    )
    stream, gate, theirs = made[0], made[1], made[6]
    came = split_exchange(with_partner(made[2:6], theirs))
    mine, theirs = run(
        mix_cols_kernel,
        [((OPS, 2 * all_, cols), F32), ((OPS, 2 * all_, cols), BF16)],
        where, *came,
        smem=(0,),
        scratch=[
            ((2 * OPS, width // (2 * OPS), rows, cols), F32),
            ((2 * OPS, width // (2 * OPS), rows, cols), F32),
            ((2 * tall, cols), F32),
        ],
    )
    mixed = run(sum_kernel, [((2 * all_, cols), BF16)] * OPS, mine, core_permute(theirs))
    mixed = split_exchange(mixed, SMALL_SPLIT)
    other = core_permute(run(pick_kernel, [((OPS * all_, cols), BF16)], *mixed)[0])
    return run(
        final_kernel,
        [((rows, cols, width), BF16)],
        where, *mixed, other, stream, gate, out_t,
        smem=(0,),
        scratch=[((rows, 2 * OPS, width // (2 * OPS), cols), F32)],
    )[0]


def fits_chips(mesh):
    return mesh.shape["narrow"] == 1 and mesh.shape["wide"] == 16


def solution(mesh):
    per_device = per_device_chips if fits_chips(mesh) else per_device_general
    return jax.shard_map(
        per_device,
        mesh=mesh,
        in_specs=(
            P(("grp", "wide"), "narrow", None),
            P("grp", "wide", None),
            P("grp"),
            P("grp"),
            P("grp", "wide"),
            P(),
            P(),
            P(),
            P(),
            P(),
        ),
        out_specs=P(("grp", "wide"), "narrow", None),
        check_vma=False,
    )
```
